32 devices in a mesh: section: 2 (over x), expert: 4 (over y, core), dp: 4 (over z).
Axes of the slice: x: 2, y: 2, z: 4, core: 2. Of those that a mesh axis runs over, the one named last changes fastest.
Arguments:
- layer_input: bfloat16 [2, 16, 128, 1536], P(None, ('expert', 'dp')), may hold values from -6 to 6
- cotangent: bfloat16 [2, 16, 128, 1536], P(None, ('expert', 'dp')), may hold values from -6 to 6
- segments: int32 [2, 16, 128], P(None, ('expert', 'dp')), may hold values from 0 to 3, never falling along the last dimension, each value on 1 to 64 neighbouring positions
- routes: int32 [2, 2, 16, 128, 4], P('section', None, ('expert', 'dp')), may hold values from 0 to 7, all different within a row; in each aligned block of 128 rows (0 to 127, 128 to 255, ..., all dimensions but the last counted through in order) at most 80 rows name the same one
- attn_gain: bfloat16 [2, 1536], P('section', ('expert', 'dp')), may hold values from 0.25 to 1.75
- w_qkv: bfloat16 [2, 1536, 2048], P('section', ('expert', 'dp')), may hold values from -0.15625 to 0.15625
- w_out: bfloat16 [2, 1536, 1536], P('section', ('expert', 'dp')), may hold values from -0.625 to 0.625
- moe_gain: bfloat16 [2, 1536], P('section', ('expert', 'dp')), may hold values from 0.25 to 1.75
- w_router: bfloat16 [2, 1536, 8], P('section', ('expert', 'dp')), may hold values from -0.078125 to 0.078125
- w_gate: bfloat16 [2, 8, 1536, 768], P('section', 'expert'), may hold values from -0.15625 to 0.15625
- w_up: bfloat16 [2, 8, 1536, 768], P('section', 'expert'), may hold values from -0.15625 to 0.15625
- w_down: bfloat16 [2, 8, 768, 1536], P('section', 'expert'), may hold values from -0.625 to 0.625
Outputs:
- section_out: bfloat16 [2, 2, 16, 128, 1536], P('section', None, ('expert', 'dp'))
- grad_in: bfloat16 [2, 2, 16, 128, 1536], P('section', None, ('expert', 'dp'))
- grad_attn_gain: float32 [2, 1536], P('section', ('expert', 'dp'))
- grad_qkv: float32 [2, 1536, 2048], P('section', ('expert', 'dp'))
- grad_out: float32 [2, 1536, 1536], P('section', ('expert', 'dp'))
- grad_moe_gain: float32 [2, 1536], P('section', ('expert', 'dp'))
- grad_router: float32 [2, 1536, 8], P('section', ('expert', 'dp'))
- grad_gate: float32 [2, 8, 1536, 768], P('section', 'expert', 'dp')
- grad_up: float32 [2, 8, 1536, 768], P('section', 'expert', 'dp')
- grad_down: float32 [2, 8, 768, 1536], P('section', 'expert', 'dp')
The draws below stay inside these ranges and needn't reach their ends.
Inputs may be any that keep to these rules, and one draw needn't show every extreme that they name: `segments`: within each pack the numbers start at 0, never fall, reach 3, and each is held by at most half of 128 positions. `routes`: A row names 4 different experts. In each aligned block of 128 rows (one pack of one micro-batch of one section) no expert is named more than 80 times, a bound that some block reaches.
All inputs are finite; a program needn't handle non-finite values.
Results may differ from the reference program's by a relative error of at most 0.024.
Values may be sent and summed in bfloat16 or wider, within the bound.
A program may use at most 256 MiB of HBM per device.

```python
import math
import jax
import jax.numpy as jnp
import numpy as np
from jax import lax

D = 1536
QUERY_HEADS = 12
KEY_VALUE_HEADS = 2
HEAD_WIDTH = 128
H = 768
TOP = 4
MB = 2
SEGS = 4
PACK_TOKENS = 128
SECTIONS = 2
PACKS = 16
EXPERTS = 8
QD = 1536
QKV = 2048
CAP = 80


def levels(key, dims, shards, least, largest):
    factor_of, own = 1.0, jax.random.fold_in(key, 6)
    for dim, shards_of in shards:
        heights = jnp.exp(jax.random.uniform(jax.random.fold_in(own, dim), (shards_of,), jnp.float32, least / len(shards), largest / len(shards)))
        factor_of = factor_of * jnp.repeat(heights, dims[dim] // shards_of).reshape([-1 if axis == dim else 1 for axis in range(len(dims))])
    return factor_of


def profile(count, total, limit, lean):
    loads = [(1 << 20) // math.isqrt(standing ** lean) + 1 for standing in range(2, count + 1)]
    surplus, counts = total - limit - (count - 1), [1] * (count - 1)
    while surplus > 0:
        movable = [i for i in range(count - 1) if counts[i] < limit]
        mass, budget = sum([loads[i] for i in movable]), surplus
        for i in movable:
            extra = min(limit - counts[i], max(1, budget * loads[i] // mass), surplus)
            counts[i] = counts[i] + extra
            surplus = surplus - extra
    return np.array([limit] + counts)


def ragged_sizes(rng, amount, total, reach, lean):
    if amount == 2:
        one = jax.random.randint(rng, (), max(1, total - reach), min(reach, total - 1) + 1)
        return jnp.stack([one, total - one])
    sizes = jnp.asarray(profile(amount, total, reach, lean), jnp.int32)
    couples = (amount - 1) // 2
    donor, taker = sizes[1:1 + 2 * couples:2], sizes[2:2 + 2 * couples:2]
    margin = jnp.minimum(donor - 1, reach - taker)
    shifted = jax.random.randint(jax.random.fold_in(rng, 1), (couples,), 0, 1 << 20) % (margin + 1)
    sizes = sizes.at[1:1 + 2 * couples:2].set(donor - shifted).at[2:2 + 2 * couples:2].set(taker + shifted)
    return sizes[jax.random.permutation(jax.random.fold_in(rng, 2), amount)]


def deal_out(key, own, number, rows, count, top, bound, lean):
    sequence = jax.random.permutation(key, count)
    heavy_load, ordinary = load_shares(count, rows * top, bound, lean, True), load_shares(count, rows * top, bound, lean, False)
    places = jnp.arange(count)

    def named(lengths, offset_by):
        used = int((lengths > 0).sum())
        fixed = max(1, used // 4)
        shifted = fixed + (places - fixed + offset_by * (used - fixed)) % max(1, count - fixed)
        return jnp.zeros((count,), jnp.int32).at[sequence[jnp.where(places < fixed, places, shifted)]].set(jnp.asarray(lengths, jnp.int32))

    lengths = jnp.where(number % 4 == 0, named(heavy_load, number // 4), named(ordinary, number - number // 4 - 1))
    mixed = jax.random.permutation(jax.random.fold_in(own, 3), count)
    donor, receiver = mixed[0:count // 2 * 2:2], mixed[1:count // 2 * 2:2]
    margin = jnp.minimum(lengths[donor] - 1, bound - lengths[receiver]) // 2
    margin = jnp.where((donor == sequence[0]) | (receiver == sequence[0]) | (lengths[receiver] == 0), 0, jnp.maximum(margin, 0))
    shifted = jax.random.randint(jax.random.fold_in(own, 4), (count // 2,), 0, 1 << 20) % (margin + 1)
    lengths = lengths.at[donor].add(-shifted).at[receiver].add(shifted)
    labels = jnp.searchsorted(jnp.cumsum(lengths), jnp.arange(rows * top), side="right").astype(jnp.int32)
    grid = labels.reshape(top, rows).T
    grid = grid[jax.random.permutation(jax.random.fold_in(own, 1), rows)]
    offset_by = jax.random.randint(jax.random.fold_in(own, 2), (rows, 1), 0, top)
    return jnp.take_along_axis(grid, (jnp.arange(top)[None, :] + offset_by) % top, axis=1)


def load_shares(amount, total, bound, lean, full):
    weights = [(1 << 20) // math.isqrt(grade ** lean) + 1 for grade in range(1, amount + 1)]
    largest = bound if full else min(bound, max(-(-total // amount), total * weights[0] // sum(weights)))
    least = 1 if total - largest >= amount - 1 else 0
    given, spare = [largest] + [least] * (amount - 1), total - largest - least * (amount - 1)
    while spare > 0:
        movable = [i for i in range(1, amount) if given[i] < largest] or [i for i in range(1, amount) if given[i] < bound]
        pool, left = sum([weights[i] for i in movable]), spare
        for i in movable:
            extra = min(bound - given[i], max(1, left * weights[i] // pool), spare)
            given[i] = given[i] + extra
            spare = spare - extra
    return np.array(given)


def normal_values(stream_key, extent, deviation, bound, cuts=(), kind=jnp.bfloat16):
    loudness = levels(stream_key, extent, cuts, -0.22, 0.18) if cuts else 1.0
    array = jax.random.normal(stream_key, extent, jnp.float32) * deviation * loudness
    return jnp.minimum(jnp.maximum(array, -bound), bound).astype(kind)


def setup_inputs(seed: int = 0) -> dict:
    key_of = jax.random.split(jax.random.key(seed), 13)
    layer_input = normal_values(key_of[0], (MB, PACKS, PACK_TOKENS, D), 1.0, 6.0, ((1, 16),))
    cotangent = normal_values(key_of[1], (MB, PACKS, PACK_TOKENS, D), 1.0, 6.0, ((1, 16),))
    segments = jax.vmap(lambda own: jnp.searchsorted(jnp.cumsum(ragged_sizes(own, SEGS, PACK_TOKENS, PACK_TOKENS // 2, 1)), jnp.arange(PACK_TOKENS), side="right"))(jax.random.split(key_of[2], MB * PACKS)).reshape((MB, PACKS, PACK_TOKENS)).astype(jnp.int32)
    routes_keys = jax.random.split(jax.random.fold_in(key_of[3], 1), SECTIONS * MB * PACKS * PACK_TOKENS // PACK_TOKENS)
    routes_turns = jax.random.permutation(jax.random.fold_in(key_of[3], 3), SECTIONS * MB * PACKS * PACK_TOKENS // PACK_TOKENS)
    routes = jax.vmap(lambda own, number: deal_out(jax.random.fold_in(key_of[3], 2), own, number, PACK_TOKENS, EXPERTS, TOP, CAP, 1))(routes_keys, routes_turns).reshape((SECTIONS, MB, PACKS, PACK_TOKENS, TOP))
    attn_gain = jnp.clip(1.0 + 0.15 * jax.random.normal(key_of[4], (SECTIONS, D), jnp.float32), 0.25, 1.75).astype(jnp.bfloat16)
    w_qkv = normal_values(key_of[5], (SECTIONS, D, QKV), D ** -0.5, 0.15625, ((0, 2), (1, 16)))
    w_out = normal_values(key_of[6], (SECTIONS, QD, D), (QD // 16) ** -0.5, 0.625, ((0, 2), (1, 16)))
    moe_gain = jnp.clip(1.0 + 0.15 * jax.random.normal(key_of[7], (SECTIONS, D), jnp.float32), 0.25, 1.75).astype(jnp.bfloat16)
    w_router = normal_values(key_of[8], (SECTIONS, D, EXPERTS), (0.5 * D ** -0.5), 0.078125, ((0, 2), (1, 16)))
    w_gate = normal_values(key_of[9], (SECTIONS, EXPERTS, D, H), D ** -0.5, 0.15625, ((0, 2), (1, 4)))
    w_up = normal_values(key_of[10], (SECTIONS, EXPERTS, D, H), D ** -0.5, 0.15625, ((0, 2), (1, 4)))
    w_down = normal_values(key_of[11], (SECTIONS, EXPERTS, H, D), (H // 8) ** -0.5, 0.625, ((0, 2), (1, 4)))
    return {"layer_input": layer_input, "cotangent": cotangent, "segments": segments, "routes": routes, "attn_gain": attn_gain, "w_qkv": w_qkv, "w_out": w_out, "moe_gain": moe_gain, "w_router": w_router, "w_gate": w_gate, "w_up": w_up, "w_down": w_down}


EPS = 1e-06
THETA = 1000000.0
HIGHEST = lax.Precision.HIGHEST
NEGATIVE = -1e+30

@jax.custom_vjp
def lower_bound(v):
    return lax.optimization_barrier(v.astype(jnp.bfloat16)).astype(jnp.float32)

@jax.custom_vjp
def low_back(v):
    return v

def low_keep(v):
    return (lower_bound(v), None)

def low_pass(kept, grad):
    return (grad,)

def back_keep(v):
    return (v, None)

def back_low(kept, grad):
    return (lower_bound(grad),)
lower_bound.defvjp(low_keep, low_pass)
low_back.defvjp(back_keep, back_low)

def rms_scale(hidden, gain):
    return hidden * lax.rsqrt(lax.optimization_barrier(jnp.mean(hidden * hidden, -1, keepdims=True)) + EPS) * gain

def rope_tables():
    places = jnp.arange(PACK_TOKENS, dtype=jnp.float32)
    inverse = THETA ** (-2.0 * jnp.arange(HEAD_WIDTH // 2, dtype=jnp.float32) / HEAD_WIDTH)
    angles = places[:, None] * inverse[None, :]
    return (jnp.cos(angles), jnp.sin(angles))

def apply_rotary(vector, cosine_table, sine_table):
    half_size = vector.shape[-1] // 2
    first_half = vector[..., :half_size]
    second_half = vector[..., half_size:]
    return jnp.concatenate([first_half * cosine_table - second_half * sine_table, second_half * cosine_table + first_half * sine_table], -1)

def attend(w_qkv_s, w_out_s, normed, segs):
    token_count = normed.shape[0]
    query_width = QUERY_HEADS * HEAD_WIDTH
    key_width = KEY_VALUE_HEADS * HEAD_WIDTH
    query_group = QUERY_HEADS // KEY_VALUE_HEADS
    cosine_table, sine_table = rope_tables()
    mixed_heads = low_back(jnp.einsum('btd,de->bte', normed, w_qkv_s, precision=HIGHEST))
    query_matrix = lower_bound(apply_rotary(mixed_heads[..., :query_width].reshape(token_count, PACK_TOKENS, KEY_VALUE_HEADS, query_group, HEAD_WIDTH), cosine_table[:, None, None, :], sine_table[:, None, None, :]))
    key_matrix = lower_bound(apply_rotary(mixed_heads[..., query_width:query_width + key_width].reshape(token_count, PACK_TOKENS, KEY_VALUE_HEADS, HEAD_WIDTH), cosine_table[:, None, :], sine_table[:, None, :]))
    value_matrix = lower_bound(mixed_heads[..., query_width + key_width:].reshape(token_count, PACK_TOKENS, KEY_VALUE_HEADS, HEAD_WIDTH))
    scores = low_back(jnp.einsum('btgih,bsgh->bgits', query_matrix, key_matrix, precision=HIGHEST) * HEAD_WIDTH ** (-0.5))
    same_doc = segs[:, :, None] == segs[:, None, :]
    order = jnp.arange(PACK_TOKENS)
    allowed = (same_doc & (order[:, None] >= order[None, :])[None])[:, None, None]
    shares = lower_bound(jax.nn.softmax(jnp.where(allowed, scores, NEGATIVE), -1))
    context = jnp.einsum('bgits,bsgh->btgih', shares, value_matrix, precision=HIGHEST).reshape(token_count, PACK_TOKENS, query_width)
    context = lower_bound(low_back(context))
    return low_back(jnp.einsum('bte,ed->btd', context, w_out_s, precision=HIGHEST))

def layer(params, hidden, segs, route):
    gain_attn, w_qkv_s, w_out_s, gain_moe, router, gate_w, up_w, down_w = params
    token_count = hidden.shape[0]
    normed = lower_bound(rms_scale(hidden, gain_attn))
    group_size = math.gcd(token_count, max(1, 4096 // PACK_TOKENS))

    def attend_group(packed):
        return attend(w_qkv_s, w_out_s, packed[0], packed[1])
    branch = lax.map(jax.checkpoint(attend_group), (normed.reshape(token_count // group_size, group_size, PACK_TOKENS, D), segs.reshape(token_count // group_size, group_size, PACK_TOKENS)))
    after_attn = hidden + branch.reshape(token_count, PACK_TOKENS, D)
    moe_in = lower_bound(rms_scale(after_attn, gain_moe)).reshape(token_count * PACK_TOKENS, D)
    logits = jnp.dot(moe_in, router, precision=HIGHEST)
    chosen = jnp.any(route[:, :, None] == jnp.arange(EXPERTS)[None, None, :], 1)
    gates = jax.nn.softmax(jnp.where(chosen, logits, NEGATIVE), -1)

    def expert_step(total, packed):
        gate_e, up_e, down_e, weight_e = packed
        copy_in = low_back(moe_in)
        gate_proj = low_back(jnp.dot(copy_in, gate_e, precision=HIGHEST))
        up_proj = low_back(jnp.dot(copy_in, up_e, precision=HIGHEST))
        inner = lower_bound(jax.nn.gelu(gate_proj, approximate=True) * up_proj)
        result = lower_bound(low_back(jnp.dot(inner, down_e, precision=HIGHEST)))
        return (total + weight_e[:, None] * result, None)
    start = jnp.zeros((token_count * PACK_TOKENS, D), jnp.float32)
    mixture, _ = lax.scan(jax.checkpoint(expert_step), start, (gate_w, up_w, down_w, gates.T))
    return after_attn + mixture.reshape(token_count, PACK_TOKENS, D)

def reference(layer_input, cotangent, segments, routes, attn_gain, w_qkv, w_out, moe_gain, w_router, w_gate, w_up, w_down):
    token_count = MB * PACKS
    first_in = layer_input.astype(jnp.float32).reshape(token_count, PACK_TOKENS, D)
    segs = segments.reshape(token_count, PACK_TOKENS)

    def params(section_no):
        return (attn_gain[section_no].astype(jnp.float32), w_qkv[section_no].astype(jnp.float32), w_out[section_no].astype(jnp.float32), moe_gain[section_no].astype(jnp.float32), w_router[section_no].astype(jnp.float32), w_gate[section_no].astype(jnp.float32), w_up[section_no].astype(jnp.float32), w_down[section_no].astype(jnp.float32))

    def section_zero(weights, hidden):
        return layer(weights, hidden, segs, routes[0].reshape(-1, TOP))

    def section_one(weights, hidden):
        return layer(weights, hidden, segs, routes[1].reshape(-1, TOP))
    out_zero, pull_zero = jax.vjp(section_zero, params(0), first_in)
    out_zero_b = out_zero.astype(jnp.bfloat16)
    out_one, pull_one = jax.vjp(section_one, params(1), out_zero_b.astype(jnp.float32))
    grads_one, grad_mid = pull_one(cotangent.astype(jnp.float32).reshape(token_count, PACK_TOKENS, D))
    grad_mid_b = grad_mid.astype(jnp.bfloat16)
    grads_zero, grad_first = pull_zero(grad_mid_b.astype(jnp.float32))
    shape = (MB, PACKS, PACK_TOKENS, D)
    section_out = jnp.stack([out_zero_b.reshape(shape), out_one.astype(jnp.bfloat16).reshape(shape)])
    grad_in = jnp.stack([grad_first.astype(jnp.bfloat16).reshape(shape), grad_mid_b.reshape(shape)])
    stacked = [jnp.stack([left, right]) for left, right in zip(grads_zero, grads_one)]
    return (section_out, grad_in, stacked[0], stacked[1], stacked[2], stacked[3], stacked[4], stacked[5], stacked[6], stacked[7])
```

```python
import functools

import jax
import jax.numpy as jnp
import numpy as np
from jax import lax
from jax.experimental import pallas as pl
from jax.experimental.pallas import tpu as pltpu
from jax.sharding import PartitionSpec as P

HEAD = 128
QUERY_HEADS = 12
KEY_VALUE_HEADS = 2
GROUP = QUERY_HEADS // KEY_VALUE_HEADS
EPS = 1e-06
THETA = 1000000.0
NEGATIVE = -1e30
SCALE = HEAD ** (-0.5)
ROUTER_ROWS = 16
SMALL_ROWS = 32
CHUNKS = 2
MESH = pl.DeviceIdType.MESH
F32 = jnp.float32
BF16 = jnp.bfloat16
GELU_C = float(np.sqrt(2.0 / np.pi))
GELU_A = 0.044715


def dot(a, b):
    return jnp.dot(a, b, preferred_element_type=F32)


def dot_nt(a, b):
    return lax.dot_general(a, b, (((1,), (1,)), ((), ())), preferred_element_type=F32)


def dot_tn(a, b):
    return lax.dot_general(a, b, (((0,), (0,)), ((), ())), preferred_element_type=F32)


def rotary_tables(tokens):
    places = np.arange(tokens, dtype=np.float64)
    inverse = THETA ** (-2.0 * np.arange(HEAD // 2, dtype=np.float64) / HEAD)
    angles = places[:, None] * inverse[None, :]
    cosine, sine = np.cos(angles), np.sin(angles)
    return (
        jnp.asarray(np.concatenate([cosine, cosine], 1), F32),
        jnp.asarray(np.concatenate([-sine, sine], 1), F32),
    )


def mask_bias(col, row):
    tokens = row.shape[1]
    ti = lax.broadcasted_iota(jnp.int32, (tokens, tokens), 0)
    ui = lax.broadcasted_iota(jnp.int32, (tokens, tokens), 1)
    return jnp.where((col == row) & (ui <= ti), 0.0, NEGATIVE).astype(F32)


def heads_of(value, first, count):
    return jnp.concatenate(
        [value[:, (first + i) * HEAD : (first + i + 1) * HEAD] for i in range(count)], 0
    )


def attention_shares(q6, k, bias6):
    scores = dot_nt(q6, k) * SCALE + bias6
    top = jnp.max(scores, -1, keepdims=True)
    raised = jnp.exp(scores - top)
    return raised / jnp.sum(raised, -1, keepdims=True)


class Place:
    def __init__(self, ny):
        self.ny = ny
        self.s = lax.axis_index("section")
        self.e = lax.axis_index("expert")
        self.d = lax.axis_index("dp")
        self.y = lax.div(self.e, 2)
        self.c = lax.rem(self.e, 2)
        self.core = (self.s, self.y * 2 + 1 - self.c, self.d)
        self.x = (1 - self.s, self.e, self.d)

    def ahead(self, r):
        return (self.s, lax.rem(self.y + r, self.ny) * 2 + self.c, self.d)

    def behind(self, r):
        return (self.s, lax.rem(self.y + self.ny - r, self.ny) * 2 + self.c, self.d)

    def pack(self, r, other):
        core = 1 - self.c if other else self.c
        return lax.rem(self.y + r, self.ny) * 2 + core

    def greet(self):
        barrier = pltpu.get_barrier_semaphore()
        partners = [self.core, self.x] + [self.ahead(r) for r in range(1, self.ny)]
        for partner in partners:
            pl.semaphore_signal(barrier, inc=1, device_id=partner, device_id_type=MESH)
        pl.semaphore_wait(barrier, len(partners))


def remote(src, dst, send, recv, device):
    return pltpu.make_async_remote_copy(
        src_ref=src, dst_ref=dst, send_sem=send, recv_sem=recv, device_id=device, device_id_type=MESH
    )


class Exchange:
    def __init__(self, place, rows_ref, retl, retc, rety, sendl, sendc, sendy, sems):
        self.place = place
        self.rows_ref = rows_ref
        self.retl, self.retc, self.rety = retl, retc, rety
        self.sendl, self.sendc, self.sendy = sendl, sendc, sendy
        self.sems = sems
        self.tokens = rows_ref.shape[2]
        self.span = self.tokens // CHUNKS

    def rows(self, q):
        return pl.ds(q * self.span, self.span)

    def core_own(self):
        g = self.place
        return remote(
            self.rows_ref.at[0, 0], self.rows_ref.at[0, 1], self.sems.cs.at[0, 0], self.sems.cr.at[0, 0], g.core
        )

    def y_own(self, r, q):
        g = self.place
        return remote(
            self.rows_ref.at[0, 0, self.rows(q)],
            self.rows_ref.at[r, 0, self.rows(q)],
            self.sems.ys.at[r, q],
            self.sems.yr.at[r, q],
            g.behind(r),
        )

    def forward(self, r, q):
        g = self.place
        return remote(
            self.rows_ref.at[r, 0, self.rows(q)],
            self.rows_ref.at[r, 1, self.rows(q)],
            self.sems.cs.at[r, q],
            self.sems.cr.at[r, q],
            g.core,
        )

    def back_local(self):
        return remote(self.sendl, self.retl, self.sems.bs.at[0, 0], self.sems.br.at[0, 0], self.place.core)

    def back_core(self, r, q):
        return remote(
            self.sendc.at[r, self.rows(q)],
            self.retc.at[r, self.rows(q)],
            self.sems.bs.at[r, q],
            self.sems.br.at[r, q],
            self.place.core,
        )

    def back_y(self, r, q):
        g = self.place
        return remote(
            self.sendy.at[r, self.rows(q)],
            self.rety.at[g.ny - r, self.rows(q)],
            self.sems.zs.at[r, q],
            self.sems.zr.at[g.ny - r, q],
            g.ahead(r),
        )

    def back_y_arrival(self, r, q):
        g = self.place
        return remote(
            self.sendy.at[r, self.rows(q)],
            self.rety.at[r, self.rows(q)],
            self.sems.zs.at[r, q],
            self.sems.zr.at[r, q],
            g.ahead(r),
        )

    def send_own(self):
        for q in range(CHUNKS):
            for r in range(1, self.place.ny):
                self.y_own(r, q).start()
        self.core_own().start()

    def run(self, local_block, remote_block):
        ny = self.place.ny
        items = [(r, q) for q in range(CHUNKS) for r in range(1, ny)]
        self.core_own().wait_recv()
        local_block()
        self.back_local().start()
        if items:
            self.y_own(*items[0]).wait_recv()
            self.forward(*items[0]).start()
        for i, (r, q) in enumerate(items):
            self.forward(r, q).wait_recv()
            own = remote_block(r, q)
            self.back_core(r, q).start()
            if i + 1 < len(items):
                self.y_own(*items[i + 1]).wait_recv()
                self.forward(*items[i + 1]).start()
            self.back_core(r, q).wait_recv()
            here = self.rows(q)
            self.sendy[r, here, :] = (own() + self.retc[r, here, :].astype(F32)).astype(BF16)
            self.back_y(r, q).start()
        self.back_local().wait_recv()

    def arrived(self, q):
        for r in range(1, self.place.ny):
            self.back_y_arrival(r, q).wait_recv()

    def finish(self):
        ny = self.place.ny
        self.core_own().wait_send()
        self.back_local().wait_send()
        for q in range(CHUNKS):
            for r in range(1, ny):
                self.y_own(r, q).wait_send()
                self.forward(r, q).wait_send()
                self.back_core(r, q).wait_send()
                self.back_y(r, q).wait_send()


class Sems:
    def __init__(self, refs, m):
        self.cs, self.cr, self.ys, self.yr, self.bs, self.br, self.zs, self.zr = [ref.at[m] for ref in refs]


def sem_shapes(micro, ny):
    return [pltpu.SemaphoreType.DMA((micro, ny, CHUNKS)) for _ in range(8)]


def chosen_gates(logits_t, route):
    experts = lax.broadcasted_iota(jnp.int32, logits_t.shape, 0)
    chosen = route[0:1, :] == experts
    for k in range(1, route.shape[0]):
        chosen = chosen | (route[k : k + 1, :] == experts)
    masked = jnp.where(chosen, logits_t, NEGATIVE)
    raised = jnp.where(chosen, jnp.exp(masked - jnp.max(masked, 0, keepdims=True)), 0.0)
    return raised / jnp.sum(raised, 0, keepdims=True)


def gate_lanes(gates_t, expert):
    rows = lax.broadcasted_iota(jnp.int32, gates_t.shape, 0)
    one = jnp.sum(jnp.where(rows == expert, gates_t, 0.0), 0, keepdims=True)
    return jnp.transpose(jnp.broadcast_to(one, (128, one.shape[1])))


def widen(lanes, width):
    return jnp.concatenate([lanes] * (width // 128), 1)


def forward_kernel(
    ny, sections,
    x_ref, segc_ref, segr_ref, route_ref, small_ref, cos_ref, sin_ref,
    wqkv_h, wout_h, wg_h, wu_h, wd_h,
    out_ref, hin_ref, h1_ref, qkv_ref, ob_ref, xm_ref, gates_ref,
    wqkv, wout, wg, wu, wd, hid, accl, accr, gl, retl, retc, rety, sendl, sendc, sendy,
    wsem, xs, xr, *sem_refs,
):
    micro, tokens, width = x_ref.shape
    hidden = wg.shape[2]
    span = tokens // CHUNKS
    loads = [
        pltpu.make_async_copy(src, dst, wsem.at[i])
        for i, (src, dst) in enumerate([(wqkv_h, wqkv), (wout_h, wout), (wg_h, wg), (wu_h, wu), (wd_h, wd)])
    ]
    for load in loads:
        load.start()
    g = Place(ny)
    g.greet()
    gain_a = small_ref[ROUTER_ROWS : ROUTER_ROWS + 1, :].astype(F32)
    gain_m = small_ref[ROUTER_ROWS + 1 : ROUTER_ROWS + 2, :].astype(F32)
    cos, sin = cos_ref[...], sin_ref[...]

    def hop(m, q):
        here = pl.ds(q * span, span)
        return remote(out_ref.at[m, here], hin_ref.at[m, here], xs.at[m, q], xr.at[m, q], g.x)

    def experts(rows, lanes, keep):
        count = rows.shape[0]
        for j in range(2):
            for n in range(hidden // 256):
                cols = slice(n * 256, (n + 1) * 256)
                a = dot(rows, wg[j, :, cols])
                b = dot(rows, wu[j, :, cols])
                act = 0.5 * a * (1.0 + jnp.tanh(GELU_C * (a + GELU_A * a * a * a)))
                hid[j, 0:count, cols] = (act * b).astype(BF16)
        for n in range(width // 512):
            cols = slice(n * 512, (n + 1) * 512)
            total = None
            for j in range(2):
                eo = dot(hid[j, 0:count, :], wd[j, :, cols]).astype(BF16).astype(F32)
                term = widen(lanes[j], 512) * eo
                total = term if total is None else total + term
            keep(cols, total)

    def body(m, carry):
        @pl.when(g.s == 0)
        def _():
            hin_ref[m] = x_ref[m]

        @pl.when(g.s > 0)
        def _():
            for q in range(CHUNKS):
                hop(m, q).wait_recv()

        h = hin_ref[m].astype(F32)
        xa = (h * lax.rsqrt(jnp.mean(h * h, -1, keepdims=True) + EPS) * gain_a).astype(BF16)

        @pl.when(m == 0)
        def _():
            loads[0].wait()

        turned = QUERY_HEADS + KEY_VALUE_HEADS
        for i in range(wqkv.shape[1] // 256):
            mixed = dot(xa, wqkv[:, i * 256 : (i + 1) * 256])
            for half in range(2):
                head = 2 * i + half
                part = mixed[:, half * HEAD : (half + 1) * HEAD]
                if head < turned:
                    part = part * cos + pltpu.roll(part, HEAD // 2, 1) * sin
                qkv_ref[m, :, head * HEAD : (head + 1) * HEAD] = part.astype(BF16)
        bias = mask_bias(segc_ref[m], segr_ref[m])
        bias6 = jnp.concatenate([bias] * GROUP, 0)
        qkv = qkv_ref.at[m]
        for kv in range(KEY_VALUE_HEADS):
            q6 = heads_of(qkv, kv * GROUP, GROUP)
            k = heads_of(qkv, QUERY_HEADS + kv, 1)
            v = heads_of(qkv, turned + kv, 1)
            shares = attention_shares(q6, k, bias6).astype(BF16)
            o6 = dot(shares, v).astype(BF16)
            for i in range(GROUP):
                head = kv * GROUP + i
                ob_ref[m, :, head * HEAD : (head + 1) * HEAD] = o6[i * tokens : (i + 1) * tokens]

        @pl.when(m == 0)
        def _():
            loads[1].wait()

        ob = ob_ref[m]
        for n in range(width // 512):
            cols = slice(n * 512, (n + 1) * 512)
            h1_ref[m, :, cols] = hin_ref[m, :, cols].astype(F32) + dot(ob, wout[:, cols])
        h1 = h1_ref[m]
        xm_ref[m, 0, 0] = (h1 * lax.rsqrt(jnp.mean(h1 * h1, -1, keepdims=True) + EPS) * gain_m).astype(BF16)

        ex = Exchange(g, xm_ref.at[m], retl, retc, rety, sendl, sendc, sendy, Sems(sem_refs, m))
        ex.send_own()

        @pl.when(m == 0)
        def _():
            for load in loads[2:]:
                load.wait()

        def gates_for(r, other, here):
            rows = xm_ref[m, r, other, here, :]
            logits_t = dot_nt(small_ref[0:ROUTER_ROWS, :], rows)
            gates_t = chosen_gates(logits_t, route_ref[g.pack(r, other), m][:, here])
            return gates_t

        def lanes_of(blocks):
            return [
                jnp.concatenate([gate_lanes(gates_t, 2 * g.e + j) for gates_t in blocks], 0) for j in range(2)
            ]

        full = slice(0, tokens)

        def local_block():
            blocks = []
            for other in range(2):
                gates_t = gates_for(0, other, full)
                gates_ref[m, 0, other] = gates_t
                blocks.append(gates_t)

            def keep(cols, total):
                accl[:, cols] = total[0:tokens]
                sendl[:, cols] = total[tokens:].astype(BF16)

            experts(xm_ref[m, 0].reshape(2 * tokens, width), lanes_of(blocks), keep)

        def remote_block(r, q):
            here = slice(q * span, (q + 1) * span)
            blocks = []
            for other in range(2):
                gates_t = gates_for(r, other, here)
                gates_ref[m, r, other, :, here] = gates_t
                blocks.append(jnp.concatenate([gates_t] * (128 // span), 1))
            lanes = [
                jnp.concatenate([gate_lanes(gates_t, 2 * g.e + j)[0:span] for gates_t in blocks], 0)
                for j in range(2)
            ]

            def keep(cols, total):
                accr[:, cols] = total[0:span]
                sendc[r, here, cols] = total[span:].astype(BF16)

            experts(xm_ref[m, r, :, here, :].reshape(2 * span, width), lanes, keep)
            return lambda: accr[...]

        ex.run(local_block, remote_block)
        for q in range(CHUNKS):
            here = slice(q * span, (q + 1) * span)
            ex.arrived(q)
            total = h1_ref[m, here, :] + accl[here, :] + retl[here, :].astype(F32)
            for r in range(1, ny):
                total = total + rety[r, here, :].astype(F32)
            out_ref[m, here, :] = total.astype(BF16)

            @pl.when(g.s < sections - 1)
            def _():
                hop(m, q).start()

        ex.finish()
        return carry

    lax.fori_loop(0, micro, body, 0)

    @pl.when(g.s < sections - 1)
    def _():
        for m in range(micro):
            for q in range(CHUNKS):
                hop(m, q).wait_send()


def backward_kernel(
    ny, sections,
    cot_ref, segc_ref, segr_ref, small_ref, cos_ref, sin_ref,
    hin_ref, h1_ref, qkv_ref, gates_ref,
    xm_h, wqkv_h, wout_h, wg_h, wu_h, wd_h,
    gin_ref, grows_ref, xa_ref, dqkv_ref, dattn_ref, gsmall_ref,
    wqkv, wout, wg, wu, wd, xm_s, hid, act_s, slope_s, da_s, db_s, accl, accr, dh1_s, n_s,
    retl, retc, rety, sendl, sendc, sendy,
    wsem, xmsem, xs, xr, *sem_refs,
):
    micro, tokens, width = cot_ref.shape
    hidden = wg.shape[2]
    span = tokens // CHUNKS
    loads = [
        pltpu.make_async_copy(src, dst, wsem.at[i])
        for i, (src, dst) in enumerate([(wg_h, wg), (wu_h, wu), (wd_h, wd), (wout_h, wout), (wqkv_h, wqkv)])
    ]
    for load in loads:
        load.start()
    g = Place(ny)
    g.greet()
    gain_a = small_ref[ROUTER_ROWS : ROUTER_ROWS + 1, :].astype(F32)
    gain_m = small_ref[ROUTER_ROWS + 1 : ROUTER_ROWS + 2, :].astype(F32)
    cos, sin = cos_ref[...], sin_ref[...]
    gsmall_ref[...] = jnp.zeros_like(gsmall_ref)

    def hop(m, q):
        here = pl.ds(q * span, span)
        return remote(gin_ref.at[m, here], grows_ref.at[m, 0, 0, here], xs.at[m, q], xr.at[m, q], g.x)

    def body(m, carry):
        load_xm = pltpu.make_async_copy(xm_h.at[m], xm_s, xmsem)
        load_xm.start()

        @pl.when(g.s == sections - 1)
        def _():
            grows_ref[m, 0, 0] = cot_ref[m]

        @pl.when(g.s < sections - 1)
        def _():
            for q in range(CHUNKS):
                hop(m, q).wait_recv()

        ex = Exchange(g, grows_ref.at[m], retl, retc, rety, sendl, sendc, sendy, Sems(sem_refs, m))
        ex.send_own()

        @pl.when(m == 0)
        def _():
            for load in loads[:3]:
                load.wait()

        load_xm.wait()

        def again(r, _):
            rows = xm_s[r].reshape(2 * tokens, width)
            for j in range(2):
                for n in range(hidden // 256):
                    cols = slice(n * 256, (n + 1) * 256)
                    a = dot(rows, wg[j, :, cols])
                    b = dot(rows, wu[j, :, cols])
                    square = a * a
                    th = jnp.tanh(GELU_C * (a + GELU_A * square * a))
                    half = 0.5 * (1.0 + th)
                    act = a * half
                    slope = half + (0.5 * GELU_C) * a * (1.0 - th * th) * (1.0 + (3.0 * GELU_A) * square)
                    shape = (2, tokens, 256)
                    hid[j, r, :, :, cols] = (act * b).astype(BF16).reshape(shape)
                    act_s[j, r, :, :, cols] = act.astype(BF16).reshape(shape)
                    slope_s[j, r, :, :, cols] = (slope * b).astype(BF16).reshape(shape)
            return 0

        lax.fori_loop(0, ny, again, 0)

        def experts(rows, r, here, keep):
            count = 2 * (here.stop - here.start)
            part = slice(0, count)
            lane = lax.broadcasted_iota(jnp.int32, (count, 128), 1)
            gate_grads = jnp.zeros((count, 128), F32)
            for j in range(2):
                expert = 2 * g.e + j
                lanes = []
                for other in range(2):
                    gates_t = gates_ref[m, r, other]
                    lanes.append(gate_lanes(gates_t, expert)[here])
                lanes = widen(jnp.concatenate(lanes, 0), 256)
                summed = jnp.zeros((count, 1), F32)
                for n in range(hidden // 256):
                    cols = slice(n * 256, (n + 1) * 256)
                    u = dot_nt(rows, wd[j, cols, :])
                    inner = hid[j, r, :, here, cols].reshape(count, 256).astype(F32)
                    summed = summed + jnp.sum(u * inner, -1, keepdims=True)
                    u = u * lanes
                    slope = slope_s[j, r, :, here, cols].reshape(count, 256).astype(F32)
                    act = act_s[j, r, :, here, cols].reshape(count, 256).astype(F32)
                    da_s[j, part, cols] = (u * slope).astype(BF16)
                    db_s[j, part, cols] = (u * act).astype(BF16)
                high = summed.astype(BF16).astype(F32)
                gate_grads = jnp.where(lane == expert, high, gate_grads)
                gate_grads = jnp.where(lane == expert + 64, summed - high, gate_grads)
            for n in range(width // 512):
                cols = slice(n * 512, (n + 1) * 512)
                total = None
                for j in range(2):
                    term = dot_nt(da_s[j, part, :], wg[j, cols, :]) + dot_nt(db_s[j, part, :], wu[j, cols, :])
                    total = term if total is None else total + term
                keep(cols, total)
            keep(slice(width, width + 128), gate_grads)

        full = slice(0, tokens)

        def local_block():
            def keep(cols, total):
                accl[:, cols] = total[0:tokens]
                sendl[:, cols] = total[tokens:].astype(BF16)

            experts(grows_ref[m, 0].reshape(2 * tokens, width), 0, full, keep)

        def remote_block(r, q):
            here = slice(q * span, (q + 1) * span)

            def keep(cols, total):
                accr[:, cols] = total[0:span]
                sendc[r, here, cols] = total[span:].astype(BF16)

            experts(grows_ref[m, r, :, here, :].reshape(2 * span, width), r, here, keep)
            return lambda: accr[...]

        ex.run(local_block, remote_block)
        for q in range(CHUNKS):
            ex.arrived(q)
        total = accl[...] + retl[...].astype(F32)
        for r in range(1, ny):
            total = total + rety[r].astype(F32)
        dgates = total[:, width:]
        dgates = dgates + pltpu.roll(dgates, 64, 1)
        gates_t = gates_ref[m, 0, 0]
        gates = jnp.transpose(
            jnp.concatenate([gates_t, jnp.zeros((128 - ROUTER_ROWS, tokens), F32)], 0)
        )
        dlog = gates * (dgates - jnp.sum(gates * dgates, -1, keepdims=True))
        dlog = dlog[:, 0:SMALL_ROWS]
        high = dlog.astype(BF16)
        low = (dlog - high.astype(F32)).astype(BF16)
        router = small_ref[...]
        dxm = total[:, 0:width] + dot(high, router) + dot(low, router)
        xm = xm_s[0, 0]
        gsmall_ref[0:ROUTER_ROWS, :] += (dot_tn(high, xm) + dot_tn(low, xm))[0:ROUTER_ROWS]
        h1 = h1_ref[m]
        rinv = lax.rsqrt(jnp.mean(h1 * h1, -1, keepdims=True) + EPS)
        n2 = h1 * rinv
        gsmall_ref[ROUTER_ROWS + 1 : ROUTER_ROWS + 2, :] += jnp.sum(dxm * n2, 0, keepdims=True)
        scaled = dxm * gain_m
        dh1 = grows_ref[m, 0, 0].astype(F32) + rinv * (scaled - n2 * jnp.mean(scaled * n2, -1, keepdims=True))
        dh1_s[...] = dh1
        dattn = dh1.astype(BF16)
        dattn_ref[m] = dattn

        @pl.when(m == 0)
        def _():
            for load in loads[3:]:
                load.wait()

        bias = mask_bias(segc_ref[m], segr_ref[m])
        bias6 = jnp.concatenate([bias] * GROUP, 0)
        qkv = qkv_ref.at[m]
        turned = QUERY_HEADS + KEY_VALUE_HEADS

        def unturn(part):
            return part * cos - pltpu.roll(part, HEAD // 2, 1) * sin

        for kv in range(KEY_VALUE_HEADS):
            wide = GROUP * HEAD
            dob = dot_nt(dattn, wout[kv * wide : (kv + 1) * wide, :]).astype(BF16)
            dob6 = heads_of(dob, 0, GROUP)
            q6 = heads_of(qkv, kv * GROUP, GROUP)
            k = heads_of(qkv, QUERY_HEADS + kv, 1)
            v = heads_of(qkv, turned + kv, 1)
            shares = attention_shares(q6, k, bias6)
            dshares = dot_nt(dob6, v)
            dv = dot_tn(shares.astype(BF16), dob6)
            ds = (shares * (dshares - jnp.sum(shares * dshares, -1, keepdims=True))).astype(BF16)
            dq6 = dot(ds, k) * SCALE
            dk = dot_tn(ds, q6) * SCALE
            for i in range(GROUP):
                head = kv * GROUP + i
                dqkv_ref[m, :, head * HEAD : (head + 1) * HEAD] = unturn(
                    dq6[i * tokens : (i + 1) * tokens]
                ).astype(BF16)
            head = QUERY_HEADS + kv
            dqkv_ref[m, :, head * HEAD : (head + 1) * HEAD] = unturn(dk).astype(BF16)
            head = turned + kv
            dqkv_ref[m, :, head * HEAD : (head + 1) * HEAD] = dv.astype(BF16)

        h = hin_ref[m].astype(F32)
        rinv = lax.rsqrt(jnp.mean(h * h, -1, keepdims=True) + EPS)
        n1 = h * rinv
        xa_ref[m] = (n1 * gain_a).astype(BF16)
        n_s[...] = n1
        dqkv = dqkv_ref[m]
        for n in range(width // 512):
            cols = slice(n * 512, (n + 1) * 512)
            accl[:, cols] = dot_nt(dqkv, wqkv[cols, :])
        dxa = accl[:, 0:width]
        n1 = n_s[...]
        gsmall_ref[ROUTER_ROWS : ROUTER_ROWS + 1, :] += jnp.sum(dxa * n1, 0, keepdims=True)
        scaled = dxa * gain_a
        grad = dh1_s[...] + rinv * (scaled - n1 * jnp.mean(scaled * n1, -1, keepdims=True))
        gin_ref[m] = grad.astype(BF16)

        @pl.when(g.s > 0)
        def _():
            for q in range(CHUNKS):
                hop(m, q).start()

        ex.finish()
        return carry

    lax.fori_loop(0, micro, body, 0)

    @pl.when(g.s > 0)
    def _():
        for m in range(micro):
            for q in range(CHUNKS):
                hop(m, q).wait_send()


VMEM = pl.BlockSpec(memory_space=pltpu.VMEM)
ANY = pl.BlockSpec(memory_space=pl.ANY)


def per_device(
    ne, sections,
    layer_input, cotangent, segments, routes, attn_gain, w_qkv, w_out, moe_gain, w_router, w_gate, w_up, w_down,
):
    ny = ne // 2
    micro, _, tokens, width = layer_input.shape
    total_experts = w_router.shape[2]
    hidden = w_gate.shape[3]
    owners = ("expert", "dp")
    shard = w_qkv.shape[1]
    small = jnp.concatenate(
        [
            jnp.pad(w_router[0], ((0, 0), (0, ROUTER_ROWS - total_experts))),
            attn_gain[0][:, None],
            moe_gain[0][:, None],
            jnp.zeros((shard, SMALL_ROWS - ROUTER_ROWS - 2), BF16),
        ],
        1,
    )
    small = lax.all_gather(small, owners, axis=0, tiled=True).T
    wqkv = lax.all_gather(w_qkv[0], owners, axis=0, tiled=True)
    wout = lax.all_gather(w_out[0], owners, axis=0, tiled=True)
    route = lax.all_gather(jnp.transpose(routes[0, :, 0], (0, 2, 1)), "expert", axis=0)
    cos, sin = rotary_tables(tokens)
    segs = segments[:, 0]
    segc, segr = segs[:, :, None], segs[:, None, :]
    x = layer_input[:, 0]
    cot = cotangent[:, 0]
    wg, wu, wd = w_gate[0], w_up[0], w_down[0]
    span = tokens // CHUNKS
    qkv_width = wqkv.shape[1]

    def shape(*dims, dtype=BF16):
        return jax.ShapeDtypeStruct(dims, dtype)

    weight_scratch = {
        "wqkv": pltpu.VMEM(wqkv.shape, BF16),
        "wout": pltpu.VMEM(wout.shape, BF16),
        "wg": pltpu.VMEM(wg.shape, BF16),
        "wu": pltpu.VMEM(wu.shape, BF16),
        "wd": pltpu.VMEM(wd.shape, BF16),
    }
    order = ("wqkv", "wout", "wg", "wu", "wd")
    hop_sems = [pltpu.SemaphoreType.DMA((micro, CHUNKS)) for _ in range(2)]

    def returns(wide):
        return [
            pltpu.VMEM((tokens, wide), BF16),
            pltpu.VMEM((ny, tokens, wide), BF16),
            pltpu.VMEM((ny, tokens, wide), BF16),
            pltpu.VMEM((tokens, wide), BF16),
            pltpu.VMEM((ny, tokens, wide), BF16),
            pltpu.VMEM((ny, tokens, wide), BF16),
        ]

    out, hin, h1, qkv, ob, xm, gates = pl.pallas_call(
        functools.partial(forward_kernel, ny, sections),
        out_shape=(
            shape(micro, tokens, width),
            shape(micro, tokens, width),
            shape(micro, tokens, width, dtype=F32),
            shape(micro, tokens, qkv_width),
            shape(micro, tokens, width),
            shape(micro, ny, 2, tokens, width),
            shape(micro, ny, 2, ROUTER_ROWS, tokens, dtype=F32),
        ),
        in_specs=[VMEM] * 7 + [ANY] * 5,
        out_specs=tuple([VMEM] * 7),
        scratch_shapes=[weight_scratch[name] for name in order]
        + [
            pltpu.VMEM((2, 2 * tokens, hidden), BF16),
            pltpu.VMEM((tokens, width), F32),
            pltpu.VMEM((span, width), F32),
            pltpu.VMEM((8, 128), F32),
        ]
        + returns(width)
        + [pltpu.SemaphoreType.DMA((5,))]
        + hop_sems
        + sem_shapes(micro, ny),
        compiler_params=pltpu.CompilerParams(
            collective_id=0, has_side_effects=True, vmem_limit_bytes=60 * 2**20
        ),
        name="layers_forward",
    )(x, segc, segr, route, small, cos, sin, wqkv, wout, wg, wu, wd)

    wide = width + 128
    every = (2, ny, 2, tokens, hidden)
    gin, grows, xa, dqkv, dattn, gsmall = pl.pallas_call(
        functools.partial(backward_kernel, ny, sections),
        out_shape=(
            shape(micro, tokens, width),
            shape(micro, ny, 2, tokens, width),
            shape(micro, tokens, width),
            shape(micro, tokens, qkv_width),
            shape(micro, tokens, width),
            shape(SMALL_ROWS, width, dtype=F32),
        ),
        in_specs=[VMEM] * 10 + [ANY] * 6,
        out_specs=tuple([VMEM] * 6),
        scratch_shapes=[weight_scratch[name] for name in order]
        + [
            pltpu.VMEM((ny, 2, tokens, width), BF16),
            pltpu.VMEM(every, BF16),
            pltpu.VMEM(every, BF16),
            pltpu.VMEM(every, BF16),
            pltpu.VMEM((2, 2 * tokens, hidden), BF16),
            pltpu.VMEM((2, 2 * tokens, hidden), BF16),
            pltpu.VMEM((tokens, wide), F32),
            pltpu.VMEM((span, wide), F32),
            pltpu.VMEM((tokens, width), F32),
            pltpu.VMEM((tokens, width), F32),
        ]
        + returns(wide)
        + [pltpu.SemaphoreType.DMA((5,)), pltpu.SemaphoreType.DMA]
        + hop_sems
        + sem_shapes(micro, ny),
        compiler_params=pltpu.CompilerParams(
            collective_id=1, has_side_effects=True, vmem_limit_bytes=62 * 2**20
        ),
        name="layers_backward",
    )(cot, segc, segr, small, cos, sin, hin, h1, qkv, gates, xm, wqkv, wout, wg, wu, wd)

    e = lax.axis_index("expert")
    packs = micro * ny * 2
    rows = xm.reshape(packs * tokens, width)
    grads = grows.reshape(packs * tokens, width)
    own = lax.dynamic_slice_in_dim(gates, 2 * e, 2, 3)
    own = jnp.transpose(own, (3, 0, 1, 2, 4)).reshape(2, packs * tokens, 1)
    a = jnp.einsum("td,jdh->jth", rows, wg, preferred_element_type=F32)
    b = jnp.einsum("td,jdh->jth", rows, wu, preferred_element_type=F32)
    u = own * jnp.einsum("td,jhd->jth", grads, wd, preferred_element_type=F32)
    th = jnp.tanh(GELU_C * (a + GELU_A * a * a * a))
    half = 0.5 * (1.0 + th)
    act = a * half
    slope = half + (0.5 * GELU_C) * a * (1.0 - th * th) * (1.0 + (3.0 * GELU_A) * a * a)
    da = (u * b * slope).astype(BF16)
    db = (u * act).astype(BF16)
    gh = (own * act * b).astype(BF16)
    grad_gate = jnp.einsum("td,jth->jdh", rows, da, preferred_element_type=F32)
    grad_up = jnp.einsum("td,jth->jdh", rows, db, preferred_element_type=F32)
    grad_down = jnp.einsum("jth,td->jhd", gh, grads, preferred_element_type=F32)

    def over_dp(value):
        return lax.psum_scatter(value.astype(BF16), "dp", scatter_dimension=1, tiled=True).astype(F32)

    grad_qkv = jnp.einsum("mtd,mte->de", xa, dqkv, preferred_element_type=F32).astype(BF16)
    grad_out = jnp.einsum("mtd,mte->de", ob, dattn, preferred_element_type=F32).astype(BF16)
    grad_qkv = lax.psum_scatter(grad_qkv, owners, scatter_dimension=0, tiled=True).astype(F32)
    grad_out = lax.psum_scatter(grad_out, owners, scatter_dimension=0, tiled=True).astype(F32)
    grad_small = lax.psum_scatter(gsmall.T, owners, scatter_dimension=0, tiled=True)
    return (
        out[None, :, None],
        gin[None, :, None],
        grad_small[:, ROUTER_ROWS][None],
        grad_qkv[None],
        grad_out[None],
        grad_small[:, ROUTER_ROWS + 1][None],
        grad_small[:, 0:total_experts][None],
        over_dp(grad_gate)[None],
        over_dp(grad_up)[None],
        over_dp(grad_down)[None],
    )


def solution(mesh):
    owners = ("expert", "dp")
    return jax.shard_map(
        functools.partial(per_device, mesh.shape["expert"], mesh.shape["section"]),
        mesh=mesh,
        in_specs=(
            P(None, owners, None, None),
            P(None, owners, None, None),
            P(None, owners, None),
            P("section", None, owners, None, None),
            P("section", owners),
            P("section", owners, None),
            P("section", owners, None),
            P("section", owners),
            P("section", owners, None),
            P("section", "expert", None, None),
            P("section", "expert", None, None),
            P("section", "expert", None, None),
        ),
        out_specs=(
            P("section", None, owners, None, None),
            P("section", None, owners, None, None),
            P("section", owners),
            P("section", owners, None),
            P("section", owners, None),
            P("section", owners),
            P("section", owners, None),
            P("section", "expert", "dp", None),
            P("section", "expert", "dp", None),
            P("section", "expert", "dp", None),
        ),
        check_vma=False,
    )
```

```python
import functools

import jax
import jax.numpy as jnp
import numpy as np
from jax import lax
from jax.experimental import pallas as pl
from jax.experimental.pallas import tpu as pltpu
from jax.sharding import PartitionSpec as P

HEAD = 128
QUERY_HEADS = 12
KEY_VALUE_HEADS = 2
GROUP = QUERY_HEADS // KEY_VALUE_HEADS
EPS = 1e-06
THETA = 1000000.0
NEGATIVE = -1e30
SCALE = HEAD ** (-0.5)
ROUTER_ROWS = 16
SMALL_ROWS = 32
CHUNKS = 2
MESH = pl.DeviceIdType.MESH
F32 = jnp.float32
BF16 = jnp.bfloat16
GELU_C = float(np.sqrt(2.0 / np.pi))
GELU_A = 0.044715


def dot(a, b):
    return jnp.dot(a, b, preferred_element_type=F32)


def dot_nt(a, b):
    return lax.dot_general(a, b, (((1,), (1,)), ((), ())), preferred_element_type=F32)


def dot_tn(a, b):
    return lax.dot_general(a, b, (((0,), (0,)), ((), ())), preferred_element_type=F32)


def rotary_tables(tokens):
    places = np.arange(tokens, dtype=np.float64)
    inverse = THETA ** (-2.0 * np.arange(HEAD // 2, dtype=np.float64) / HEAD)
    angles = places[:, None] * inverse[None, :]
    cosine, sine = np.cos(angles), np.sin(angles)
    return (
        jnp.asarray(np.concatenate([cosine, cosine], 1), F32),
        jnp.asarray(np.concatenate([-sine, sine], 1), F32),
    )


def mask_bias(col, row):
    tokens = row.shape[1]
    ti = lax.broadcasted_iota(jnp.int32, (tokens, tokens), 0)
    ui = lax.broadcasted_iota(jnp.int32, (tokens, tokens), 1)
    return jnp.where((col == row) & (ui <= ti), 0.0, NEGATIVE).astype(F32)


def heads_of(value, first, count):
    return jnp.concatenate(
        [value[:, (first + i) * HEAD : (first + i + 1) * HEAD] for i in range(count)], 0
    )


def attention_shares(q6, k, bias6):
    scores = dot_nt(q6, k) * SCALE + bias6
    top = jnp.max(scores, -1, keepdims=True)
    raised = jnp.exp(scores - top)
    return raised / jnp.sum(raised, -1, keepdims=True)


class Place:
    def __init__(self, ny, nz):
        self.ny = ny
        self.nz = nz
        self.s = lax.axis_index("section")
        self.e = lax.axis_index("expert")
        self.d = lax.axis_index("dp")
        self.y = lax.div(self.e, 2)
        self.c = lax.rem(self.e, 2)
        self.core = (self.s, self.y * 2 + 1 - self.c, self.d)
        self.x = (1 - self.s, self.e, self.d)

    def ahead(self, r):
        return (self.s, lax.rem(self.y + r, self.ny) * 2 + self.c, self.d)

    def behind(self, r):
        return (self.s, lax.rem(self.y + self.ny - r, self.ny) * 2 + self.c, self.d)

    def pack(self, r, other):
        core = 1 - self.c if other else self.c
        return lax.rem(self.y + r, self.ny) * 2 + core

    def z_of(self, k):
        return lax.rem(self.d + k, self.nz)

    def z_ahead(self, k):
        return (self.s, self.e, self.z_of(k))

    def z_behind(self, k):
        return (self.s, self.e, self.z_of(self.nz - k))

    def greet(self, with_x=True):
        barrier = pltpu.get_barrier_semaphore()
        partners = [self.core] + ([self.x] if with_x else [])
        partners += [self.ahead(r) for r in range(1, self.ny)]
        partners += [self.z_ahead(k) for k in range(1, self.nz)]
        for partner in partners:
            pl.semaphore_signal(barrier, inc=1, device_id=partner, device_id_type=MESH)
        pl.semaphore_wait(barrier, len(partners))


def remote(src, dst, send, recv, device):
    return pltpu.make_async_remote_copy(
        src_ref=src, dst_ref=dst, send_sem=send, recv_sem=recv, device_id=device, device_id_type=MESH
    )


class Gather:
    def __init__(self, place, buf, send, recv, local):
        self.place, self.buf, self.send, self.recv, self.local = place, buf, send, recv, local

    def one(self, i, k, r, src):
        return remote(
            src, self.buf.at[i, k, r], self.send.at[i, k, r], self.recv.at[i, k, r], self.place.z_behind(k)
        )

    def away(self, i, r, src):
        return [self.one(i, k, r, src) for k in range(1, self.place.nz)]

    def near(self, i, r, src):
        return pltpu.make_async_copy(src, self.buf.at[i, 0, r], self.local.at[i, r])

    def push(self, i, r, src, keep=True):
        if keep:
            self.near(i, r, src).start()
        for copy in self.away(i, r, src):
            copy.start()

    def across(self, i, k, r):
        g = self.place
        return remote(
            self.buf.at[i, k, 0], self.buf.at[i, k, r], self.send.at[i, k, r], self.recv.at[i, k, r], g.behind(r)
        )

    def pass_on(self, i):
        for k in range(1, self.place.nz):
            self.one(i, k, 0, self.buf.at[i, 0, 0]).wait_recv()
            for r in range(1, self.place.ny):
                self.across(i, k, r).start()

    def drain(self, i, keep=True):
        for r in range(self.place.ny):
            src = self.buf.at[i, 0, r]
            if keep or r == 0:
                self.near(i, r, src).wait()
            for copy in self.away(i, r, src):
                copy.wait()

    def drain_passed(self, i):
        g = self.place
        for r in range(g.ny):
            self.near(i, r, self.buf.at[i, 0, r]).wait()
        for copy in self.away(i, 0, self.buf.at[i, 0, 0]):
            copy.wait_send()
        for k in range(1, g.nz):
            for r in range(1, g.ny):
                self.across(i, k, r).wait()


class Exchange:
    def __init__(self, place, rows_ref, retl, retc, rety, sendl, sendc, sendy, sems):
        self.place = place
        self.rows_ref = rows_ref
        self.retl, self.retc, self.rety = retl, retc, rety
        self.sendl, self.sendc, self.sendy = sendl, sendc, sendy
        self.sems = sems
        self.tokens = rows_ref.shape[2]
        self.span = self.tokens // CHUNKS

    def rows(self, q):
        return pl.ds(q * self.span, self.span)

    def core_own(self):
        g = self.place
        return remote(
            self.rows_ref.at[0, 0], self.rows_ref.at[0, 1], self.sems.cs.at[0, 0], self.sems.cr.at[0, 0], g.core
        )

    def y_own(self, r, q):
        g = self.place
        return remote(
            self.rows_ref.at[0, 0, self.rows(q)],
            self.rows_ref.at[r, 0, self.rows(q)],
            self.sems.ys.at[r, q],
            self.sems.yr.at[r, q],
            g.behind(r),
        )

    def forward(self, r, q):
        g = self.place
        return remote(
            self.rows_ref.at[r, 0, self.rows(q)],
            self.rows_ref.at[r, 1, self.rows(q)],
            self.sems.cs.at[r, q],
            self.sems.cr.at[r, q],
            g.core,
        )

    def back_local(self):
        return remote(self.sendl, self.retl, self.sems.bs.at[0, 0], self.sems.br.at[0, 0], self.place.core)

    def back_core(self, r, q):
        return remote(
            self.sendc.at[r - 1, self.rows(q)],
            self.retc.at[r - 1, self.rows(q)],
            self.sems.bs.at[r, q],
            self.sems.br.at[r, q],
            self.place.core,
        )

    def back_y(self, r, q):
        g = self.place
        return remote(
            self.sendy.at[r - 1, self.rows(q)],
            self.rety.at[g.ny - r - 1, self.rows(q)],
            self.sems.zs.at[r, q],
            self.sems.zr.at[g.ny - r, q],
            g.ahead(r),
        )

    def back_y_arrival(self, r, q):
        g = self.place
        return remote(
            self.sendy.at[r - 1, self.rows(q)],
            self.rety.at[r - 1, self.rows(q)],
            self.sems.zs.at[r, q],
            self.sems.zr.at[r, q],
            g.ahead(r),
        )

    def send_own(self):
        for q in range(CHUNKS):
            for r in range(1, self.place.ny):
                self.y_own(r, q).start()
        self.core_own().start()

    def run(self, local_block, remote_block, complete):
        ny = self.place.ny
        items = [(r, q) for q in range(CHUNKS) for r in range(1, ny)]
        self.core_own().wait_recv()
        local_block()
        self.back_local().start()

        def arrive(r, q):
            self.y_own(r, q).wait_recv()
            self.forward(r, q).start()
            if q == CHUNKS - 1:
                complete(r)

        if items:
            arrive(*items[0])
        for i, (r, q) in enumerate(items):
            self.forward(r, q).wait_recv()
            own = remote_block(r, q)
            self.back_core(r, q).start()
            if i + 1 < len(items):
                arrive(*items[i + 1])
            self.back_core(r, q).wait_recv()
            here = self.rows(q)
            self.sendy[r - 1, here, :] = (own() + self.retc[r - 1, here, :].astype(F32)).astype(BF16)
            self.back_y(r, q).start()
        self.back_local().wait_recv()

    def arrived(self, q):
        for r in range(1, self.place.ny):
            self.back_y_arrival(r, q).wait_recv()

    def finish(self):
        ny = self.place.ny
        self.core_own().wait_send()
        self.back_local().wait_send()
        for q in range(CHUNKS):
            for r in range(1, ny):
                self.y_own(r, q).wait_send()
                self.forward(r, q).wait_send()
                self.back_core(r, q).wait_send()
                self.back_y(r, q).wait_send()


class Sems:
    def __init__(self, refs, m):
        self.cs, self.cr, self.ys, self.yr, self.bs, self.br, self.zs, self.zr = [ref.at[m] for ref in refs]


def sem_shapes(micro, ny):
    return [pltpu.SemaphoreType.DMA((micro, ny, CHUNKS)) for _ in range(8)]


def chosen_gates(logits_t, route):
    experts = lax.broadcasted_iota(jnp.int32, logits_t.shape, 0)
    chosen = route[0:1, :] == experts
    for k in range(1, route.shape[0]):
        chosen = chosen | (route[k : k + 1, :] == experts)
    masked = jnp.where(chosen, logits_t, NEGATIVE)
    raised = jnp.where(chosen, jnp.exp(masked - jnp.max(masked, 0, keepdims=True)), 0.0)
    return raised / jnp.sum(raised, 0, keepdims=True)


def gate_lanes(gates_t, expert):
    rows = lax.broadcasted_iota(jnp.int32, gates_t.shape, 0)
    one = jnp.sum(jnp.where(rows == expert, gates_t, 0.0), 0, keepdims=True)
    return jnp.transpose(jnp.broadcast_to(one, (128, one.shape[1])))


def widen(lanes, width):
    return jnp.concatenate([lanes] * (width // 128), 1)


def forward_kernel(
    ny, nz, sections,
    x_ref, segc_ref, segr_ref, route_ref, small_ref, cos_ref, sin_ref,
    cot_h, slices_h, wqkv_h, wout_h, wg_h, wu_h, wd_h,
    out_ref, hin_ref, h1_ref, qkv_ref, obb_ref, xm_ref, gates_ref, zf_h, partner_h,
    wqkv, wout, wg, wu, wd, ob_s, hid, accl, accr, retl, retc, rety, sendl, sendc, sendy,
    wsem, zs, zr, zl, ps, pr, gs, gr, xs, xr, *sem_refs,
):
    micro, tokens, width = x_ref.shape
    hidden = wg.shape[2]
    span = tokens // CHUNKS
    loads = [
        pltpu.make_async_copy(src, dst, wsem.at[i])
        for i, (src, dst) in enumerate([(wqkv_h, wqkv), (wout_h, wout), (wg_h, wg), (wu_h, wu), (wd_h, wd)])
    ]
    for load in loads:
        load.start()
    g = Place(ny, nz)
    g.greet()
    gain_a = small_ref[ROUTER_ROWS : ROUTER_ROWS + 1, :].astype(F32)
    gain_m = small_ref[ROUTER_ROWS + 1 : ROUTER_ROWS + 2, :].astype(F32)
    cos, sin = cos_ref[...], sin_ref[...]
    gather = Gather(g, zf_h, zs, zr, zl)
    first, last = g.s == 0, g.s == sections - 1

    partner_copy = remote(slices_h, partner_h, ps, pr, g.core)
    partner_copy.start()

    def cot_copy(r):
        return remote(cot_h.at[0], zf_h.at[0, 0, r], gs.at[r], gr.at[r], g.behind(r))

    @pl.when(last)
    def _():
        for r in range(1, ny):
            cot_copy(r).start()
        gather.push(0, 0, cot_h.at[0])
        for r in range(1, ny):
            cot_copy(r).wait_recv()
            gather.push(0, r, zf_h.at[0, 0, r], keep=False)

    def hop(m, q):
        here = pl.ds(q * span, span)
        return remote(out_ref.at[m, here], hin_ref.at[m, here], xs.at[m, q], xr.at[m, q], g.x)

    def experts(rows, lanes, keep):
        count = rows.shape[0]
        for j in range(2):
            for n in range(hidden // 256):
                cols = slice(n * 256, (n + 1) * 256)
                a = dot(rows, wg[j, :, cols])
                b = dot(rows, wu[j, :, cols])
                act = 0.5 * a * (1.0 + jnp.tanh(GELU_C * (a + GELU_A * a * a * a)))
                hid[j, 0:count, cols] = (act * b).astype(BF16)
        for n in range(width // 512):
            cols = slice(n * 512, (n + 1) * 512)
            total = None
            for j in range(2):
                eo = dot(hid[j, 0:count, :], wd[j, :, cols]).astype(BF16).astype(F32)
                term = widen(lanes[j], 512) * eo
                total = term if total is None else total + term
            keep(cols, total)

    def body(m, carry):
        @pl.when(g.s == 0)
        def _():
            hin_ref[m] = x_ref[m]

        @pl.when(g.s > 0)
        def _():
            for q in range(CHUNKS):
                hop(m, q).wait_recv()

        h = hin_ref[m].astype(F32)
        xa = (h * lax.rsqrt(jnp.mean(h * h, -1, keepdims=True) + EPS) * gain_a).astype(BF16)

        @pl.when(m == 0)
        def _():
            loads[0].wait()

        turned = QUERY_HEADS + KEY_VALUE_HEADS
        for i in range(wqkv.shape[1] // 256):
            mixed = dot(xa, wqkv[:, i * 256 : (i + 1) * 256])
            for half in range(2):
                head = 2 * i + half
                part = mixed[:, half * HEAD : (half + 1) * HEAD]
                if head < turned:
                    part = part * cos + pltpu.roll(part, HEAD // 2, 1) * sin
                qkv_ref[m, :, head * HEAD : (head + 1) * HEAD] = part.astype(BF16)
        bias = mask_bias(segc_ref[m], segr_ref[m])
        bias6 = jnp.concatenate([bias] * GROUP, 0)
        qkv = qkv_ref.at[m]
        for kv in range(KEY_VALUE_HEADS):
            q6 = heads_of(qkv, kv * GROUP, GROUP)
            k = heads_of(qkv, QUERY_HEADS + kv, 1)
            v = heads_of(qkv, turned + kv, 1)
            shares = attention_shares(q6, k, bias6).astype(BF16)
            o6 = dot(shares, v).astype(BF16)
            for i in range(GROUP):
                head = kv * GROUP + i
                ob_s[:, head * HEAD : (head + 1) * HEAD] = o6[i * tokens : (i + 1) * tokens]

        @pl.when(m == 0)
        def _():
            loads[1].wait()

        ob = ob_s[...]
        block = obb_ref.shape[3]
        for i in range(2 * ny):
            obb_ref[m, i] = ob[:, i * block : (i + 1) * block]
        for n in range(width // 512):
            cols = slice(n * 512, (n + 1) * 512)
            h1_ref[m, :, cols] = hin_ref[m, :, cols].astype(F32) + dot(ob, wout[:, cols])
        h1 = h1_ref[m]
        xm_ref[m, 0, 0] = (h1 * lax.rsqrt(jnp.mean(h1 * h1, -1, keepdims=True) + EPS) * gain_m).astype(BF16)

        ex = Exchange(g, xm_ref.at[m], retl, retc, rety, sendl, sendc, sendy, Sems(sem_refs, m))
        ex.send_own()

        def complete(r):
            @pl.when(first & (m == 0))
            def _():
                gather.push(0, r, xm_ref.at[0, r, 0])

        complete(0)

        @pl.when(m == 0)
        def _():
            for load in loads[2:]:
                load.wait()

        def gates_for(r, other, here):
            rows = xm_ref[m, r, other, here, :]
            logits_t = dot_nt(small_ref[0:ROUTER_ROWS, :], rows)
            gates_t = chosen_gates(logits_t, route_ref[g.pack(r, other), m][:, here])
            return gates_t

        def lanes_of(blocks):
            return [
                jnp.concatenate([gate_lanes(gates_t, 2 * g.e + j) for gates_t in blocks], 0) for j in range(2)
            ]

        full = slice(0, tokens)

        def local_block():
            blocks = []
            for other in range(2):
                gates_t = gates_for(0, other, full)
                gates_ref[m, 0, other] = gates_t
                blocks.append(gates_t)

            def keep(cols, total):
                accl[:, cols] = total[0:tokens]
                sendl[:, cols] = total[tokens:].astype(BF16)

            experts(xm_ref[m, 0].reshape(2 * tokens, width), lanes_of(blocks), keep)

        def remote_block(r, q):
            here = slice(q * span, (q + 1) * span)
            blocks = []
            for other in range(2):
                gates_t = gates_for(r, other, here)
                gates_ref[m, r, other, :, here] = gates_t
                blocks.append(jnp.concatenate([gates_t] * (128 // span), 1))
            lanes = [
                jnp.concatenate([gate_lanes(gates_t, 2 * g.e + j)[0:span] for gates_t in blocks], 0)
                for j in range(2)
            ]

            def keep(cols, total):
                accr[:, cols] = total[0:span]
                sendc[r - 1, here, cols] = total[span:].astype(BF16)

            experts(xm_ref[m, r, :, here, :].reshape(2 * span, width), lanes, keep)
            return lambda: accr[...]

        ex.run(local_block, remote_block, complete)
        for q in range(CHUNKS):
            here = slice(q * span, (q + 1) * span)
            ex.arrived(q)
            total = h1_ref[m, here, :] + accl[here, :] + retl[here, :].astype(F32)
            for r in range(1, ny):
                total = total + rety[r - 1, here, :].astype(F32)
            out_ref[m, here, :] = total.astype(BF16)

            @pl.when(g.s < sections - 1)
            def _():
                hop(m, q).start()

        ex.finish()
        return carry

    lax.fori_loop(0, micro, body, 0)
    partner_copy.wait()

    @pl.when(g.s < sections - 1)
    def _():
        for m in range(micro):
            for q in range(CHUNKS):
                hop(m, q).wait_send()

    @pl.when(first)
    def _():
        gather.drain(0)

    @pl.when(last)
    def _():
        for r in range(1, ny):
            cot_copy(r).wait_send()
        gather.drain(0, keep=False)


def backward_kernel(
    ny, nz, sections,
    cot_ref, segc_ref, segr_ref, small_ref, cos_ref, sin_ref,
    hin_ref, h1_ref, qkv_ref, gates_ref,
    xm_h, wqkv_h, wout_h, wg_h, wu_h, wd_h,
    gin_ref, grows_ref, xab_ref, dqkv_ref, dattn_ref, gsmall_ref, zb_h,
    wqkv, wout, wg, wu, wd, xm_s, hid, act_s, slope_s, da_s, db_s, accl, accr, dh1_s, n_s,
    retl, retc, rety, sendl, sendc, sendy,
    wsem, xmsem, zs, zr, zl, xs, xr, *sem_refs,
):
    micro, tokens, width = cot_ref.shape
    hidden = wg.shape[2]
    span = tokens // CHUNKS
    loads = [
        pltpu.make_async_copy(src, dst, wsem.at[i])
        for i, (src, dst) in enumerate([(wg_h, wg), (wu_h, wu), (wd_h, wd), (wout_h, wout), (wqkv_h, wqkv)])
    ]
    for load in loads:
        load.start()
    g = Place(ny, nz)
    g.greet()
    gain_a = small_ref[ROUTER_ROWS : ROUTER_ROWS + 1, :].astype(F32)
    gain_m = small_ref[ROUTER_ROWS + 1 : ROUTER_ROWS + 2, :].astype(F32)
    cos, sin = cos_ref[...], sin_ref[...]
    gsmall_ref[...] = jnp.zeros_like(gsmall_ref)
    gather = Gather(g, zb_h, zs, zr, zl)
    first, last = g.s == 0, g.s == sections - 1

    @pl.when(first)
    def _():
        for m in range(1, micro):
            for r in range(ny):
                gather.push(micro + m, r, xm_h.at[m, r, 0])

    @pl.when(last)
    def _():
        for m in range(micro):
            gather.push(m, 0, xm_h.at[m, 0, 0])
            for r in range(1, ny):
                gather.near(m, r, xm_h.at[m, r, 0]).start()

    def hop(m, q):
        here = pl.ds(q * span, span)
        return remote(gin_ref.at[m, here], grows_ref.at[m, 0, 0, here], xs.at[m, q], xr.at[m, q], g.x)

    def body(m, carry):
        load_xm = pltpu.make_async_copy(xm_h.at[m], xm_s, xmsem)
        load_xm.start()

        @pl.when(g.s == sections - 1)
        def _():
            grows_ref[m, 0, 0] = cot_ref[m]

        @pl.when(g.s < sections - 1)
        def _():
            for q in range(CHUNKS):
                hop(m, q).wait_recv()

        ex = Exchange(g, grows_ref.at[m], retl, retc, rety, sendl, sendc, sendy, Sems(sem_refs, m))
        ex.send_own()

        def complete(r):
            src = grows_ref.at[m, r, 0]

            @pl.when(first)
            def _():
                if r == 0:
                    gather.push(m, 0, src)
                else:
                    gather.near(m, r, src).start()

            @pl.when(last & (m > 0))
            def _():
                gather.push(micro + m, r, src)

        complete(0)

        @pl.when(m == 0)
        def _():
            for load in loads[:3]:
                load.wait()

        load_xm.wait()

        def again(r, _):
            rows = xm_s[r].reshape(2 * tokens, width)
            for j in range(2):
                for n in range(hidden // 256):
                    cols = slice(n * 256, (n + 1) * 256)
                    a = dot(rows, wg[j, :, cols])
                    b = dot(rows, wu[j, :, cols])
                    square = a * a
                    th = jnp.tanh(GELU_C * (a + GELU_A * square * a))
                    half = 0.5 * (1.0 + th)
                    act = a * half
                    slope = half + (0.5 * GELU_C) * a * (1.0 - th * th) * (1.0 + (3.0 * GELU_A) * square)
                    shape = (2, tokens, 256)
                    hid[j, r, :, :, cols] = (act * b).astype(BF16).reshape(shape)
                    act_s[j, r, :, :, cols] = act.astype(BF16).reshape(shape)
                    slope_s[j, r, :, :, cols] = (slope * b).astype(BF16).reshape(shape)
            return 0

        lax.fori_loop(0, ny, again, 0)

        def experts(rows, r, here, keep):
            count = 2 * (here.stop - here.start)
            part = slice(0, count)
            lane = lax.broadcasted_iota(jnp.int32, (count, 128), 1)
            gate_grads = jnp.zeros((count, 128), F32)
            for j in range(2):
                expert = 2 * g.e + j
                lanes = []
                for other in range(2):
                    gates_t = gates_ref[m, r, other]
                    lanes.append(gate_lanes(gates_t, expert)[here])
                lanes = widen(jnp.concatenate(lanes, 0), 256)
                summed = jnp.zeros((count, 1), F32)
                for n in range(hidden // 256):
                    cols = slice(n * 256, (n + 1) * 256)
                    u = dot_nt(rows, wd[j, cols, :])
                    inner = hid[j, r, :, here, cols].reshape(count, 256).astype(F32)
                    summed = summed + jnp.sum(u * inner, -1, keepdims=True)
                    u = u * lanes
                    slope = slope_s[j, r, :, here, cols].reshape(count, 256).astype(F32)
                    act = act_s[j, r, :, here, cols].reshape(count, 256).astype(F32)
                    da_s[j, part, cols] = (u * slope).astype(BF16)
                    db_s[j, part, cols] = (u * act).astype(BF16)
                high = summed.astype(BF16).astype(F32)
                gate_grads = jnp.where(lane == expert, high, gate_grads)
                gate_grads = jnp.where(lane == expert + 64, summed - high, gate_grads)
            for n in range(width // 512):
                cols = slice(n * 512, (n + 1) * 512)
                total = None
                for j in range(2):
                    term = dot_nt(da_s[j, part, :], wg[j, cols, :]) + dot_nt(db_s[j, part, :], wu[j, cols, :])
                    total = term if total is None else total + term
                keep(cols, total)
            keep(slice(width, width + 128), gate_grads)

        full = slice(0, tokens)

        def local_block():
            def keep(cols, total):
                accl[:, cols] = total[0:tokens]
                sendl[:, cols] = total[tokens:].astype(BF16)

            experts(grows_ref[m, 0].reshape(2 * tokens, width), 0, full, keep)

        def remote_block(r, q):
            here = slice(q * span, (q + 1) * span)

            def keep(cols, total):
                accr[:, cols] = total[0:span]
                sendc[r - 1, here, cols] = total[span:].astype(BF16)

            experts(grows_ref[m, r, :, here, :].reshape(2 * span, width), r, here, keep)
            return lambda: accr[...]

        ex.run(local_block, remote_block, complete)
        for q in range(CHUNKS):
            ex.arrived(q)
        total = accl[...] + retl[...].astype(F32)
        for r in range(1, ny):
            total = total + rety[r - 1].astype(F32)
        dgates = total[:, width:]
        dgates = dgates + pltpu.roll(dgates, 64, 1)
        gates_t = gates_ref[m, 0, 0]
        gates = jnp.transpose(
            jnp.concatenate([gates_t, jnp.zeros((128 - ROUTER_ROWS, tokens), F32)], 0)
        )
        dlog = gates * (dgates - jnp.sum(gates * dgates, -1, keepdims=True))
        dlog = dlog[:, 0:SMALL_ROWS]
        high = dlog.astype(BF16)
        low = (dlog - high.astype(F32)).astype(BF16)
        router = small_ref[...]
        dxm = total[:, 0:width] + dot(high, router) + dot(low, router)
        xm = xm_s[0, 0]
        gsmall_ref[0:ROUTER_ROWS, :] += (dot_tn(high, xm) + dot_tn(low, xm))[0:ROUTER_ROWS]
        h1 = h1_ref[m]
        rinv = lax.rsqrt(jnp.mean(h1 * h1, -1, keepdims=True) + EPS)
        n2 = h1 * rinv
        gsmall_ref[ROUTER_ROWS + 1 : ROUTER_ROWS + 2, :] += jnp.sum(dxm * n2, 0, keepdims=True)
        scaled = dxm * gain_m
        dh1 = grows_ref[m, 0, 0].astype(F32) + rinv * (scaled - n2 * jnp.mean(scaled * n2, -1, keepdims=True))
        dh1_s[...] = dh1
        dattn = dh1.astype(BF16)
        dattn_ref[m] = dattn

        @pl.when(m == 0)
        def _():
            for load in loads[3:]:
                load.wait()

        gather.pass_on(m)
        bias = mask_bias(segc_ref[m], segr_ref[m])
        bias6 = jnp.concatenate([bias] * GROUP, 0)
        qkv = qkv_ref.at[m]
        turned = QUERY_HEADS + KEY_VALUE_HEADS

        def unturn(part):
            return part * cos - pltpu.roll(part, HEAD // 2, 1) * sin

        for kv in range(KEY_VALUE_HEADS):
            wide = GROUP * HEAD
            dob = dot_nt(dattn, wout[kv * wide : (kv + 1) * wide, :]).astype(BF16)
            dob6 = heads_of(dob, 0, GROUP)
            q6 = heads_of(qkv, kv * GROUP, GROUP)
            k = heads_of(qkv, QUERY_HEADS + kv, 1)
            v = heads_of(qkv, turned + kv, 1)
            shares = attention_shares(q6, k, bias6)
            dshares = dot_nt(dob6, v)
            dv = dot_tn(shares.astype(BF16), dob6)
            ds = (shares * (dshares - jnp.sum(shares * dshares, -1, keepdims=True))).astype(BF16)
            dq6 = dot(ds, k) * SCALE
            dk = dot_tn(ds, q6) * SCALE
            for i in range(GROUP):
                head = kv * GROUP + i
                dqkv_ref[m, :, head * HEAD : (head + 1) * HEAD] = unturn(
                    dq6[i * tokens : (i + 1) * tokens]
                ).astype(BF16)
            head = QUERY_HEADS + kv
            dqkv_ref[m, :, head * HEAD : (head + 1) * HEAD] = unturn(dk).astype(BF16)
            head = turned + kv
            dqkv_ref[m, :, head * HEAD : (head + 1) * HEAD] = dv.astype(BF16)

        h = hin_ref[m].astype(F32)
        rinv = lax.rsqrt(jnp.mean(h * h, -1, keepdims=True) + EPS)
        n1 = h * rinv
        xa = (n1 * gain_a).astype(BF16)
        block = xab_ref.shape[3]
        for i in range(2 * ny):
            xab_ref[m, i] = xa[:, i * block : (i + 1) * block]
        n_s[...] = n1
        dqkv = dqkv_ref[m]
        for n in range(width // 512):
            cols = slice(n * 512, (n + 1) * 512)
            accl[:, cols] = dot_nt(dqkv, wqkv[cols, :])
        dxa = accl[:, 0:width]
        n1 = n_s[...]
        gsmall_ref[ROUTER_ROWS : ROUTER_ROWS + 1, :] += jnp.sum(dxa * n1, 0, keepdims=True)
        scaled = dxa * gain_a
        grad = dh1_s[...] + rinv * (scaled - n1 * jnp.mean(scaled * n1, -1, keepdims=True))
        gin_ref[m] = grad.astype(BF16)

        @pl.when(g.s > 0)
        def _():
            for q in range(CHUNKS):
                hop(m, q).start()

        ex.finish()
        return carry

    lax.fori_loop(0, micro, body, 0)

    @pl.when(g.s > 0)
    def _():
        for m in range(micro):
            for q in range(CHUNKS):
                hop(m, q).wait_send()

    for m in range(micro):
        gather.drain_passed(m)
    for m in range(1, micro):
        gather.drain(micro + m)


def tail_kernel(
    ny, nz, sections, span,
    route_ref, small_ref, gsmall_ref,
    zf_h, zb_h, slices_h, partner_h, xab_h, obb_h, dqkv_h, dattn_h,
    gate_ref, up_ref, down_ref, attn_ref, small_out,
    w4, x_s, g_s, da_s, db_s, gh_s, acc_g, acc_u, acc_d, csend, cland, dsend, dland,
    xa_s, ob_s, dq_s, dt_s, own_s, ysend, yland, zland, sm_s, smy, smz,
    wsem, xsem, asem, as_, ar, ss, sr, cs, cr, ts, tr, ys, yr, zs, zr,
):
    micro, tokens, width = dqkv_h.shape[0], zf_h.shape[3], zf_h.shape[4]
    half = slices_h.shape[1]
    slice_h = half // 2
    both = 2 * half
    tile = 256 if both % 256 == 0 else 128
    qkv_width = dqkv_h.shape[2]
    shard = width // (2 * ny * nz)
    part = width // nz
    rows = span * ny * tokens
    groups = nz // span
    g = Place(ny, nz)
    first = g.s == 0
    mine = [pltpu.make_async_copy(src, w4.at[:, i * half : (i + 1) * half], wsem.at[i])
            for i, src in enumerate((slices_h, partner_h))]

    def load(i):
        m, k = lax.div(i, groups), pl.ds(lax.rem(i, groups) * span, span)
        early = [(first, x_s, 0), (jnp.logical_not(first), g_s, 1)]
        late = [(first, g_s, 1), (jnp.logical_not(first), x_s, 0)]
        copies = [(when, pltpu.make_async_copy(zb_h.at[m, k], dst, xsem.at[n])) for when, dst, n in late]
        for when, dst, n in early:
            copies.append((when & (m == 0), pltpu.make_async_copy(zf_h.at[0, k], dst, xsem.at[n])))
            copies.append((when & (m > 0), pltpu.make_async_copy(zb_h.at[micro + m, k], dst, xsem.at[n])))
        return copies

    def start_load(i):
        for when, copy in load(i):
            @pl.when(when)
            def _():
                copy.start()

    def wait_load():
        pltpu.make_async_copy(zf_h.at[0, pl.ds(0, span)], x_s, xsem.at[0]).wait()
        pltpu.make_async_copy(zf_h.at[0, pl.ds(0, span)], g_s, xsem.at[1]).wait()

    for copy in mine:
        copy.start()
    start_load(0)
    g.greet(with_x=False)

    away, here = [], []
    for m in range(micro):
        for yy in range(ny):
            other = yy * 2 + 1 - g.c
            own = yy * 2 + g.c
            for n, (src, dst) in enumerate(((xab_h, xa_s), (obb_h, ob_s))):
                i = (m * ny + yy) * 2 + n
                away.append(remote(src.at[m, other], dst.at[yy, 1, m], as_.at[i], ar.at[i], g.core))
                here.append(pltpu.make_async_copy(src.at[m, own], dst.at[yy, 0, m], asem.at[i]))
    base = 2 * ny * micro
    for n, (src, dst) in enumerate(((dqkv_h, dq_s), (dattn_h, dt_s))):
        i = base + n
        away.append(remote(src, dst.at[1], as_.at[i], ar.at[i], g.core))
        here.append(pltpu.make_async_copy(src, dst.at[0], asem.at[i]))
    for copy in away + here:
        copy.start()
    sm_core = remote(gsmall_ref, sm_s.at[1], ss.at[0], sr.at[0], g.core)
    sm_core.start()

    def sm_y(r):
        return remote(sm_s.at[0], smy.at[ny - r], ss.at[r], sr.at[ny - r], g.ahead(r))

    def sm_y_arrival(r):
        return remote(sm_s.at[0], smy.at[r], ss.at[r], sr.at[r], g.ahead(r))

    def sm_z(k):
        return remote(sm_s.at[1], smz.at[k], ss.at[ny + k], sr.at[ny + k], g.z_behind(k))

    for copy in away:
        copy.wait_recv()
    for copy in here:
        copy.wait()

    count = 2 * micro * tokens

    def attn_rows(yy, dst):
        for src, grad, at in ((xa_s, dq_s, 0), (ob_s, dt_s, qkv_width)):
            left = src[yy].reshape(count, shard * nz)
            wide = grad.shape[3]
            for n in range(wide // 512):
                cols = slice(n * 512, (n + 1) * 512)
                got = dot_tn(left, grad[:, :, :, cols].reshape(count, 512)).astype(BF16)
                for zi in range(nz):
                    dst[zi, 0:shard, at + n * 512 : at + (n + 1) * 512] = got[zi * shard : (zi + 1) * shard]

    def y_copy(r, k):
        zi = g.z_of(k)
        return remote(ysend.at[r - 1, zi], yland.at[ny - r - 1, zi], ys.at[r, k], yr.at[ny - r, k], g.ahead(r))

    def y_arrival(r, k):
        zi = g.z_of(k)
        return remote(ysend.at[r - 1, zi], yland.at[r - 1, zi], ys.at[r, k], yr.at[r, k], g.ahead(r))

    order = list(range(1, nz)) + [0]
    for r in range(1, ny):
        attn_rows(lax.rem(g.y + r, ny), ysend.at[r - 1])
    for k in order:
        for r in range(1, ny):
            y_copy(r, k).start()
    sm_core.wait_recv()
    sm_s[0] = gsmall_ref[...] + sm_s[1]
    sm_core.wait_send()
    for r in range(1, ny):
        sm_y(r).start()
    attn_rows(g.y, own_s)

    def z_copy(k):
        return remote(own_s.at[g.z_of(k)], zland.at[nz - k - 1], zs.at[0, k], zr.at[0, nz - k], g.z_ahead(k))

    def z_arrival(k):
        return remote(own_s.at[g.d], zland.at[k - 1], zs.at[0, k], zr.at[0, k], g.z_ahead(k))

    def attn_sum(k):
        for r in range(1, ny):
            y_arrival(r, k).wait_recv()
        zi = g.z_of(k)
        total = own_s[zi].astype(F32)
        for r in range(1, ny):
            total = total + yland[r - 1, zi].astype(F32)
        own_s[zi] = total.astype(BF16)
        if k:
            z_copy(k).start()

    for copy in mine:
        copy.wait()
    acc_g[...] = jnp.zeros_like(acc_g)
    acc_u[...] = jnp.zeros_like(acc_u)
    acc_d[...] = jnp.zeros_like(acc_d)
    column = lax.broadcasted_iota(jnp.int32, (ROUTER_ROWS, both), 1)
    expert = lax.broadcasted_iota(jnp.int32, (ROUTER_ROWS, both), 0)
    owner = jnp.where(column < half, g.e, 2 * g.y + 1 - g.c)
    local = jnp.where(column < half, column, column - half)
    chosen = 2 * owner + jnp.where(local < slice_h, 0, 1)
    spread = jnp.where(expert == chosen, 1.0, 0.0).astype(BF16)

    def group(i, carry):
        m = lax.div(i, groups)
        wait_load()

        def block(b, carry):
            k = lax.rem(i, groups) * span + lax.div(b, ny)
            r = lax.rem(b, ny)
            place = (lax.rem(g.y + r, ny) * 2 + g.c) * nz + g.z_of(k)
            x = x_s[lax.div(b, ny), r]
            gr = g_s[lax.div(b, ny), r]
            gates_t = chosen_gates(dot_nt(small_ref[0:ROUTER_ROWS, :], x), route_ref[place, m])
            high = gates_t.astype(BF16)
            low = (gates_t - high.astype(F32)).astype(BF16)
            here = pl.ds(pl.multiple_of(b * tokens, tokens), tokens)
            for n in range(both // tile):
                cols = slice(n * tile, (n + 1) * tile)
                a = dot_nt(x, w4[0, cols])
                bb = dot_nt(x, w4[1, cols])
                gate = dot_tn(high, spread[:, cols]) + dot_tn(low, spread[:, cols])
                u = dot_nt(gr, w4[2, cols]) * gate
                square = a * a
                th = jnp.tanh(GELU_C * (a + GELU_A * square * a))
                hf = 0.5 * (1.0 + th)
                act = a * hf
                slope = hf + (0.5 * GELU_C) * a * (1.0 - th * th) * (1.0 + (3.0 * GELU_A) * square)
                da_s[here, cols] = (u * slope * bb).astype(BF16)
                db_s[here, cols] = (u * act).astype(BF16)
                gh_s[here, cols] = ((act * bb).astype(BF16).astype(F32) * gate).astype(BF16)
            return carry

        lax.fori_loop(0, span * ny, block, 0)

        def columns(n, carry):
            cols = pl.ds(pl.multiple_of(n * 256, 256), 256)
            x = x_s[:, :, :, cols].reshape(rows, 256)
            acc_g[cols, :] += dot_tn(x, da_s[...])
            acc_u[cols, :] += dot_tn(x, db_s[...])
            acc_d[:, cols] += dot_tn(gh_s[...], g_s[:, :, :, cols].reshape(rows, 256))
            return carry

        lax.fori_loop(0, width // 256, columns, 0)

        @pl.when(i + 1 < micro * groups)
        def _():
            start_load(i + 1)

        return carry

    lax.fori_loop(0, micro * groups, group, 0)

    def core_copy(n, k):
        return remote(csend.at[n, k], cland.at[n, k], cs.at[n, k], cr.at[n, k], g.core)

    def turn_copy(n, k):
        dst = (gate_ref, up_ref)[n]
        return remote(cland.at[n, k], dst.at[g.d], ts.at[n, k], tr.at[n, k], g.z_ahead(k))

    def turn_near(n):
        return pltpu.make_async_copy(cland.at[n, 0], (gate_ref, up_ref)[n].at[g.d], ts.at[n, 0])

    def turn_arrival(n, k):
        dst = (gate_ref, up_ref)[n]
        return remote(cland.at[n, k], dst.at[g.z_of(nz - k)], ts.at[n, k], tr.at[n, k], g.z_behind(k))

    def width_rows(k):
        return pl.ds(pl.multiple_of(g.z_of(k) * part, part), part)

    down_copy = remote(dsend, dland, cs.at[2, 0], cr.at[2, 0], g.core)
    accs = (acc_g, acc_u)
    for n in range(2):
        for k in order:
            csend[n, k] = accs[n][width_rows(k), half:both].astype(BF16)
            core_copy(n, k).start()
    dsend[...] = acc_d[half:both, :].astype(BF16)
    down_copy.start()
    for k in order[:-1]:
        attn_sum(k)
        for n in range(2):
            core_copy(n, k).wait_recv()
            total = accs[n][width_rows(k), 0:half] + cland[n, k].astype(F32)
            cland[n, k] = total.astype(BF16)
            turn_copy(n, k).start()
    for n in range(2):
        core_copy(n, 0).wait_recv()
        cland[n, 0] = (accs[n][width_rows(0), 0:half] + cland[n, 0].astype(F32)).astype(BF16)
        turn_near(n).start()
    down_copy.wait_recv()
    down_ref[...] = (acc_d[0:half, :] + dland[...].astype(F32)).astype(BF16)
    attn_sum(0)

    for r in range(1, ny):
        sm_y_arrival(r).wait_recv()
    total = sm_s[0]
    for r in range(1, ny):
        total = total + smy[r]
    sm_s[1] = total
    for k in range(1, nz):
        sm_z(k).start()
    for k in range(1, nz):
        sm_z(k).wait_recv()
        total = total + smz[k]
    small_out[...] = total

    for k in range(1, nz):
        z_arrival(k).wait_recv()
    total = own_s[g.d].astype(F32)
    for k in range(1, nz):
        total = total + zland[k - 1].astype(F32)
    attn_ref[...] = total
    for k in range(1, nz):
        for n in range(2):
            turn_arrival(n, k).wait_recv()

    for copy in away:
        copy.wait_send()
    for r in range(1, ny):
        sm_y(r).wait_send()
        for k in range(nz):
            y_copy(r, k).wait_send()
    for k in range(1, nz):
        sm_z(k).wait_send()
        z_copy(k).wait_send()
        for n in range(2):
            turn_copy(n, k).wait_send()
    for n in range(2):
        for k in range(nz):
            core_copy(n, k).wait_send()
    down_copy.wait_send()
    for n in range(2):
        turn_near(n).wait()


VMEM = pl.BlockSpec(memory_space=pltpu.VMEM)
ANY = pl.BlockSpec(memory_space=pl.ANY)
DMA = pltpu.SemaphoreType.DMA


def per_device(
    ne, nz, sections,
    layer_input, cotangent, segments, routes, attn_gain, w_qkv, w_out, moe_gain, w_router, w_gate, w_up, w_down,
):
    ny = ne // 2
    micro, _, tokens, width = layer_input.shape
    total_experts = w_router.shape[2]
    hidden = w_gate.shape[3]
    owners = ("expert", "dp")
    shard = w_qkv.shape[1]
    place_e, place_d = lax.axis_index("expert"), lax.axis_index("dp")
    small = jnp.concatenate(
        [
            jnp.pad(w_router[0], ((0, 0), (0, ROUTER_ROWS - total_experts))),
            attn_gain[0][:, None],
            moe_gain[0][:, None],
            jnp.zeros((shard, SMALL_ROWS - ROUTER_ROWS - 2), BF16),
        ],
        1,
    )
    small = lax.all_gather(small, owners, axis=0, tiled=True).T
    wqkv = lax.all_gather(w_qkv[0], owners, axis=0, tiled=True)
    wout = lax.all_gather(w_out[0], owners, axis=0, tiled=True)
    routes_all = lax.all_gather(jnp.transpose(routes[0, :, 0], (0, 2, 1)), owners, axis=0)
    route = lax.dynamic_index_in_dim(
        routes_all.reshape((ne, nz) + routes_all.shape[1:]), place_d, 1, keepdims=False
    )
    cos, sin = rotary_tables(tokens)
    segs = segments[:, 0]
    segc, segr = segs[:, :, None], segs[:, None, :]
    x = layer_input[:, 0]
    cot = cotangent[:, 0]
    wg, wu, wd = w_gate[0], w_up[0], w_down[0]
    span = tokens // CHUNKS
    qkv_width = wqkv.shape[1]
    slice_h = hidden // nz
    half = 2 * slice_h
    at = place_d * slice_h
    slices = jnp.stack(
        [
            jnp.swapaxes(lax.dynamic_slice_in_dim(wg, at, slice_h, 2), 1, 2).reshape(half, width),
            jnp.swapaxes(lax.dynamic_slice_in_dim(wu, at, slice_h, 2), 1, 2).reshape(half, width),
            lax.dynamic_slice_in_dim(wd, at, slice_h, 1).reshape(half, width),
        ]
    )

    def shape(*dims, dtype=BF16):
        return jax.ShapeDtypeStruct(dims, dtype)

    weights = [pltpu.VMEM(w.shape, BF16) for w in (wqkv, wout, wg, wu, wd)]
    hop_sems = [DMA((micro, CHUNKS)) for _ in range(2)]
    block = width // ne

    def gather_sems(count):
        return [DMA((count, nz, ny)), DMA((count, nz, ny)), DMA((count, ny))]

    def returns(wide):
        return [
            pltpu.VMEM((tokens, wide), BF16),
            pltpu.VMEM((max(1, ny - 1), tokens, wide), BF16),
            pltpu.VMEM((max(1, ny - 1), tokens, wide), BF16),
            pltpu.VMEM((tokens, wide), BF16),
            pltpu.VMEM((max(1, ny - 1), tokens, wide), BF16),
            pltpu.VMEM((max(1, ny - 1), tokens, wide), BF16),
        ]

    out, hin, h1, qkv, obb, xm, gates, zf, partner = pl.pallas_call(
        functools.partial(forward_kernel, ny, nz, sections),
        out_shape=(
            shape(micro, tokens, width),
            shape(micro, tokens, width),
            shape(micro, tokens, width, dtype=F32),
            shape(micro, tokens, qkv_width),
            shape(micro, ne, tokens, block),
            shape(micro, ny, 2, tokens, width),
            shape(micro, ny, 2, ROUTER_ROWS, tokens, dtype=F32),
            shape(1, nz, ny, tokens, width),
            shape(3, half, width),
        ),
        in_specs=[VMEM] * 7 + [ANY] * 7,
        out_specs=tuple([VMEM] * 7 + [ANY] * 2),
        scratch_shapes=weights
        + [
            pltpu.VMEM((tokens, width), BF16),
            pltpu.VMEM((2, 2 * tokens, hidden), BF16),
            pltpu.VMEM((tokens, width), F32),
            pltpu.VMEM((span, width), F32),
        ]
        + returns(width)
        + [DMA((5,))]
        + gather_sems(1)
        + [DMA, DMA, DMA((ny,)), DMA((ny,))]
        + hop_sems
        + sem_shapes(micro, ny),
        compiler_params=pltpu.CompilerParams(
            collective_id=0, has_side_effects=True, vmem_limit_bytes=60 * 2**20
        ),
        name="layers_forward",
    )(x, segc, segr, route, small, cos, sin, cot, slices, wqkv, wout, wg, wu, wd)

    wide = width + 128
    every = (2, ny, 2, tokens, hidden)
    gin, grows, xab, dqkv, dattn, gsmall, zb = pl.pallas_call(
        functools.partial(backward_kernel, ny, nz, sections),
        out_shape=(
            shape(micro, tokens, width),
            shape(micro, ny, 2, tokens, width),
            shape(micro, ne, tokens, block),
            shape(micro, tokens, qkv_width),
            shape(micro, tokens, width),
            shape(SMALL_ROWS, width, dtype=F32),
            shape(2 * micro, nz, ny, tokens, width),
        ),
        in_specs=[VMEM] * 10 + [ANY] * 6,
        out_specs=tuple([VMEM] * 6 + [ANY]),
        scratch_shapes=weights
        + [
            pltpu.VMEM((ny, 2, tokens, width), BF16),
            pltpu.VMEM(every, BF16),
            pltpu.VMEM(every, BF16),
            pltpu.VMEM(every, BF16),
            pltpu.VMEM((2, 2 * tokens, hidden), BF16),
            pltpu.VMEM((2, 2 * tokens, hidden), BF16),
            pltpu.VMEM((tokens, wide), F32),
            pltpu.VMEM((span, wide), F32),
            pltpu.VMEM((tokens, width), F32),
            pltpu.VMEM((tokens, width), F32),
        ]
        + returns(wide)
        + [DMA((5,)), DMA]
        + gather_sems(2 * micro)
        + hop_sems
        + sem_shapes(micro, ny),
        compiler_params=pltpu.CompilerParams(
            collective_id=1, has_side_effects=True, vmem_limit_bytes=62 * 2**20
        ),
        name="layers_backward",
    )(cot, segc, segr, small, cos, sin, hin, h1, qkv, gates, xm, wqkv, wout, wg, wu, wd)

    span_z = max(1, min(nz, 1024 // (ny * tokens)))
    rows = span_z * ny * tokens
    padded = -(-shard // 16) * 16
    attn_width = qkv_width + width
    part = width // nz
    small_shape = (SMALL_ROWS, width)
    gate_g, up_g, down_g, attn_g, small_g = pl.pallas_call(
        functools.partial(tail_kernel, ny, nz, sections, span_z),
        out_shape=(
            shape(nz, part, half),
            shape(nz, part, half),
            shape(half, width),
            shape(padded, attn_width, dtype=F32),
            shape(*small_shape, dtype=F32),
        ),
        in_specs=[VMEM] * 3 + [ANY] * 8,
        out_specs=tuple([ANY] * 2 + [VMEM] * 3),
        scratch_shapes=[
            pltpu.VMEM((3, 2 * half, width), BF16),
            pltpu.VMEM((span_z, ny, tokens, width), BF16),
            pltpu.VMEM((span_z, ny, tokens, width), BF16),
            pltpu.VMEM((rows, 2 * half), BF16),
            pltpu.VMEM((rows, 2 * half), BF16),
            pltpu.VMEM((rows, 2 * half), BF16),
            pltpu.VMEM((width, 2 * half), F32),
            pltpu.VMEM((width, 2 * half), F32),
            pltpu.VMEM((2 * half, width), F32),
            pltpu.VMEM((2, nz, part, half), BF16),
            pltpu.VMEM((2, nz, part, half), BF16),
            pltpu.VMEM((half, width), BF16),
            pltpu.VMEM((half, width), BF16),
            pltpu.VMEM((ny, 2, micro, tokens, block), BF16),
            pltpu.VMEM((ny, 2, micro, tokens, block), BF16),
            pltpu.VMEM((2, micro, tokens, qkv_width), BF16),
            pltpu.VMEM((2, micro, tokens, width), BF16),
            pltpu.VMEM((nz, padded, attn_width), BF16),
            pltpu.VMEM((max(1, ny - 1), nz, padded, attn_width), BF16),
            pltpu.VMEM((max(1, ny - 1), nz, padded, attn_width), BF16),
            pltpu.VMEM((max(1, nz - 1), padded, attn_width), BF16),
            pltpu.VMEM((2,) + small_shape, F32),
            pltpu.VMEM((ny,) + small_shape, F32),
            pltpu.VMEM((nz,) + small_shape, F32),
            DMA((2,)), DMA((2,)),
            DMA((2 * ny * micro + 2,)), DMA((2 * ny * micro + 2,)), DMA((2 * ny * micro + 2,)),
            DMA((ny + nz,)), DMA((ny + nz,)),
            DMA((3, nz)), DMA((3, nz)),
            DMA((2, nz)), DMA((2, nz)),
            DMA((ny, nz)), DMA((ny, nz)),
            DMA((1, nz)), DMA((1, nz)),
        ],
        compiler_params=pltpu.CompilerParams(
            collective_id=2, has_side_effects=True, vmem_limit_bytes=62 * 2**20
        ),
        name="weight_gradients",
    )(routes_all, small, gsmall, zf, zb, slices, partner, xab, obb, dqkv, dattn)

    def unturned(value):
        value = value.reshape(nz, part, 2, slice_h)
        return jnp.transpose(value, (2, 1, 0, 3)).reshape(1, 2, part, hidden).astype(F32)

    mine = lax.dynamic_slice_in_dim(small_g, (place_e * nz + place_d) * shard, shard, 1)
    return (
        out[None, :, None],
        gin[None, :, None],
        mine[ROUTER_ROWS][None],
        attn_g[None, 0:shard, 0:qkv_width],
        attn_g[None, 0:shard, qkv_width:],
        mine[ROUTER_ROWS + 1][None],
        mine[0:total_experts].T[None],
        unturned(gate_g),
        unturned(up_g),
        down_g.reshape(1, 2, slice_h, width).astype(F32),
    )


def solution(mesh):
    owners = ("expert", "dp")
    return jax.shard_map(
        functools.partial(per_device, mesh.shape["expert"], mesh.shape["dp"], mesh.shape["section"]),
        mesh=mesh,
        in_specs=(
            P(None, owners, None, None),
            P(None, owners, None, None),
            P(None, owners, None),
            P("section", None, owners, None, None),
            P("section", owners),
            P("section", owners, None),
            P("section", owners, None),
            P("section", owners),
            P("section", owners, None),
            P("section", "expert", None, None),
            P("section", "expert", None, None),
            P("section", "expert", None, None),
        ),
        out_specs=(
            P("section", None, owners, None, None),
            P("section", None, owners, None, None),
            P("section", owners),
            P("section", owners, None),
            P("section", owners, None),
            P("section", owners),
            P("section", owners, None),
            P("section", "expert", "dp", None),
            P("section", "expert", "dp", None),
            P("section", "expert", "dp", None),
        ),
        check_vma=False,
    )
```

```python
import functools

import jax
import jax.numpy as jnp
import numpy as np
from jax import lax
from jax.experimental import pallas as pl
from jax.experimental.pallas import tpu as pltpu
from jax.sharding import PartitionSpec as P

HEAD = 128
QUERY_HEADS = 12
KEY_VALUE_HEADS = 2
GROUP = QUERY_HEADS // KEY_VALUE_HEADS
EPS = 1e-06
THETA = 1000000.0
NEGATIVE = -1e30
SCALE = HEAD ** (-0.5)
ROUTER_ROWS = 16
SMALL_ROWS = 32
FORWARD_CHUNKS = 2
BACKWARD_CHUNKS = 1
HOP_CHUNKS = 2
MESH = pl.DeviceIdType.MESH
F32 = jnp.float32
BF16 = jnp.bfloat16
GELU_C = float(np.sqrt(2.0 / np.pi))
GELU_A = 0.044715


def dot(a, b):
    return jnp.dot(a, b, preferred_element_type=F32)


def dot_nt(a, b):
    return lax.dot_general(a, b, (((1,), (1,)), ((), ())), preferred_element_type=F32)


def dot_tn(a, b):
    return lax.dot_general(a, b, (((0,), (0,)), ((), ())), preferred_element_type=F32)


def rotary_tables(tokens):
    places = np.arange(tokens, dtype=np.float64)
    inverse = THETA ** (-2.0 * np.arange(HEAD // 2, dtype=np.float64) / HEAD)
    angles = places[:, None] * inverse[None, :]
    cosine, sine = np.cos(angles), np.sin(angles)
    return (
        jnp.asarray(np.concatenate([cosine, cosine], 1), F32),
        jnp.asarray(np.concatenate([-sine, sine], 1), F32),
    )


def mask_bias(col, row):
    tokens = row.shape[1]
    ti = lax.broadcasted_iota(jnp.int32, (tokens, tokens), 0)
    ui = lax.broadcasted_iota(jnp.int32, (tokens, tokens), 1)
    return jnp.where((col == row) & (ui <= ti), 0.0, NEGATIVE).astype(F32)


def heads_of(value, first, count):
    return jnp.concatenate(
        [value[:, (first + i) * HEAD : (first + i + 1) * HEAD] for i in range(count)], 0
    )


def attention_shares(q6, k, bias6):
    scores = dot_nt(q6, k) * SCALE + bias6
    top = jnp.max(scores, -1, keepdims=True)
    raised = jnp.exp(scores - top)
    return raised / jnp.sum(raised, -1, keepdims=True)


class Place:
    def __init__(self, ny, nz):
        self.ny = ny
        self.nz = nz
        self.s = lax.axis_index("section")
        self.e = lax.axis_index("expert")
        self.d = lax.axis_index("dp")
        self.y = lax.div(self.e, 2)
        self.c = lax.rem(self.e, 2)
        self.core = (self.s, self.y * 2 + 1 - self.c, self.d)
        self.x = (1 - self.s, self.e, self.d)

    def ahead(self, r):
        return (self.s, lax.rem(self.y + r, self.ny) * 2 + self.c, self.d)

    def behind(self, r):
        return (self.s, lax.rem(self.y + self.ny - r, self.ny) * 2 + self.c, self.d)

    def pack(self, r, other):
        core = 1 - self.c if other else self.c
        return lax.rem(self.y + r, self.ny) * 2 + core

    def z_of(self, k):
        return lax.rem(self.d + k, self.nz)

    def z_ahead(self, k):
        return (self.s, self.e, self.z_of(k))

    def z_behind(self, k):
        return (self.s, self.e, self.z_of(self.nz - k))

    def greet(self, with_x=True):
        barrier = pltpu.get_barrier_semaphore()
        partners = [self.core] + ([self.x] if with_x else [])
        partners += [self.ahead(r) for r in range(1, self.ny)]
        partners += [self.z_ahead(k) for k in range(1, self.nz)]
        for partner in partners:
            pl.semaphore_signal(barrier, inc=1, device_id=partner, device_id_type=MESH)
        pl.semaphore_wait(barrier, len(partners))


def remote(src, dst, send, recv, device):
    return pltpu.make_async_remote_copy(
        src_ref=src, dst_ref=dst, send_sem=send, recv_sem=recv, device_id=device, device_id_type=MESH
    )


class Line:
    def __init__(self, place, slot, send, recv):
        self.place, self.slot, self.send, self.recv = place, slot, send, recv

    def origin(self, way, h):
        return self.place.d - h if way == 0 else self.place.d + h

    def comes(self, way, h):
        return self.place.d >= h if way == 0 else self.place.d + h < self.place.nz

    def leaves(self, way, h):
        d, nz = self.place.d, self.place.nz
        return (d + 1 < nz) & (d >= h - 1) if way == 0 else (d >= 1) & (d + h - 1 < nz)

    def out(self, way, h, src=None):
        g = self.place
        at = self.slot(self.origin(way, h - 1))
        next_door = (g.s, g.e, g.d + 1 if way == 0 else g.d - 1)
        return remote(at if src is None else src, at, self.send.at[way, h], self.recv.at[way, h], next_door)

    def came(self, way, h):
        g = self.place
        at = self.slot(self.origin(way, h))
        return remote(at, at, self.send.at[way, h], self.recv.at[way, h], g.core)

    def start(self, src):
        for way in range(2):
            @pl.when(self.leaves(way, 1))
            def _():
                self.out(way, 1, src).start()

    def step(self, h, then=None):
        for way in range(2):
            @pl.when(self.comes(way, h))
            def _():
                self.came(way, h).wait_recv()
                if h + 1 < self.place.nz:
                    @pl.when(self.leaves(way, h + 1))
                    def _():
                        self.out(way, h + 1).start()
                if then is not None:
                    then(way, h)

    def finish(self):
        for way in range(2):
            for h in range(1, self.place.nz):
                @pl.when(self.leaves(way, h))
                def _():
                    self.out(way, h).wait_send()


class Gather:
    def __init__(self, place, buf, send, recv, ysend, yrecv, local):
        self.place, self.buf, self.local = place, buf, local
        self.send, self.recv, self.ysend, self.yrecv = send, recv, ysend, yrecv

    def line(self, i, r):
        return Line(self.place, lambda zz: self.buf.at[i, zz, r], self.send.at[i, r], self.recv.at[i, r])

    def near(self, i, r, src):
        return pltpu.make_async_copy(src, self.buf.at[i, self.place.d, r], self.local.at[i, r])

    def across(self, i, way, h, r):
        at = self.line(i, 0).origin(way, h)
        return remote(
            self.buf.at[i, at, 0], self.buf.at[i, at, r],
            self.ysend.at[i, way, h, r], self.yrecv.at[i, way, h, r], self.place.behind(r),
        )

    def start(self, i, r, src, keep=True):
        if keep:
            self.near(i, r, src).start()
        self.line(i, r).start(src)

    def pass_one(self, i, way, h):
        for r in range(1, self.place.ny):
            self.across(i, way, h, r).start()

    def step(self, i, h, slots):
        for r in slots:
            self.line(i, r).step(h)

    def passes(self, i, early):
        line, d = self.line(i, 0), self.place.d
        for h in range(1, self.place.nz):
            for way in range(2):
                soon = (way == 0) | (d == 0) if h == 1 else False
                here = soon if early else jnp.logical_not(soon)

                @pl.when(line.comes(way, h) & here)
                def _():
                    self.pass_one(i, way, h)

    def pass_early(self, i):
        self.passes(i, True)

    def pass_rest(self, i):
        self.passes(i, False)

    def finish(self, i, slots, kept):
        g = self.place
        for r in kept:
            self.near(i, r, self.buf.at[i, g.d, r]).wait()
        for r in slots:
            self.line(i, r).finish()
        line = self.line(i, 0)
        for r in range(g.ny):
            if r not in slots:
                for h in range(1, g.nz):
                    for way in range(2):
                        @pl.when(line.comes(way, h))
                        def _():
                            self.across(i, way, h, r).wait()


class Exchange:
    def __init__(self, place, chunks, rows_ref, retl, retc, rety, sendl, sendc, sendy, sems):
        self.place, self.chunks = place, chunks
        self.rows_ref = rows_ref
        self.retl, self.retc, self.rety = retl, retc, rety
        self.sendl, self.sendc, self.sendy = sendl, sendc, sendy
        self.sems = sems
        self.tokens = rows_ref.shape[2]
        self.span = self.tokens // chunks

    def rows(self, q):
        return pl.ds(q * self.span, self.span)

    def core_own(self):
        g = self.place
        return remote(
            self.rows_ref.at[0, 0], self.rows_ref.at[0, 1], self.sems.cs.at[0, 0], self.sems.cr.at[0, 0], g.core
        )

    def y_own(self, r, q):
        g = self.place
        return remote(
            self.rows_ref.at[0, 0, self.rows(q)],
            self.rows_ref.at[r, 0, self.rows(q)],
            self.sems.ys.at[r, q],
            self.sems.yr.at[r, q],
            g.behind(r),
        )

    def forward(self, r, q):
        g = self.place
        return remote(
            self.rows_ref.at[r, 0, self.rows(q)],
            self.rows_ref.at[r, 1, self.rows(q)],
            self.sems.cs.at[r, q],
            self.sems.cr.at[r, q],
            g.core,
        )

    def back_local(self):
        return remote(self.sendl, self.retl, self.sems.bs.at[0, 0], self.sems.br.at[0, 0], self.place.core)

    def back_core(self, r, q):
        return remote(
            self.sendc.at[r - 1, self.rows(q)],
            self.retc.at[r - 1, self.rows(q)],
            self.sems.bs.at[r, q],
            self.sems.br.at[r, q],
            self.place.core,
        )

    def back_y(self, r, q):
        g = self.place
        return remote(
            self.sendy.at[r - 1, self.rows(q)],
            self.rety.at[g.ny - r - 1, self.rows(q)],
            self.sems.zs.at[r, q],
            self.sems.zr.at[g.ny - r, q],
            g.ahead(r),
        )

    def back_y_arrival(self, r, q):
        g = self.place
        return remote(
            self.sendy.at[r - 1, self.rows(q)],
            self.rety.at[r - 1, self.rows(q)],
            self.sems.zs.at[r, q],
            self.sems.zr.at[r, q],
            g.ahead(r),
        )

    def send_own(self):
        for q in range(self.chunks):
            for r in range(1, self.place.ny):
                self.y_own(r, q).start()
        self.core_own().start()

    def run(self, local_block, remote_block, complete, meanwhile=None):
        ny = self.place.ny
        items = [(r, q) for q in range(self.chunks) for r in range(1, ny)]
        self.core_own().wait_recv()
        local_block()
        self.back_local().start()

        def arrive(r, q):
            self.y_own(r, q).wait_recv()
            self.forward(r, q).start()
            if q == self.chunks - 1:
                complete(r)

        if items:
            arrive(*items[0])
        if meanwhile is not None:
            meanwhile()
        for i, (r, q) in enumerate(items):
            self.forward(r, q).wait_recv()
            own = remote_block(r, q)
            self.back_core(r, q).start()
            if i + 1 < len(items):
                arrive(*items[i + 1])
            self.back_core(r, q).wait_recv()
            here = self.rows(q)
            self.sendy[r - 1, here, :] = (own() + self.retc[r - 1, here, :].astype(F32)).astype(BF16)
            self.back_y(r, q).start()
        self.back_local().wait_recv()

    def arrived(self, q):
        for r in range(1, self.place.ny):
            self.back_y_arrival(r, q).wait_recv()

    def finish(self):
        ny = self.place.ny
        self.core_own().wait_send()
        self.back_local().wait_send()
        for q in range(self.chunks):
            for r in range(1, ny):
                self.y_own(r, q).wait_send()
                self.forward(r, q).wait_send()
                self.back_core(r, q).wait_send()
                self.back_y(r, q).wait_send()


class Sems:
    def __init__(self, refs, m):
        self.cs, self.cr, self.ys, self.yr, self.bs, self.br, self.zs, self.zr = [ref.at[m] for ref in refs]


def sem_shapes(micro, ny, chunks):
    return [pltpu.SemaphoreType.DMA((micro, ny, chunks)) for _ in range(8)]


def chosen_gates(logits_t, route):
    experts = lax.broadcasted_iota(jnp.int32, logits_t.shape, 0)
    chosen = route[0:1, :] == experts
    for k in range(1, route.shape[0]):
        chosen = chosen | (route[k : k + 1, :] == experts)
    masked = jnp.where(chosen, logits_t, NEGATIVE)
    raised = jnp.where(chosen, jnp.exp(masked - jnp.max(masked, 0, keepdims=True)), 0.0)
    return raised / jnp.sum(raised, 0, keepdims=True)


def gate_lanes(gates_t, expert):
    rows = lax.broadcasted_iota(jnp.int32, gates_t.shape, 0)
    one = jnp.sum(jnp.where(rows == expert, gates_t, 0.0), 0, keepdims=True)
    return jnp.transpose(jnp.broadcast_to(one, (128, one.shape[1])))


def widen(lanes, width):
    return jnp.concatenate([lanes] * (width // 128), 1)


def gather_kernel(
    ny, nz,
    small_ref, route_h, wqkv_h, wout_h, wg_h, wu_h, wd_h,
    small_t, route_o, wqkv_o, wout_o, slices_o, partner_o,
    small_s, wg, wu, turned,
    lsem, own_sem, cs, cr, ys, yr, zs, zr, sls, pls, plr,
):
    g = Place(ny, nz)
    hidden, width = turned.shape[2], turned.shape[3]
    slice_h = hidden // nz
    loads = [pltpu.make_async_copy(src, dst, lsem.at[i]) for i, (src, dst) in enumerate(((wg_h, wg), (wu_h, wu)))]
    for copy in loads:
        copy.start()
    g.greet(with_x=False)
    arrays = ((small_ref, small_s), (route_h, route_o), (wqkv_h, wqkv_o), (wout_h, wout_o))
    count = len(arrays)

    def near(n):
        src, dst = arrays[n]
        return pltpu.make_async_copy(src, dst.at[g.e, g.d], own_sem.at[n])

    lines = [Line(g, lambda zz, dst=dst: dst.at[g.e, zz], zs.at[n], zr.at[n]) for n, (_, dst) in enumerate(arrays)]

    def along_y(n, way, h, r):
        src, dst = arrays[n]
        at = dst.at[g.e, lines[n].origin(way, h)]
        return remote(src if h == 0 else at, at, ys.at[n, way, h, r], yr.at[n, way, h, r], g.behind(r))

    def to_core(n, way, h, r):
        src, dst = arrays[n]
        at = dst.at[g.pack(r, False), lines[n].origin(way, h)]
        own = h == 0 and r == 0
        return remote(src if own else at, at, cs.at[n, way, h, r], cr.at[n, way, h, r], g.core)

    for n in range(count):
        for r in range(1, ny):
            along_y(n, 0, 0, r).start()
        lines[n].start(arrays[n][0])
        near(n).start()
        to_core(n, 0, 0, 0).start()

    def got_z(n, h):
        def then(way, h):
            for r in range(1, ny):
                along_y(n, way, h, r).start()
            to_core(n, way, h, 0).start()

        lines[n].step(h, then)

    def got_y(n, h):
        for way in range(1 if h == 0 else 2):
            def pass_on():
                for r in range(1, ny):
                    along_y(n, way, h, r).wait_recv()
                    to_core(n, way, h, r).start()

            if h == 0:
                pass_on()
            else:
                pl.when(lines[n].comes(way, h))(pass_on)

    parts = []
    here = pl.ds(pl.multiple_of(g.d * slice_h, slice_h), slice_h)
    for i in range(3):
        for j in range(2):
            src = wd_h.at[j, here] if i == 2 else turned.at[i, j, here]
            to = slice(j * slice_h, (j + 1) * slice_h)
            parts.append(pltpu.make_async_copy(src, slices_o.at[i, to], sls.at[i, j]))
            parts.append(remote(src, partner_o.at[i, to], pls.at[i, j], plr.at[i, j], g.core))

    def turn(i, j, n):
        src = (wg, wu)[i]
        if j == 0 and n == 0:
            loads[i].wait()
        cols = slice(n * 256, (n + 1) * 256)
        turned[i, j, cols, :] = jnp.transpose(src[j, :, cols])

    turns = [(i, j, n) for i in range(2) for j in range(2) for n in range(hidden // 256)]

    z_items = [(n, h) for h in range(1, nz) for n in range(count)]
    y_items = [(n, 0) for n in range(count)] + z_items
    done = 0
    for i, item in enumerate(z_items):
        got_z(*item)
        if i % 2 == 1 or i >= count:
            got_y(*y_items[done])
            done += 1
        for piece in turns[:2]:
            turn(*piece)
        turns = turns[2:]
        if not turns and parts:
            for copy in parts:
                copy.start()
            started, parts = parts, []
    for item in y_items[done:]:
        got_y(*item)

    def each(act):
        for n in range(count):
            for h in range(nz):
                for way in range(1 if h == 0 else 2):
                    if h == 0:
                        act(n, way, h)
                    else:
                        pl.when(lines[n].comes(way, h))(lambda: act(n, way, h))

    def arrived(n, way, h):
        for r in range(ny):
            to_core(n, way, h, r).wait_recv()

    def sent(n, way, h):
        for r in range(ny):
            to_core(n, way, h, r).wait_send()
            if r:
                along_y(n, way, h, r).wait_send()

    each(arrived)
    for n in range(count):
        near(n).wait()
    gathered = small_s[...].reshape(width, small_s.shape[3])
    small_t[...] = jnp.transpose(gathered)[0:SMALL_ROWS].astype(BF16)
    each(sent)
    for line in lines:
        line.finish()
    for copy in started:
        copy.wait()


def forward_kernel(
    ny, nz, sections,
    x_ref, segc_ref, segr_ref, route_ref, small_ref, cos_ref, sin_ref,
    cot_h, wqkv_h, wout_h, wg_h, wu_h, wd_h,
    out_ref, hin_ref, h1_ref, qkv_ref, obb_ref, xm_ref, gates_ref, zf_h,
    wqkv, wout, wg, wu, wd, ob_s, hid, accl, accr, retl, retc, rety, sendl, sendc, sendy,
    wsem, zs, zr, zys, zyr, zl, gs, gr, xs, xr, *sem_refs,
):
    micro, tokens, width = x_ref.shape
    hidden = wg.shape[2]
    span = tokens // FORWARD_CHUNKS
    loads = [
        pltpu.make_async_copy(src, dst, wsem.at[i])
        for i, (src, dst) in enumerate([(wqkv_h, wqkv), (wout_h, wout), (wg_h, wg), (wu_h, wu), (wd_h, wd)])
    ]
    for load in loads:
        load.start()
    g = Place(ny, nz)
    g.greet()
    gain_a = small_ref[ROUTER_ROWS : ROUTER_ROWS + 1, :].astype(F32)
    gain_m = small_ref[ROUTER_ROWS + 1 : ROUTER_ROWS + 2, :].astype(F32)
    cos, sin = cos_ref[...], sin_ref[...]
    gather = Gather(g, zf_h, zs, zr, zys, zyr, zl)
    every = range(ny)
    first, last = g.s == 0, g.s == sections - 1

    def cot_copy(r):
        return remote(cot_h.at[0], zf_h.at[0, g.d, r], gs.at[r], gr.at[r], g.behind(r))

    @pl.when(last)
    def _():
        for r in range(1, ny):
            cot_copy(r).start()
        gather.start(0, 0, cot_h.at[0])
        for r in range(1, ny):
            cot_copy(r).wait_recv()
            gather.start(0, r, zf_h.at[0, g.d, r], keep=False)
        gather.step(0, 1, every)

    def hop(m, q):
        here = pl.ds(q * (tokens // HOP_CHUNKS), tokens // HOP_CHUNKS)
        return remote(out_ref.at[m, here], hin_ref.at[m, here], xs.at[m, q], xr.at[m, q], g.x)

    def experts(rows, lanes, keep):
        count = rows.shape[0]
        for j in range(2):
            for n in range(hidden // 256):
                cols = slice(n * 256, (n + 1) * 256)
                a = dot(rows, wg[j, :, cols])
                b = dot(rows, wu[j, :, cols])
                act = 0.5 * a * (1.0 + jnp.tanh(GELU_C * (a + GELU_A * a * a * a)))
                hid[j, 0:count, cols] = (act * b).astype(BF16)
        for n in range(width // 512):
            cols = slice(n * 512, (n + 1) * 512)
            total = None
            for j in range(2):
                eo = dot(hid[j, 0:count, :], wd[j, :, cols]).astype(BF16).astype(F32)
                term = widen(lanes[j], 512) * eo
                total = term if total is None else total + term
            keep(cols, total)

    def body(m, carry):
        @pl.when(g.s == 0)
        def _():
            hin_ref[m] = x_ref[m]

        @pl.when(g.s > 0)
        def _():
            for q in range(HOP_CHUNKS):
                hop(m, q).wait_recv()

        h = hin_ref[m].astype(F32)
        xa = (h * lax.rsqrt(jnp.mean(h * h, -1, keepdims=True) + EPS) * gain_a).astype(BF16)

        @pl.when(m == 0)
        def _():
            loads[0].wait()

        turned = QUERY_HEADS + KEY_VALUE_HEADS
        for i in range(wqkv.shape[1] // 256):
            mixed = dot(xa, wqkv[:, i * 256 : (i + 1) * 256])
            for half in range(2):
                head = 2 * i + half
                part = mixed[:, half * HEAD : (half + 1) * HEAD]
                if head < turned:
                    part = part * cos + pltpu.roll(part, HEAD // 2, 1) * sin
                qkv_ref[m, :, head * HEAD : (head + 1) * HEAD] = part.astype(BF16)
        bias = mask_bias(segc_ref[m], segr_ref[m])
        bias6 = jnp.concatenate([bias] * GROUP, 0)
        qkv = qkv_ref.at[m]
        for kv in range(KEY_VALUE_HEADS):
            q6 = heads_of(qkv, kv * GROUP, GROUP)
            k = heads_of(qkv, QUERY_HEADS + kv, 1)
            v = heads_of(qkv, turned + kv, 1)
            shares = attention_shares(q6, k, bias6).astype(BF16)
            o6 = dot(shares, v).astype(BF16)
            for i in range(GROUP):
                head = kv * GROUP + i
                ob_s[:, head * HEAD : (head + 1) * HEAD] = o6[i * tokens : (i + 1) * tokens]

        @pl.when(m == 0)
        def _():
            loads[1].wait()

        ob = ob_s[...]
        block = obb_ref.shape[3]
        for i in range(2 * ny):
            obb_ref[m, i] = ob[:, i * block : (i + 1) * block]
        for n in range(width // 512):
            cols = slice(n * 512, (n + 1) * 512)
            h1_ref[m, :, cols] = hin_ref[m, :, cols].astype(F32) + dot(ob, wout[:, cols])
        h1 = h1_ref[m]
        xm_ref[m, 0, 0] = (h1 * lax.rsqrt(jnp.mean(h1 * h1, -1, keepdims=True) + EPS) * gain_m).astype(BF16)

        ex = Exchange(g, FORWARD_CHUNKS, xm_ref.at[m], retl, retc, rety, sendl, sendc, sendy, Sems(sem_refs, m))
        ex.send_own()

        def complete(r):
            @pl.when(first & (m == 0))
            def _():
                gather.start(0, r, xm_ref.at[0, r, 0])

        def move(h):
            if h + 1 < nz:
                @pl.when(last & (m == 0))
                def _():
                    gather.step(0, h + 1, every)

            if h < nz:
                @pl.when(first & (m == 1))
                def _():
                    gather.step(0, h, every)

        complete(0)
        move(1)

        @pl.when(m == 0)
        def _():
            for load in loads[2:]:
                load.wait()

        def gates_for(r, other, here):
            rows = xm_ref[m, r, other, here, :]
            logits_t = dot_nt(small_ref[0:ROUTER_ROWS, :], rows)
            gates_t = chosen_gates(logits_t, route_ref[g.pack(r, other) * nz + g.d, m][:, here])
            return gates_t

        def lanes_of(blocks):
            return [
                jnp.concatenate([gate_lanes(gates_t, 2 * g.e + j) for gates_t in blocks], 0) for j in range(2)
            ]

        full = slice(0, tokens)

        def local_block():
            blocks = []
            for other in range(2):
                gates_t = gates_for(0, other, full)
                gates_ref[m, 0, other] = gates_t
                blocks.append(gates_t)

            def keep(cols, total):
                accl[:, cols] = total[0:tokens]
                sendl[:, cols] = total[tokens:].astype(BF16)

            experts(xm_ref[m, 0].reshape(2 * tokens, width), lanes_of(blocks), keep)

        def remote_block(r, q):
            here = slice(q * span, (q + 1) * span)
            blocks = []
            for other in range(2):
                gates_t = gates_for(r, other, here)
                gates_ref[m, r, other, :, here] = gates_t
                blocks.append(jnp.concatenate([gates_t] * (128 // span), 1))
            lanes = [
                jnp.concatenate([gate_lanes(gates_t, 2 * g.e + j)[0:span] for gates_t in blocks], 0)
                for j in range(2)
            ]

            def keep(cols, total):
                accr[:, cols] = total[0:span]
                sendc[r - 1, here, cols] = total[span:].astype(BF16)

            experts(xm_ref[m, r, :, here, :].reshape(2 * span, width), lanes, keep)
            return lambda: accr[...]

        ex.run(local_block, remote_block, complete)
        for q in range(HOP_CHUNKS):
            here = slice(q * span, (q + 1) * span)
            ex.arrived(q)
            total = h1_ref[m, here, :] + accl[here, :] + retl[here, :].astype(F32)
            for r in range(1, ny):
                total = total + rety[r - 1, here, :].astype(F32)
            out_ref[m, here, :] = total.astype(BF16)

            @pl.when(g.s < sections - 1)
            def _():
                hop(m, q).start()

        ex.finish()
        move(2)
        return carry

    lax.fori_loop(0, micro, body, 0)

    @pl.when(g.s < sections - 1)
    def _():
        for m in range(micro):
            for q in range(HOP_CHUNKS):
                hop(m, q).wait_send()

    @pl.when(first)
    def _():
        for h in range(3, nz):
            gather.step(0, h, every)
        gather.finish(0, every, every)

    @pl.when(last)
    def _():
        for r in range(1, ny):
            cot_copy(r).wait_send()
        for h in range(4, nz):
            gather.step(0, h, every)
        gather.finish(0, every, [0])


def backward_kernel(
    ny, nz, sections,
    cot_ref, segc_ref, segr_ref, small_ref, cos_ref, sin_ref,
    hin_ref, h1_ref, qkv_ref, gates_ref,
    xm_h, wqkv_h, wout_h, wg_h, wu_h, wd_h,
    gin_ref, grows_ref, xab_ref, dqkv_ref, dattn_ref, gsmall_ref, zb_h,
    wqkv, wout, wg, wu, wd, xm_s, hid, act_s, slope_s, da_s, db_s, accl, accr, dh1_s, n_s,
    retl, retc, rety, sendl, sendc, sendy,
    wsem, xmsem, zs, zr, zys, zyr, zl, xs, xr, *sem_refs,
):
    micro, tokens, width = cot_ref.shape
    hidden = wg.shape[2]
    span = tokens // BACKWARD_CHUNKS
    loads = [
        pltpu.make_async_copy(src, dst, wsem.at[i])
        for i, (src, dst) in enumerate([(wg_h, wg), (wu_h, wu), (wd_h, wd), (wout_h, wout), (wqkv_h, wqkv)])
    ]
    for load in loads:
        load.start()
    g = Place(ny, nz)
    g.greet()
    gain_a = small_ref[ROUTER_ROWS : ROUTER_ROWS + 1, :].astype(F32)
    gain_m = small_ref[ROUTER_ROWS + 1 : ROUTER_ROWS + 2, :].astype(F32)
    cos, sin = cos_ref[...], sin_ref[...]
    gsmall_ref[...] = jnp.zeros_like(gsmall_ref)
    gather = Gather(g, zb_h, zs, zr, zys, zyr, zl)
    every = range(ny)
    first, last = g.s == 0, g.s == sections - 1

    @pl.when(first)
    def _():
        for m in range(1, micro):
            for r in every:
                gather.start(micro + m, r, xm_h.at[m, r, 0])
            for h in range(1, nz):
                gather.step(micro + m, h, every)

    def hop(m, q):
        here = pl.ds(q * (tokens // HOP_CHUNKS), tokens // HOP_CHUNKS)
        return remote(gin_ref.at[m, here], grows_ref.at[m, 0, 0, here], xs.at[m, q], xr.at[m, q], g.x)

    def body(m, carry):
        load_xm = pltpu.make_async_copy(xm_h.at[m], xm_s, xmsem)
        load_xm.start()

        @pl.when(last)
        def _():
            grows_ref[m, 0, 0] = cot_ref[m]
            gather.start(m, 0, xm_h.at[m, 0, 0])
            for r in range(1, ny):
                gather.near(m, r, xm_h.at[m, r, 0]).start()

        @pl.when(g.s < sections - 1)
        def _():
            for q in range(HOP_CHUNKS):
                hop(m, q).wait_recv()

        ex = Exchange(g, BACKWARD_CHUNKS, grows_ref.at[m], retl, retc, rety, sendl, sendc, sendy, Sems(sem_refs, m))
        ex.send_own()

        def complete(r):
            src = grows_ref.at[m, r, 0]

            @pl.when(first)
            def _():
                if r == 0:
                    gather.start(m, 0, src)
                else:
                    gather.near(m, r, src).start()

        def move(hops):
            for h in hops:
                gather.step(m, h, [0])

        complete(0)

        @pl.when(m == 0)
        def _():
            for load in loads[:3]:
                load.wait()

        load_xm.wait()

        def again(r, _):
            rows = xm_s[r].reshape(2 * tokens, width)
            for j in range(2):
                for n in range(hidden // 256):
                    cols = slice(n * 256, (n + 1) * 256)
                    a = dot(rows, wg[j, :, cols])
                    b = dot(rows, wu[j, :, cols])
                    square = a * a
                    th = jnp.tanh(GELU_C * (a + GELU_A * square * a))
                    half = 0.5 * (1.0 + th)
                    act = a * half
                    slope = half + (0.5 * GELU_C) * a * (1.0 - th * th) * (1.0 + (3.0 * GELU_A) * square)
                    shape = (2, tokens, 256)
                    hid[j, r, :, :, cols] = (act * b).astype(BF16).reshape(shape)
                    act_s[j, r, :, :, cols] = act.astype(BF16).reshape(shape)
                    slope_s[j, r, :, :, cols] = (slope * b).astype(BF16).reshape(shape)
            return 0

        lax.fori_loop(0, ny, again, 0)

        def experts(rows, r, here, keep):
            count = 2 * (here.stop - here.start)
            part = slice(0, count)
            lane = lax.broadcasted_iota(jnp.int32, (count, 128), 1)
            gate_grads = jnp.zeros((count, 128), F32)
            for j in range(2):
                expert = 2 * g.e + j
                lanes = []
                for other in range(2):
                    gates_t = gates_ref[m, r, other]
                    lanes.append(gate_lanes(gates_t, expert)[here])
                lanes = widen(jnp.concatenate(lanes, 0), 256)
                summed = jnp.zeros((count, 1), F32)
                for n in range(hidden // 256):
                    cols = slice(n * 256, (n + 1) * 256)
                    u = dot_nt(rows, wd[j, cols, :])
                    inner = hid[j, r, :, here, cols].reshape(count, 256).astype(F32)
                    summed = summed + jnp.sum(u * inner, -1, keepdims=True)
                    u = u * lanes
                    slope = slope_s[j, r, :, here, cols].reshape(count, 256).astype(F32)
                    act = act_s[j, r, :, here, cols].reshape(count, 256).astype(F32)
                    da_s[j, part, cols] = (u * slope).astype(BF16)
                    db_s[j, part, cols] = (u * act).astype(BF16)
                high = summed.astype(BF16).astype(F32)
                gate_grads = jnp.where(lane == expert, high, gate_grads)
                gate_grads = jnp.where(lane == expert + 64, summed - high, gate_grads)
            for n in range(width // 512):
                cols = slice(n * 512, (n + 1) * 512)
                total = None
                for j in range(2):
                    term = dot_nt(da_s[j, part, :], wg[j, cols, :]) + dot_nt(db_s[j, part, :], wu[j, cols, :])
                    total = term if total is None else total + term
                keep(cols, total)
            keep(slice(width, width + 128), gate_grads)

        full = slice(0, tokens)

        def local_block():
            def keep(cols, total):
                accl[:, cols] = total[0:tokens]
                sendl[:, cols] = total[tokens:].astype(BF16)

            experts(grows_ref[m, 0].reshape(2 * tokens, width), 0, full, keep)

        def remote_block(r, q):
            here = slice(q * span, (q + 1) * span)

            def keep(cols, total):
                accr[:, cols] = total[0:span]
                sendc[r - 1, here, cols] = total[span:].astype(BF16)

            experts(grows_ref[m, r, :, here, :].reshape(2 * span, width), r, here, keep)
            return lambda: accr[...]

        def meanwhile():
            move(range(1, 2))

            @pl.when(first)
            def _():
                gather.pass_early(m)

        ex.run(local_block, remote_block, complete, meanwhile)
        move(range(2, min(3, nz)))
        for q in range(BACKWARD_CHUNKS):
            ex.arrived(q)
        total = accl[...] + retl[...].astype(F32)
        for r in range(1, ny):
            total = total + rety[r - 1].astype(F32)
        dgates = total[:, width:]
        dgates = dgates + pltpu.roll(dgates, 64, 1)
        gates_t = gates_ref[m, 0, 0]
        gates = jnp.transpose(
            jnp.concatenate([gates_t, jnp.zeros((128 - ROUTER_ROWS, tokens), F32)], 0)
        )
        dlog = gates * (dgates - jnp.sum(gates * dgates, -1, keepdims=True))
        dlog = dlog[:, 0:SMALL_ROWS]
        high = dlog.astype(BF16)
        low = (dlog - high.astype(F32)).astype(BF16)
        router = small_ref[...]
        dxm = total[:, 0:width] + dot(high, router) + dot(low, router)
        xm = xm_s[0, 0]
        gsmall_ref[0:ROUTER_ROWS, :] += (dot_tn(high, xm) + dot_tn(low, xm))[0:ROUTER_ROWS]
        h1 = h1_ref[m]
        rinv = lax.rsqrt(jnp.mean(h1 * h1, -1, keepdims=True) + EPS)
        n2 = h1 * rinv
        gsmall_ref[ROUTER_ROWS + 1 : ROUTER_ROWS + 2, :] += jnp.sum(dxm * n2, 0, keepdims=True)
        scaled = dxm * gain_m
        dh1 = grows_ref[m, 0, 0].astype(F32) + rinv * (scaled - n2 * jnp.mean(scaled * n2, -1, keepdims=True))
        dh1_s[...] = dh1
        dattn = dh1.astype(BF16)
        dattn_ref[m] = dattn

        @pl.when(m == 0)
        def _():
            for load in loads[3:]:
                load.wait()

        @pl.when(first)
        def _():
            move(range(3, nz))
            gather.pass_rest(m)

        bias = mask_bias(segc_ref[m], segr_ref[m])
        bias6 = jnp.concatenate([bias] * GROUP, 0)
        qkv = qkv_ref.at[m]
        turned = QUERY_HEADS + KEY_VALUE_HEADS

        def unturn(part):
            return part * cos - pltpu.roll(part, HEAD // 2, 1) * sin

        for kv in range(KEY_VALUE_HEADS):
            wide = GROUP * HEAD
            dob = dot_nt(dattn, wout[kv * wide : (kv + 1) * wide, :]).astype(BF16)
            dob6 = heads_of(dob, 0, GROUP)
            q6 = heads_of(qkv, kv * GROUP, GROUP)
            k = heads_of(qkv, QUERY_HEADS + kv, 1)
            v = heads_of(qkv, turned + kv, 1)
            shares = attention_shares(q6, k, bias6)
            dshares = dot_nt(dob6, v)
            dv = dot_tn(shares.astype(BF16), dob6)
            ds = (shares * (dshares - jnp.sum(shares * dshares, -1, keepdims=True))).astype(BF16)
            dq6 = dot(ds, k) * SCALE
            dk = dot_tn(ds, q6) * SCALE
            for i in range(GROUP):
                head = kv * GROUP + i
                dqkv_ref[m, :, head * HEAD : (head + 1) * HEAD] = unturn(
                    dq6[i * tokens : (i + 1) * tokens]
                ).astype(BF16)
            head = QUERY_HEADS + kv
            dqkv_ref[m, :, head * HEAD : (head + 1) * HEAD] = unturn(dk).astype(BF16)
            head = turned + kv
            dqkv_ref[m, :, head * HEAD : (head + 1) * HEAD] = dv.astype(BF16)

        h = hin_ref[m].astype(F32)
        rinv = lax.rsqrt(jnp.mean(h * h, -1, keepdims=True) + EPS)
        n1 = h * rinv
        xa = (n1 * gain_a).astype(BF16)
        block = xab_ref.shape[3]
        for i in range(2 * ny):
            xab_ref[m, i] = xa[:, i * block : (i + 1) * block]
        n_s[...] = n1
        dqkv = dqkv_ref[m]
        for n in range(width // 512):
            cols = slice(n * 512, (n + 1) * 512)
            accl[:, cols] = dot_nt(dqkv, wqkv[cols, :])
        dxa = accl[:, 0:width]
        n1 = n_s[...]
        gsmall_ref[ROUTER_ROWS : ROUTER_ROWS + 1, :] += jnp.sum(dxa * n1, 0, keepdims=True)
        scaled = dxa * gain_a
        grad = dh1_s[...] + rinv * (scaled - n1 * jnp.mean(scaled * n1, -1, keepdims=True))
        gin_ref[m] = grad.astype(BF16)

        @pl.when(g.s > 0)
        def _():
            for q in range(HOP_CHUNKS):
                hop(m, q).start()
            move(range(3, nz))

        ex.finish()
        return carry

    lax.fori_loop(0, micro, body, 0)

    @pl.when(g.s > 0)
    def _():
        for m in range(micro):
            for q in range(HOP_CHUNKS):
                hop(m, q).wait_send()

    @pl.when(last)
    def _():
        for m in range(micro):
            gather.pass_early(m)
            gather.pass_rest(m)
        for m in range(1, micro):
            for r in every:
                gather.start(micro + m, r, grows_ref.at[m, r, 0])
            for h in range(1, nz):
                gather.step(micro + m, h, every)

    for m in range(micro):
        gather.finish(m, [0], every)
    for m in range(1, micro):
        gather.finish(micro + m, every, every)


def tail_kernel(
    ny, nz, sections, span,
    route_ref, small_ref, gsmall_ref,
    zf_h, zb_h, slices_h, partner_h, xab_h, obb_h, dqkv_h, dattn_h,
    gate_ref, up_ref, down_ref, attn_ref, small_out,
    w4, x_s, g_s, da_s, db_s, gh_s, acc_g, acc_u, acc_d, csend, cland, dsend, dland,
    xa_s, ob_s, dq_s, dt_s, own_s, ysend, yland, zland, sm_s, smy, smz,
    wsem, xsem, asem, as_, ar, ss, sr, cs, cr, ts, tr, ys, yr, zs, zr,
):
    micro, tokens, width = dqkv_h.shape[0], zf_h.shape[3], zf_h.shape[4]
    half = slices_h.shape[1]
    slice_h = half // 2
    both = 2 * half
    tile = 256 if both % 256 == 0 else 128
    qkv_width = dqkv_h.shape[2]
    shard = width // (2 * ny * nz)
    part = width // nz
    rows = span * ny * tokens
    groups = nz // span
    g = Place(ny, nz)
    first = g.s == 0
    mine = [pltpu.make_async_copy(src, w4.at[:, i * half : (i + 1) * half], wsem.at[i])
            for i, src in enumerate((slices_h, partner_h))]

    def load(i):
        m, k = lax.div(i, groups), pl.ds(lax.rem(i, groups) * span, span)
        early = [(first, x_s, 0), (jnp.logical_not(first), g_s, 1)]
        late = [(first, g_s, 1), (jnp.logical_not(first), x_s, 0)]
        copies = [(when, pltpu.make_async_copy(zb_h.at[m, k], dst, xsem.at[n])) for when, dst, n in late]
        for when, dst, n in early:
            copies.append((when & (m == 0), pltpu.make_async_copy(zf_h.at[0, k], dst, xsem.at[n])))
            copies.append((when & (m > 0), pltpu.make_async_copy(zb_h.at[micro + m, k], dst, xsem.at[n])))
        return copies

    def start_load(i):
        for when, copy in load(i):
            @pl.when(when)
            def _():
                copy.start()

    def wait_load():
        pltpu.make_async_copy(zf_h.at[0, pl.ds(0, span)], x_s, xsem.at[0]).wait()
        pltpu.make_async_copy(zf_h.at[0, pl.ds(0, span)], g_s, xsem.at[1]).wait()

    for copy in mine:
        copy.start()
    start_load(0)
    g.greet(with_x=False)

    away, here = [], []
    for m in range(micro):
        for yy in range(ny):
            other = yy * 2 + 1 - g.c
            own = yy * 2 + g.c
            for n, (src, dst) in enumerate(((xab_h, xa_s), (obb_h, ob_s))):
                i = (m * ny + yy) * 2 + n
                away.append(remote(src.at[m, other], dst.at[yy, 1, m], as_.at[i], ar.at[i], g.core))
                here.append(pltpu.make_async_copy(src.at[m, own], dst.at[yy, 0, m], asem.at[i]))
    base = 2 * ny * micro
    for n, (src, dst) in enumerate(((dqkv_h, dq_s), (dattn_h, dt_s))):
        i = base + n
        away.append(remote(src, dst.at[1], as_.at[i], ar.at[i], g.core))
        here.append(pltpu.make_async_copy(src, dst.at[0], asem.at[i]))
    for copy in away + here:
        copy.start()
    sm_core = remote(gsmall_ref, sm_s.at[1], ss.at[0], sr.at[0], g.core)
    sm_core.start()

    def sm_y(r):
        return remote(sm_s.at[0], smy.at[ny - r], ss.at[r], sr.at[ny - r], g.ahead(r))

    def sm_y_arrival(r):
        return remote(sm_s.at[0], smy.at[r], ss.at[r], sr.at[r], g.ahead(r))

    def sm_z(k):
        return remote(sm_s.at[1], smz.at[k], ss.at[ny + k], sr.at[ny + k], g.z_behind(k))

    for copy in away:
        copy.wait_recv()
    for copy in here:
        copy.wait()

    count = 2 * micro * tokens

    def attn_rows(yy, dst):
        for src, grad, at in ((xa_s, dq_s, 0), (ob_s, dt_s, qkv_width)):
            left = src[yy].reshape(count, shard * nz)
            wide = grad.shape[3]
            for n in range(wide // 512):
                cols = slice(n * 512, (n + 1) * 512)
                got = dot_tn(left, grad[:, :, :, cols].reshape(count, 512)).astype(BF16)
                for zi in range(nz):
                    dst[zi, 0:shard, at + n * 512 : at + (n + 1) * 512] = got[zi * shard : (zi + 1) * shard]

    def flipped(mask):
        place = g.d
        for b in range(nz.bit_length()):
            if mask >> b & 1:
                place = place + (1 << b) - (2 << b) * lax.rem(lax.div(g.d, 1 << b), 2)
        return place

    def y_copy(r, k):
        zi = flipped(k)
        return remote(ysend.at[r - 1, zi], yland.at[ny - r - 1, zi], ys.at[r, k], yr.at[ny - r, k], g.ahead(r))

    def y_arrival(r, k):
        zi = flipped(k)
        return remote(ysend.at[r - 1, zi], yland.at[r - 1, zi], ys.at[r, k], yr.at[r, k], g.ahead(r))

    order = list(range(1, nz)) + [0]
    masks = list(range(nz - 1, -1, -1))

    def y_start(k):
        for r in range(1, ny):
            y_copy(r, k).start()

    for r in range(1, ny):
        attn_rows(lax.rem(g.y + r, ny), ysend.at[r - 1])
    y_start(masks[0])
    sm_core.wait_recv()
    sm_s[0] = gsmall_ref[...] + sm_s[1]
    sm_core.wait_send()
    for r in range(1, ny):
        sm_y(r).start()
    attn_rows(g.y, own_s)

    bits = nz.bit_length() - 1

    def low(mask):
        return (mask & -mask).bit_length() - 1 if mask else bits

    landings = [(mask, b) for mask in range(nz) for b in range(low(mask))]

    def z_copy(mask):
        b = low(mask)
        at = landings.index((mask - (1 << b), b))
        device = (g.s, g.e, flipped(1 << b))
        return remote(own_s.at[flipped(mask)], zland.at[at], zs.at[0, mask], zr.at[0, at], device)

    def z_arrival(mask, b):
        at = landings.index((mask, b))
        device = (g.s, g.e, flipped(1 << b))
        return remote(own_s.at[flipped(mask)], zland.at[at], zs.at[0, mask], zr.at[0, at], device)

    def advance(mask):
        for r in range(1, ny):
            y_arrival(r, mask).wait_recv()
        zi = flipped(mask)
        for b in range(low(mask)):
            z_arrival(mask, b).wait_recv()
        for n in range((qkv_width + width) // 512):
            cols = slice(n * 512, (n + 1) * 512)
            total = own_s[zi, :, cols].astype(F32)
            for r in range(1, ny):
                total = total + yland[r - 1, zi, :, cols].astype(F32)
            for b in range(low(mask)):
                total = total + zland[landings.index((mask, b)), :, cols].astype(F32)
            if mask:
                own_s[zi, :, cols] = total.astype(BF16)
            else:
                attn_ref[:, cols] = total
        if mask:
            z_copy(mask).start()

    for copy in mine:
        copy.wait()
    acc_g[...] = jnp.zeros_like(acc_g)
    acc_u[...] = jnp.zeros_like(acc_u)
    acc_d[...] = jnp.zeros_like(acc_d)
    column = lax.broadcasted_iota(jnp.int32, (ROUTER_ROWS, both), 1)
    expert = lax.broadcasted_iota(jnp.int32, (ROUTER_ROWS, both), 0)
    owner = jnp.where(column < half, g.e, 2 * g.y + 1 - g.c)
    local = jnp.where(column < half, column, column - half)
    chosen = 2 * owner + jnp.where(local < slice_h, 0, 1)
    spread = jnp.where(expert == chosen, 1.0, 0.0).astype(BF16)

    blocks = span * ny
    total_blocks = micro * groups * blocks
    polls = (total_blocks * 7 // 16, total_blocks * 10 // 16)

    def group(i, carry):
        m = lax.div(i, groups)
        wait_load()

        def block(b, carry):
            k = lax.rem(i, groups) * span + lax.div(b, ny)
            r = lax.rem(b, ny)
            place = (lax.rem(g.y + r, ny) * 2 + g.c) * nz + k
            x = x_s[lax.div(b, ny), r]
            gr = g_s[lax.div(b, ny), r]
            gates_t = chosen_gates(dot_nt(small_ref[0:ROUTER_ROWS, :], x), route_ref[place, m])
            high = gates_t.astype(BF16)
            low = (gates_t - high.astype(F32)).astype(BF16)
            here = pl.ds(pl.multiple_of(b * tokens, tokens), tokens)
            for n in range(both // tile):
                cols = slice(n * tile, (n + 1) * tile)
                a = dot_nt(x, w4[0, cols])
                bb = dot_nt(x, w4[1, cols])
                gate = dot_tn(high, spread[:, cols]) + dot_tn(low, spread[:, cols])
                u = dot_nt(gr, w4[2, cols]) * gate
                square = a * a
                th = jnp.tanh(GELU_C * (a + GELU_A * square * a))
                hf = 0.5 * (1.0 + th)
                act = a * hf
                slope = hf + (0.5 * GELU_C) * a * (1.0 - th * th) * (1.0 + (3.0 * GELU_A) * square)
                da_s[here, cols] = (u * slope * bb).astype(BF16)
                db_s[here, cols] = (u * act).astype(BF16)
                gh_s[here, cols] = ((act * bb).astype(BF16).astype(F32) * gate).astype(BF16)
            for n, poll in enumerate(polls):
                @pl.when(i * blocks + b == poll - 1)
                def _():
                    y_start(masks[n + 1])

                @pl.when(i * blocks + b == poll)
                def _():
                    advance(masks[n])

            return carry

        lax.fori_loop(0, blocks, block, 0)

        def columns(n, carry):
            cols = pl.ds(pl.multiple_of(n * 256, 256), 256)
            x = x_s[:, :, :, cols].reshape(rows, 256)
            acc_g[cols, :] += dot_tn(x, da_s[...])
            acc_u[cols, :] += dot_tn(x, db_s[...])
            acc_d[:, cols] += dot_tn(gh_s[...], g_s[:, :, :, cols].reshape(rows, 256))
            return carry

        lax.fori_loop(0, width // 256, columns, 0)

        @pl.when(i + 1 < micro * groups)
        def _():
            start_load(i + 1)

        return carry

    lax.fori_loop(0, micro * groups, group, 0)
    for mask in masks[3:]:
        y_start(mask)
    for mask in masks[2:-1]:
        advance(mask)

    def core_copy(n, k):
        return remote(csend.at[n, k], cland.at[n, k], cs.at[n, k], cr.at[n, k], g.core)

    def turn_copy(n, k):
        dst = (gate_ref, up_ref)[n]
        return remote(cland.at[n, k], dst.at[g.d], ts.at[n, k], tr.at[n, k], g.z_ahead(k))

    def turn_near(n):
        return pltpu.make_async_copy(cland.at[n, 0], (gate_ref, up_ref)[n].at[g.d], ts.at[n, 0])

    def turn_arrival(n, k):
        dst = (gate_ref, up_ref)[n]
        return remote(cland.at[n, k], dst.at[g.z_of(nz - k)], ts.at[n, k], tr.at[n, k], g.z_behind(k))

    def width_rows(k):
        return pl.ds(pl.multiple_of(g.z_of(k) * part, part), part)

    down_copy = remote(dsend, dland, cs.at[2, 0], cr.at[2, 0], g.core)
    accs = (acc_g, acc_u)
    for n in range(2):
        for k in order:
            csend[n, k] = accs[n][width_rows(k), half:both].astype(BF16)
            core_copy(n, k).start()
    dsend[...] = acc_d[half:both, :].astype(BF16)
    down_copy.start()
    for k in order[:-1]:
        for n in range(2):
            core_copy(n, k).wait_recv()
            total = accs[n][width_rows(k), 0:half] + cland[n, k].astype(F32)
            cland[n, k] = total.astype(BF16)
            turn_copy(n, k).start()
    for n in range(2):
        core_copy(n, 0).wait_recv()
        cland[n, 0] = (accs[n][width_rows(0), 0:half] + cland[n, 0].astype(F32)).astype(BF16)
        turn_near(n).start()
    down_copy.wait_recv()
    dland[...] = (acc_d[0:half, :] + dland[...].astype(F32)).astype(BF16)
    down_near = pltpu.make_async_copy(dland, down_ref, ts.at[0, nz])
    down_near.start()

    for r in range(1, ny):
        sm_y_arrival(r).wait_recv()
    total = sm_s[0]
    for r in range(1, ny):
        total = total + smy[r]
    sm_s[1] = total
    for k in range(1, nz):
        sm_z(k).start()
    for k in range(1, nz):
        sm_z(k).wait_recv()
        total = total + smz[k]
    small_out[...] = total

    advance(0)
    for k in range(1, nz):
        for n in range(2):
            turn_arrival(n, k).wait_recv()

    for copy in away:
        copy.wait_send()
    for r in range(1, ny):
        sm_y(r).wait_send()
        for k in range(nz):
            y_copy(r, k).wait_send()
    for k in range(1, nz):
        sm_z(k).wait_send()
        z_copy(k).wait_send()
        for n in range(2):
            turn_copy(n, k).wait_send()
    for n in range(2):
        for k in range(nz):
            core_copy(n, k).wait_send()
    down_copy.wait_send()
    for n in range(2):
        turn_near(n).wait()
    down_near.wait()


def finish_kernel(nz, experts, gate_in, up_in, down_in, attn_in, small_in, gate, up, down, qkv, out, router, again, mgain):
    slice_h = gate_in.shape[2] // 2
    for src, dst in ((gate_in, gate), (up_in, up)):
        for j in range(2):
            cols = slice(j * slice_h, (j + 1) * slice_h)
            dst[0, j] = jnp.concatenate([src[z, :, cols].astype(F32) for z in range(nz)], 1)
    down[0, 0] = down_in[...].astype(F32)
    shard, split = qkv.shape[1], qkv.shape[2]
    qkv[0] = attn_in[0:shard, 0:split]
    out[0] = attn_in[0:shard, split:]
    rows, width = small_in.shape
    base = (lax.axis_index("expert") * nz + lax.axis_index("dp")) * shard
    at = lax.broadcasted_iota(jnp.int32, (width, 128), 0)
    lane = lax.broadcasted_iota(jnp.int32, (width, 128), 1)
    pick = jnp.where(at == base + lane, 1.0, 0.0).astype(F32)
    got = jnp.dot(small_in[...], pick, precision=lax.Precision.HIGHEST, preferred_element_type=F32)
    again[...] = got[ROUTER_ROWS : ROUTER_ROWS + 1, 0:shard]
    mgain[...] = got[ROUTER_ROWS + 1 : ROUTER_ROWS + 2, 0:shard]
    turned = jnp.transpose(jnp.concatenate([got, jnp.zeros((128 - rows, 128), F32)], 0))
    router[0] = turned[0:shard, 0:experts]


VMEM = pl.BlockSpec(memory_space=pltpu.VMEM)
ANY = pl.BlockSpec(memory_space=pl.ANY)
DMA = pltpu.SemaphoreType.DMA


def per_device(
    ne, nz, sections,
    layer_input, cotangent, segments, routes, attn_gain, w_qkv, w_out, moe_gain, w_router, w_gate, w_up, w_down,
):
    ny = ne // 2
    micro, _, tokens, width = layer_input.shape
    total_experts = w_router.shape[2]
    hidden = w_gate.shape[3]
    owners = ("expert", "dp")
    shard = w_qkv.shape[1]
    place_e, place_d = lax.axis_index("expert"), lax.axis_index("dp")
    small = jnp.concatenate(
        [
            w_router[0],
            jnp.zeros((shard, ROUTER_ROWS - total_experts), BF16),
            attn_gain[0][:, None],
            moe_gain[0][:, None],
            jnp.zeros((shard, 128 - ROUTER_ROWS - 2), BF16),
        ],
        1,
    ).astype(F32)
    own_routes = jnp.transpose(routes[0, :, 0], (0, 2, 1))
    cos, sin = rotary_tables(tokens)
    segs = segments[:, 0]
    segc, segr = segs[:, :, None], segs[:, None, :]
    x = layer_input[:, 0]
    cot = cotangent[:, 0]
    wg, wu, wd = w_gate[0], w_up[0], w_down[0]
    qkv_width = w_qkv.shape[2]
    slice_h = hidden // nz
    half = 2 * slice_h

    def shape(*dims, dtype=BF16):
        return jax.ShapeDtypeStruct(dims, dtype)

    grid_sems = [DMA((4, 2, nz, ny)) for _ in range(4)]
    small, routes_all, wqkv, wout, slices, partner = pl.pallas_call(
        functools.partial(gather_kernel, ny, nz),
        out_shape=(
            shape(SMALL_ROWS, width),
            shape(ne, nz, *own_routes.shape, dtype=jnp.int32),
            shape(ne, nz, shard, qkv_width),
            shape(ne, nz, shard, width),
            shape(3, half, width),
            shape(3, half, width),
        ),
        in_specs=[VMEM] + [ANY] * 6,
        out_specs=tuple([VMEM] + [ANY] * 5),
        scratch_shapes=[
            pltpu.VMEM((ne, nz, shard, 128), F32),
            pltpu.VMEM(wg.shape, BF16),
            pltpu.VMEM(wu.shape, BF16),
            pltpu.VMEM((2, 2, hidden, width), BF16),
            DMA((2,)), DMA((4,)),
        ]
        + grid_sems
        + [DMA((4, 2, nz)), DMA((4, 2, nz)), DMA((3, 2)), DMA((3, 2)), DMA((3, 2))],
        compiler_params=pltpu.CompilerParams(
            collective_id=3, has_side_effects=True, vmem_limit_bytes=60 * 2**20
        ),
        name="gather_weights",
    )(small, own_routes, w_qkv[0], w_out[0], wg, wu, wd)
    wqkv = wqkv.reshape(width, qkv_width)
    wout = wout.reshape(width, width)
    routes_all = routes_all.reshape((ne * nz,) + own_routes.shape)
    weights = [pltpu.VMEM(w.shape, BF16) for w in (wqkv, wout, wg, wu, wd)]
    hop_sems = [DMA((micro, HOP_CHUNKS)) for _ in range(2)]
    block = width // ne

    def gather_sems(count):
        return [DMA((count, ny, 2, nz))] * 2 + [DMA((count, 2, nz, ny))] * 2 + [DMA((count, ny))]

    def returns(wide):
        return [
            pltpu.VMEM((tokens, wide), BF16),
            pltpu.VMEM((max(1, ny - 1), tokens, wide), BF16),
            pltpu.VMEM((max(1, ny - 1), tokens, wide), BF16),
            pltpu.VMEM((tokens, wide), BF16),
            pltpu.VMEM((max(1, ny - 1), tokens, wide), BF16),
            pltpu.VMEM((max(1, ny - 1), tokens, wide), BF16),
        ]

    out, hin, h1, qkv, obb, xm, gates, zf = pl.pallas_call(
        functools.partial(forward_kernel, ny, nz, sections),
        out_shape=(
            shape(micro, tokens, width),
            shape(micro, tokens, width),
            shape(micro, tokens, width, dtype=F32),
            shape(micro, tokens, qkv_width),
            shape(micro, ne, tokens, block),
            shape(micro, ny, 2, tokens, width),
            shape(micro, ny, 2, ROUTER_ROWS, tokens, dtype=F32),
            shape(1, nz, ny, tokens, width),
        ),
        in_specs=[VMEM] * 7 + [ANY] * 6,
        out_specs=tuple([VMEM] * 7 + [ANY]),
        scratch_shapes=weights
        + [
            pltpu.VMEM((tokens, width), BF16),
            pltpu.VMEM((2, 2 * tokens, hidden), BF16),
            pltpu.VMEM((tokens, width), F32),
            pltpu.VMEM((tokens // FORWARD_CHUNKS, width), F32),
        ]
        + returns(width)
        + [DMA((5,))]
        + gather_sems(1)
        + [DMA((ny,)), DMA((ny,))]
        + hop_sems
        + sem_shapes(micro, ny, FORWARD_CHUNKS),
        compiler_params=pltpu.CompilerParams(
            collective_id=0, has_side_effects=True, vmem_limit_bytes=60 * 2**20
        ),
        name="layers_forward",
    )(x, segc, segr, routes_all, small, cos, sin, cot, wqkv, wout, wg, wu, wd)

    wide = width + 128
    every = (2, ny, 2, tokens, hidden)
    gin, grows, xab, dqkv, dattn, gsmall, zb = pl.pallas_call(
        functools.partial(backward_kernel, ny, nz, sections),
        out_shape=(
            shape(micro, tokens, width),
            shape(micro, ny, 2, tokens, width),
            shape(micro, ne, tokens, block),
            shape(micro, tokens, qkv_width),
            shape(micro, tokens, width),
            shape(SMALL_ROWS, width, dtype=F32),
            shape(2 * micro, nz, ny, tokens, width),
        ),
        in_specs=[VMEM] * 10 + [ANY] * 6,
        out_specs=tuple([VMEM] * 6 + [ANY]),
        scratch_shapes=weights
        + [
            pltpu.VMEM((ny, 2, tokens, width), BF16),
            pltpu.VMEM(every, BF16),
            pltpu.VMEM(every, BF16),
            pltpu.VMEM(every, BF16),
            pltpu.VMEM((2, 2 * tokens, hidden), BF16),
            pltpu.VMEM((2, 2 * tokens, hidden), BF16),
            pltpu.VMEM((tokens, wide), F32),
            pltpu.VMEM((tokens // BACKWARD_CHUNKS, wide), F32),
            pltpu.VMEM((tokens, width), F32),
            pltpu.VMEM((tokens, width), F32),
        ]
        + returns(wide)
        + [DMA((5,)), DMA]
        + gather_sems(2 * micro)
        + hop_sems
        + sem_shapes(micro, ny, BACKWARD_CHUNKS),
        compiler_params=pltpu.CompilerParams(
            collective_id=1, has_side_effects=True, vmem_limit_bytes=62 * 2**20
        ),
        name="layers_backward",
    )(cot, segc, segr, small, cos, sin, hin, h1, qkv, gates, xm, wqkv, wout, wg, wu, wd)

    span_z = max(1, min(nz, 1024 // (ny * tokens)))
    rows = span_z * ny * tokens
    padded = -(-shard // 16) * 16
    attn_width = qkv_width + width
    part = width // nz
    small_shape = (SMALL_ROWS, width)
    gate_g, up_g, down_g, attn_g, small_g = pl.pallas_call(
        functools.partial(tail_kernel, ny, nz, sections, span_z),
        out_shape=(
            shape(nz, part, half),
            shape(nz, part, half),
            shape(half, width),
            shape(padded, attn_width, dtype=F32),
            shape(*small_shape, dtype=F32),
        ),
        in_specs=[VMEM] * 3 + [ANY] * 8,
        out_specs=tuple([ANY] * 3 + [VMEM] * 2),
        scratch_shapes=[
            pltpu.VMEM((3, 2 * half, width), BF16),
            pltpu.VMEM((span_z, ny, tokens, width), BF16),
            pltpu.VMEM((span_z, ny, tokens, width), BF16),
            pltpu.VMEM((rows, 2 * half), BF16),
            pltpu.VMEM((rows, 2 * half), BF16),
            pltpu.VMEM((rows, 2 * half), BF16),
            pltpu.VMEM((width, 2 * half), F32),
            pltpu.VMEM((width, 2 * half), F32),
            pltpu.VMEM((2 * half, width), F32),
            pltpu.VMEM((2, nz, part, half), BF16),
            pltpu.VMEM((2, nz, part, half), BF16),
            pltpu.VMEM((half, width), BF16),
            pltpu.VMEM((half, width), BF16),
            pltpu.VMEM((ny, 2, micro, tokens, block), BF16),
            pltpu.VMEM((ny, 2, micro, tokens, block), BF16),
            pltpu.VMEM((2, micro, tokens, qkv_width), BF16),
            pltpu.VMEM((2, micro, tokens, width), BF16),
            pltpu.VMEM((nz, padded, attn_width), BF16),
            pltpu.VMEM((max(1, ny - 1), nz, padded, attn_width), BF16),
            pltpu.VMEM((max(1, ny - 1), nz, padded, attn_width), BF16),
            pltpu.VMEM((max(1, nz - 1), padded, attn_width), BF16),
            pltpu.VMEM((2,) + small_shape, F32),
            pltpu.VMEM((ny,) + small_shape, F32),
            pltpu.VMEM((nz,) + small_shape, F32),
            DMA((2,)), DMA((2,)),
            DMA((2 * ny * micro + 2,)), DMA((2 * ny * micro + 2,)), DMA((2 * ny * micro + 2,)),
            DMA((ny + nz,)), DMA((ny + nz,)),
            DMA((3, nz)), DMA((3, nz)),
            DMA((2, nz + 1)), DMA((2, nz)),
            DMA((ny, nz)), DMA((ny, nz)),
            DMA((1, nz)), DMA((1, nz)),
        ],
        compiler_params=pltpu.CompilerParams(
            collective_id=2, has_side_effects=True, vmem_limit_bytes=62 * 2**20
        ),
        name="weight_gradients",
    )(routes_all, small, gsmall, zf, zb, slices, partner, xab, obb, dqkv, dattn)

    steps = 2
    finals = pl.pallas_call(
        functools.partial(finish_kernel, nz, total_experts),
        grid=(steps,),
        out_shape=(
            shape(1, 2, part, hidden, dtype=F32),
            shape(1, 2, part, hidden, dtype=F32),
            shape(1, 2, slice_h, width, dtype=F32),
            shape(1, shard, qkv_width, dtype=F32),
            shape(1, shard, width, dtype=F32),
            shape(1, shard, total_experts, dtype=F32),
            shape(1, shard, dtype=F32),
            shape(1, shard, dtype=F32),
        ),
        in_specs=[
            pl.BlockSpec((nz, part // steps, half), lambda i: (0, i, 0)),
            pl.BlockSpec((nz, part // steps, half), lambda i: (0, i, 0)),
            pl.BlockSpec((slice_h, width), lambda i: (i, 0)),
            pl.BlockSpec((padded, attn_width), lambda i: (0, 0)),
            pl.BlockSpec(small_shape, lambda i: (0, 0)),
        ],
        out_specs=(
            pl.BlockSpec((1, 2, part // steps, hidden), lambda i: (0, 0, i, 0)),
            pl.BlockSpec((1, 2, part // steps, hidden), lambda i: (0, 0, i, 0)),
            pl.BlockSpec((1, 1, slice_h, width), lambda i: (0, i, 0, 0)),
            pl.BlockSpec((1, shard, qkv_width), lambda i: (0, 0, 0)),
            pl.BlockSpec((1, shard, width), lambda i: (0, 0, 0)),
            pl.BlockSpec((1, shard, total_experts), lambda i: (0, 0, 0)),
            pl.BlockSpec((1, shard), lambda i: (0, 0)),
            pl.BlockSpec((1, shard), lambda i: (0, 0)),
        ),
        compiler_params=pltpu.CompilerParams(vmem_limit_bytes=60 * 2**20),
        name="finish_gradients",
    )(gate_g, up_g, down_g, attn_g, small_g)
    grad_gate, grad_up, grad_down, grad_qkv, grad_out, grad_router, grad_again, grad_mgain = finals
    return (
        out[None, :, None],
        gin[None, :, None],
        grad_again,
        grad_qkv,
        grad_out,
        grad_mgain,
        grad_router,
        grad_gate,
        grad_up,
        grad_down,
    )


def solution(mesh):
    owners = ("expert", "dp")
    return jax.shard_map(
        functools.partial(per_device, mesh.shape["expert"], mesh.shape["dp"], mesh.shape["section"]),
        mesh=mesh,
        in_specs=(
            P(None, owners, None, None),
            P(None, owners, None, None),
            P(None, owners, None),
            P("section", None, owners, None, None),
            P("section", owners),
            P("section", owners, None),
            P("section", owners, None),
            P("section", owners),
            P("section", owners, None),
            P("section", "expert", None, None),
            P("section", "expert", None, None),
            P("section", "expert", None, None),
        ),
        out_specs=(
            P("section", None, owners, None, None),
            P("section", None, owners, None, None),
            P("section", owners),
            P("section", owners, None),
            P("section", owners, None),
            P("section", owners),
            P("section", owners, None),
            P("section", "expert", "dp", None),
            P("section", "expert", "dp", None),
            P("section", "expert", "dp", None),
        ),
        check_vma=False,
    )
```

```python
import functools

import jax
import jax.numpy as jnp
import numpy as np
from jax import lax
from jax.experimental import pallas as pl
from jax.experimental.pallas import tpu as pltpu
from jax.sharding import PartitionSpec as P

HEAD = 128
QUERY_HEADS = 12
KEY_VALUE_HEADS = 2
GROUP = QUERY_HEADS // KEY_VALUE_HEADS
EPS = 1e-06
THETA = 1000000.0
NEGATIVE = -1e30
SCALE = HEAD ** (-0.5)
ROUTER_ROWS = 16
SMALL_ROWS = 32
FORWARD_CHUNKS = 2
BACKWARD_CHUNKS = 1
HOP_CHUNKS = 2
MESH = pl.DeviceIdType.MESH
F32 = jnp.float32
BF16 = jnp.bfloat16
GELU_C = float(np.sqrt(2.0 / np.pi))
GELU_A = 0.044715


def dot(a, b):
    return jnp.dot(a, b, preferred_element_type=F32)


def dot_nt(a, b):
    return lax.dot_general(a, b, (((1,), (1,)), ((), ())), preferred_element_type=F32)


def dot_tn(a, b):
    return lax.dot_general(a, b, (((0,), (0,)), ((), ())), preferred_element_type=F32)


def rotary_tables(tokens):
    places = np.arange(tokens, dtype=np.float64)
    inverse = THETA ** (-2.0 * np.arange(HEAD // 2, dtype=np.float64) / HEAD)
    angles = places[:, None] * inverse[None, :]
    cosine, sine = np.cos(angles), np.sin(angles)
    return (
        jnp.asarray(np.concatenate([cosine, cosine], 1), F32),
        jnp.asarray(np.concatenate([-sine, sine], 1), F32),
    )


def mask_bias(col, row):
    tokens = row.shape[1]
    ti = lax.broadcasted_iota(jnp.int32, (tokens, tokens), 0)
    ui = lax.broadcasted_iota(jnp.int32, (tokens, tokens), 1)
    return jnp.where((col == row) & (ui <= ti), 0.0, NEGATIVE).astype(F32)


def heads_of(value, first, count):
    return jnp.concatenate(
        [value[:, (first + i) * HEAD : (first + i + 1) * HEAD] for i in range(count)], 0
    )


def attention_shares(q6, k, bias6):
    scores = dot_nt(q6, k) * SCALE + bias6
    top = jnp.max(scores, -1, keepdims=True)
    raised = jnp.exp(scores - top)
    return raised / jnp.sum(raised, -1, keepdims=True)


class Place:
    def __init__(self, ny, nz):
        self.ny = ny
        self.nz = nz
        self.s = lax.axis_index("section")
        self.e = lax.axis_index("expert")
        self.d = lax.axis_index("dp")
        self.y = lax.div(self.e, 2)
        self.c = lax.rem(self.e, 2)
        self.core = (self.s, self.y * 2 + 1 - self.c, self.d)
        self.x = (1 - self.s, self.e, self.d)

    def ahead(self, r):
        return (self.s, lax.rem(self.y + r, self.ny) * 2 + self.c, self.d)

    def behind(self, r):
        return (self.s, lax.rem(self.y + self.ny - r, self.ny) * 2 + self.c, self.d)

    def pack(self, r, other):
        core = 1 - self.c if other else self.c
        return lax.rem(self.y + r, self.ny) * 2 + core

    def z_of(self, k):
        return lax.rem(self.d + k, self.nz)

    def z_ahead(self, k):
        return (self.s, self.e, self.z_of(k))

    def z_behind(self, k):
        return (self.s, self.e, self.z_of(self.nz - k))

    def greet(self, with_x=True):
        barrier = pltpu.get_barrier_semaphore()
        partners = [self.core] + ([self.x] if with_x else [])
        partners += [self.ahead(r) for r in range(1, self.ny)]
        partners += [self.z_ahead(k) for k in range(1, self.nz)]
        for partner in partners:
            pl.semaphore_signal(barrier, inc=1, device_id=partner, device_id_type=MESH)
        pl.semaphore_wait(barrier, len(partners))


def remote(src, dst, send, recv, device):
    return pltpu.make_async_remote_copy(
        src_ref=src, dst_ref=dst, send_sem=send, recv_sem=recv, device_id=device, device_id_type=MESH
    )


class Line:
    def __init__(self, place, slot, send, recv):
        self.place, self.slot, self.send, self.recv = place, slot, send, recv

    def origin(self, way, h):
        return self.place.d - h if way == 0 else self.place.d + h

    def comes(self, way, h):
        return self.place.d >= h if way == 0 else self.place.d + h < self.place.nz

    def leaves(self, way, h):
        d, nz = self.place.d, self.place.nz
        return (d + 1 < nz) & (d >= h - 1) if way == 0 else (d >= 1) & (d + h - 1 < nz)

    def out(self, way, h, src=None):
        g = self.place
        at = self.slot(self.origin(way, h - 1))
        next_door = (g.s, g.e, g.d + 1 if way == 0 else g.d - 1)
        return remote(at if src is None else src, at, self.send.at[way, h], self.recv.at[way, h], next_door)

    def came(self, way, h):
        g = self.place
        at = self.slot(self.origin(way, h))
        return remote(at, at, self.send.at[way, h], self.recv.at[way, h], g.core)

    def start(self, src):
        for way in range(2):
            @pl.when(self.leaves(way, 1))
            def _():
                self.out(way, 1, src).start()

    def go_on(self, h):
        for way in range(2):
            @pl.when(self.leaves(way, h))
            def _():
                self.out(way, h).start()

    def step(self, h, then=None, forward=True):
        for way in range(2):
            @pl.when(self.comes(way, h))
            def _():
                self.came(way, h).wait_recv()
                if forward and h + 1 < self.place.nz:
                    @pl.when(self.leaves(way, h + 1))
                    def _():
                        self.out(way, h + 1).start()
                if then is not None:
                    then(way, h)

    def finish(self, hops=None):
        for way in range(2):
            for h in range(1, self.place.nz) if hops is None else hops:
                @pl.when(self.leaves(way, h))
                def _():
                    self.out(way, h).wait_send()


class Gather:
    def __init__(self, place, buf, send, recv, ysend, yrecv, local):
        self.place, self.buf, self.local = place, buf, local
        self.send, self.recv, self.ysend, self.yrecv = send, recv, ysend, yrecv
        self.tokens = buf.shape[3]
        self.cut = self.tokens // 2

    def rows(self, r, whole):
        return pl.ds(0, self.tokens if whole or r == 0 else self.cut)

    def line(self, i, r, whole=True):
        rows = self.rows(r, whole)
        return Line(self.place, lambda zz: self.buf.at[i, zz, r, rows], self.send.at[i, r], self.recv.at[i, r])

    def near(self, i, r, src):
        return pltpu.make_async_copy(src, self.buf.at[i, self.place.d, r], self.local.at[i, r])

    def across(self, i, way, h, r):
        at = self.line(i, 0).origin(way, h)
        rest = pl.ds(self.cut, self.tokens - self.cut)
        return remote(
            self.buf.at[i, at, 0, rest], self.buf.at[i, at, r, rest],
            self.ysend.at[i, way, h, r], self.yrecv.at[i, way, h, r], self.place.behind(r),
        )

    def start(self, i, r, src, keep=True, whole=True):
        if keep:
            self.near(i, r, src).start()
        self.line(i, r, whole).start(src.at[self.rows(r, whole)])

    def step(self, i, h, whole=True, forward=True):
        for r in range(self.place.ny):
            self.line(i, r, whole).step(h, forward=forward)

    def go_on(self, i, h, whole=True):
        for r in range(self.place.ny):
            self.line(i, r, whole).go_on(h)

    def passes(self, i, hops):
        line = self.line(i, 0)
        for h in hops:
            for way in range(2):
                @pl.when(line.comes(way, h))
                def _():
                    for r in range(1, self.place.ny):
                        self.across(i, way, h, r).start()

    def finish(self, i, kept, whole=True, hops=None):
        for r in kept:
            self.near(i, r, self.buf.at[i, self.place.d, r]).wait()
        for r in range(self.place.ny):
            self.line(i, r, whole).finish(hops)
        if not whole:
            self.finish_passes(i, hops)

    def finish_passes(self, i, hops=None):
        g = self.place
        line = self.line(i, 0)
        for h in range(1, g.nz) if hops is None else hops:
            for way in range(2):
                @pl.when(line.comes(way, h))
                def _():
                    for r in range(1, g.ny):
                        self.across(i, way, h, r).wait()


class Exchange:
    def __init__(self, place, chunks, rows_ref, retl, retc, rety, sendl, sendc, sendy, sems, parts=1):
        self.place, self.chunks, self.parts = place, chunks, parts
        self.rows_ref = rows_ref
        self.retl, self.retc, self.rety = retl, retc, rety
        self.sendl, self.sendc, self.sendy = sendl, sendc, sendy
        self.sems = sems
        self.tokens = rows_ref.shape[2]
        self.span = self.tokens // chunks

    def rows(self, q):
        return pl.ds(q * self.span, self.span)

    def core_own(self):
        g = self.place
        return remote(
            self.rows_ref.at[0, 0], self.rows_ref.at[0, 1], self.sems.cs.at[0, 0], self.sems.cr.at[0, 0], g.core
        )

    def y_part(self, r, i):
        g = self.place
        size = self.span // self.parts
        rows = pl.ds(i * size, size)
        return remote(
            self.rows_ref.at[0, 0, rows],
            self.rows_ref.at[r, 0, rows],
            self.sems.ys.at[r, i],
            self.sems.yr.at[r, i],
            g.behind(r),
        )

    def y_parts(self, r, q):
        return [self.y_part(r, q * self.parts + p) for p in range(self.parts)]

    def forward(self, r, q):
        g = self.place
        return remote(
            self.rows_ref.at[r, 0, self.rows(q)],
            self.rows_ref.at[r, 1, self.rows(q)],
            self.sems.cs.at[r, q],
            self.sems.cr.at[r, q],
            g.core,
        )

    def back_local(self):
        return remote(self.sendl, self.retl, self.sems.bs.at[0, 0], self.sems.br.at[0, 0], self.place.core)

    def back_core(self, r, q):
        return remote(
            self.sendc.at[r - 1, self.rows(q)],
            self.retc.at[r - 1, self.rows(q)],
            self.sems.bs.at[r, q],
            self.sems.br.at[r, q],
            self.place.core,
        )

    def back_y(self, r, q):
        g = self.place
        return remote(
            self.sendy.at[r - 1, self.rows(q)],
            self.rety.at[g.ny - r - 1, self.rows(q)],
            self.sems.zs.at[r, q],
            self.sems.zr.at[g.ny - r, q],
            g.ahead(r),
        )

    def back_y_arrival(self, r, q):
        g = self.place
        return remote(
            self.sendy.at[r - 1, self.rows(q)],
            self.rety.at[r - 1, self.rows(q)],
            self.sems.zs.at[r, q],
            self.sems.zr.at[r, q],
            g.ahead(r),
        )

    def send_own(self):
        for i in range(self.chunks * self.parts):
            self.send_part(i)
        self.core_own().start()

    def send_part(self, i):
        for r in range(1, self.place.ny):
            self.y_part(r, i).start()

    def run(self, local_block, remote_block, complete, early=None):
        ny = self.place.ny
        items = [(r, q) for q in range(self.chunks) for r in range(1, ny)]
        def arrive(r, q):
            for part in self.y_parts(r, q):
                part.wait_recv()
            self.forward(r, q).start()
            if q == self.chunks - 1:
                complete(r)

        if items and early is not None:
            @pl.when(early)
            def _():
                arrive(*items[0])

        self.core_own().wait_recv()
        local_block()
        self.back_local().start()
        if items and early is None:
            arrive(*items[0])
        if items and early is not None:
            @pl.when(jnp.logical_not(early))
            def _():
                arrive(*items[0])

        for i, (r, q) in enumerate(items):
            self.forward(r, q).wait_recv()
            own = remote_block(r, q)
            self.back_core(r, q).start()
            if i + 1 < len(items):
                arrive(*items[i + 1])
            self.back_core(r, q).wait_recv()
            here = self.rows(q)
            self.sendy[r - 1, here, :] = (own() + self.retc[r - 1, here, :].astype(F32)).astype(BF16)
            self.back_y(r, q).start()
        self.back_local().wait_recv()

    def arrived(self, q):
        for r in range(1, self.place.ny):
            self.back_y_arrival(r, q).wait_recv()

    def finish(self):
        ny = self.place.ny
        self.core_own().wait_send()
        self.back_local().wait_send()
        for q in range(self.chunks):
            for r in range(1, ny):
                for part in self.y_parts(r, q):
                    part.wait_send()
                self.forward(r, q).wait_send()
                self.back_core(r, q).wait_send()
                self.back_y(r, q).wait_send()


class Sems:
    def __init__(self, refs, m):
        self.cs, self.cr, self.ys, self.yr, self.bs, self.br, self.zs, self.zr = [ref.at[m] for ref in refs]


def sem_shapes(micro, ny, chunks):
    return [pltpu.SemaphoreType.DMA((micro, ny, chunks)) for _ in range(8)]


def chosen_gates(logits_t, route):
    experts = lax.broadcasted_iota(jnp.int32, logits_t.shape, 0)
    chosen = route[0:1, :] == experts
    for k in range(1, route.shape[0]):
        chosen = chosen | (route[k : k + 1, :] == experts)
    masked = jnp.where(chosen, logits_t, NEGATIVE)
    raised = jnp.where(chosen, jnp.exp(masked - jnp.max(masked, 0, keepdims=True)), 0.0)
    return raised / jnp.sum(raised, 0, keepdims=True)


def gate_lanes(gates_t, expert):
    rows = lax.broadcasted_iota(jnp.int32, gates_t.shape, 0)
    one = jnp.sum(jnp.where(rows == expert, gates_t, 0.0), 0, keepdims=True)
    return jnp.transpose(jnp.broadcast_to(one, (128, one.shape[1])))


def widen(lanes, width):
    return jnp.concatenate([lanes] * (width // 128), 1)


def gather_kernel(
    ny, nz,
    small_ref, route_h, wqkv_h, wout_h, wg_h, wu_h, wd_h,
    small_t, route_o, wqkv_o, wout_o, slices_o, partner_o,
    small_s, wg, wu, turned,
    lsem, own_sem, cs, cr, ys, yr, zs, zr, sls, pls, plr,
):
    g = Place(ny, nz)
    hidden, width = turned.shape[2], turned.shape[3]
    slice_h = hidden // nz
    loads = [pltpu.make_async_copy(src, dst, lsem.at[i]) for i, (src, dst) in enumerate(((wg_h, wg), (wu_h, wu)))]
    for copy in loads:
        copy.start()
    g.greet(with_x=False)
    arrays = ((small_ref, small_s), (route_h, route_o), (wqkv_h, wqkv_o), (wout_h, wout_o))
    count = len(arrays)

    def near(n):
        src, dst = arrays[n]
        return pltpu.make_async_copy(src, dst.at[g.e, g.d], own_sem.at[n])

    lines = [Line(g, lambda zz, dst=dst: dst.at[g.e, zz], zs.at[n], zr.at[n]) for n, (_, dst) in enumerate(arrays)]

    def along_y(n, way, h, r):
        src, dst = arrays[n]
        at = dst.at[g.e, lines[n].origin(way, h)]
        return remote(src if h == 0 else at, at, ys.at[n, way, h, r], yr.at[n, way, h, r], g.behind(r))

    def to_core(n, way, h, r):
        src, dst = arrays[n]
        at = dst.at[g.pack(r, False), lines[n].origin(way, h)]
        own = h == 0 and r == 0
        return remote(src if own else at, at, cs.at[n, way, h, r], cr.at[n, way, h, r], g.core)

    for n in range(count):
        for r in range(1, ny):
            along_y(n, 0, 0, r).start()
        lines[n].start(arrays[n][0])
        near(n).start()
        to_core(n, 0, 0, 0).start()

    def got_z(n, h):
        def then(way, h):
            for r in range(1, ny):
                along_y(n, way, h, r).start()
            to_core(n, way, h, 0).start()

        lines[n].step(h, then)

    def got_y(n, h):
        for way in range(1 if h == 0 else 2):
            def pass_on():
                for r in range(1, ny):
                    along_y(n, way, h, r).wait_recv()
                    to_core(n, way, h, r).start()

            if h == 0:
                pass_on()
            else:
                pl.when(lines[n].comes(way, h))(pass_on)

    parts = []
    here = pl.ds(pl.multiple_of(g.d * slice_h, slice_h), slice_h)
    for i in range(3):
        for j in range(2):
            src = wd_h.at[j, here] if i == 2 else turned.at[i, j, here]
            to = slice(j * slice_h, (j + 1) * slice_h)
            parts.append(pltpu.make_async_copy(src, slices_o.at[i, to], sls.at[i, j]))
            parts.append(remote(src, partner_o.at[i, to], pls.at[i, j], plr.at[i, j], g.core))

    def turn(i, j, n):
        src = (wg, wu)[i]
        if j == 0 and n == 0:
            loads[i].wait()
        cols = slice(n * 256, (n + 1) * 256)
        turned[i, j, cols, :] = jnp.transpose(src[j, :, cols])

    turns = [(i, j, n) for i in range(2) for j in range(2) for n in range(hidden // 256)]

    z_items = [(n, h) for h in range(1, nz) for n in range(count)]
    y_items = [(n, 0) for n in range(count)] + z_items
    done = 0
    for i, item in enumerate(z_items):
        got_z(*item)
        if i % 2 == 1 or i >= count:
            got_y(*y_items[done])
            done += 1
        for piece in turns[:2]:
            turn(*piece)
        turns = turns[2:]
        if not turns and parts:
            for copy in parts:
                copy.start()
            started, parts = parts, []
    for item in y_items[done:]:
        got_y(*item)

    def each(act):
        for n in range(count):
            for h in range(nz):
                for way in range(1 if h == 0 else 2):
                    if h == 0:
                        act(n, way, h)
                    else:
                        pl.when(lines[n].comes(way, h))(lambda: act(n, way, h))

    def arrived(n, way, h):
        for r in range(ny):
            to_core(n, way, h, r).wait_recv()

    def sent(n, way, h):
        for r in range(ny):
            to_core(n, way, h, r).wait_send()
            if r:
                along_y(n, way, h, r).wait_send()

    each(arrived)
    for n in range(count):
        near(n).wait()
    gathered = small_s[...].reshape(width, small_s.shape[3])
    small_t[...] = jnp.transpose(gathered)[0:SMALL_ROWS].astype(BF16)
    each(sent)
    for line in lines:
        line.finish()
    for copy in started:
        copy.wait()


def forward_kernel(
    ny, nz, sections,
    x_ref, segc_ref, segr_ref, route_ref, small_ref, cos_ref, sin_ref,
    cot_h, wqkv_h, wout_h, wg_h, wu_h, wd_h,
    out_ref, hin_ref, h1_ref, qkv_ref, obb_ref, xm_ref, gates_ref, zf_h, obp_h,
    wqkv, wout, wg, wu, wd, ob_s, hid, accl, accr, retl, retc, rety, sendl, sendc, sendy,
    wsem, zs, zr, zys, zyr, zl, gs, gr, xs, xr, ps, pr, *sem_refs,
):
    micro, tokens, width = x_ref.shape
    hidden = wg.shape[2]
    span = tokens // FORWARD_CHUNKS
    loads = [
        pltpu.make_async_copy(src, dst, wsem.at[i])
        for i, (src, dst) in enumerate([(wqkv_h, wqkv), (wout_h, wout), (wg_h, wg), (wu_h, wu), (wd_h, wd)])
    ]
    for load in loads:
        load.start()
    g = Place(ny, nz)
    g.greet()
    gain_a = small_ref[ROUTER_ROWS : ROUTER_ROWS + 1, :].astype(F32)
    gain_m = small_ref[ROUTER_ROWS + 1 : ROUTER_ROWS + 2, :].astype(F32)
    cos, sin = cos_ref[...], sin_ref[...]
    gather = Gather(g, zf_h, zs, zr, zys, zyr, zl)
    every = range(ny)
    first, last = g.s == 0, g.s == sections - 1

    def cot_copy(r):
        return remote(cot_h.at[0], zf_h.at[0, g.d, r], gs.at[r], gr.at[r], g.behind(r))

    @pl.when(last)
    def _():
        for r in range(1, ny):
            cot_copy(r).start()
        gather.start(0, 0, cot_h.at[0])
        for r in range(1, ny):
            cot_copy(r).wait_recv()
            gather.start(0, r, zf_h.at[0, g.d, r], keep=False)
        gather.step(0, 1)

    def hop(m, q):
        here = pl.ds(q * (tokens // HOP_CHUNKS), tokens // HOP_CHUNKS)
        return remote(out_ref.at[m, here], hin_ref.at[m, here], xs.at[m, q], xr.at[m, q], g.x)

    def experts(rows, lanes, keep):
        count = rows.shape[0]
        for j in range(2):
            for n in range(hidden // 256):
                cols = slice(n * 256, (n + 1) * 256)
                a = dot(rows, wg[j, :, cols])
                b = dot(rows, wu[j, :, cols])
                act = 0.5 * a * (1.0 + jnp.tanh(GELU_C * (a + GELU_A * a * a * a)))
                hid[j, 0:count, cols] = (act * b).astype(BF16)
        for n in range(width // 512):
            cols = slice(n * 512, (n + 1) * 512)
            total = None
            for j in range(2):
                eo = dot(hid[j, 0:count, :], wd[j, :, cols]).astype(BF16).astype(F32)
                term = widen(lanes[j], 512) * eo
                total = term if total is None else total + term
            keep(cols, total)

    def partner(m, yy):
        return remote(obb_ref.at[m, yy * 2 + 1 - g.c], obp_h.at[m, yy], ps.at[m, yy], pr.at[m, yy], g.core)

    def body(m, carry):
        @pl.when(g.s == 0)
        def _():
            hin_ref[m] = x_ref[m]

        @pl.when(g.s > 0)
        def _():
            for q in range(HOP_CHUNKS):
                hop(m, q).wait_recv()

        h = hin_ref[m].astype(F32)
        xa = (h * lax.rsqrt(jnp.mean(h * h, -1, keepdims=True) + EPS) * gain_a).astype(BF16)

        @pl.when(m == 0)
        def _():
            loads[0].wait()

        turned = QUERY_HEADS + KEY_VALUE_HEADS
        for i in range(wqkv.shape[1] // 256):
            mixed = dot(xa, wqkv[:, i * 256 : (i + 1) * 256])
            for half in range(2):
                head = 2 * i + half
                part = mixed[:, half * HEAD : (half + 1) * HEAD]
                if head < turned:
                    part = part * cos + pltpu.roll(part, HEAD // 2, 1) * sin
                qkv_ref[m, :, head * HEAD : (head + 1) * HEAD] = part.astype(BF16)
        bias = mask_bias(segc_ref[m], segr_ref[m])
        bias6 = jnp.concatenate([bias] * GROUP, 0)
        qkv = qkv_ref.at[m]
        for kv in range(KEY_VALUE_HEADS):
            q6 = heads_of(qkv, kv * GROUP, GROUP)
            k = heads_of(qkv, QUERY_HEADS + kv, 1)
            v = heads_of(qkv, turned + kv, 1)
            shares = attention_shares(q6, k, bias6).astype(BF16)
            o6 = dot(shares, v).astype(BF16)
            for i in range(GROUP):
                head = kv * GROUP + i
                ob_s[:, head * HEAD : (head + 1) * HEAD] = o6[i * tokens : (i + 1) * tokens]

        @pl.when(m == 0)
        def _():
            loads[1].wait()

        ob = ob_s[...]
        block = obb_ref.shape[3]
        for i in range(2 * ny):
            obb_ref[m, i] = ob[:, i * block : (i + 1) * block]
        for n in range(width // 512):
            cols = slice(n * 512, (n + 1) * 512)
            h1_ref[m, :, cols] = hin_ref[m, :, cols].astype(F32) + dot(ob, wout[:, cols])
        h1 = h1_ref[m]
        xm_ref[m, 0, 0] = (h1 * lax.rsqrt(jnp.mean(h1 * h1, -1, keepdims=True) + EPS) * gain_m).astype(BF16)

        ex = Exchange(g, FORWARD_CHUNKS, xm_ref.at[m], retl, retc, rety, sendl, sendc, sendy, Sems(sem_refs, m))
        ex.send_own()

        def complete(r):
            @pl.when(first & (m == 0))
            def _():
                gather.start(0, r, xm_ref.at[0, r, 0])

        def move(h):
            if h + 1 < nz:
                @pl.when(last & (m == 0))
                def _():
                    gather.step(0, h + 1)

            if h < nz:
                @pl.when(first & (m == 1))
                def _():
                    gather.step(0, h)

        complete(0)
        move(1)

        @pl.when(m == 0)
        def _():
            for load in loads[2:]:
                load.wait()

        def gates_for(r, other, here):
            rows = xm_ref[m, r, other, here, :]
            logits_t = dot_nt(small_ref[0:ROUTER_ROWS, :], rows)
            gates_t = chosen_gates(logits_t, route_ref[g.pack(r, other) * nz + g.d, m][:, here])
            return gates_t

        def lanes_of(blocks):
            return [
                jnp.concatenate([gate_lanes(gates_t, 2 * g.e + j) for gates_t in blocks], 0) for j in range(2)
            ]

        full = slice(0, tokens)

        def local_block():
            blocks = []
            for other in range(2):
                gates_t = gates_for(0, other, full)
                gates_ref[m, 0, other] = gates_t
                blocks.append(gates_t)

            def keep(cols, total):
                accl[:, cols] = total[0:tokens]
                sendl[:, cols] = total[tokens:].astype(BF16)

            experts(xm_ref[m, 0].reshape(2 * tokens, width), lanes_of(blocks), keep)

        def remote_block(r, q):
            here = slice(q * span, (q + 1) * span)
            blocks = []
            for other in range(2):
                gates_t = gates_for(r, other, here)
                gates_ref[m, r, other, :, here] = gates_t
                blocks.append(jnp.concatenate([gates_t] * (128 // span), 1))
            lanes = [
                jnp.concatenate([gate_lanes(gates_t, 2 * g.e + j)[0:span] for gates_t in blocks], 0)
                for j in range(2)
            ]

            def keep(cols, total):
                accr[:, cols] = total[0:span]
                sendc[r - 1, here, cols] = total[span:].astype(BF16)

            experts(xm_ref[m, r, :, here, :].reshape(2 * span, width), lanes, keep)
            return lambda: accr[...]

        ex.run(local_block, remote_block, complete)
        for q in range(HOP_CHUNKS):
            here = slice(q * span, (q + 1) * span)
            ex.arrived(q)
            total = h1_ref[m, here, :] + accl[here, :] + retl[here, :].astype(F32)
            for r in range(1, ny):
                total = total + rety[r - 1, here, :].astype(F32)
            out_ref[m, here, :] = total.astype(BF16)

            @pl.when(g.s < sections - 1)
            def _():
                hop(m, q).start()

        ex.finish()
        for yy in range(ny):
            partner(m, yy).start()
        move(2)
        return carry

    lax.fori_loop(0, micro, body, 0)
    for m in range(micro):
        for yy in range(ny):
            partner(m, yy).wait()

    @pl.when(g.s < sections - 1)
    def _():
        for m in range(micro):
            for q in range(HOP_CHUNKS):
                hop(m, q).wait_send()

    @pl.when(first)
    def _():
        for h in range(3, nz):
            gather.step(0, h)
        gather.finish(0, every)

    @pl.when(last)
    def _():
        for r in range(1, ny):
            cot_copy(r).wait_send()
        for h in range(4, nz):
            gather.step(0, h)
        gather.finish(0, [0])


def backward_kernel(
    ny, nz, sections,
    cot_ref, segc_ref, segr_ref, small_ref, cos_ref, sin_ref,
    hin_ref, h1_ref, qkv_ref, gates_ref,
    xm_h, wqkv_h, wout_h, wg_h, wu_h, wd_h,
    gin_ref, grows_ref, xab_ref, dqkv_ref, dattn_ref, gsmall_ref, zb_h, xap_h, dqp_h, dtp_h,
    wqkv, wout, wg, wu, wd, xm_s, hid, act_s, slope_s, da_s, db_s, accl, accr, dh1_s, n_s,
    retl, retc, rety, sendl, sendc, sendy,
    wsem, xmsem, zs, zr, zys, zyr, zl, xs, xr, ps, pr, *sem_refs,
):
    micro, tokens, width = cot_ref.shape
    hidden = wg.shape[2]
    span = tokens // BACKWARD_CHUNKS
    loads = [
        pltpu.make_async_copy(src, dst, wsem.at[i])
        for i, (src, dst) in enumerate([(wg_h, wg), (wu_h, wu), (wd_h, wd), (wout_h, wout), (wqkv_h, wqkv)])
    ]
    for load in loads:
        load.start()
    g = Place(ny, nz)
    g.greet()
    gain_a = small_ref[ROUTER_ROWS : ROUTER_ROWS + 1, :].astype(F32)
    gain_m = small_ref[ROUTER_ROWS + 1 : ROUTER_ROWS + 2, :].astype(F32)
    cos, sin = cos_ref[...], sin_ref[...]
    gsmall_ref[...] = jnp.zeros_like(gsmall_ref)
    gather = Gather(g, zb_h, zs, zr, zys, zyr, zl)
    every = range(ny)
    first, last = g.s == 0, g.s == sections - 1

    @pl.when(first)
    def _():
        for m in range(1, micro):
            for r in every:
                gather.start(micro + m, r, xm_h.at[m, r, 0])
            for h in range(1, nz):
                gather.step(micro + m, h)

    def hop(m, q):
        here = pl.ds(q * (tokens // HOP_CHUNKS), tokens // HOP_CHUNKS)
        return remote(gin_ref.at[m, here], grows_ref.at[m, 0, 0, here], xs.at[m, q], xr.at[m, q], g.x)

    def partner(m):
        pairs = [(dattn_ref.at[m], dtp_h.at[m]), (dqkv_ref.at[m], dqp_h.at[m])]
        pairs += [(xab_ref.at[m, yy * 2 + 1 - g.c], xap_h.at[m, yy]) for yy in range(ny)]
        return [remote(src, dst, ps.at[m, n], pr.at[m, n], g.core) for n, (src, dst) in enumerate(pairs)]

    def late(m):
        for h in range(3, nz):
            gather.step(m, h, whole=False)

    def body(m, carry):
        load_xm = pltpu.make_async_copy(xm_h.at[m], xm_s, xmsem)
        load_xm.start()

        @pl.when(last)
        def _():
            grows_ref[m, 0, 0] = cot_ref[m]
            for r in every:
                gather.start(m, r, xm_h.at[m, r, 0], whole=False)

        ex = Exchange(
            g, BACKWARD_CHUNKS, grows_ref.at[m], retl, retc, rety, sendl, sendc, sendy, Sems(sem_refs, m), HOP_CHUNKS
        )

        @pl.when(last)
        def _():
            ex.send_own()

        @pl.when(m == 0)
        def _():
            for load in loads[:3]:
                load.wait()

        load_xm.wait()

        def again(r, _):
            rows = xm_s[r].reshape(2 * tokens, width)
            for j in range(2):
                for n in range(hidden // 256):
                    cols = slice(n * 256, (n + 1) * 256)
                    a = dot(rows, wg[j, :, cols])
                    b = dot(rows, wu[j, :, cols])
                    square = a * a
                    th = jnp.tanh(GELU_C * (a + GELU_A * square * a))
                    half = 0.5 * (1.0 + th)
                    act = a * half
                    slope = half + (0.5 * GELU_C) * a * (1.0 - th * th) * (1.0 + (3.0 * GELU_A) * square)
                    shape = (2, tokens, 256)
                    hid[j, r, :, :, cols] = (act * b).astype(BF16).reshape(shape)
                    act_s[j, r, :, :, cols] = act.astype(BF16).reshape(shape)
                    slope_s[j, r, :, :, cols] = (slope * b).astype(BF16).reshape(shape)
            return 0

        @pl.when(first)
        def _():
            lax.fori_loop(0, ny, again, 0)

            @pl.when(m > 0)
            def _():
                late(m - 1)

            for q in range(HOP_CHUNKS):
                hop(m, q).wait_recv()
                ex.send_part(q)
            ex.core_own().start()

        def complete(r):
            src = grows_ref.at[m, r, 0]

            @pl.when(first)
            def _():
                gather.start(m, r, src, whole=False)

        open_end = first & (m == micro - 1)

        def move(hops):
            for h in hops:
                gather.step(m, h, whole=False)

        complete(0)

        @pl.when(last)
        def _():
            lax.fori_loop(0, ny, again, 0)


        def experts(rows, r, here, keep):
            count = 2 * (here.stop - here.start)
            part = slice(0, count)
            lane = lax.broadcasted_iota(jnp.int32, (count, 128), 1)
            gate_grads = jnp.zeros((count, 128), F32)
            for j in range(2):
                expert = 2 * g.e + j
                lanes = []
                for other in range(2):
                    gates_t = gates_ref[m, r, other]
                    lanes.append(gate_lanes(gates_t, expert)[here])
                lanes = widen(jnp.concatenate(lanes, 0), 256)
                summed = jnp.zeros((count, 1), F32)
                for n in range(hidden // 256):
                    cols = slice(n * 256, (n + 1) * 256)
                    u = dot_nt(rows, wd[j, cols, :])
                    inner = hid[j, r, :, here, cols].reshape(count, 256).astype(F32)
                    summed = summed + jnp.sum(u * inner, -1, keepdims=True)
                    u = u * lanes
                    slope = slope_s[j, r, :, here, cols].reshape(count, 256).astype(F32)
                    act = act_s[j, r, :, here, cols].reshape(count, 256).astype(F32)
                    da_s[j, part, cols] = (u * slope).astype(BF16)
                    db_s[j, part, cols] = (u * act).astype(BF16)
                high = summed.astype(BF16).astype(F32)
                gate_grads = jnp.where(lane == expert, high, gate_grads)
                gate_grads = jnp.where(lane == expert + 64, summed - high, gate_grads)
            for n in range(width // 512):
                cols = slice(n * 512, (n + 1) * 512)
                total = None
                for j in range(2):
                    term = dot_nt(da_s[j, part, :], wg[j, cols, :]) + dot_nt(db_s[j, part, :], wu[j, cols, :])
                    total = term if total is None else total + term
                keep(cols, total)
            keep(slice(width, width + 128), gate_grads)

        full = slice(0, tokens)

        def local_block():
            def keep(cols, total):
                accl[:, cols] = total[0:tokens]
                sendl[:, cols] = total[tokens:].astype(BF16)

            experts(grows_ref[m, 0].reshape(2 * tokens, width), 0, full, keep)

        def remote_block(r, q):
            here = slice(q * span, (q + 1) * span)

            def keep(cols, total):
                accr[:, cols] = total[0:span]
                sendc[r - 1, here, cols] = total[span:].astype(BF16)

            experts(grows_ref[m, r, :, here, :].reshape(2 * span, width), r, here, keep)
            return lambda: accr[...]

        ex.run(local_block, remote_block, complete, last)
        move(range(1, 2))
        for q in range(BACKWARD_CHUNKS):
            ex.arrived(q)
        total = accl[...] + retl[...].astype(F32)
        for r in range(1, ny):
            total = total + rety[r - 1].astype(F32)
        dgates = total[:, width:]
        dgates = dgates + pltpu.roll(dgates, 64, 1)
        gates_t = gates_ref[m, 0, 0]
        gates = jnp.transpose(
            jnp.concatenate([gates_t, jnp.zeros((128 - ROUTER_ROWS, tokens), F32)], 0)
        )
        dlog = gates * (dgates - jnp.sum(gates * dgates, -1, keepdims=True))
        dlog = dlog[:, 0:SMALL_ROWS]
        high = dlog.astype(BF16)
        low = (dlog - high.astype(F32)).astype(BF16)
        router = small_ref[...]
        dxm = total[:, 0:width] + dot(high, router) + dot(low, router)
        xm = xm_s[0, 0]
        gsmall_ref[0:ROUTER_ROWS, :] += (dot_tn(high, xm) + dot_tn(low, xm))[0:ROUTER_ROWS]
        h1 = h1_ref[m]
        rinv = lax.rsqrt(jnp.mean(h1 * h1, -1, keepdims=True) + EPS)
        n2 = h1 * rinv
        gsmall_ref[ROUTER_ROWS + 1 : ROUTER_ROWS + 2, :] += jnp.sum(dxm * n2, 0, keepdims=True)
        scaled = dxm * gain_m
        dh1 = grows_ref[m, 0, 0].astype(F32) + rinv * (scaled - n2 * jnp.mean(scaled * n2, -1, keepdims=True))
        dh1_s[...] = dh1
        dattn = dh1.astype(BF16)
        dattn_ref[m] = dattn

        @pl.when(m == 0)
        def _():
            for load in loads[3:]:
                load.wait()

        @pl.when(jnp.logical_not(open_end))
        def _():
            move(range(2, min(3, nz)))

        @pl.when(first)
        def _():
            gather.passes(m, range(1, 2))

        @pl.when(first & (m > 0))
        def _():
            gather.passes(m - 1, range(3, nz))

        @pl.when(first & (m < micro - 1))
        def _():
            gather.passes(m, range(2, min(3, nz)))

        for copy in partner(m)[:1]:
            copy.start()
        bias = mask_bias(segc_ref[m], segr_ref[m])
        bias6 = jnp.concatenate([bias] * GROUP, 0)
        qkv = qkv_ref.at[m]
        turned = QUERY_HEADS + KEY_VALUE_HEADS

        def unturn(part):
            return part * cos - pltpu.roll(part, HEAD // 2, 1) * sin

        for kv in range(KEY_VALUE_HEADS):
            wide = GROUP * HEAD
            dob = dot_nt(dattn, wout[kv * wide : (kv + 1) * wide, :]).astype(BF16)
            dob6 = heads_of(dob, 0, GROUP)
            q6 = heads_of(qkv, kv * GROUP, GROUP)
            k = heads_of(qkv, QUERY_HEADS + kv, 1)
            v = heads_of(qkv, turned + kv, 1)
            shares = attention_shares(q6, k, bias6)
            dshares = dot_nt(dob6, v)
            dv = dot_tn(shares.astype(BF16), dob6)
            ds = (shares * (dshares - jnp.sum(shares * dshares, -1, keepdims=True))).astype(BF16)
            dq6 = dot(ds, k) * SCALE
            dk = dot_tn(ds, q6) * SCALE
            for i in range(GROUP):
                head = kv * GROUP + i
                dqkv_ref[m, :, head * HEAD : (head + 1) * HEAD] = unturn(
                    dq6[i * tokens : (i + 1) * tokens]
                ).astype(BF16)
            head = QUERY_HEADS + kv
            dqkv_ref[m, :, head * HEAD : (head + 1) * HEAD] = unturn(dk).astype(BF16)
            head = turned + kv
            dqkv_ref[m, :, head * HEAD : (head + 1) * HEAD] = dv.astype(BF16)

        h = hin_ref[m].astype(F32)
        rinv = lax.rsqrt(jnp.mean(h * h, -1, keepdims=True) + EPS)
        n1 = h * rinv
        xa = (n1 * gain_a).astype(BF16)
        block = xab_ref.shape[3]
        for i in range(2 * ny):
            xab_ref[m, i] = xa[:, i * block : (i + 1) * block]
        n_s[...] = n1
        dqkv = dqkv_ref[m]
        for n in range(width // 512):
            cols = slice(n * 512, (n + 1) * 512)
            accl[:, cols] = dot_nt(dqkv, wqkv[cols, :])
        dxa = accl[:, 0:width]
        n1 = n_s[...]
        gsmall_ref[ROUTER_ROWS : ROUTER_ROWS + 1, :] += jnp.sum(dxa * n1, 0, keepdims=True)
        scaled = dxa * gain_a
        grad = dh1_s[...] + rinv * (scaled - n1 * jnp.mean(scaled * n1, -1, keepdims=True))
        gin_ref[m] = grad.astype(BF16)

        @pl.when(g.s > 0)
        def _():
            for q in range(HOP_CHUNKS):
                hop(m, q).start()

        for copy in partner(m)[1:]:
            copy.start()

        @pl.when(last)
        def _():
            move(range(3, nz))

        @pl.when(open_end)
        def _():
            for h in range(2, min(3, nz)):
                gather.step(m, h, whole=False, forward=False)

        ex.finish()
        return carry

    lax.fori_loop(0, micro, body, 0)

    @pl.when(g.s > 0)
    def _():
        for m in range(micro):
            for q in range(HOP_CHUNKS):
                hop(m, q).wait_send()

    few = range(1, min(3, nz))

    @pl.when(last)
    def _():
        for m in range(micro):
            gather.passes(m, range(1, nz))
        for m in range(1, micro):
            for r in every:
                gather.start(micro + m, r, grows_ref.at[m, r, 0])
            for h in few:
                gather.step(micro + m, h, forward=m < micro - 1 or h < few[-1])
            if m < micro - 1:
                for h in range(3, nz):
                    gather.step(micro + m, h)

    for m in range(micro - 1):
        gather.finish(m, every, whole=False)
    for m in range(1, micro - 1):
        gather.finish(micro + m, every)

    @pl.when(first)
    def _():
        for r in every:
            gather.near(micro - 1, r, grows_ref.at[micro - 1, r, 0]).wait()
        for r in every:
            gather.line(micro - 1, r, False).finish(few)
        gather.finish_passes(micro - 1, range(1, 2))
        gather.finish(2 * micro - 1, every)

    @pl.when(last)
    def _():
        gather.finish(micro - 1, every, whole=False)
        gather.finish(2 * micro - 1, every, hops=few)

    for m in range(micro):
        for copy in partner(m):
            copy.wait()


def tail_kernel(
    ny, nz, sections, span,
    route_ref, small_ref, gsmall_ref,
    zf_h, zb_in, slices_h, partner_h, xab_h, obb_h, dqkv_h, dattn_h, xap_h, obp_h, dqp_h, dtp_h,
    gate_ref, up_ref, down_ref, attn_ref, small_out, zb_h,
    w4, x_s, g_s, da_s, db_s, gh_s, acc_g, acc_u, acc_d, csend, cland, dsend, dland,
    xa_s, ob_s, dq_s, dt_s, own_s, ysend, yland, zland, sm_s, smy, smz,
    wsem, xsem, asem, ss, sr, cs, cr, ts, tr, ys, yr, zs, zr, hs, hr, hys, hyr, hl,
):
    micro, tokens, width = dqkv_h.shape[0], zf_h.shape[3], zf_h.shape[4]
    half = slices_h.shape[1]
    slice_h = half // 2
    both = 2 * half
    tile = 256 if both % 256 == 0 else 128
    qkv_width = dqkv_h.shape[2]
    shard = width // (2 * ny * nz)
    part = width // nz
    rows = span * ny * tokens
    groups = nz // span
    g = Place(ny, nz)
    first = g.s == 0
    mine = [pltpu.make_async_copy(src, w4.at[:, i * half : (i + 1) * half], wsem.at[i])
            for i, src in enumerate((slices_h, partner_h))]

    def load(i):
        m, k = lax.div(i, groups), pl.ds(lax.rem(i, groups) * span, span)
        early = [(first, x_s, 0), (jnp.logical_not(first), g_s, 1)]
        late = [(first, g_s, 1), (jnp.logical_not(first), x_s, 0)]
        copies = [(when, pltpu.make_async_copy(zb_h.at[m, k], dst, xsem.at[n])) for when, dst, n in late]
        for when, dst, n in early:
            copies.append((when & (m == 0), pltpu.make_async_copy(zf_h.at[0, k], dst, xsem.at[n])))
            copies.append((when & (m > 0), pltpu.make_async_copy(zb_h.at[micro + m, k], dst, xsem.at[n])))
        return copies

    def start_load(i):
        for when, copy in load(i):
            @pl.when(when)
            def _():
                copy.start()

    def wait_load():
        pltpu.make_async_copy(zf_h.at[0, pl.ds(0, span)], x_s, xsem.at[0]).wait()
        pltpu.make_async_copy(zf_h.at[0, pl.ds(0, span)], g_s, xsem.at[1]).wait()

    acts = []
    for m in range(micro):
        for yy in range(ny):
            own = yy * 2 + g.c
            acts.append((xab_h.at[m, own], xa_s.at[yy, 0, m]))
            acts.append((xap_h.at[m, yy], xa_s.at[yy, 1, m]))
            acts.append((obb_h.at[m, own], ob_s.at[yy, 0, m]))
            acts.append((obp_h.at[m, yy], ob_s.at[yy, 1, m]))
    acts += [(dqkv_h, dq_s.at[0]), (dqp_h, dq_s.at[1]), (dattn_h, dt_s.at[0]), (dtp_h, dt_s.at[1])]
    acts = [pltpu.make_async_copy(src, dst, asem.at[i]) for i, (src, dst) in enumerate(acts)]
    for copy in acts:
        copy.start()
    g.greet(with_x=False)
    gather = Gather(g, zb_h, hs, hr, hys, hyr, hl)
    late_hops = range(3, nz)
    newest = micro - 1

    @pl.when(first)
    def _():
        gather.passes(newest, range(2, min(3, nz)))
        for h in late_hops[:1]:
            gather.go_on(newest, h, whole=False)

    @pl.when(jnp.logical_not(first))
    def _():
        for h in late_hops[:1]:
            gather.go_on(micro + newest, h)
    sm_core = remote(gsmall_ref, sm_s.at[1], ss.at[0], sr.at[0], g.core)
    sm_core.start()

    def sm_y(r):
        return remote(sm_s.at[0], smy.at[ny - r], ss.at[r], sr.at[ny - r], g.ahead(r))

    def sm_y_arrival(r):
        return remote(sm_s.at[0], smy.at[r], ss.at[r], sr.at[r], g.ahead(r))

    def sm_z(k):
        return remote(sm_s.at[1], smz.at[k], ss.at[ny + k], sr.at[ny + k], g.z_behind(k))

    for copy in acts:
        copy.wait()
    for copy in mine:
        copy.start()
    start_load(0)

    count = 2 * micro * tokens

    def attn_rows(yy, dst):
        for src, grad, at in ((xa_s, dq_s, 0), (ob_s, dt_s, qkv_width)):
            left = src[yy].reshape(count, shard * nz)
            wide = grad.shape[3]
            for n in range(wide // 512):
                cols = slice(n * 512, (n + 1) * 512)
                got = dot_tn(left, grad[:, :, :, cols].reshape(count, 512)).astype(BF16)
                for zi in range(nz):
                    dst[zi, 0:shard, at + n * 512 : at + (n + 1) * 512] = got[zi * shard : (zi + 1) * shard]

    def flipped(mask):
        place = g.d
        for b in range(nz.bit_length()):
            if mask >> b & 1:
                place = place + (1 << b) - (2 << b) * lax.rem(lax.div(g.d, 1 << b), 2)
        return place

    def y_copy(r, k):
        zi = flipped(k)
        return remote(ysend.at[r - 1, zi], yland.at[ny - r - 1, zi], ys.at[r, k], yr.at[ny - r, k], g.ahead(r))

    def y_arrival(r, k):
        zi = flipped(k)
        return remote(ysend.at[r - 1, zi], yland.at[r - 1, zi], ys.at[r, k], yr.at[r, k], g.ahead(r))

    order = list(range(1, nz)) + [0]
    masks = list(range(nz - 1, -1, -1))

    def y_start(k):
        for r in range(1, ny):
            y_copy(r, k).start()

    for r in range(1, ny):
        attn_rows(lax.rem(g.y + r, ny), ysend.at[r - 1])
    y_start(masks[0])
    sm_core.wait_recv()
    sm_s[0] = gsmall_ref[...] + sm_s[1]
    sm_core.wait_send()
    for r in range(1, ny):
        sm_y(r).start()
    attn_rows(g.y, own_s)

    bits = nz.bit_length() - 1

    def low(mask):
        return (mask & -mask).bit_length() - 1 if mask else bits

    landings = [(mask, b) for mask in range(nz) for b in range(low(mask))]

    def z_copy(mask):
        b = low(mask)
        at = landings.index((mask - (1 << b), b))
        device = (g.s, g.e, flipped(1 << b))
        return remote(own_s.at[flipped(mask)], zland.at[at], zs.at[0, mask], zr.at[0, at], device)

    def z_arrival(mask, b):
        at = landings.index((mask, b))
        device = (g.s, g.e, flipped(1 << b))
        return remote(own_s.at[flipped(mask)], zland.at[at], zs.at[0, mask], zr.at[0, at], device)

    def advance(mask):
        for r in range(1, ny):
            y_arrival(r, mask).wait_recv()
        zi = flipped(mask)
        for b in range(low(mask)):
            z_arrival(mask, b).wait_recv()
        for n in range((qkv_width + width) // 512):
            cols = slice(n * 512, (n + 1) * 512)
            total = own_s[zi, :, cols].astype(F32)
            for r in range(1, ny):
                total = total + yland[r - 1, zi, :, cols].astype(F32)
            for b in range(low(mask)):
                total = total + zland[landings.index((mask, b)), :, cols].astype(F32)
            if mask:
                own_s[zi, :, cols] = total.astype(BF16)
            else:
                attn_ref[:, cols] = total
        if mask:
            z_copy(mask).start()

    for copy in mine:
        copy.wait()
    acc_g[...] = jnp.zeros_like(acc_g)
    acc_u[...] = jnp.zeros_like(acc_u)
    acc_d[...] = jnp.zeros_like(acc_d)
    column = lax.broadcasted_iota(jnp.int32, (ROUTER_ROWS, both), 1)
    expert = lax.broadcasted_iota(jnp.int32, (ROUTER_ROWS, both), 0)
    owner = jnp.where(column < half, g.e, 2 * g.y + 1 - g.c)
    local = jnp.where(column < half, column, column - half)
    chosen = 2 * owner + jnp.where(local < slice_h, 0, 1)
    spread = jnp.where(expert == chosen, 1.0, 0.0).astype(BF16)

    last_group = micro * groups - 1
    half_way = (micro * groups) // 2 - 1

    def core_copy(n, k):
        return remote(csend.at[n, k], cland.at[n, k], cs.at[n, k], cr.at[n, k], g.core)

    def width_rows(k):
        return pl.ds(pl.multiple_of(g.z_of(k) * part, part), part)

    accs = (acc_g, acc_u)

    def give_half(n):
        for k in order:
            csend[n, k] = accs[n][width_rows(k), half:both].astype(BF16)
            core_copy(n, k).start()

    def small_z():
        for r in range(1, ny):
            sm_y_arrival(r).wait_recv()
        total = sm_s[0]
        for r in range(1, ny):
            total = total + smy[r]
        sm_s[1] = total
        for k in range(1, nz):
            sm_z(k).start()

    def group(i, carry):
        m = lax.div(i, groups)
        wait_load()

        def block(b, carry):
            k = lax.rem(i, groups) * span + b
            x = x_s[b].reshape(ny * tokens, width)
            gr = g_s[b].reshape(ny * tokens, width)
            places = [(lax.rem(g.y + r, ny) * 2 + g.c) * nz + k for r in range(ny)]
            route = jnp.concatenate([route_ref[place, m] for place in places], 1)
            gates_t = chosen_gates(dot_nt(small_ref[0:ROUTER_ROWS, :], x), route)
            high = gates_t.astype(BF16)
            low_part = (gates_t - high.astype(F32)).astype(BF16)
            here = pl.ds(pl.multiple_of(b * ny * tokens, ny * tokens), ny * tokens)
            for n in range(both // tile):
                cols = slice(n * tile, (n + 1) * tile)
                a = dot_nt(x, w4[0, cols])
                bb = dot_nt(x, w4[1, cols])
                gate = dot_tn(high, spread[:, cols]) + dot_tn(low_part, spread[:, cols])
                u = dot_nt(gr, w4[2, cols]) * gate
                square = a * a
                th = jnp.tanh(GELU_C * (a + GELU_A * square * a))
                hf = 0.5 * (1.0 + th)
                act = a * hf
                slope = hf + (0.5 * GELU_C) * a * (1.0 - th * th) * (1.0 + (3.0 * GELU_A) * square)
                da_s[here, cols] = (u * slope * bb).astype(BF16)
                db_s[here, cols] = (u * act).astype(BF16)
                gh_s[here, cols] = ((act * bb).astype(BF16).astype(F32) * gate).astype(BF16)

            @pl.when((i == half_way) & (b == span // 2 - 1))
            def _():
                advance(masks[0])
                y_start(masks[1])

            @pl.when((i == last_group) & (b == span // 2 - 1))
            def _():
                advance(masks[2])
                y_start(masks[3])

            return carry

        lax.fori_loop(0, span, block, 0)

        @pl.when(first & (i == newest * groups - 1))
        def _():
            for h in late_hops:
                gather.step(newest, h, whole=False)
            gather.passes(newest, late_hops)

        @pl.when(jnp.logical_not(first) & (i == newest * groups - 1))
        def _():
            for h in late_hops:
                gather.step(micro + newest, h)

        def gate_rows(cols):
            acc_g[cols, :] += dot_tn(x_s[:, :, :, cols].reshape(rows, 256), da_s[...])

        def up_rows(cols):
            acc_u[cols, :] += dot_tn(x_s[:, :, :, cols].reshape(rows, 256), db_s[...])

        def down_rows(cols):
            acc_d[cols, :] += dot_tn(gh_s[:, cols], g_s[...].reshape(rows, width))

        def over(act, extent, size):
            def columns(n, carry):
                act(pl.ds(pl.multiple_of(n * size, size), size))
                return carry

            lax.fori_loop(0, extent // size, columns, 0)

        over(gate_rows, width, 256)

        @pl.when(i == last_group)
        def _():
            give_half(0)

        over(up_rows, width, 256)

        @pl.when(i == half_way)
        def _():
            advance(masks[1])
            y_start(masks[2])

        @pl.when(i == last_group)
        def _():
            give_half(1)

        over(down_rows, both, tile)

        @pl.when(first & (i == newest * groups - 1))
        def _():
            for r in range(ny):
                gather.line(newest, r, False).finish(late_hops)
            gather.finish_passes(newest, range(2, nz))

        @pl.when(jnp.logical_not(first) & (i == newest * groups - 1))
        def _():
            gather.finish(micro + newest, [], hops=late_hops)

        @pl.when(i < last_group)
        def _():
            start_load(i + 1)

        @pl.when(i == half_way)
        def _():
            small_z()

        return carry

    lax.fori_loop(0, micro * groups, group, 0)
    for mask in masks[4:]:
        y_start(mask)

    def turn_copy(n, k):
        dst = (gate_ref, up_ref)[n]
        return remote(cland.at[n, k], dst.at[g.d], ts.at[n, k], tr.at[n, k], g.z_ahead(k))

    def turn_near(n):
        return pltpu.make_async_copy(cland.at[n, 0], (gate_ref, up_ref)[n].at[g.d], ts.at[n, 0])

    def turn_arrival(n, k):
        dst = (gate_ref, up_ref)[n]
        return remote(cland.at[n, k], dst.at[g.z_of(nz - k)], ts.at[n, k], tr.at[n, k], g.z_behind(k))

    down_copy = remote(dsend, dland, cs.at[2, 0], cr.at[2, 0], g.core)
    dsend[...] = acc_d[half:both, :].astype(BF16)
    down_copy.start()
    for n in range(2):
        for k in order[:-1]:
            core_copy(n, k).wait_recv()
            total = accs[n][width_rows(k), 0:half] + cland[n, k].astype(F32)
            cland[n, k] = total.astype(BF16)
            turn_copy(n, k).start()
    for mask in masks[3:-1]:
        advance(mask)
    for n in range(2):
        core_copy(n, 0).wait_recv()
        cland[n, 0] = (accs[n][width_rows(0), 0:half] + cland[n, 0].astype(F32)).astype(BF16)
        turn_near(n).start()
    down_copy.wait_recv()
    dland[...] = (acc_d[0:half, :] + dland[...].astype(F32)).astype(BF16)
    down_near = pltpu.make_async_copy(dland, down_ref, ts.at[0, nz])
    down_near.start()

    total = sm_s[1]
    for k in range(1, nz):
        sm_z(k).wait_recv()
        total = total + smz[k]
    small_out[...] = total

    advance(0)
    for k in range(1, nz):
        for n in range(2):
            turn_arrival(n, k).wait_recv()

    for r in range(1, ny):
        sm_y(r).wait_send()
        for k in range(nz):
            y_copy(r, k).wait_send()
    for k in range(1, nz):
        sm_z(k).wait_send()
        z_copy(k).wait_send()
        for n in range(2):
            turn_copy(n, k).wait_send()
    for n in range(2):
        for k in range(nz):
            core_copy(n, k).wait_send()
    down_copy.wait_send()
    for n in range(2):
        turn_near(n).wait()
    down_near.wait()


def finish_kernel(nz, experts, gate_in, up_in, down_in, attn_in, small_in, gate, up, down, qkv, out, router, again, mgain):
    slice_h = gate_in.shape[2] // 2
    for src, dst in ((gate_in, gate), (up_in, up)):
        for j in range(2):
            cols = slice(j * slice_h, (j + 1) * slice_h)
            dst[0, j] = jnp.concatenate([src[z, :, cols].astype(F32) for z in range(nz)], 1)
    down[0, 0] = down_in[...].astype(F32)
    shard, split = qkv.shape[1], qkv.shape[2]
    qkv[0] = attn_in[0:shard, 0:split]
    out[0] = attn_in[0:shard, split:]
    rows, width = small_in.shape
    base = (lax.axis_index("expert") * nz + lax.axis_index("dp")) * shard
    at = lax.broadcasted_iota(jnp.int32, (width, 128), 0)
    lane = lax.broadcasted_iota(jnp.int32, (width, 128), 1)
    pick = jnp.where(at == base + lane, 1.0, 0.0).astype(F32)
    got = jnp.dot(small_in[...], pick, precision=lax.Precision.HIGHEST, preferred_element_type=F32)
    again[...] = got[ROUTER_ROWS : ROUTER_ROWS + 1, 0:shard]
    mgain[...] = got[ROUTER_ROWS + 1 : ROUTER_ROWS + 2, 0:shard]
    turned = jnp.transpose(jnp.concatenate([got, jnp.zeros((128 - rows, 128), F32)], 0))
    router[0] = turned[0:shard, 0:experts]


VMEM = pl.BlockSpec(memory_space=pltpu.VMEM)
ANY = pl.BlockSpec(memory_space=pl.ANY)
DMA = pltpu.SemaphoreType.DMA


def per_device(
    ne, nz, sections,
    layer_input, cotangent, segments, routes, attn_gain, w_qkv, w_out, moe_gain, w_router, w_gate, w_up, w_down,
):
    ny = ne // 2
    micro, _, tokens, width = layer_input.shape
    total_experts = w_router.shape[2]
    hidden = w_gate.shape[3]
    owners = ("expert", "dp")
    shard = w_qkv.shape[1]
    place_e, place_d = lax.axis_index("expert"), lax.axis_index("dp")
    small = jnp.concatenate(
        [
            w_router[0],
            jnp.zeros((shard, ROUTER_ROWS - total_experts), BF16),
            attn_gain[0][:, None],
            moe_gain[0][:, None],
            jnp.zeros((shard, 128 - ROUTER_ROWS - 2), BF16),
        ],
        1,
    ).astype(F32)
    own_routes = jnp.transpose(routes[0, :, 0], (0, 2, 1))
    cos, sin = rotary_tables(tokens)
    segs = segments[:, 0]
    segc, segr = segs[:, :, None], segs[:, None, :]
    x = layer_input[:, 0]
    cot = cotangent[:, 0]
    wg, wu, wd = w_gate[0], w_up[0], w_down[0]
    qkv_width = w_qkv.shape[2]
    slice_h = hidden // nz
    half = 2 * slice_h

    def shape(*dims, dtype=BF16):
        return jax.ShapeDtypeStruct(dims, dtype)

    grid_sems = [DMA((4, 2, nz, ny)) for _ in range(4)]
    small, routes_all, wqkv, wout, slices, partner = pl.pallas_call(
        functools.partial(gather_kernel, ny, nz),
        out_shape=(
            shape(SMALL_ROWS, width),
            shape(ne, nz, *own_routes.shape, dtype=jnp.int32),
            shape(ne, nz, shard, qkv_width),
            shape(ne, nz, shard, width),
            shape(3, half, width),
            shape(3, half, width),
        ),
        in_specs=[VMEM] + [ANY] * 6,
        out_specs=tuple([VMEM] + [ANY] * 5),
        scratch_shapes=[
            pltpu.VMEM((ne, nz, shard, 128), F32),
            pltpu.VMEM(wg.shape, BF16),
            pltpu.VMEM(wu.shape, BF16),
            pltpu.VMEM((2, 2, hidden, width), BF16),
            DMA((2,)), DMA((4,)),
        ]
        + grid_sems
        + [DMA((4, 2, nz)), DMA((4, 2, nz)), DMA((3, 2)), DMA((3, 2)), DMA((3, 2))],
        compiler_params=pltpu.CompilerParams(
            collective_id=3, has_side_effects=True, vmem_limit_bytes=60 * 2**20
        ),
        name="gather_weights",
    )(small, own_routes, w_qkv[0], w_out[0], wg, wu, wd)
    wqkv = wqkv.reshape(width, qkv_width)
    wout = wout.reshape(width, width)
    routes_all = routes_all.reshape((ne * nz,) + own_routes.shape)
    weights = [pltpu.VMEM(w.shape, BF16) for w in (wqkv, wout, wg, wu, wd)]
    hop_sems = [DMA((micro, HOP_CHUNKS)) for _ in range(2)]
    block = width // ne

    def gather_sems(count):
        return [DMA((count, ny, 2, nz))] * 2 + [DMA((count, 2, nz, ny))] * 2 + [DMA((count, ny))]

    def returns(wide):
        return [
            pltpu.VMEM((tokens, wide), BF16),
            pltpu.VMEM((max(1, ny - 1), tokens, wide), BF16),
            pltpu.VMEM((max(1, ny - 1), tokens, wide), BF16),
            pltpu.VMEM((tokens, wide), BF16),
            pltpu.VMEM((max(1, ny - 1), tokens, wide), BF16),
            pltpu.VMEM((max(1, ny - 1), tokens, wide), BF16),
        ]

    out, hin, h1, qkv, obb, xm, gates, zf, obp = pl.pallas_call(
        functools.partial(forward_kernel, ny, nz, sections),
        out_shape=(
            shape(micro, tokens, width),
            shape(micro, tokens, width),
            shape(micro, tokens, width, dtype=F32),
            shape(micro, tokens, qkv_width),
            shape(micro, ne, tokens, block),
            shape(micro, ny, 2, tokens, width),
            shape(micro, ny, 2, ROUTER_ROWS, tokens, dtype=F32),
            shape(1, nz, ny, tokens, width),
            shape(micro, ny, tokens, block),
        ),
        in_specs=[VMEM] * 7 + [ANY] * 6,
        out_specs=tuple([VMEM] * 7 + [ANY] * 2),
        scratch_shapes=weights
        + [
            pltpu.VMEM((tokens, width), BF16),
            pltpu.VMEM((2, 2 * tokens, hidden), BF16),
            pltpu.VMEM((tokens, width), F32),
            pltpu.VMEM((tokens // FORWARD_CHUNKS, width), F32),
        ]
        + returns(width)
        + [DMA((5,))]
        + gather_sems(1)
        + [DMA((ny,)), DMA((ny,))]
        + hop_sems
        + [DMA((micro, ny))] * 2
        + sem_shapes(micro, ny, FORWARD_CHUNKS),
        compiler_params=pltpu.CompilerParams(
            collective_id=0, has_side_effects=True, vmem_limit_bytes=60 * 2**20
        ),
        name="layers_forward",
    )(x, segc, segr, routes_all, small, cos, sin, cot, wqkv, wout, wg, wu, wd)

    wide = width + 128
    every = (2, ny, 2, tokens, hidden)
    gin, grows, xab, dqkv, dattn, gsmall, zb, xap, dqp, dtp = pl.pallas_call(
        functools.partial(backward_kernel, ny, nz, sections),
        out_shape=(
            shape(micro, tokens, width),
            shape(micro, ny, 2, tokens, width),
            shape(micro, ne, tokens, block),
            shape(micro, tokens, qkv_width),
            shape(micro, tokens, width),
            shape(SMALL_ROWS, width, dtype=F32),
            shape(2 * micro, nz, ny, tokens, width),
            shape(micro, ny, tokens, block),
            shape(micro, tokens, qkv_width),
            shape(micro, tokens, width),
        ),
        in_specs=[VMEM] * 10 + [ANY] * 6,
        out_specs=tuple([VMEM] * 6 + [ANY] * 4),
        scratch_shapes=weights
        + [
            pltpu.VMEM((ny, 2, tokens, width), BF16),
            pltpu.VMEM(every, BF16),
            pltpu.VMEM(every, BF16),
            pltpu.VMEM(every, BF16),
            pltpu.VMEM((2, 2 * tokens, hidden), BF16),
            pltpu.VMEM((2, 2 * tokens, hidden), BF16),
            pltpu.VMEM((tokens, wide), F32),
            pltpu.VMEM((tokens // BACKWARD_CHUNKS, wide), F32),
            pltpu.VMEM((tokens, width), F32),
            pltpu.VMEM((tokens, width), F32),
        ]
        + returns(wide)
        + [DMA((5,)), DMA]
        + gather_sems(2 * micro)
        + hop_sems
        + [DMA((micro, ny + 2))] * 2
        + sem_shapes(micro, ny, BACKWARD_CHUNKS * HOP_CHUNKS),
        compiler_params=pltpu.CompilerParams(
            collective_id=1, has_side_effects=True, vmem_limit_bytes=62 * 2**20
        ),
        name="layers_backward",
    )(cot, segc, segr, small, cos, sin, hin, h1, qkv, gates, xm, wqkv, wout, wg, wu, wd)

    span_z = max(1, min(nz, 1024 // (ny * tokens)))
    rows = span_z * ny * tokens
    padded = -(-shard // 16) * 16
    attn_width = qkv_width + width
    part = width // nz
    small_shape = (SMALL_ROWS, width)
    gate_g, up_g, down_g, attn_g, small_g, _ = pl.pallas_call(
        functools.partial(tail_kernel, ny, nz, sections, span_z),
        out_shape=(
            shape(nz, part, half),
            shape(nz, part, half),
            shape(half, width),
            shape(padded, attn_width, dtype=F32),
            shape(*small_shape, dtype=F32),
            shape(*zb.shape),
        ),
        in_specs=[VMEM] * 3 + [ANY] * 12,
        out_specs=tuple([ANY] * 3 + [VMEM] * 2 + [ANY]),
        input_output_aliases={4: 5},
        scratch_shapes=[
            pltpu.VMEM((3, 2 * half, width), BF16),
            pltpu.VMEM((span_z, ny, tokens, width), BF16),
            pltpu.VMEM((span_z, ny, tokens, width), BF16),
            pltpu.VMEM((rows, 2 * half), BF16),
            pltpu.VMEM((rows, 2 * half), BF16),
            pltpu.VMEM((rows, 2 * half), BF16),
            pltpu.VMEM((width, 2 * half), F32),
            pltpu.VMEM((width, 2 * half), F32),
            pltpu.VMEM((2 * half, width), F32),
            pltpu.VMEM((2, nz, part, half), BF16),
            pltpu.VMEM((2, nz, part, half), BF16),
            pltpu.VMEM((half, width), BF16),
            pltpu.VMEM((half, width), BF16),
            pltpu.VMEM((ny, 2, micro, tokens, block), BF16),
            pltpu.VMEM((ny, 2, micro, tokens, block), BF16),
            pltpu.VMEM((2, micro, tokens, qkv_width), BF16),
            pltpu.VMEM((2, micro, tokens, width), BF16),
            pltpu.VMEM((nz, padded, attn_width), BF16),
            pltpu.VMEM((max(1, ny - 1), nz, padded, attn_width), BF16),
            pltpu.VMEM((max(1, ny - 1), nz, padded, attn_width), BF16),
            pltpu.VMEM((max(1, nz - 1), padded, attn_width), BF16),
            pltpu.VMEM((2,) + small_shape, F32),
            pltpu.VMEM((ny,) + small_shape, F32),
            pltpu.VMEM((nz,) + small_shape, F32),
            DMA((2,)), DMA((2,)),
            DMA((4 * ny * micro + 4,)),
            DMA((ny + nz,)), DMA((ny + nz,)),
            DMA((3, nz)), DMA((3, nz)),
            DMA((2, nz + 1)), DMA((2, nz)),
            DMA((ny, nz)), DMA((ny, nz)),
            DMA((1, nz)), DMA((1, nz)),
        ]
        + gather_sems(2 * micro),
        compiler_params=pltpu.CompilerParams(
            collective_id=2, has_side_effects=True, vmem_limit_bytes=62 * 2**20
        ),
        name="weight_gradients",
    )(routes_all, small, gsmall, zf, zb, slices, partner, xab, obb, dqkv, dattn, xap, obp, dqp, dtp)

    steps = 2
    finals = pl.pallas_call(
        functools.partial(finish_kernel, nz, total_experts),
        grid=(steps,),
        out_shape=(
            shape(1, 2, part, hidden, dtype=F32),
            shape(1, 2, part, hidden, dtype=F32),
            shape(1, 2, slice_h, width, dtype=F32),
            shape(1, shard, qkv_width, dtype=F32),
            shape(1, shard, width, dtype=F32),
            shape(1, shard, total_experts, dtype=F32),
            shape(1, shard, dtype=F32),
            shape(1, shard, dtype=F32),
        ),
        in_specs=[
            pl.BlockSpec((nz, part // steps, half), lambda i: (0, i, 0)),
            pl.BlockSpec((nz, part // steps, half), lambda i: (0, i, 0)),
            pl.BlockSpec((slice_h, width), lambda i: (i, 0)),
            pl.BlockSpec((padded, attn_width), lambda i: (0, 0)),
            pl.BlockSpec(small_shape, lambda i: (0, 0)),
        ],
        out_specs=(
            pl.BlockSpec((1, 2, part // steps, hidden), lambda i: (0, 0, i, 0)),
            pl.BlockSpec((1, 2, part // steps, hidden), lambda i: (0, 0, i, 0)),
            pl.BlockSpec((1, 1, slice_h, width), lambda i: (0, i, 0, 0)),
            pl.BlockSpec((1, shard, qkv_width), lambda i: (0, 0, 0)),
            pl.BlockSpec((1, shard, width), lambda i: (0, 0, 0)),
            pl.BlockSpec((1, shard, total_experts), lambda i: (0, 0, 0)),
            pl.BlockSpec((1, shard), lambda i: (0, 0)),
            pl.BlockSpec((1, shard), lambda i: (0, 0)),
        ),
        compiler_params=pltpu.CompilerParams(vmem_limit_bytes=60 * 2**20),
        name="finish_gradients",
    )(gate_g, up_g, down_g, attn_g, small_g)
    grad_gate, grad_up, grad_down, grad_qkv, grad_out, grad_router, grad_again, grad_mgain = finals
    return (
        out[None, :, None],
        gin[None, :, None],
        grad_again,
        grad_qkv,
        grad_out,
        grad_mgain,
        grad_router,
        grad_gate,
        grad_up,
        grad_down,
    )


def solution(mesh):
    owners = ("expert", "dp")
    return jax.shard_map(
        functools.partial(per_device, mesh.shape["expert"], mesh.shape["dp"], mesh.shape["section"]),
        mesh=mesh,
        in_specs=(
            P(None, owners, None, None),
            P(None, owners, None, None),
            P(None, owners, None),
            P("section", None, owners, None, None),
            P("section", owners),
            P("section", owners, None),
            P("section", owners, None),
            P("section", owners),
            P("section", owners, None),
            P("section", "expert", None, None),
            P("section", "expert", None, None),
            P("section", "expert", None, None),
        ),
        out_specs=(
            P("section", None, owners, None, None),
            P("section", None, owners, None, None),
            P("section", owners),
            P("section", owners, None),
            P("section", owners, None),
            P("section", owners),
            P("section", owners, None),
            P("section", "expert", "dp", None),
            P("section", "expert", "dp", None),
            P("section", "expert", "dp", None),
        ),
        check_vma=False,
    )
```

```python
import functools

import jax
import jax.numpy as jnp
import numpy as np
from jax import lax
from jax.experimental import pallas as pl
from jax.experimental.pallas import tpu as pltpu
from jax.sharding import PartitionSpec as P

HEAD = 128
QUERY_HEADS = 12
KEY_VALUE_HEADS = 2
GROUP = QUERY_HEADS // KEY_VALUE_HEADS
EPS = 1e-06
THETA = 1000000.0
NEGATIVE = -1e30
SCALE = HEAD ** (-0.5)
ROUTER_ROWS = 16
SMALL_ROWS = 32
FORWARD_CHUNKS = 2
BACKWARD_CHUNKS = 1
HOP_CHUNKS = 2
MESH = pl.DeviceIdType.MESH
F32 = jnp.float32
BF16 = jnp.bfloat16
GELU_C = float(np.sqrt(2.0 / np.pi))
GELU_A = 0.044715


def dot(a, b):
    return jnp.dot(a, b, preferred_element_type=F32)


def dot_nt(a, b):
    return lax.dot_general(a, b, (((1,), (1,)), ((), ())), preferred_element_type=F32)


def dot_tn(a, b):
    return lax.dot_general(a, b, (((0,), (0,)), ((), ())), preferred_element_type=F32)


def rotary_tables(tokens):
    places = np.arange(tokens, dtype=np.float64)
    inverse = THETA ** (-2.0 * np.arange(HEAD // 2, dtype=np.float64) / HEAD)
    angles = places[:, None] * inverse[None, :]
    cosine, sine = np.cos(angles), np.sin(angles)
    return (
        jnp.asarray(np.concatenate([cosine, cosine], 1), F32),
        jnp.asarray(np.concatenate([-sine, sine], 1), F32),
    )


def mask_bias(col, row):
    tokens = row.shape[1]
    ti = lax.broadcasted_iota(jnp.int32, (tokens, tokens), 0)
    ui = lax.broadcasted_iota(jnp.int32, (tokens, tokens), 1)
    return jnp.where((col == row) & (ui <= ti), 0.0, NEGATIVE).astype(F32)


def heads_of(value, first, count):
    return jnp.concatenate(
        [value[:, (first + i) * HEAD : (first + i + 1) * HEAD] for i in range(count)], 0
    )


def attention_shares(q6, k, bias6):
    scores = dot_nt(q6, k) * SCALE + bias6
    top = jnp.max(scores, -1, keepdims=True)
    raised = jnp.exp(scores - top)
    return raised / jnp.sum(raised, -1, keepdims=True)


class Place:
    def __init__(self, ny, nz):
        self.ny = ny
        self.nz = nz
        self.s = lax.axis_index("section")
        self.e = lax.axis_index("expert")
        self.d = lax.axis_index("dp")
        self.y = lax.div(self.e, 2)
        self.c = lax.rem(self.e, 2)
        self.core = (self.s, self.y * 2 + 1 - self.c, self.d)
        self.x = (1 - self.s, self.e, self.d)

    def ahead(self, r):
        return (self.s, lax.rem(self.y + r, self.ny) * 2 + self.c, self.d)

    def behind(self, r):
        return (self.s, lax.rem(self.y + self.ny - r, self.ny) * 2 + self.c, self.d)

    def pack(self, r, other):
        core = 1 - self.c if other else self.c
        return lax.rem(self.y + r, self.ny) * 2 + core

    def z_of(self, k):
        return lax.rem(self.d + k, self.nz)

    def z_ahead(self, k):
        return (self.s, self.e, self.z_of(k))

    def z_behind(self, k):
        return (self.s, self.e, self.z_of(self.nz - k))

    def greet(self, with_x=True):
        barrier = pltpu.get_barrier_semaphore()
        partners = [self.core] + ([self.x] if with_x else [])
        partners += [self.ahead(r) for r in range(1, self.ny)]
        partners += [self.z_ahead(k) for k in range(1, self.nz)]
        for partner in partners:
            pl.semaphore_signal(barrier, inc=1, device_id=partner, device_id_type=MESH)
        pl.semaphore_wait(barrier, len(partners))


def remote(src, dst, send, recv, device):
    return pltpu.make_async_remote_copy(
        src_ref=src, dst_ref=dst, send_sem=send, recv_sem=recv, device_id=device, device_id_type=MESH
    )


class Line:
    def __init__(self, place, slot, send, recv):
        self.place, self.slot, self.send, self.recv = place, slot, send, recv

    def origin(self, way, h):
        return self.place.d - h if way == 0 else self.place.d + h

    def comes(self, way, h):
        return self.place.d >= h if way == 0 else self.place.d + h < self.place.nz

    def leaves(self, way, h):
        d, nz = self.place.d, self.place.nz
        return (d + 1 < nz) & (d >= h - 1) if way == 0 else (d >= 1) & (d + h - 1 < nz)

    def out(self, way, h, src=None):
        g = self.place
        at = self.slot(self.origin(way, h - 1))
        next_door = (g.s, g.e, g.d + 1 if way == 0 else g.d - 1)
        return remote(at if src is None else src, at, self.send.at[way, h], self.recv.at[way, h], next_door)

    def came(self, way, h):
        g = self.place
        at = self.slot(self.origin(way, h))
        return remote(at, at, self.send.at[way, h], self.recv.at[way, h], g.core)

    def start(self, src):
        for way in range(2):
            @pl.when(self.leaves(way, 1))
            def _():
                self.out(way, 1, src).start()

    def go_on(self, h):
        for way in range(2):
            @pl.when(self.leaves(way, h))
            def _():
                self.out(way, h).start()

    def step(self, h, then=None, forward=True):
        for way in range(2):
            @pl.when(self.comes(way, h))
            def _():
                self.came(way, h).wait_recv()
                if forward and h + 1 < self.place.nz:
                    @pl.when(self.leaves(way, h + 1))
                    def _():
                        self.out(way, h + 1).start()
                if then is not None:
                    then(way, h)

    def finish(self, hops=None):
        for way in range(2):
            for h in range(1, self.place.nz) if hops is None else hops:
                @pl.when(self.leaves(way, h))
                def _():
                    self.out(way, h).wait_send()


class Gather:
    def __init__(self, place, buf, send, recv, ysend, yrecv, local):
        self.place, self.buf, self.local = place, buf, local
        self.send, self.recv, self.ysend, self.yrecv = send, recv, ysend, yrecv
        self.tokens = buf.shape[3]
        self.cut = self.tokens // 2

    def rows(self, r, whole):
        return pl.ds(0, self.tokens if whole or r == 0 else self.cut)

    def line(self, i, r, whole=True):
        rows = self.rows(r, whole)
        return Line(self.place, lambda zz: self.buf.at[i, zz, r, rows], self.send.at[i, r], self.recv.at[i, r])

    def near(self, i, r, src):
        return pltpu.make_async_copy(src, self.buf.at[i, self.place.d, r], self.local.at[i, r])

    def across(self, i, way, h, r):
        at = self.line(i, 0).origin(way, h)
        rest = pl.ds(self.cut, self.tokens - self.cut)
        return remote(
            self.buf.at[i, at, 0, rest], self.buf.at[i, at, r, rest],
            self.ysend.at[i, way, h, r], self.yrecv.at[i, way, h, r], self.place.behind(r),
        )

    def start(self, i, r, src, keep=True, whole=True):
        if keep:
            self.near(i, r, src).start()
        self.line(i, r, whole).start(src.at[self.rows(r, whole)])

    def step(self, i, h, whole=True, forward=True):
        for r in range(self.place.ny):
            self.line(i, r, whole).step(h, forward=forward)

    def go_on(self, i, h, whole=True):
        for r in range(self.place.ny):
            self.line(i, r, whole).go_on(h)

    def passes(self, i, hops):
        line = self.line(i, 0)
        for h in hops:
            for way in range(2):
                @pl.when(line.comes(way, h))
                def _():
                    for r in range(1, self.place.ny):
                        self.across(i, way, h, r).start()

    def finish(self, i, kept, whole=True, hops=None):
        for r in kept:
            self.near(i, r, self.buf.at[i, self.place.d, r]).wait()
        for r in range(self.place.ny):
            self.line(i, r, whole).finish(hops)
        if not whole:
            self.finish_passes(i, hops)

    def finish_passes(self, i, hops=None):
        g = self.place
        line = self.line(i, 0)
        for h in range(1, g.nz) if hops is None else hops:
            for way in range(2):
                @pl.when(line.comes(way, h))
                def _():
                    for r in range(1, g.ny):
                        self.across(i, way, h, r).wait()


class Exchange:
    def __init__(self, place, chunks, rows_ref, retl, retc, rety, sendl, sendc, sendy, sems, parts=1):
        self.place, self.chunks, self.parts = place, chunks, parts
        self.rows_ref = rows_ref
        self.retl, self.retc, self.rety = retl, retc, rety
        self.sendl, self.sendc, self.sendy = sendl, sendc, sendy
        self.sems = sems
        self.tokens = rows_ref.shape[2]
        self.span = self.tokens // chunks

    def rows(self, q):
        return pl.ds(q * self.span, self.span)

    def core_own(self):
        g = self.place
        return remote(
            self.rows_ref.at[0, 0], self.rows_ref.at[0, 1], self.sems.cs.at[0, 0], self.sems.cr.at[0, 0], g.core
        )

    def y_part(self, r, i):
        g = self.place
        size = self.span // self.parts
        rows = pl.ds(i * size, size)
        return remote(
            self.rows_ref.at[0, 0, rows],
            self.rows_ref.at[r, 0, rows],
            self.sems.ys.at[r, i],
            self.sems.yr.at[r, i],
            g.behind(r),
        )

    def y_parts(self, r, q):
        return [self.y_part(r, q * self.parts + p) for p in range(self.parts)]

    def forward(self, r, q):
        g = self.place
        return remote(
            self.rows_ref.at[r, 0, self.rows(q)],
            self.rows_ref.at[r, 1, self.rows(q)],
            self.sems.cs.at[r, q],
            self.sems.cr.at[r, q],
            g.core,
        )

    def back_local(self):
        return remote(self.sendl, self.retl, self.sems.bs.at[0, 0], self.sems.br.at[0, 0], self.place.core)

    def back_core(self, r, q):
        return remote(
            self.sendc.at[r - 1, self.rows(q)],
            self.retc.at[r - 1, self.rows(q)],
            self.sems.bs.at[r, q],
            self.sems.br.at[r, q],
            self.place.core,
        )

    def back_y(self, r, q):
        g = self.place
        return remote(
            self.sendy.at[r - 1, self.rows(q)],
            self.rety.at[g.ny - r - 1, self.rows(q)],
            self.sems.zs.at[r, q],
            self.sems.zr.at[g.ny - r, q],
            g.ahead(r),
        )

    def back_y_arrival(self, r, q):
        g = self.place
        return remote(
            self.sendy.at[r - 1, self.rows(q)],
            self.rety.at[r - 1, self.rows(q)],
            self.sems.zs.at[r, q],
            self.sems.zr.at[r, q],
            g.ahead(r),
        )

    def send_own(self):
        for i in range(self.chunks * self.parts):
            self.send_part(i)
        self.core_own().start()

    def send_part(self, i):
        for r in range(1, self.place.ny):
            self.y_part(r, i).start()

    def run(self, local_block, remote_block, complete, early=None):
        ny = self.place.ny
        items = [(r, q) for q in range(self.chunks) for r in range(1, ny)]
        def arrive(r, q):
            for part in self.y_parts(r, q):
                part.wait_recv()
            self.forward(r, q).start()
            if q == self.chunks - 1:
                complete(r)

        if items and early is not None:
            @pl.when(early)
            def _():
                arrive(*items[0])

        self.core_own().wait_recv()
        local_block()
        self.back_local().start()
        if items and early is None:
            arrive(*items[0])
        if items and early is not None:
            @pl.when(jnp.logical_not(early))
            def _():
                arrive(*items[0])

        for i, (r, q) in enumerate(items):
            self.forward(r, q).wait_recv()
            own = remote_block(r, q)
            self.back_core(r, q).start()
            if i + 1 < len(items):
                arrive(*items[i + 1])
            self.back_core(r, q).wait_recv()
            here = self.rows(q)
            self.sendy[r - 1, here, :] = (own() + self.retc[r - 1, here, :].astype(F32)).astype(BF16)
            self.back_y(r, q).start()
        self.back_local().wait_recv()

    def arrived(self, q):
        for r in range(1, self.place.ny):
            self.back_y_arrival(r, q).wait_recv()

    def finish(self):
        ny = self.place.ny
        self.core_own().wait_send()
        self.back_local().wait_send()
        for q in range(self.chunks):
            for r in range(1, ny):
                for part in self.y_parts(r, q):
                    part.wait_send()
                self.forward(r, q).wait_send()
                self.back_core(r, q).wait_send()
                self.back_y(r, q).wait_send()


class Sems:
    def __init__(self, refs, m):
        self.cs, self.cr, self.ys, self.yr, self.bs, self.br, self.zs, self.zr = [ref.at[m] for ref in refs]


def sem_shapes(micro, ny, chunks):
    return [pltpu.SemaphoreType.DMA((micro, ny, chunks)) for _ in range(8)]


def chosen_gates(logits_t, route):
    experts = lax.broadcasted_iota(jnp.int32, logits_t.shape, 0)
    chosen = route[0:1, :] == experts
    for k in range(1, route.shape[0]):
        chosen = chosen | (route[k : k + 1, :] == experts)
    masked = jnp.where(chosen, logits_t, NEGATIVE)
    raised = jnp.where(chosen, jnp.exp(masked - jnp.max(masked, 0, keepdims=True)), 0.0)
    return raised / jnp.sum(raised, 0, keepdims=True)


def gate_lanes(gates_t, expert):
    rows = lax.broadcasted_iota(jnp.int32, gates_t.shape, 0)
    one = jnp.sum(jnp.where(rows == expert, gates_t, 0.0), 0, keepdims=True)
    return jnp.transpose(jnp.broadcast_to(one, (128, one.shape[1])))


def widen(lanes, width):
    return jnp.concatenate([lanes] * (width // 128), 1)


def gather_kernel(
    ny, nz,
    small_ref, route_h, wqkv_h, wout_h, wg_h, wu_h,
    small_t, route_o, wqkv_o, wout_o, slices_o,
    small_s, wg, wu, turned,
    lsem, own_sem, cs, cr, ys, yr, zs, zr, sls,
):
    g = Place(ny, nz)
    hidden, width = turned.shape[2], turned.shape[3]
    slice_h = hidden // nz
    loads = [pltpu.make_async_copy(src, dst, lsem.at[i]) for i, (src, dst) in enumerate(((wg_h, wg), (wu_h, wu)))]
    for copy in loads:
        copy.start()
    g.greet(with_x=False)
    arrays = ((small_ref, small_s), (route_h, route_o), (wqkv_h, wqkv_o), (wout_h, wout_o))
    count = len(arrays)

    def near(n):
        src, dst = arrays[n]
        return pltpu.make_async_copy(src, dst.at[g.e, g.d], own_sem.at[n])

    lines = [Line(g, lambda zz, dst=dst: dst.at[g.e, zz], zs.at[n], zr.at[n]) for n, (_, dst) in enumerate(arrays)]

    def along_y(n, way, h, r):
        src, dst = arrays[n]
        at = dst.at[g.e, lines[n].origin(way, h)]
        return remote(src if h == 0 else at, at, ys.at[n, way, h, r], yr.at[n, way, h, r], g.behind(r))

    def to_core(n, way, h, r):
        src, dst = arrays[n]
        at = dst.at[g.pack(r, False), lines[n].origin(way, h)]
        own = h == 0 and r == 0
        return remote(src if own else at, at, cs.at[n, way, h, r], cr.at[n, way, h, r], g.core)

    for n in range(count):
        for r in range(1, ny):
            along_y(n, 0, 0, r).start()
        lines[n].start(arrays[n][0])
        near(n).start()
        to_core(n, 0, 0, 0).start()

    def got_z(n, h):
        def then(way, h):
            for r in range(1, ny):
                along_y(n, way, h, r).start()
            to_core(n, way, h, 0).start()

        lines[n].step(h, then)

    def got_y(n, h):
        for way in range(1 if h == 0 else 2):
            def pass_on():
                for r in range(1, ny):
                    along_y(n, way, h, r).wait_recv()
                    to_core(n, way, h, r).start()

            if h == 0:
                pass_on()
            else:
                pl.when(lines[n].comes(way, h))(pass_on)

    parts = []
    for i in range(2):
        for t in range(nz // 2):
            here = pl.ds(pl.multiple_of(g.z_of(2 * t) * slice_h, slice_h), slice_h)
            for j in range(2):
                n = 2 * t + j
                to = slice(n * slice_h, (n + 1) * slice_h)
                parts.append(pltpu.make_async_copy(turned.at[i, j, here], slices_o.at[i, to], sls.at[i, n]))

    def turn(i, j, n):
        src = (wg, wu)[i]
        if j == 0 and n == 0:
            loads[i].wait()
        cols = slice(n * 256, (n + 1) * 256)
        turned[i, j, cols, :] = jnp.transpose(src[j, :, cols])

    turns = [(i, j, n) for i in range(2) for j in range(2) for n in range(hidden // 256)]

    z_items = [(n, h) for h in range(1, nz) for n in range(count)]
    y_items = [(n, 0) for n in range(count)] + z_items
    done = 0
    for i, item in enumerate(z_items):
        got_z(*item)
        if i % 2 == 1 or i >= count:
            got_y(*y_items[done])
            done += 1
        for piece in turns[:2]:
            turn(*piece)
        turns = turns[2:]
        if not turns and parts:
            for copy in parts:
                copy.start()
            started, parts = parts, []
    for item in y_items[done:]:
        got_y(*item)

    def each(act):
        for n in range(count):
            for h in range(nz):
                for way in range(1 if h == 0 else 2):
                    if h == 0:
                        act(n, way, h)
                    else:
                        pl.when(lines[n].comes(way, h))(lambda: act(n, way, h))

    def arrived(n, way, h):
        for r in range(ny):
            to_core(n, way, h, r).wait_recv()

    def sent(n, way, h):
        for r in range(ny):
            to_core(n, way, h, r).wait_send()
            if r:
                along_y(n, way, h, r).wait_send()

    each(arrived)
    for n in range(count):
        near(n).wait()
    gathered = small_s[...].reshape(width, small_s.shape[3])
    small_t[...] = jnp.transpose(gathered)[0:SMALL_ROWS].astype(BF16)
    each(sent)
    for line in lines:
        line.finish()
    for copy in started:
        copy.wait()


def forward_kernel(
    ny, nz, sections,
    x_ref, segc_ref, segr_ref, route_ref, small_ref, cos_ref, sin_ref,
    cot_h, slices_h, wqkv_h, wout_h, wg_h, wu_h, wd_h,
    out_ref, hin_ref, h1_ref, qkv_ref, obb_ref, xm_ref, gates_ref, zf_h, obp_h, share_h,
    wqkv, wout, wg, wu, wd, ob_s, hid, accl, accr, retl, retc, rety, sendl, sendc, sendy,
    wsem, zs, zr, zys, zyr, zl, gs, gr, xs, xr, ps, pr, hs, hr, *sem_refs,
):
    micro, tokens, width = x_ref.shape
    hidden = wg.shape[2]
    span = tokens // FORWARD_CHUNKS
    loads = [
        pltpu.make_async_copy(src, dst, wsem.at[i])
        for i, (src, dst) in enumerate([(wqkv_h, wqkv), (wout_h, wout), (wg_h, wg), (wu_h, wu), (wd_h, wd)])
    ]
    for load in loads:
        load.start()
    g = Place(ny, nz)
    g.greet()
    gain_a = small_ref[ROUTER_ROWS : ROUTER_ROWS + 1, :].astype(F32)
    gain_m = small_ref[ROUTER_ROWS + 1 : ROUTER_ROWS + 2, :].astype(F32)
    cos, sin = cos_ref[...], sin_ref[...]
    gather = Gather(g, zf_h, zs, zr, zys, zyr, zl)
    every = range(ny)
    first, last = g.s == 0, g.s == sections - 1

    slice_h = hidden // nz
    shares = [remote(slices_h.at[i], share_h.at[i], hs.at[i], hr.at[i], g.core) for i in range(2)]
    for t in range(nz // 2):
        here = pl.ds(pl.multiple_of(g.z_of(2 * t) * slice_h, slice_h), slice_h)
        for j in range(2):
            n = 2 * t + j
            to = slice(n * slice_h, (n + 1) * slice_h)
            shares.append(remote(wd_h.at[j, here], share_h.at[2, to], hs.at[2 + n], hr.at[2 + n], g.core))

    def cot_copy(r):
        return remote(cot_h.at[0], zf_h.at[0, g.d, r], gs.at[r], gr.at[r], g.behind(r))

    @pl.when(last)
    def _():
        for r in range(1, ny):
            cot_copy(r).start()
        gather.start(0, 0, cot_h.at[0])
        for r in range(1, ny):
            cot_copy(r).wait_recv()
            gather.start(0, r, zf_h.at[0, g.d, r], keep=False)
        for copy in shares:
            copy.start()
        gather.step(0, 1)

    def hop(m, q):
        here = pl.ds(q * (tokens // HOP_CHUNKS), tokens // HOP_CHUNKS)
        return remote(out_ref.at[m, here], hin_ref.at[m, here], xs.at[m, q], xr.at[m, q], g.x)

    def experts(rows, lanes, keep):
        count = rows.shape[0]
        for j in range(2):
            for n in range(hidden // 256):
                cols = slice(n * 256, (n + 1) * 256)
                a = dot(rows, wg[j, :, cols])
                b = dot(rows, wu[j, :, cols])
                act = 0.5 * a * (1.0 + jnp.tanh(GELU_C * (a + GELU_A * a * a * a)))
                hid[j, 0:count, cols] = (act * b).astype(BF16)
        for n in range(width // 512):
            cols = slice(n * 512, (n + 1) * 512)
            total = None
            for j in range(2):
                eo = dot(hid[j, 0:count, :], wd[j, :, cols]).astype(BF16).astype(F32)
                term = widen(lanes[j], 512) * eo
                total = term if total is None else total + term
            keep(cols, total)

    def partner(m, yy):
        return remote(obb_ref.at[m, yy * 2 + 1 - g.c], obp_h.at[m, yy], ps.at[m, yy], pr.at[m, yy], g.core)

    def body(m, carry):
        @pl.when(g.s == 0)
        def _():
            hin_ref[m] = x_ref[m]

        @pl.when(g.s > 0)
        def _():
            for q in range(HOP_CHUNKS):
                hop(m, q).wait_recv()

        h = hin_ref[m].astype(F32)
        xa = (h * lax.rsqrt(jnp.mean(h * h, -1, keepdims=True) + EPS) * gain_a).astype(BF16)

        @pl.when(m == 0)
        def _():
            loads[0].wait()

        turned = QUERY_HEADS + KEY_VALUE_HEADS
        for i in range(wqkv.shape[1] // 256):
            mixed = dot(xa, wqkv[:, i * 256 : (i + 1) * 256])
            for half in range(2):
                head = 2 * i + half
                part = mixed[:, half * HEAD : (half + 1) * HEAD]
                if head < turned:
                    part = part * cos + pltpu.roll(part, HEAD // 2, 1) * sin
                qkv_ref[m, :, head * HEAD : (head + 1) * HEAD] = part.astype(BF16)
        bias = mask_bias(segc_ref[m], segr_ref[m])
        bias6 = jnp.concatenate([bias] * GROUP, 0)
        qkv = qkv_ref.at[m]
        for kv in range(KEY_VALUE_HEADS):
            q6 = heads_of(qkv, kv * GROUP, GROUP)
            k = heads_of(qkv, QUERY_HEADS + kv, 1)
            v = heads_of(qkv, turned + kv, 1)
            shares = attention_shares(q6, k, bias6).astype(BF16)
            o6 = dot(shares, v).astype(BF16)
            for i in range(GROUP):
                head = kv * GROUP + i
                ob_s[:, head * HEAD : (head + 1) * HEAD] = o6[i * tokens : (i + 1) * tokens]

        @pl.when(m == 0)
        def _():
            loads[1].wait()

        ob = ob_s[...]
        block = obb_ref.shape[3]
        for i in range(2 * ny):
            obb_ref[m, i] = ob[:, i * block : (i + 1) * block]
        for n in range(width // 512):
            cols = slice(n * 512, (n + 1) * 512)
            h1_ref[m, :, cols] = hin_ref[m, :, cols].astype(F32) + dot(ob, wout[:, cols])
        h1 = h1_ref[m]
        xm_ref[m, 0, 0] = (h1 * lax.rsqrt(jnp.mean(h1 * h1, -1, keepdims=True) + EPS) * gain_m).astype(BF16)

        ex = Exchange(g, FORWARD_CHUNKS, xm_ref.at[m], retl, retc, rety, sendl, sendc, sendy, Sems(sem_refs, m))
        ex.send_own()

        def complete(r):
            @pl.when(first & (m == 0))
            def _():
                gather.start(0, r, xm_ref.at[0, r, 0])

        def move(h):
            if h + 1 < nz:
                @pl.when(last & (m == 0))
                def _():
                    gather.step(0, h + 1)

            if h < nz:
                @pl.when(first & (m == 1))
                def _():
                    gather.step(0, h)

        complete(0)
        move(1)

        @pl.when(m == 0)
        def _():
            for load in loads[2:]:
                load.wait()

        def gates_for(r, other, here):
            rows = xm_ref[m, r, other, here, :]
            logits_t = dot_nt(small_ref[0:ROUTER_ROWS, :], rows)
            gates_t = chosen_gates(logits_t, route_ref[g.pack(r, other) * nz + g.d, m][:, here])
            return gates_t

        def lanes_of(blocks):
            return [
                jnp.concatenate([gate_lanes(gates_t, 2 * g.e + j) for gates_t in blocks], 0) for j in range(2)
            ]

        full = slice(0, tokens)

        def local_block():
            blocks = []
            for other in range(2):
                gates_t = gates_for(0, other, full)
                gates_ref[m, 0, other] = gates_t
                blocks.append(gates_t)

            def keep(cols, total):
                accl[:, cols] = total[0:tokens]
                sendl[:, cols] = total[tokens:].astype(BF16)

            experts(xm_ref[m, 0].reshape(2 * tokens, width), lanes_of(blocks), keep)

        def remote_block(r, q):
            here = slice(q * span, (q + 1) * span)
            blocks = []
            for other in range(2):
                gates_t = gates_for(r, other, here)
                gates_ref[m, r, other, :, here] = gates_t
                blocks.append(jnp.concatenate([gates_t] * (128 // span), 1))
            lanes = [
                jnp.concatenate([gate_lanes(gates_t, 2 * g.e + j)[0:span] for gates_t in blocks], 0)
                for j in range(2)
            ]

            def keep(cols, total):
                accr[:, cols] = total[0:span]
                sendc[r - 1, here, cols] = total[span:].astype(BF16)

            experts(xm_ref[m, r, :, here, :].reshape(2 * span, width), lanes, keep)
            return lambda: accr[...]

        ex.run(local_block, remote_block, complete)
        for q in range(HOP_CHUNKS):
            here = slice(q * span, (q + 1) * span)
            ex.arrived(q)
            total = h1_ref[m, here, :] + accl[here, :] + retl[here, :].astype(F32)
            for r in range(1, ny):
                total = total + rety[r - 1, here, :].astype(F32)
            out_ref[m, here, :] = total.astype(BF16)

            @pl.when(g.s < sections - 1)
            def _():
                hop(m, q).start()

        ex.finish()
        for yy in range(ny):
            partner(m, yy).start()
        move(2)
        return carry

    lax.fori_loop(0, micro, body, 0)

    @pl.when(jnp.logical_not(last))
    def _():
        for copy in shares:
            copy.start()

    for m in range(micro):
        for yy in range(ny):
            partner(m, yy).wait()

    @pl.when(g.s < sections - 1)
    def _():
        for m in range(micro):
            for q in range(HOP_CHUNKS):
                hop(m, q).wait_send()

    @pl.when(first)
    def _():
        for h in range(3, nz):
            gather.step(0, h)
        gather.finish(0, every)

    for copy in shares:
        copy.wait()

    @pl.when(last)
    def _():
        for r in range(1, ny):
            cot_copy(r).wait_send()
        for h in range(4, nz):
            gather.step(0, h)
        gather.finish(0, [0])


def backward_kernel(
    ny, nz, sections,
    cot_ref, segc_ref, segr_ref, small_ref, cos_ref, sin_ref,
    hin_ref, h1_ref, qkv_ref, gates_ref,
    xm_h, wqkv_h, wout_h, wg_h, wu_h, wd_h,
    gin_ref, grows_ref, xab_ref, dqkv_ref, dattn_ref, gsmall_ref, zb_h, xap_h, dqp_h, dtp_h,
    wqkv, wout, wg, wu, wd, xm_s, hid, act_s, slope_s, da_s, db_s, accl, accr, dh1_s, n_s,
    retl, retc, rety, sendl, sendc, sendy,
    wsem, xmsem, zs, zr, zys, zyr, zl, xs, xr, ps, pr, *sem_refs,
):
    micro, tokens, width = cot_ref.shape
    hidden = wg.shape[2]
    span = tokens // BACKWARD_CHUNKS
    loads = [
        pltpu.make_async_copy(src, dst, wsem.at[i])
        for i, (src, dst) in enumerate([(wg_h, wg), (wu_h, wu), (wd_h, wd), (wout_h, wout), (wqkv_h, wqkv)])
    ]
    for load in loads:
        load.start()
    g = Place(ny, nz)
    g.greet()
    gain_a = small_ref[ROUTER_ROWS : ROUTER_ROWS + 1, :].astype(F32)
    gain_m = small_ref[ROUTER_ROWS + 1 : ROUTER_ROWS + 2, :].astype(F32)
    cos, sin = cos_ref[...], sin_ref[...]
    gsmall_ref[...] = jnp.zeros_like(gsmall_ref)
    gather = Gather(g, zb_h, zs, zr, zys, zyr, zl)
    every = range(ny)
    first, last = g.s == 0, g.s == sections - 1

    @pl.when(first)
    def _():
        for m in range(1, micro):
            for r in every:
                gather.start(micro + m, r, xm_h.at[m, r, 0])
            for h in range(1, nz):
                gather.step(micro + m, h)

    def hop(m, q):
        here = pl.ds(q * (tokens // HOP_CHUNKS), tokens // HOP_CHUNKS)
        return remote(gin_ref.at[m, here], grows_ref.at[m, 0, 0, here], xs.at[m, q], xr.at[m, q], g.x)

    def partner(m):
        pairs = [(dattn_ref.at[m], dtp_h.at[m]), (dqkv_ref.at[m], dqp_h.at[m])]
        pairs += [(xab_ref.at[m, yy * 2 + 1 - g.c], xap_h.at[m, yy]) for yy in range(ny)]
        return [remote(src, dst, ps.at[m, n], pr.at[m, n], g.core) for n, (src, dst) in enumerate(pairs)]

    def late(m):
        for h in range(3, nz):
            gather.step(m, h, whole=False)

    def body(m, carry):
        load_xm = pltpu.make_async_copy(xm_h.at[m], xm_s, xmsem)
        load_xm.start()

        @pl.when(last)
        def _():
            grows_ref[m, 0, 0] = cot_ref[m]
            for r in every:
                gather.start(m, r, xm_h.at[m, r, 0], whole=False)

        ex = Exchange(
            g, BACKWARD_CHUNKS, grows_ref.at[m], retl, retc, rety, sendl, sendc, sendy, Sems(sem_refs, m), HOP_CHUNKS
        )

        @pl.when(last)
        def _():
            ex.send_own()

        @pl.when(m == 0)
        def _():
            for load in loads[:3]:
                load.wait()

        load_xm.wait()

        def again(r, _):
            rows = xm_s[r].reshape(2 * tokens, width)
            for j in range(2):
                for n in range(hidden // 256):
                    cols = slice(n * 256, (n + 1) * 256)
                    a = dot(rows, wg[j, :, cols])
                    b = dot(rows, wu[j, :, cols])
                    square = a * a
                    th = jnp.tanh(GELU_C * (a + GELU_A * square * a))
                    half = 0.5 * (1.0 + th)
                    act = a * half
                    slope = half + (0.5 * GELU_C) * a * (1.0 - th * th) * (1.0 + (3.0 * GELU_A) * square)
                    shape = (2, tokens, 256)
                    hid[j, r, :, :, cols] = (act * b).astype(BF16).reshape(shape)
                    act_s[j, r, :, :, cols] = act.astype(BF16).reshape(shape)
                    slope_s[j, r, :, :, cols] = (slope * b).astype(BF16).reshape(shape)
            return 0

        @pl.when(first)
        def _():
            lax.fori_loop(0, ny, again, 0)

            @pl.when(m > 0)
            def _():
                late(m - 1)

            for q in range(HOP_CHUNKS):
                hop(m, q).wait_recv()
                ex.send_part(q)
            ex.core_own().start()

        def complete(r):
            src = grows_ref.at[m, r, 0]

            @pl.when(first)
            def _():
                gather.start(m, r, src, whole=False)

        open_end = first & (m == micro - 1)

        def move(hops):
            for h in hops:
                gather.step(m, h, whole=False)

        complete(0)

        @pl.when(last)
        def _():
            lax.fori_loop(0, ny, again, 0)


        def experts(rows, r, here, keep):
            count = 2 * (here.stop - here.start)
            part = slice(0, count)
            lane = lax.broadcasted_iota(jnp.int32, (count, 128), 1)
            gate_grads = jnp.zeros((count, 128), F32)
            for j in range(2):
                expert = 2 * g.e + j
                lanes = []
                for other in range(2):
                    gates_t = gates_ref[m, r, other]
                    lanes.append(gate_lanes(gates_t, expert)[here])
                lanes = widen(jnp.concatenate(lanes, 0), 256)
                summed = jnp.zeros((count, 1), F32)
                for n in range(hidden // 256):
                    cols = slice(n * 256, (n + 1) * 256)
                    u = dot_nt(rows, wd[j, cols, :])
                    inner = hid[j, r, :, here, cols].reshape(count, 256).astype(F32)
                    summed = summed + jnp.sum(u * inner, -1, keepdims=True)
                    u = u * lanes
                    slope = slope_s[j, r, :, here, cols].reshape(count, 256).astype(F32)
                    act = act_s[j, r, :, here, cols].reshape(count, 256).astype(F32)
                    da_s[j, part, cols] = (u * slope).astype(BF16)
                    db_s[j, part, cols] = (u * act).astype(BF16)
                high = summed.astype(BF16).astype(F32)
                gate_grads = jnp.where(lane == expert, high, gate_grads)
                gate_grads = jnp.where(lane == expert + 64, summed - high, gate_grads)
            for n in range(width // 512):
                cols = slice(n * 512, (n + 1) * 512)
                total = None
                for j in range(2):
                    term = dot_nt(da_s[j, part, :], wg[j, cols, :]) + dot_nt(db_s[j, part, :], wu[j, cols, :])
                    total = term if total is None else total + term
                keep(cols, total)
            keep(slice(width, width + 128), gate_grads)

        full = slice(0, tokens)

        def local_block():
            def keep(cols, total):
                accl[:, cols] = total[0:tokens]
                sendl[:, cols] = total[tokens:].astype(BF16)

            experts(grows_ref[m, 0].reshape(2 * tokens, width), 0, full, keep)

        def remote_block(r, q):
            here = slice(q * span, (q + 1) * span)

            def keep(cols, total):
                accr[:, cols] = total[0:span]
                sendc[r - 1, here, cols] = total[span:].astype(BF16)

            experts(grows_ref[m, r, :, here, :].reshape(2 * span, width), r, here, keep)
            return lambda: accr[...]

        ex.run(local_block, remote_block, complete, last)
        move(range(1, 2))
        for q in range(BACKWARD_CHUNKS):
            ex.arrived(q)
        total = accl[...] + retl[...].astype(F32)
        for r in range(1, ny):
            total = total + rety[r - 1].astype(F32)
        dgates = total[:, width:]
        dgates = dgates + pltpu.roll(dgates, 64, 1)
        gates_t = gates_ref[m, 0, 0]
        gates = jnp.transpose(
            jnp.concatenate([gates_t, jnp.zeros((128 - ROUTER_ROWS, tokens), F32)], 0)
        )
        dlog = gates * (dgates - jnp.sum(gates * dgates, -1, keepdims=True))
        dlog = dlog[:, 0:SMALL_ROWS]
        high = dlog.astype(BF16)
        low = (dlog - high.astype(F32)).astype(BF16)
        router = small_ref[...]
        dxm = total[:, 0:width] + dot(high, router) + dot(low, router)
        xm = xm_s[0, 0]
        gsmall_ref[0:ROUTER_ROWS, :] += (dot_tn(high, xm) + dot_tn(low, xm))[0:ROUTER_ROWS]
        h1 = h1_ref[m]
        rinv = lax.rsqrt(jnp.mean(h1 * h1, -1, keepdims=True) + EPS)
        n2 = h1 * rinv
        gsmall_ref[ROUTER_ROWS + 1 : ROUTER_ROWS + 2, :] += jnp.sum(dxm * n2, 0, keepdims=True)
        scaled = dxm * gain_m
        dh1 = grows_ref[m, 0, 0].astype(F32) + rinv * (scaled - n2 * jnp.mean(scaled * n2, -1, keepdims=True))
        dh1_s[...] = dh1
        dattn = dh1.astype(BF16)
        dattn_ref[m] = dattn

        @pl.when(m == 0)
        def _():
            for load in loads[3:]:
                load.wait()

        @pl.when(jnp.logical_not(open_end))
        def _():
            move(range(2, min(3, nz)))

        @pl.when(first)
        def _():
            gather.passes(m, range(1, 2))

        @pl.when(first & (m > 0))
        def _():
            gather.passes(m - 1, range(3, nz))

        @pl.when(first & (m < micro - 1))
        def _():
            gather.passes(m, range(2, min(3, nz)))

        for copy in partner(m)[:1]:
            copy.start()
        bias = mask_bias(segc_ref[m], segr_ref[m])
        bias6 = jnp.concatenate([bias] * GROUP, 0)
        qkv = qkv_ref.at[m]
        turned = QUERY_HEADS + KEY_VALUE_HEADS

        def unturn(part):
            return part * cos - pltpu.roll(part, HEAD // 2, 1) * sin

        for kv in range(KEY_VALUE_HEADS):
            wide = GROUP * HEAD
            dob = dot_nt(dattn, wout[kv * wide : (kv + 1) * wide, :]).astype(BF16)
            dob6 = heads_of(dob, 0, GROUP)
            q6 = heads_of(qkv, kv * GROUP, GROUP)
            k = heads_of(qkv, QUERY_HEADS + kv, 1)
            v = heads_of(qkv, turned + kv, 1)
            shares = attention_shares(q6, k, bias6)
            dshares = dot_nt(dob6, v)
            dv = dot_tn(shares.astype(BF16), dob6)
            ds = (shares * (dshares - jnp.sum(shares * dshares, -1, keepdims=True))).astype(BF16)
            dq6 = dot(ds, k) * SCALE
            dk = dot_tn(ds, q6) * SCALE
            for i in range(GROUP):
                head = kv * GROUP + i
                dqkv_ref[m, :, head * HEAD : (head + 1) * HEAD] = unturn(
                    dq6[i * tokens : (i + 1) * tokens]
                ).astype(BF16)
            head = QUERY_HEADS + kv
            dqkv_ref[m, :, head * HEAD : (head + 1) * HEAD] = unturn(dk).astype(BF16)
            head = turned + kv
            dqkv_ref[m, :, head * HEAD : (head + 1) * HEAD] = dv.astype(BF16)

        h = hin_ref[m].astype(F32)
        rinv = lax.rsqrt(jnp.mean(h * h, -1, keepdims=True) + EPS)
        n1 = h * rinv
        xa = (n1 * gain_a).astype(BF16)
        block = xab_ref.shape[3]
        for i in range(2 * ny):
            xab_ref[m, i] = xa[:, i * block : (i + 1) * block]
        n_s[...] = n1
        dqkv = dqkv_ref[m]
        for n in range(width // 512):
            cols = slice(n * 512, (n + 1) * 512)
            accl[:, cols] = dot_nt(dqkv, wqkv[cols, :])
        dxa = accl[:, 0:width]
        n1 = n_s[...]
        gsmall_ref[ROUTER_ROWS : ROUTER_ROWS + 1, :] += jnp.sum(dxa * n1, 0, keepdims=True)
        scaled = dxa * gain_a
        grad = dh1_s[...] + rinv * (scaled - n1 * jnp.mean(scaled * n1, -1, keepdims=True))
        gin_ref[m] = grad.astype(BF16)

        @pl.when(g.s > 0)
        def _():
            for q in range(HOP_CHUNKS):
                hop(m, q).start()

        for copy in partner(m)[1:]:
            copy.start()

        @pl.when(last)
        def _():
            move(range(3, nz))

        @pl.when(open_end)
        def _():
            for h in range(2, min(3, nz)):
                gather.step(m, h, whole=False, forward=False)

        ex.finish()
        return carry

    lax.fori_loop(0, micro, body, 0)

    @pl.when(g.s > 0)
    def _():
        for m in range(micro):
            for q in range(HOP_CHUNKS):
                hop(m, q).wait_send()

    few = range(1, min(3, nz))

    @pl.when(last)
    def _():
        for m in range(micro):
            gather.passes(m, range(1, nz))
        for m in range(1, micro):
            for r in every:
                gather.start(micro + m, r, grows_ref.at[m, r, 0])
            for h in few:
                gather.step(micro + m, h, forward=m < micro - 1 or h < few[-1])
            if m < micro - 1:
                for h in range(3, nz):
                    gather.step(micro + m, h)

    for m in range(micro - 1):
        gather.finish(m, every, whole=False)
    for m in range(1, micro - 1):
        gather.finish(micro + m, every)

    @pl.when(first)
    def _():
        for r in every:
            gather.near(micro - 1, r, grows_ref.at[micro - 1, r, 0]).wait()
        for r in every:
            gather.line(micro - 1, r, False).finish(few)
        gather.finish_passes(micro - 1, range(1, 2))
        gather.finish(2 * micro - 1, every)

    @pl.when(last)
    def _():
        gather.finish(micro - 1, every, whole=False)
        gather.finish(2 * micro - 1, every, hops=few)

    for m in range(micro):
        for copy in partner(m):
            copy.wait()


def tail_kernel(
    ny, nz, sections, span,
    route_ref, small_ref, gsmall_ref,
    zf_h, zb_in, slices_h, partner_h, wd_h, xab_h, obb_h, dqkv_h, dattn_h, xap_h, obp_h, dqp_h, dtp_h,
    gate_ref, up_ref, down_ref, attn_ref, small_out, zb_h,
    w4, x_s, g_s, da_s, db_s, gh_s, acc_g, acc_u, acc_d, csend, cland, dsend, dland,
    xa_s, ob_s, dq_s, dt_s, own_s, ysend, yland, zland, sm_s, smy, smz,
    wsem, xsem, asem, ss, sr, cs, cr, ts, tr, ys, yr, zs, zr, hs, hr, hys, hyr, hl,
):
    micro, tokens, width = dqkv_h.shape[0], zf_h.shape[3], zf_h.shape[4]
    hidden = slices_h.shape[1]
    turns = nz // 2
    half = hidden // turns
    slice_h = half // 2
    both = 2 * half
    wide = 2 * hidden
    tile = 256 if both % 256 == 0 else 128
    qkv_width = dqkv_h.shape[2]
    shard = width // (2 * ny * nz)
    part = width // nz
    rows = span * ny * tokens
    groups = nz // span
    g = Place(ny, nz)
    first = g.s == 0
    pieces = []
    for t in range(turns):
        own, other = 2 * t, 2 * t + 1
        rows_t = slice(t * half, (t + 1) * half)
        pieces.append((slices_h.at[:, rows_t], w4.at[0:2, own * half : (own + 1) * half]))
        pieces.append((partner_h.at[:, rows_t], w4.at[:, other * half : (other + 1) * half]))
        here = pl.ds(pl.multiple_of(g.z_of(2 * t) * slice_h, slice_h), slice_h)
        for j in range(2):
            at = own * half + j * slice_h
            pieces.append((wd_h.at[j, here], w4.at[2, at : at + slice_h]))
    mine = [pltpu.make_async_copy(src, dst, wsem.at[n]) for n, (src, dst) in enumerate(pieces)]

    def load(i):
        m, k = lax.div(i, groups), pl.ds(lax.rem(i, groups) * span, span)
        early = [(first, x_s, 0), (jnp.logical_not(first), g_s, 1)]
        late = [(first, g_s, 1), (jnp.logical_not(first), x_s, 0)]
        copies = [(when, pltpu.make_async_copy(zb_h.at[m, k], dst, xsem.at[n])) for when, dst, n in late]
        for when, dst, n in early:
            copies.append((when & (m == 0), pltpu.make_async_copy(zf_h.at[0, k], dst, xsem.at[n])))
            copies.append((when & (m > 0), pltpu.make_async_copy(zb_h.at[micro + m, k], dst, xsem.at[n])))
        return copies

    def start_load(i):
        for when, copy in load(i):
            @pl.when(when)
            def _():
                copy.start()

    def wait_load():
        pltpu.make_async_copy(zf_h.at[0, pl.ds(0, span)], x_s, xsem.at[0]).wait()
        pltpu.make_async_copy(zf_h.at[0, pl.ds(0, span)], g_s, xsem.at[1]).wait()

    acts = []
    for m in range(micro):
        for yy in range(ny):
            own = yy * 2 + g.c
            acts.append((xab_h.at[m, own], xa_s.at[yy, 0, m]))
            acts.append((xap_h.at[m, yy], xa_s.at[yy, 1, m]))
            acts.append((obb_h.at[m, own], ob_s.at[yy, 0, m]))
            acts.append((obp_h.at[m, yy], ob_s.at[yy, 1, m]))
    acts += [(dqkv_h, dq_s.at[0]), (dqp_h, dq_s.at[1]), (dattn_h, dt_s.at[0]), (dtp_h, dt_s.at[1])]
    acts = [pltpu.make_async_copy(src, dst, asem.at[i]) for i, (src, dst) in enumerate(acts)]
    for copy in acts:
        copy.start()
    g.greet(with_x=False)
    gather = Gather(g, zb_h, hs, hr, hys, hyr, hl)
    late_hops = range(3, nz)
    newest = micro - 1

    @pl.when(first)
    def _():
        gather.passes(newest, range(2, min(3, nz)))
        for h in late_hops[:1]:
            gather.go_on(newest, h, whole=False)

    @pl.when(jnp.logical_not(first))
    def _():
        for h in late_hops[:1]:
            gather.go_on(micro + newest, h)
    sm_core = remote(gsmall_ref, sm_s.at[1], ss.at[0], sr.at[0], g.core)
    sm_core.start()

    def sm_y(r):
        return remote(sm_s.at[0], smy.at[ny - r], ss.at[r], sr.at[ny - r], g.ahead(r))

    def sm_y_arrival(r):
        return remote(sm_s.at[0], smy.at[r], ss.at[r], sr.at[r], g.ahead(r))

    def sm_z(k):
        return remote(sm_s.at[1], smz.at[k], ss.at[ny + k], sr.at[ny + k], g.z_behind(k))

    for copy in acts:
        copy.wait()
    for copy in mine:
        copy.start()
    start_load(0)

    count = 2 * micro * tokens

    def attn_rows(yy, dst):
        for src, grad, at in ((xa_s, dq_s, 0), (ob_s, dt_s, qkv_width)):
            left = src[yy].reshape(count, shard * nz)
            wide = grad.shape[3]
            for n in range(wide // 512):
                cols = slice(n * 512, (n + 1) * 512)
                got = dot_tn(left, grad[:, :, :, cols].reshape(count, 512)).astype(BF16)
                for zi in range(nz):
                    dst[zi, 0:shard, at + n * 512 : at + (n + 1) * 512] = got[zi * shard : (zi + 1) * shard]

    def flipped(mask):
        place = g.d
        for b in range(nz.bit_length()):
            if mask >> b & 1:
                place = place + (1 << b) - (2 << b) * lax.rem(lax.div(g.d, 1 << b), 2)
        return place

    def y_copy(r, k):
        zi = flipped(k)
        return remote(ysend.at[r - 1, zi], yland.at[ny - r - 1, zi], ys.at[r, k], yr.at[ny - r, k], g.ahead(r))

    def y_arrival(r, k):
        zi = flipped(k)
        return remote(ysend.at[r - 1, zi], yland.at[r - 1, zi], ys.at[r, k], yr.at[r, k], g.ahead(r))

    order = list(range(1, nz)) + [0]
    masks = list(range(nz - 1, -1, -1))

    def y_start(k):
        for r in range(1, ny):
            y_copy(r, k).start()

    for r in range(1, ny):
        attn_rows(lax.rem(g.y + r, ny), ysend.at[r - 1])
    y_start(masks[0])
    sm_core.wait_recv()
    sm_s[0] = gsmall_ref[...] + sm_s[1]
    sm_core.wait_send()
    for r in range(1, ny):
        sm_y(r).start()
    attn_rows(g.y, own_s)

    bits = nz.bit_length() - 1

    def low(mask):
        return (mask & -mask).bit_length() - 1 if mask else bits

    landings = [(mask, b) for mask in range(nz) for b in range(low(mask))]

    def z_copy(mask):
        b = low(mask)
        at = landings.index((mask - (1 << b), b))
        device = (g.s, g.e, flipped(1 << b))
        return remote(own_s.at[flipped(mask)], zland.at[at], zs.at[0, mask], zr.at[0, at], device)

    def z_arrival(mask, b):
        at = landings.index((mask, b))
        device = (g.s, g.e, flipped(1 << b))
        return remote(own_s.at[flipped(mask)], zland.at[at], zs.at[0, mask], zr.at[0, at], device)

    def advance(mask):
        for r in range(1, ny):
            y_arrival(r, mask).wait_recv()
        zi = flipped(mask)
        for b in range(low(mask)):
            z_arrival(mask, b).wait_recv()
        for n in range((qkv_width + width) // 512):
            cols = slice(n * 512, (n + 1) * 512)
            total = own_s[zi, :, cols].astype(F32)
            for r in range(1, ny):
                total = total + yland[r - 1, zi, :, cols].astype(F32)
            for b in range(low(mask)):
                total = total + zland[landings.index((mask, b)), :, cols].astype(F32)
            own_s[zi, :, cols] = total.astype(BF16)
        if mask:
            z_copy(mask).start()

    for copy in mine:
        copy.wait()
    acc_g[...] = jnp.zeros_like(acc_g)
    acc_u[...] = jnp.zeros_like(acc_u)
    acc_d[...] = jnp.zeros_like(acc_d)
    column = lax.rem(lax.broadcasted_iota(jnp.int32, (ROUTER_ROWS, wide), 1), both)
    expert = lax.broadcasted_iota(jnp.int32, (ROUTER_ROWS, wide), 0)
    owner = jnp.where(column < half, g.e, 2 * g.y + 1 - g.c)
    local = jnp.where(column < half, column, column - half)
    chosen = 2 * owner + jnp.where(local < slice_h, 0, 1)
    spread = jnp.where(expert == chosen, 1.0, 0.0).astype(BF16)

    last_group = micro * groups - 1
    accs = (acc_g, acc_u)
    parity = lax.rem(g.d, 2)

    def rows_of(x):
        at = parity if x == 0 else 1 - parity
        return pl.ds(pl.multiple_of(at * part, part), part)

    def cols_of(t, o):
        return slice((2 * t + o) * half, (2 * t + o + 1) * half)

    def core_copy(n, x, t):
        return remote(csend.at[n, x, t], cland.at[n, x, t], cs.at[n, x * turns + t], cr.at[n, x * turns + t], g.core)

    def give_half(n):
        for x in (1, 0):
            for t in range(turns):
                csend[n, x, t] = accs[n][rows_of(x), cols_of(t, 1)].astype(BF16)
                core_copy(n, x, t).start()

    def turn_copy(n, t):
        dst = (gate_ref, up_ref)[n]
        device = (g.s, g.e, flipped(1))
        return remote(cland.at[n, 1, t], dst.at[g.z_of(2 * t)], ts.at[n, t], tr.at[n, t], device)

    def turn_arrival(n, t):
        dst = (gate_ref, up_ref)[n]
        device = (g.s, g.e, flipped(1))
        return remote(cland.at[n, 1, t], dst.at[lax.rem(flipped(1) + 2 * t, nz)], ts.at[n, t], tr.at[n, t], device)

    def turn_near(n, t):
        dst = (gate_ref, up_ref)[n]
        return pltpu.make_async_copy(cland.at[n, 0, t], dst.at[g.z_of(2 * t)], ts.at[n, turns + t])

    def take_half(n):
        for x in (1, 0):
            for t in range(turns):
                core_copy(n, x, t).wait_recv()
                total = accs[n][rows_of(x), cols_of(t, 0)] + cland[n, x, t].astype(F32)
                cland[n, x, t] = total.astype(BF16)
                if x:
                    turn_copy(n, t).start()
                else:
                    turn_near(n, t).start()

    def small_z():
        for r in range(1, ny):
            sm_y_arrival(r).wait_recv()
        total = sm_s[0]
        for r in range(1, ny):
            total = total + smy[r]
        sm_s[1] = total
        for k in range(1, nz):
            sm_z(k).start()

    def group(i, carry):
        m = lax.div(i, groups)
        wait_load()

        def block(b, carry):
            k = lax.rem(i, groups) * span + b
            x = x_s[b].reshape(ny * tokens, width)
            gr = g_s[b].reshape(ny * tokens, width)
            places = [(lax.rem(g.y + r, ny) * 2 + g.c) * nz + k for r in range(ny)]
            route = jnp.concatenate([route_ref[place, m] for place in places], 1)
            gates_t = chosen_gates(dot_nt(small_ref[0:ROUTER_ROWS, :], x), route)
            high = gates_t.astype(BF16)
            low_part = (gates_t - high.astype(F32)).astype(BF16)
            here = pl.ds(pl.multiple_of(b * ny * tokens, ny * tokens), ny * tokens)
            for n in range(wide // tile):
                cols = slice(n * tile, (n + 1) * tile)
                a = dot_nt(x, w4[0, cols])
                bb = dot_nt(x, w4[1, cols])
                gate = dot_tn(high, spread[:, cols]) + dot_tn(low_part, spread[:, cols])
                u = dot_nt(gr, w4[2, cols]) * gate
                square = a * a
                th = jnp.tanh(GELU_C * (a + GELU_A * square * a))
                hf = 0.5 * (1.0 + th)
                act = a * hf
                slope = hf + (0.5 * GELU_C) * a * (1.0 - th * th) * (1.0 + (3.0 * GELU_A) * square)
                da_s[here, cols] = (u * slope * bb).astype(BF16)
                db_s[here, cols] = (u * act).astype(BF16)
                if (n + 1) * tile <= both:
                    gh_s[here, cols] = ((act * bb).astype(BF16).astype(F32) * gate).astype(BF16)
            return carry

        lax.fori_loop(0, span, block, 0)

        @pl.when(first & (i == newest * groups - 1))
        def _():
            for h in late_hops:
                gather.step(newest, h, whole=False)
            gather.passes(newest, late_hops)

        @pl.when(jnp.logical_not(first) & (i == newest * groups - 1))
        def _():
            for h in late_hops:
                gather.step(micro + newest, h)

        size = 256 if (2 * part) % 256 == 0 else 128
        base = lax.div(g.d, 2) * (2 * part)

        def x_columns(n):
            cols = pl.ds(pl.multiple_of(base + n * size, size), size)
            return x_s[:, :, :, cols].reshape(rows, size)

        def sum_rows(acc, right):
            def columns(n, carry):
                at = pl.ds(pl.multiple_of(n * size, size), size)
                acc[at, :] += dot_tn(x_columns(n), right[...])
                return carry

            lax.fori_loop(0, 2 * part // size, columns, 0)

        def down():
            def columns(n, carry):
                cols = pl.ds(pl.multiple_of(n * tile, tile), tile)
                acc_d[cols, :] += dot_tn(gh_s[:, cols], g_s[...].reshape(rows, width))
                return carry

            lax.fori_loop(0, both // tile, columns, 0)

        sum_rows(acc_g, da_s)

        @pl.when(i == last_group)
        def _():
            give_half(0)

        sum_rows(acc_u, db_s)

        @pl.when(i == last_group)
        def _():
            give_half(1)
            take_half(0)

        down()

        @pl.when(first & (i == newest * groups - 1))
        def _():
            for r in range(ny):
                gather.line(newest, r, False).finish(late_hops)
            gather.finish_passes(newest, range(2, nz))

        @pl.when(jnp.logical_not(first) & (i == newest * groups - 1))
        def _():
            gather.finish(micro + newest, [], hops=late_hops)

        @pl.when(i < last_group)
        def _():
            start_load(i + 1)

        for n in range(min(3, last_group)):
            @pl.when(i == n)
            def _():
                advance(masks[n])
                y_start(masks[n + 1])
                if n == 1:
                    small_z()

        return carry

    lax.fori_loop(0, micro * groups, group, 0)
    polled = min(3, last_group)
    for mask in masks[polled + 1 :]:
        y_start(mask)

    down_copy = remote(dsend, dland, cs.at[2, 0], cr.at[2, 0], g.core)
    dsend[...] = acc_d[half:both, :].astype(BF16)
    down_copy.start()
    take_half(1)
    for mask in masks[polled:-1]:
        advance(mask)
    down_copy.wait_recv()
    dland[...] = (acc_d[0:half, :] + dland[...].astype(F32)).astype(BF16)
    down_near = pltpu.make_async_copy(dland, down_ref, ts.at[0, nz])
    down_near.start()

    total = sm_s[1]
    for k in range(1, nz):
        sm_z(k).wait_recv()
        total = total + smz[k]
    small_out[...] = total

    advance(0)
    attn_near = pltpu.make_async_copy(own_s.at[g.d], attn_ref, ts.at[1, nz])
    attn_near.start()
    for t in range(turns):
        for n in range(2):
            turn_arrival(n, t).wait_recv()

    for r in range(1, ny):
        sm_y(r).wait_send()
        for k in range(nz):
            y_copy(r, k).wait_send()
    for k in range(1, nz):
        sm_z(k).wait_send()
        z_copy(k).wait_send()
    for n in range(2):
        for t in range(turns):
            turn_copy(n, t).wait_send()
            turn_near(n, t).wait()
            for x in range(2):
                core_copy(n, x, t).wait_send()
    down_copy.wait_send()
    down_near.wait()
    attn_near.wait()


def finish_kernel(nz, experts, gate_in, up_in, down_in, attn_in, small_in, gate, up, down, qkv, out, router, again, mgain):
    slice_h = gate_in.shape[2] // 2
    for src, dst in ((gate_in, gate), (up_in, up)):
        for j in range(2):
            cols = slice(j * slice_h, (j + 1) * slice_h)
            dst[0, j] = jnp.concatenate([src[z, :, cols].astype(F32) for z in range(nz)], 1)
    down[0, 0] = down_in[...].astype(F32)
    shard, split = qkv.shape[1], qkv.shape[2]
    qkv[0] = attn_in[0:shard, 0:split].astype(F32)
    out[0] = attn_in[0:shard, split:].astype(F32)
    rows, width = small_in.shape
    base = (lax.axis_index("expert") * nz + lax.axis_index("dp")) * shard
    at = lax.broadcasted_iota(jnp.int32, (width, 128), 0)
    lane = lax.broadcasted_iota(jnp.int32, (width, 128), 1)
    pick = jnp.where(at == base + lane, 1.0, 0.0).astype(F32)
    got = jnp.dot(small_in[...], pick, precision=lax.Precision.HIGHEST, preferred_element_type=F32)
    again[...] = got[ROUTER_ROWS : ROUTER_ROWS + 1, 0:shard]
    mgain[...] = got[ROUTER_ROWS + 1 : ROUTER_ROWS + 2, 0:shard]
    turned = jnp.transpose(jnp.concatenate([got, jnp.zeros((128 - rows, 128), F32)], 0))
    router[0] = turned[0:shard, 0:experts]


VMEM = pl.BlockSpec(memory_space=pltpu.VMEM)
ANY = pl.BlockSpec(memory_space=pl.ANY)
DMA = pltpu.SemaphoreType.DMA


def per_device(
    ne, nz, sections,
    layer_input, cotangent, segments, routes, attn_gain, w_qkv, w_out, moe_gain, w_router, w_gate, w_up, w_down,
):
    ny = ne // 2
    micro, _, tokens, width = layer_input.shape
    total_experts = w_router.shape[2]
    hidden = w_gate.shape[3]
    owners = ("expert", "dp")
    shard = w_qkv.shape[1]
    place_e, place_d = lax.axis_index("expert"), lax.axis_index("dp")
    small = jnp.concatenate(
        [
            w_router[0],
            jnp.zeros((shard, ROUTER_ROWS - total_experts), BF16),
            attn_gain[0][:, None],
            moe_gain[0][:, None],
            jnp.zeros((shard, 128 - ROUTER_ROWS - 2), BF16),
        ],
        1,
    ).astype(F32)
    own_routes = jnp.transpose(routes[0, :, 0], (0, 2, 1))
    cos, sin = rotary_tables(tokens)
    segs = segments[:, 0]
    segc, segr = segs[:, :, None], segs[:, None, :]
    x = layer_input[:, 0]
    cot = cotangent[:, 0]
    wg, wu, wd = w_gate[0], w_up[0], w_down[0]
    qkv_width = w_qkv.shape[2]
    slice_h = hidden // nz
    half = 2 * slice_h

    def shape(*dims, dtype=BF16):
        return jax.ShapeDtypeStruct(dims, dtype)

    grid_sems = [DMA((4, 2, nz, ny)) for _ in range(4)]
    small, routes_all, wqkv, wout, slices = pl.pallas_call(
        functools.partial(gather_kernel, ny, nz),
        out_shape=(
            shape(SMALL_ROWS, width),
            shape(ne, nz, *own_routes.shape, dtype=jnp.int32),
            shape(ne, nz, shard, qkv_width),
            shape(ne, nz, shard, width),
            shape(2, hidden, width),
        ),
        in_specs=[VMEM] + [ANY] * 5,
        out_specs=tuple([VMEM] + [ANY] * 4),
        scratch_shapes=[
            pltpu.VMEM((ne, nz, shard, 128), F32),
            pltpu.VMEM(wg.shape, BF16),
            pltpu.VMEM(wu.shape, BF16),
            pltpu.VMEM((2, 2, hidden, width), BF16),
            DMA((2,)), DMA((4,)),
        ]
        + grid_sems
        + [DMA((4, 2, nz)), DMA((4, 2, nz)), DMA((2, nz))],
        compiler_params=pltpu.CompilerParams(
            collective_id=3, has_side_effects=True, vmem_limit_bytes=60 * 2**20
        ),
        name="gather_weights",
    )(small, own_routes, w_qkv[0], w_out[0], wg, wu)
    wqkv = wqkv.reshape(width, qkv_width)
    wout = wout.reshape(width, width)
    routes_all = routes_all.reshape((ne * nz,) + own_routes.shape)
    weights = [pltpu.VMEM(w.shape, BF16) for w in (wqkv, wout, wg, wu, wd)]
    hop_sems = [DMA((micro, HOP_CHUNKS)) for _ in range(2)]
    block = width // ne

    def gather_sems(count):
        return [DMA((count, ny, 2, nz))] * 2 + [DMA((count, 2, nz, ny))] * 2 + [DMA((count, ny))]

    def returns(wide):
        return [
            pltpu.VMEM((tokens, wide), BF16),
            pltpu.VMEM((max(1, ny - 1), tokens, wide), BF16),
            pltpu.VMEM((max(1, ny - 1), tokens, wide), BF16),
            pltpu.VMEM((tokens, wide), BF16),
            pltpu.VMEM((max(1, ny - 1), tokens, wide), BF16),
            pltpu.VMEM((max(1, ny - 1), tokens, wide), BF16),
        ]

    out, hin, h1, qkv, obb, xm, gates, zf, obp, partner = pl.pallas_call(
        functools.partial(forward_kernel, ny, nz, sections),
        out_shape=(
            shape(micro, tokens, width),
            shape(micro, tokens, width),
            shape(micro, tokens, width, dtype=F32),
            shape(micro, tokens, qkv_width),
            shape(micro, ne, tokens, block),
            shape(micro, ny, 2, tokens, width),
            shape(micro, ny, 2, ROUTER_ROWS, tokens, dtype=F32),
            shape(1, nz, ny, tokens, width),
            shape(micro, ny, tokens, block),
            shape(3, hidden, width),
        ),
        in_specs=[VMEM] * 7 + [ANY] * 7,
        out_specs=tuple([VMEM] * 7 + [ANY] * 3),
        scratch_shapes=weights
        + [
            pltpu.VMEM((tokens, width), BF16),
            pltpu.VMEM((2, 2 * tokens, hidden), BF16),
            pltpu.VMEM((tokens, width), F32),
            pltpu.VMEM((tokens // FORWARD_CHUNKS, width), F32),
        ]
        + returns(width)
        + [DMA((5,))]
        + gather_sems(1)
        + [DMA((ny,)), DMA((ny,))]
        + hop_sems
        + [DMA((micro, ny))] * 2
        + [DMA((nz + 2,))] * 2
        + sem_shapes(micro, ny, FORWARD_CHUNKS),
        compiler_params=pltpu.CompilerParams(
            collective_id=0, has_side_effects=True, vmem_limit_bytes=60 * 2**20
        ),
        name="layers_forward",
    )(x, segc, segr, routes_all, small, cos, sin, cot, slices, wqkv, wout, wg, wu, wd)

    wide = width + 128
    every = (2, ny, 2, tokens, hidden)
    gin, grows, xab, dqkv, dattn, gsmall, zb, xap, dqp, dtp = pl.pallas_call(
        functools.partial(backward_kernel, ny, nz, sections),
        out_shape=(
            shape(micro, tokens, width),
            shape(micro, ny, 2, tokens, width),
            shape(micro, ne, tokens, block),
            shape(micro, tokens, qkv_width),
            shape(micro, tokens, width),
            shape(SMALL_ROWS, width, dtype=F32),
            shape(2 * micro, nz, ny, tokens, width),
            shape(micro, ny, tokens, block),
            shape(micro, tokens, qkv_width),
            shape(micro, tokens, width),
        ),
        in_specs=[VMEM] * 10 + [ANY] * 6,
        out_specs=tuple([VMEM] * 6 + [ANY] * 4),
        scratch_shapes=weights
        + [
            pltpu.VMEM((ny, 2, tokens, width), BF16),
            pltpu.VMEM(every, BF16),
            pltpu.VMEM(every, BF16),
            pltpu.VMEM(every, BF16),
            pltpu.VMEM((2, 2 * tokens, hidden), BF16),
            pltpu.VMEM((2, 2 * tokens, hidden), BF16),
            pltpu.VMEM((tokens, wide), F32),
            pltpu.VMEM((tokens // BACKWARD_CHUNKS, wide), F32),
            pltpu.VMEM((tokens, width), F32),
            pltpu.VMEM((tokens, width), F32),
        ]
        + returns(wide)
        + [DMA((5,)), DMA]
        + gather_sems(2 * micro)
        + hop_sems
        + [DMA((micro, ny + 2))] * 2
        + sem_shapes(micro, ny, BACKWARD_CHUNKS * HOP_CHUNKS),
        compiler_params=pltpu.CompilerParams(
            collective_id=1, has_side_effects=True, vmem_limit_bytes=62 * 2**20
        ),
        name="layers_backward",
    )(cot, segc, segr, small, cos, sin, hin, h1, qkv, gates, xm, wqkv, wout, wg, wu, wd)

    span_z = max(1, min(nz, 512 // (ny * tokens)))
    rows = span_z * ny * tokens
    padded = -(-shard // 16) * 16
    attn_width = qkv_width + width
    part = width // nz
    small_shape = (SMALL_ROWS, width)
    gate_g, up_g, down_g, attn_g, small_g, _ = pl.pallas_call(
        functools.partial(tail_kernel, ny, nz, sections, span_z),
        out_shape=(
            shape(nz, part, half),
            shape(nz, part, half),
            shape(half, width),
            shape(padded, attn_width),
            shape(*small_shape, dtype=F32),
            shape(*zb.shape),
        ),
        in_specs=[VMEM] * 3 + [ANY] * 13,
        out_specs=tuple([ANY] * 4 + [VMEM] + [ANY]),
        input_output_aliases={4: 5},
        scratch_shapes=[
            pltpu.VMEM((3, 2 * hidden, width), BF16),
            pltpu.VMEM((span_z, ny, tokens, width), BF16),
            pltpu.VMEM((span_z, ny, tokens, width), BF16),
            pltpu.VMEM((rows, 2 * hidden), BF16),
            pltpu.VMEM((rows, 2 * hidden), BF16),
            pltpu.VMEM((rows, 2 * half), BF16),
            pltpu.VMEM((2 * part, 2 * hidden), F32),
            pltpu.VMEM((2 * part, 2 * hidden), F32),
            pltpu.VMEM((2 * half, width), F32),
            pltpu.VMEM((2, 2, nz // 2, part, half), BF16),
            pltpu.VMEM((2, 2, nz // 2, part, half), BF16),
            pltpu.VMEM((half, width), BF16),
            pltpu.VMEM((half, width), BF16),
            pltpu.VMEM((ny, 2, micro, tokens, block), BF16),
            pltpu.VMEM((ny, 2, micro, tokens, block), BF16),
            pltpu.VMEM((2, micro, tokens, qkv_width), BF16),
            pltpu.VMEM((2, micro, tokens, width), BF16),
            pltpu.VMEM((nz, padded, attn_width), BF16),
            pltpu.VMEM((max(1, ny - 1), nz, padded, attn_width), BF16),
            pltpu.VMEM((max(1, ny - 1), nz, padded, attn_width), BF16),
            pltpu.VMEM((max(1, nz - 1), padded, attn_width), BF16),
            pltpu.VMEM((2,) + small_shape, F32),
            pltpu.VMEM((ny,) + small_shape, F32),
            pltpu.VMEM((nz,) + small_shape, F32),
            DMA((2 * nz,)), DMA((2,)),
            DMA((4 * ny * micro + 4,)),
            DMA((ny + nz,)), DMA((ny + nz,)),
            DMA((3, nz)), DMA((3, nz)),
            DMA((2, nz + 1)), DMA((2, nz)),
            DMA((ny, nz)), DMA((ny, nz)),
            DMA((1, nz)), DMA((1, nz)),
        ]
        + gather_sems(2 * micro),
        compiler_params=pltpu.CompilerParams(
            collective_id=2, has_side_effects=True, vmem_limit_bytes=62 * 2**20
        ),
        name="weight_gradients",
    )(routes_all, small, gsmall, zf, zb, slices, partner, wd, xab, obb, dqkv, dattn, xap, obp, dqp, dtp)

    steps = 2
    finals = pl.pallas_call(
        functools.partial(finish_kernel, nz, total_experts),
        grid=(steps,),
        out_shape=(
            shape(1, 2, part, hidden, dtype=F32),
            shape(1, 2, part, hidden, dtype=F32),
            shape(1, 2, slice_h, width, dtype=F32),
            shape(1, shard, qkv_width, dtype=F32),
            shape(1, shard, width, dtype=F32),
            shape(1, shard, total_experts, dtype=F32),
            shape(1, shard, dtype=F32),
            shape(1, shard, dtype=F32),
        ),
        in_specs=[
            pl.BlockSpec((nz, part // steps, half), lambda i: (0, i, 0)),
            pl.BlockSpec((nz, part // steps, half), lambda i: (0, i, 0)),
            pl.BlockSpec((slice_h, width), lambda i: (i, 0)),
            pl.BlockSpec((padded, attn_width), lambda i: (0, 0)),
            pl.BlockSpec(small_shape, lambda i: (0, 0)),
        ],
        out_specs=(
            pl.BlockSpec((1, 2, part // steps, hidden), lambda i: (0, 0, i, 0)),
            pl.BlockSpec((1, 2, part // steps, hidden), lambda i: (0, 0, i, 0)),
            pl.BlockSpec((1, 1, slice_h, width), lambda i: (0, i, 0, 0)),
            pl.BlockSpec((1, shard, qkv_width), lambda i: (0, 0, 0)),
            pl.BlockSpec((1, shard, width), lambda i: (0, 0, 0)),
            pl.BlockSpec((1, shard, total_experts), lambda i: (0, 0, 0)),
            pl.BlockSpec((1, shard), lambda i: (0, 0)),
            pl.BlockSpec((1, shard), lambda i: (0, 0)),
        ),
        compiler_params=pltpu.CompilerParams(vmem_limit_bytes=60 * 2**20),
        name="finish_gradients",
    )(gate_g, up_g, down_g, attn_g, small_g)
    grad_gate, grad_up, grad_down, grad_qkv, grad_out, grad_router, grad_again, grad_mgain = finals
    return (
        out[None, :, None],
        gin[None, :, None],
        grad_again,
        grad_qkv,
        grad_out,
        grad_mgain,
        grad_router,
        grad_gate,
        grad_up,
        grad_down,
    )


def solution(mesh):
    owners = ("expert", "dp")
    return jax.shard_map(
        functools.partial(per_device, mesh.shape["expert"], mesh.shape["dp"], mesh.shape["section"]),
        mesh=mesh,
        in_specs=(
            P(None, owners, None, None),
            P(None, owners, None, None),
            P(None, owners, None),
            P("section", None, owners, None, None),
            P("section", owners),
            P("section", owners, None),
            P("section", owners, None),
            P("section", owners),
            P("section", owners, None),
            P("section", "expert", None, None),
            P("section", "expert", None, None),
            P("section", "expert", None, None),
        ),
        out_specs=(
            P("section", None, owners, None, None),
            P("section", None, owners, None, None),
            P("section", owners),
            P("section", owners, None),
            P("section", owners, None),
            P("section", owners),
            P("section", owners, None),
            P("section", "expert", "dp", None),
            P("section", "expert", "dp", None),
            P("section", "expert", "dp", None),
        ),
        check_vma=False,
    )
```

```python
import functools

import jax
import jax.numpy as jnp
import numpy as np
from jax import lax
from jax.experimental import pallas as pl
from jax.experimental.pallas import tpu as pltpu
from jax.sharding import PartitionSpec as P

HEAD = 128
QUERY_HEADS = 12
KEY_VALUE_HEADS = 2
GROUP = QUERY_HEADS // KEY_VALUE_HEADS
EPS = 1e-06
THETA = 1000000.0
NEGATIVE = -1e30
SCALE = HEAD ** (-0.5)
ROUTER_ROWS = 16
SMALL_ROWS = 32
FORWARD_CHUNKS = 2
BACKWARD_CHUNKS = 1
HOP_CHUNKS = 2
MESH = pl.DeviceIdType.MESH
F32 = jnp.float32
BF16 = jnp.bfloat16
GELU_C = float(np.sqrt(2.0 / np.pi))
GELU_A = 0.044715


def dot(a, b):
    return jnp.dot(a, b, preferred_element_type=F32)


def dot_nt(a, b):
    return lax.dot_general(a, b, (((1,), (1,)), ((), ())), preferred_element_type=F32)


def dot_tn(a, b):
    return lax.dot_general(a, b, (((0,), (0,)), ((), ())), preferred_element_type=F32)


def rotary_tables(tokens):
    places = np.arange(tokens, dtype=np.float64)
    inverse = THETA ** (-2.0 * np.arange(HEAD // 2, dtype=np.float64) / HEAD)
    angles = places[:, None] * inverse[None, :]
    cosine, sine = np.cos(angles), np.sin(angles)
    return (
        jnp.asarray(np.concatenate([cosine, cosine], 1), F32),
        jnp.asarray(np.concatenate([-sine, sine], 1), F32),
    )


def mask_bias(col, row):
    tokens = row.shape[1]
    ti = lax.broadcasted_iota(jnp.int32, (tokens, tokens), 0)
    ui = lax.broadcasted_iota(jnp.int32, (tokens, tokens), 1)
    return jnp.where((col == row) & (ui <= ti), 0.0, NEGATIVE).astype(F32)


def heads_of(value, first, count):
    return jnp.concatenate(
        [value[:, (first + i) * HEAD : (first + i + 1) * HEAD] for i in range(count)], 0
    )


def attention_shares(q6, k, bias6):
    scores = dot_nt(q6, k) * SCALE + bias6
    top = jnp.max(scores, -1, keepdims=True)
    raised = jnp.exp(scores - top)
    return raised / jnp.sum(raised, -1, keepdims=True)


class Place:
    def __init__(self, ny, nz):
        self.ny = ny
        self.nz = nz
        self.s = lax.axis_index("section")
        self.e = lax.axis_index("expert")
        self.d = lax.axis_index("dp")
        self.y = lax.div(self.e, 2)
        self.c = lax.rem(self.e, 2)
        self.core = (self.s, self.y * 2 + 1 - self.c, self.d)
        self.x = (1 - self.s, self.e, self.d)

    def ahead(self, r):
        return (self.s, lax.rem(self.y + r, self.ny) * 2 + self.c, self.d)

    def behind(self, r):
        return (self.s, lax.rem(self.y + self.ny - r, self.ny) * 2 + self.c, self.d)

    def pack(self, r, other):
        core = 1 - self.c if other else self.c
        return lax.rem(self.y + r, self.ny) * 2 + core

    def z_of(self, k):
        return lax.rem(self.d + k, self.nz)

    def z_ahead(self, k):
        return (self.s, self.e, self.z_of(k))

    def z_behind(self, k):
        return (self.s, self.e, self.z_of(self.nz - k))

    def greet(self, with_x=True):
        barrier = pltpu.get_barrier_semaphore()
        partners = [self.core] + ([self.x] if with_x else [])
        partners += [self.ahead(r) for r in range(1, self.ny)]
        partners += [self.z_ahead(k) for k in range(1, self.nz)]
        for partner in partners:
            pl.semaphore_signal(barrier, inc=1, device_id=partner, device_id_type=MESH)
        pl.semaphore_wait(barrier, len(partners))


def remote(src, dst, send, recv, device):
    return pltpu.make_async_remote_copy(
        src_ref=src, dst_ref=dst, send_sem=send, recv_sem=recv, device_id=device, device_id_type=MESH
    )


class Line:
    def __init__(self, place, slot, send, recv):
        self.place, self.slot, self.send, self.recv = place, slot, send, recv

    def origin(self, way, h):
        return self.place.d - h if way == 0 else self.place.d + h

    def comes(self, way, h):
        return self.place.d >= h if way == 0 else self.place.d + h < self.place.nz

    def leaves(self, way, h):
        d, nz = self.place.d, self.place.nz
        return (d + 1 < nz) & (d >= h - 1) if way == 0 else (d >= 1) & (d + h - 1 < nz)

    def out(self, way, h, src=None):
        g = self.place
        at = self.slot(self.origin(way, h - 1))
        next_door = (g.s, g.e, g.d + 1 if way == 0 else g.d - 1)
        return remote(at if src is None else src, at, self.send.at[way, h], self.recv.at[way, h], next_door)

    def came(self, way, h):
        g = self.place
        at = self.slot(self.origin(way, h))
        return remote(at, at, self.send.at[way, h], self.recv.at[way, h], g.core)

    def start(self, src):
        for way in range(2):
            @pl.when(self.leaves(way, 1))
            def _():
                self.out(way, 1, src).start()

    def go_on(self, h):
        for way in range(2):
            @pl.when(self.leaves(way, h))
            def _():
                self.out(way, h).start()

    def step(self, h, then=None, forward=True):
        for way in range(2):
            @pl.when(self.comes(way, h))
            def _():
                self.came(way, h).wait_recv()
                if forward and h + 1 < self.place.nz:
                    @pl.when(self.leaves(way, h + 1))
                    def _():
                        self.out(way, h + 1).start()
                if then is not None:
                    then(way, h)

    def finish(self, hops=None):
        for way in range(2):
            for h in range(1, self.place.nz) if hops is None else hops:
                @pl.when(self.leaves(way, h))
                def _():
                    self.out(way, h).wait_send()


class Gather:
    def __init__(self, place, buf, send, recv, ysend, yrecv, local):
        self.place, self.buf, self.local = place, buf, local
        self.send, self.recv, self.ysend, self.yrecv = send, recv, ysend, yrecv
        self.tokens = buf.shape[3]
        self.cut = self.tokens // 2

    def rows(self, r, whole):
        return pl.ds(0, self.tokens if whole or r == 0 else self.cut)

    def line(self, i, r, whole=True):
        rows = self.rows(r, whole)
        return Line(self.place, lambda zz: self.buf.at[i, zz, r, rows], self.send.at[i, r], self.recv.at[i, r])

    def near(self, i, r, src):
        return pltpu.make_async_copy(src, self.buf.at[i, self.place.d, r], self.local.at[i, r])

    def across(self, i, way, h, r):
        at = self.line(i, 0).origin(way, h)
        rest = pl.ds(self.cut, self.tokens - self.cut)
        return remote(
            self.buf.at[i, at, 0, rest], self.buf.at[i, at, r, rest],
            self.ysend.at[i, way, h, r], self.yrecv.at[i, way, h, r], self.place.behind(r),
        )

    def start(self, i, r, src, keep=True, whole=True):
        if keep:
            self.near(i, r, src).start()
        self.line(i, r, whole).start(src.at[self.rows(r, whole)])

    def step(self, i, h, whole=True, forward=True):
        for r in range(self.place.ny):
            self.line(i, r, whole).step(h, forward=forward)

    def go_on(self, i, h, whole=True):
        for r in range(self.place.ny):
            self.line(i, r, whole).go_on(h)

    def passes(self, i, hops):
        line = self.line(i, 0)
        for h in hops:
            for way in range(2):
                @pl.when(line.comes(way, h))
                def _():
                    for r in range(1, self.place.ny):
                        self.across(i, way, h, r).start()

    def finish(self, i, kept, whole=True, hops=None):
        for r in kept:
            self.near(i, r, self.buf.at[i, self.place.d, r]).wait()
        for r in range(self.place.ny):
            self.line(i, r, whole).finish(hops)
        if not whole:
            self.finish_passes(i, hops)

    def finish_passes(self, i, hops=None):
        g = self.place
        line = self.line(i, 0)
        for h in range(1, g.nz) if hops is None else hops:
            for way in range(2):
                @pl.when(line.comes(way, h))
                def _():
                    for r in range(1, g.ny):
                        self.across(i, way, h, r).wait()


class Exchange:
    def __init__(self, place, chunks, rows_ref, retl, retc, rety, sendl, sendc, sendy, sems, parts=1):
        self.place, self.chunks, self.parts = place, chunks, parts
        self.rows_ref = rows_ref
        self.retl, self.retc, self.rety = retl, retc, rety
        self.sendl, self.sendc, self.sendy = sendl, sendc, sendy
        self.sems = sems
        self.tokens = rows_ref.shape[2]
        self.span = self.tokens // chunks

    def rows(self, q):
        return pl.ds(q * self.span, self.span)

    def core_own(self):
        g = self.place
        return remote(
            self.rows_ref.at[0, 0], self.rows_ref.at[0, 1], self.sems.cs.at[0, 0], self.sems.cr.at[0, 0], g.core
        )

    def y_part(self, r, i):
        g = self.place
        size = self.span // self.parts
        rows = pl.ds(i * size, size)
        return remote(
            self.rows_ref.at[0, 0, rows],
            self.rows_ref.at[r, 0, rows],
            self.sems.ys.at[r, i],
            self.sems.yr.at[r, i],
            g.behind(r),
        )

    def y_parts(self, r, q):
        return [self.y_part(r, q * self.parts + p) for p in range(self.parts)]

    def forward(self, r, q):
        g = self.place
        return remote(
            self.rows_ref.at[r, 0, self.rows(q)],
            self.rows_ref.at[r, 1, self.rows(q)],
            self.sems.cs.at[r, q],
            self.sems.cr.at[r, q],
            g.core,
        )

    def back_local(self):
        return remote(self.sendl, self.retl, self.sems.bs.at[0, 0], self.sems.br.at[0, 0], self.place.core)

    def back_core(self, r, q):
        return remote(
            self.sendc.at[r - 1, self.rows(q)],
            self.retc.at[r - 1, self.rows(q)],
            self.sems.bs.at[r, q],
            self.sems.br.at[r, q],
            self.place.core,
        )

    def back_y(self, r, q):
        g = self.place
        return remote(
            self.sendy.at[r - 1, self.rows(q)],
            self.rety.at[g.ny - r - 1, self.rows(q)],
            self.sems.zs.at[r, q],
            self.sems.zr.at[g.ny - r, q],
            g.ahead(r),
        )

    def back_y_arrival(self, r, q):
        g = self.place
        return remote(
            self.sendy.at[r - 1, self.rows(q)],
            self.rety.at[r - 1, self.rows(q)],
            self.sems.zs.at[r, q],
            self.sems.zr.at[r, q],
            g.ahead(r),
        )

    def send_own(self):
        for i in range(self.chunks * self.parts):
            self.send_part(i)
        self.core_own().start()

    def send_part(self, i):
        for r in range(1, self.place.ny):
            self.y_part(r, i).start()

    def run(self, local_block, remote_block, complete, early=None):
        ny = self.place.ny
        items = [(r, q) for q in range(self.chunks) for r in range(1, ny)]
        def arrive(r, q):
            for part in self.y_parts(r, q):
                part.wait_recv()
            self.forward(r, q).start()
            if q == self.chunks - 1:
                complete(r)

        if items and early is not None:
            @pl.when(early)
            def _():
                arrive(*items[0])

        self.core_own().wait_recv()
        local_block()
        self.back_local().start()
        if items and early is None:
            arrive(*items[0])
        if items and early is not None:
            @pl.when(jnp.logical_not(early))
            def _():
                arrive(*items[0])

        for i, (r, q) in enumerate(items):
            self.forward(r, q).wait_recv()
            own = remote_block(r, q)
            self.back_core(r, q).start()
            if i + 1 < len(items):
                arrive(*items[i + 1])
            self.back_core(r, q).wait_recv()
            here = self.rows(q)
            self.sendy[r - 1, here, :] = (own() + self.retc[r - 1, here, :].astype(F32)).astype(BF16)
            self.back_y(r, q).start()
        self.back_local().wait_recv()

    def arrived(self, q):
        for r in range(1, self.place.ny):
            self.back_y_arrival(r, q).wait_recv()

    def finish(self):
        ny = self.place.ny
        self.core_own().wait_send()
        self.back_local().wait_send()
        for q in range(self.chunks):
            for r in range(1, ny):
                for part in self.y_parts(r, q):
                    part.wait_send()
                self.forward(r, q).wait_send()
                self.back_core(r, q).wait_send()
                self.back_y(r, q).wait_send()


class Sems:
    def __init__(self, refs, m):
        self.cs, self.cr, self.ys, self.yr, self.bs, self.br, self.zs, self.zr = [ref.at[m] for ref in refs]


def sem_shapes(micro, ny, chunks):
    return [pltpu.SemaphoreType.DMA((micro, ny, chunks)) for _ in range(8)]


def chosen_gates(logits_t, route):
    experts = lax.broadcasted_iota(jnp.int32, logits_t.shape, 0)
    chosen = route[0:1, :] == experts
    for k in range(1, route.shape[0]):
        chosen = chosen | (route[k : k + 1, :] == experts)
    masked = jnp.where(chosen, logits_t, NEGATIVE)
    raised = jnp.where(chosen, jnp.exp(masked - jnp.max(masked, 0, keepdims=True)), 0.0)
    return raised / jnp.sum(raised, 0, keepdims=True)


def gate_lanes(gates_t, expert):
    rows = lax.broadcasted_iota(jnp.int32, gates_t.shape, 0)
    one = jnp.sum(jnp.where(rows == expert, gates_t, 0.0), 0, keepdims=True)
    return jnp.transpose(jnp.broadcast_to(one, (128, one.shape[1])))


def widen(lanes, width):
    return jnp.concatenate([lanes] * (width // 128), 1)


def gather_kernel(
    ny, nz,
    small_ref, route_h, wqkv_h, wout_h, wg_h, wu_h,
    small_t, route_o, wqkv_o, wout_o, slices_o,
    small_s, wg, wu, turned,
    lsem, own_sem, cs, cr, ys, yr, zs, zr, sls,
):
    g = Place(ny, nz)
    hidden, width = turned.shape[2], turned.shape[3]
    slice_h = hidden // nz
    loads = [pltpu.make_async_copy(src, dst, lsem.at[i]) for i, (src, dst) in enumerate(((wg_h, wg), (wu_h, wu)))]
    for copy in loads:
        copy.start()
    g.greet(with_x=False)
    split = width * 2 // 3
    arrays = (
        (small_ref, lambda e, zz: small_s.at[e, zz]),
        (route_h, lambda e, zz: route_o.at[e, zz]),
        (wqkv_h, lambda e, zz: wqkv_o.at[e, zz]),
        (wout_h.at[:, 0:split], lambda e, zz: wout_o.at[e, zz, :, 0:split]),
        (wout_h.at[:, split:width], lambda e, zz: wout_o.at[e, zz, :, split:width]),
    )
    count = len(arrays)
    turned_way = count - 1
    plain = range(turned_way)

    def near(n):
        src, slot = arrays[n]
        return pltpu.make_async_copy(src, slot(g.e, g.d), own_sem.at[n])

    lines = [
        Line(g, lambda zz, slot=slot: slot(g.e, zz), zs.at[n, 0], zr.at[n, 0]) for n, (_, slot) in enumerate(arrays)
    ]
    turned_lines = [
        Line(g, lambda zz, r=r: arrays[turned_way][1](g.pack(r, False), zz), zs.at[turned_way, r], zr.at[turned_way, r])
        for r in range(ny)
    ]

    def along_y(n, way, h, r):
        src, slot = arrays[n]
        at = slot(g.e, lines[n].origin(way, h))
        return remote(src if h == 0 else at, at, ys.at[n, way, h, r], yr.at[n, way, h, r], g.behind(r))

    def to_core(n, way, h, r):
        src, slot = arrays[n]
        at = slot(g.pack(r, False), lines[n].origin(way, h))
        own = h == 0 and r == 0
        return remote(src if own else at, at, cs.at[n, way, h, r], cr.at[n, way, h, r], g.core)

    for n in [turned_way] + list(plain):
        for r in range(1, ny):
            along_y(n, 0, 0, r).start()
        lines[n].start(arrays[n][0])
        near(n).start()
        to_core(n, 0, 0, 0).start()

    def got_z(n, h):
        if n == turned_way:
            for r, line in enumerate(turned_lines):
                line.step(h, lambda way, h, r=r: to_core(n, way, h, r).start())
            return

        def then(way, h):
            for r in range(1, ny):
                along_y(n, way, h, r).start()
            to_core(n, way, h, 0).start()

        lines[n].step(h, then)

    def got_y(n, h):
        for way in range(1 if h == 0 else 2):
            def pass_on():
                for r in range(1, ny):
                    along_y(n, way, h, r).wait_recv()
                    to_core(n, way, h, r).start()
                    if n == turned_way:
                        turned_lines[r].start(arrays[n][1](g.pack(r, False), g.d))

            if h == 0:
                pass_on()
            else:
                pl.when(lines[n].comes(way, h))(pass_on)

    parts = []
    for i in range(2):
        for t in range(nz // 2):
            here = pl.ds(pl.multiple_of(g.z_of(2 * t) * slice_h, slice_h), slice_h)
            for j in range(2):
                n = 2 * t + j
                to = slice(n * slice_h, (n + 1) * slice_h)
                parts.append(pltpu.make_async_copy(turned.at[i, j, here], slices_o.at[i, to], sls.at[i, n]))

    def turn(i, j, n):
        src = (wg, wu)[i]
        if j == 0 and n == 0:
            loads[i].wait()
        cols = slice(n * 256, (n + 1) * 256)
        turned[i, j, cols, :] = jnp.transpose(src[j, :, cols])

    turns = [(i, j, n) for i in range(2) for j in range(2) for n in range(hidden // 256)]

    z_items = [(n, h) for h in range(1, nz) for n in range(count)]
    y_items = [(n, h) for h in range(nz) for n in plain]
    done = 0
    for i, item in enumerate(z_items):
        if item == (2, 1):
            got_y(turned_way, 0)
        got_z(*item)
        if (i % 2 == 1 or i >= count) and item[0] != turned_way:
            got_y(*y_items[done])
            done += 1
        for piece in turns[:2]:
            turn(*piece)
        turns = turns[2:]
        if not turns and parts:
            for copy in parts:
                copy.start()
            started, parts = parts, []
    for item in y_items[done:]:
        got_y(*item)

    def each(act):
        for n in range(count):
            for h in range(nz):
                for way in range(1 if h == 0 else 2):
                    if h == 0:
                        act(n, way, h)
                    else:
                        pl.when(lines[n].comes(way, h))(lambda: act(n, way, h))

    def arrived(n, way, h):
        for r in range(ny):
            to_core(n, way, h, r).wait_recv()

    def sent(n, way, h):
        for r in range(ny):
            to_core(n, way, h, r).wait_send()
            if r and (h == 0 or n != turned_way):
                along_y(n, way, h, r).wait_send()

    each(arrived)
    for n in range(count):
        near(n).wait()
    gathered = small_s[...].reshape(width, small_s.shape[3])
    small_t[...] = jnp.transpose(gathered)[0:SMALL_ROWS].astype(BF16)
    each(sent)
    for line in lines[:turned_way] + turned_lines:
        line.finish()
    for copy in started:
        copy.wait()


def forward_kernel(
    ny, nz, sections,
    x_ref, segc_ref, segr_ref, route_ref, small_ref, cos_ref, sin_ref,
    cot_h, slices_h, wqkv_h, wout_h, wg_h, wu_h, wd_h,
    out_ref, hin_ref, h1_ref, qkv_ref, obb_ref, xm_ref, gates_ref, zf_h, obp_h, share_h,
    wqkv, wout, wg, wu, wd, ob_s, hid, accl, accr, retl, retc, rety, sendl, sendc, sendy,
    wsem, zs, zr, zys, zyr, zl, gs, gr, xs, xr, ps, pr, hs, hr, *sem_refs,
):
    micro, tokens, width = x_ref.shape
    hidden = wg.shape[2]
    span = tokens // FORWARD_CHUNKS
    loads = [
        pltpu.make_async_copy(src, dst, wsem.at[i])
        for i, (src, dst) in enumerate([(wqkv_h, wqkv), (wout_h, wout), (wg_h, wg), (wu_h, wu), (wd_h, wd)])
    ]
    for load in loads:
        load.start()
    g = Place(ny, nz)
    g.greet()
    gain_a = small_ref[ROUTER_ROWS : ROUTER_ROWS + 1, :].astype(F32)
    gain_m = small_ref[ROUTER_ROWS + 1 : ROUTER_ROWS + 2, :].astype(F32)
    cos, sin = cos_ref[...], sin_ref[...]
    gather = Gather(g, zf_h, zs, zr, zys, zyr, zl)
    every = range(ny)
    first, last = g.s == 0, g.s == sections - 1

    slice_h = hidden // nz
    shares = [remote(slices_h.at[i], share_h.at[i], hs.at[i], hr.at[i], g.core) for i in range(2)]
    for t in range(nz // 2):
        here = pl.ds(pl.multiple_of(g.z_of(2 * t) * slice_h, slice_h), slice_h)
        for j in range(2):
            n = 2 * t + j
            to = slice(n * slice_h, (n + 1) * slice_h)
            shares.append(remote(wd_h.at[j, here], share_h.at[2, to], hs.at[2 + n], hr.at[2 + n], g.core))

    def cot_copy(r):
        return remote(cot_h.at[0], zf_h.at[0, g.d, r], gs.at[r], gr.at[r], g.behind(r))

    @pl.when(last)
    def _():
        for r in range(1, ny):
            cot_copy(r).start()
        gather.start(0, 0, cot_h.at[0])
        for r in range(1, ny):
            cot_copy(r).wait_recv()
            gather.start(0, r, zf_h.at[0, g.d, r], keep=False)
        for copy in shares:
            copy.start()
        gather.step(0, 1)

    def hop(m, q):
        here = pl.ds(q * (tokens // HOP_CHUNKS), tokens // HOP_CHUNKS)
        return remote(out_ref.at[m, here], hin_ref.at[m, here], xs.at[m, q], xr.at[m, q], g.x)

    def experts(rows, lanes, keep):
        count = rows.shape[0]
        for j in range(2):
            for n in range(hidden // 256):
                cols = slice(n * 256, (n + 1) * 256)
                a = dot(rows, wg[j, :, cols])
                b = dot(rows, wu[j, :, cols])
                act = 0.5 * a * (1.0 + jnp.tanh(GELU_C * (a + GELU_A * a * a * a)))
                hid[j, 0:count, cols] = (act * b).astype(BF16)
        for n in range(width // 512):
            cols = slice(n * 512, (n + 1) * 512)
            total = None
            for j in range(2):
                eo = dot(hid[j, 0:count, :], wd[j, :, cols]).astype(BF16).astype(F32)
                term = widen(lanes[j], 512) * eo
                total = term if total is None else total + term
            keep(cols, total)

    def partner(m, yy):
        return remote(obb_ref.at[m, yy * 2 + 1 - g.c], obp_h.at[m, yy], ps.at[m, yy], pr.at[m, yy], g.core)

    def body(m, carry):
        @pl.when(g.s == 0)
        def _():
            hin_ref[m] = x_ref[m]

        @pl.when(g.s > 0)
        def _():
            for q in range(HOP_CHUNKS):
                hop(m, q).wait_recv()

        h = hin_ref[m].astype(F32)
        xa = (h * lax.rsqrt(jnp.mean(h * h, -1, keepdims=True) + EPS) * gain_a).astype(BF16)

        @pl.when(m == 0)
        def _():
            loads[0].wait()

        turned = QUERY_HEADS + KEY_VALUE_HEADS
        for i in range(wqkv.shape[1] // 256):
            mixed = dot(xa, wqkv[:, i * 256 : (i + 1) * 256])
            for half in range(2):
                head = 2 * i + half
                part = mixed[:, half * HEAD : (half + 1) * HEAD]
                if head < turned:
                    part = part * cos + pltpu.roll(part, HEAD // 2, 1) * sin
                qkv_ref[m, :, head * HEAD : (head + 1) * HEAD] = part.astype(BF16)
        bias = mask_bias(segc_ref[m], segr_ref[m])
        bias6 = jnp.concatenate([bias] * GROUP, 0)
        qkv = qkv_ref.at[m]
        for kv in range(KEY_VALUE_HEADS):
            q6 = heads_of(qkv, kv * GROUP, GROUP)
            k = heads_of(qkv, QUERY_HEADS + kv, 1)
            v = heads_of(qkv, turned + kv, 1)
            shares = attention_shares(q6, k, bias6).astype(BF16)
            o6 = dot(shares, v).astype(BF16)
            for i in range(GROUP):
                head = kv * GROUP + i
                ob_s[:, head * HEAD : (head + 1) * HEAD] = o6[i * tokens : (i + 1) * tokens]

        @pl.when(m == 0)
        def _():
            loads[1].wait()

        ob = ob_s[...]
        block = obb_ref.shape[3]
        for i in range(2 * ny):
            obb_ref[m, i] = ob[:, i * block : (i + 1) * block]
        for n in range(width // 512):
            cols = slice(n * 512, (n + 1) * 512)
            h1_ref[m, :, cols] = hin_ref[m, :, cols].astype(F32) + dot(ob, wout[:, cols])
        h1 = h1_ref[m]
        xm_ref[m, 0, 0] = (h1 * lax.rsqrt(jnp.mean(h1 * h1, -1, keepdims=True) + EPS) * gain_m).astype(BF16)

        ex = Exchange(g, FORWARD_CHUNKS, xm_ref.at[m], retl, retc, rety, sendl, sendc, sendy, Sems(sem_refs, m))
        ex.send_own()

        def complete(r):
            @pl.when(first & (m == 0))
            def _():
                gather.start(0, r, xm_ref.at[0, r, 0])

        def move(h):
            if h + 1 < nz:
                @pl.when(last & (m == 0))
                def _():
                    gather.step(0, h + 1)

            if h < nz:
                @pl.when(first & (m == 1))
                def _():
                    gather.step(0, h)

        complete(0)
        move(1)

        @pl.when(m == 0)
        def _():
            for load in loads[2:]:
                load.wait()

        def gates_for(r, other, here):
            rows = xm_ref[m, r, other, here, :]
            logits_t = dot_nt(small_ref[0:ROUTER_ROWS, :], rows)
            gates_t = chosen_gates(logits_t, route_ref[g.pack(r, other) * nz + g.d, m][:, here])
            return gates_t

        def lanes_of(blocks):
            return [
                jnp.concatenate([gate_lanes(gates_t, 2 * g.e + j) for gates_t in blocks], 0) for j in range(2)
            ]

        full = slice(0, tokens)

        def local_block():
            blocks = []
            for other in range(2):
                gates_t = gates_for(0, other, full)
                gates_ref[m, 0, other] = gates_t
                blocks.append(gates_t)

            def keep(cols, total):
                accl[:, cols] = total[0:tokens]
                sendl[:, cols] = total[tokens:].astype(BF16)

            experts(xm_ref[m, 0].reshape(2 * tokens, width), lanes_of(blocks), keep)

        def remote_block(r, q):
            here = slice(q * span, (q + 1) * span)
            blocks = []
            for other in range(2):
                gates_t = gates_for(r, other, here)
                gates_ref[m, r, other, :, here] = gates_t
                blocks.append(jnp.concatenate([gates_t] * (128 // span), 1))
            lanes = [
                jnp.concatenate([gate_lanes(gates_t, 2 * g.e + j)[0:span] for gates_t in blocks], 0)
                for j in range(2)
            ]

            def keep(cols, total):
                accr[:, cols] = total[0:span]
                sendc[r - 1, here, cols] = total[span:].astype(BF16)

            experts(xm_ref[m, r, :, here, :].reshape(2 * span, width), lanes, keep)
            return lambda: accr[...]

        ex.run(local_block, remote_block, complete)
        for q in range(HOP_CHUNKS):
            here = slice(q * span, (q + 1) * span)
            ex.arrived(q)
            total = h1_ref[m, here, :] + accl[here, :] + retl[here, :].astype(F32)
            for r in range(1, ny):
                total = total + rety[r - 1, here, :].astype(F32)
            out_ref[m, here, :] = total.astype(BF16)

            @pl.when(g.s < sections - 1)
            def _():
                hop(m, q).start()

        ex.finish()
        for yy in range(ny):
            partner(m, yy).start()
        move(2)
        return carry

    lax.fori_loop(0, micro, body, 0)

    @pl.when(jnp.logical_not(last))
    def _():
        for copy in shares:
            copy.start()

    for m in range(micro):
        for yy in range(ny):
            partner(m, yy).wait()

    @pl.when(g.s < sections - 1)
    def _():
        for m in range(micro):
            for q in range(HOP_CHUNKS):
                hop(m, q).wait_send()

    @pl.when(first)
    def _():
        for h in range(3, nz):
            gather.step(0, h)
        gather.finish(0, every)

    for copy in shares:
        copy.wait()

    @pl.when(last)
    def _():
        for r in range(1, ny):
            cot_copy(r).wait_send()
        for h in range(4, nz):
            gather.step(0, h)
        gather.finish(0, [0])


def backward_kernel(
    ny, nz, sections,
    cot_ref, segc_ref, segr_ref, small_ref, cos_ref, sin_ref,
    hin_ref, h1_ref, qkv_ref, gates_ref,
    xm_h, wqkv_h, wout_h, wg_h, wu_h, wd_h,
    gin_ref, grows_ref, xab_ref, dqkv_ref, dattn_ref, gsmall_ref, zb_h, xap_h, dqp_h, dtp_h,
    wqkv, wout, wg, wu, wd, xm_s, hid, act_s, slope_s, da_s, db_s, accl, accr, dh1_s, n_s,
    retl, retc, rety, sendl, sendc, sendy,
    wsem, xmsem, zs, zr, zys, zyr, zl, xs, xr, ps, pr, *sem_refs,
):
    micro, tokens, width = cot_ref.shape
    hidden = wg.shape[2]
    span = tokens // BACKWARD_CHUNKS
    loads = [
        pltpu.make_async_copy(src, dst, wsem.at[i])
        for i, (src, dst) in enumerate([(wg_h, wg), (wu_h, wu), (wd_h, wd), (wout_h, wout), (wqkv_h, wqkv)])
    ]
    for load in loads:
        load.start()
    g = Place(ny, nz)
    g.greet()
    gain_a = small_ref[ROUTER_ROWS : ROUTER_ROWS + 1, :].astype(F32)
    gain_m = small_ref[ROUTER_ROWS + 1 : ROUTER_ROWS + 2, :].astype(F32)
    cos, sin = cos_ref[...], sin_ref[...]
    gsmall_ref[...] = jnp.zeros_like(gsmall_ref)
    gather = Gather(g, zb_h, zs, zr, zys, zyr, zl)
    every = range(ny)
    first, last = g.s == 0, g.s == sections - 1

    @pl.when(first)
    def _():
        for m in range(1, micro):
            for r in every:
                gather.start(micro + m, r, xm_h.at[m, r, 0])
            for h in range(1, nz):
                gather.step(micro + m, h)

    def hop(m, q):
        here = pl.ds(q * (tokens // HOP_CHUNKS), tokens // HOP_CHUNKS)
        return remote(gin_ref.at[m, here], grows_ref.at[m, 0, 0, here], xs.at[m, q], xr.at[m, q], g.x)

    def partner(m):
        pairs = [(dattn_ref.at[m], dtp_h.at[m]), (dqkv_ref.at[m], dqp_h.at[m])]
        pairs += [(xab_ref.at[m, yy * 2 + 1 - g.c], xap_h.at[m, yy]) for yy in range(ny)]
        return [remote(src, dst, ps.at[m, n], pr.at[m, n], g.core) for n, (src, dst) in enumerate(pairs)]

    def late(m):
        for h in range(3, nz):
            gather.step(m, h, whole=False)

    def body(m, carry):
        load_xm = pltpu.make_async_copy(xm_h.at[m], xm_s, xmsem)
        load_xm.start()

        @pl.when(last)
        def _():
            grows_ref[m, 0, 0] = cot_ref[m]
            for r in every:
                gather.start(m, r, xm_h.at[m, r, 0], whole=False)

        ex = Exchange(
            g, BACKWARD_CHUNKS, grows_ref.at[m], retl, retc, rety, sendl, sendc, sendy, Sems(sem_refs, m), HOP_CHUNKS
        )

        @pl.when(last)
        def _():
            ex.send_own()

        @pl.when(m == 0)
        def _():
            for load in loads[:3]:
                load.wait()

        load_xm.wait()

        def again(r, _):
            rows = xm_s[r].reshape(2 * tokens, width)
            for j in range(2):
                for n in range(hidden // 256):
                    cols = slice(n * 256, (n + 1) * 256)
                    a = dot(rows, wg[j, :, cols])
                    b = dot(rows, wu[j, :, cols])
                    square = a * a
                    th = jnp.tanh(GELU_C * (a + GELU_A * square * a))
                    half = 0.5 * (1.0 + th)
                    act = a * half
                    slope = half + (0.5 * GELU_C) * a * (1.0 - th * th) * (1.0 + (3.0 * GELU_A) * square)
                    shape = (2, tokens, 256)
                    hid[j, r, :, :, cols] = (act * b).astype(BF16).reshape(shape)
                    act_s[j, r, :, :, cols] = act.astype(BF16).reshape(shape)
                    slope_s[j, r, :, :, cols] = (slope * b).astype(BF16).reshape(shape)
            return 0

        @pl.when(first)
        def _():
            lax.fori_loop(0, ny, again, 0)

            @pl.when(m > 0)
            def _():
                late(m - 1)

            for q in range(HOP_CHUNKS):
                hop(m, q).wait_recv()
                ex.send_part(q)
            ex.core_own().start()

        def complete(r):
            src = grows_ref.at[m, r, 0]

            @pl.when(first)
            def _():
                gather.start(m, r, src, whole=False)

        open_end = first & (m == micro - 1)

        def move(hops):
            for h in hops:
                gather.step(m, h, whole=False)

        complete(0)

        @pl.when(last)
        def _():
            lax.fori_loop(0, ny, again, 0)


        def experts(rows, r, here, keep):
            count = 2 * (here.stop - here.start)
            part = slice(0, count)
            lane = lax.broadcasted_iota(jnp.int32, (count, 128), 1)
            gate_grads = jnp.zeros((count, 128), F32)
            for j in range(2):
                expert = 2 * g.e + j
                lanes = []
                for other in range(2):
                    gates_t = gates_ref[m, r, other]
                    lanes.append(gate_lanes(gates_t, expert)[here])
                lanes = widen(jnp.concatenate(lanes, 0), 256)
                summed = jnp.zeros((count, 1), F32)
                for n in range(hidden // 256):
                    cols = slice(n * 256, (n + 1) * 256)
                    u = dot_nt(rows, wd[j, cols, :])
                    inner = hid[j, r, :, here, cols].reshape(count, 256).astype(F32)
                    summed = summed + jnp.sum(u * inner, -1, keepdims=True)
                    u = u * lanes
                    slope = slope_s[j, r, :, here, cols].reshape(count, 256).astype(F32)
                    act = act_s[j, r, :, here, cols].reshape(count, 256).astype(F32)
                    da_s[j, part, cols] = (u * slope).astype(BF16)
                    db_s[j, part, cols] = (u * act).astype(BF16)
                high = summed.astype(BF16).astype(F32)
                gate_grads = jnp.where(lane == expert, high, gate_grads)
                gate_grads = jnp.where(lane == expert + 64, summed - high, gate_grads)
            for n in range(width // 512):
                cols = slice(n * 512, (n + 1) * 512)
                total = None
                for j in range(2):
                    term = dot_nt(da_s[j, part, :], wg[j, cols, :]) + dot_nt(db_s[j, part, :], wu[j, cols, :])
                    total = term if total is None else total + term
                keep(cols, total)
            keep(slice(width, width + 128), gate_grads)

        full = slice(0, tokens)

        def local_block():
            def keep(cols, total):
                accl[:, cols] = total[0:tokens]
                sendl[:, cols] = total[tokens:].astype(BF16)

            experts(grows_ref[m, 0].reshape(2 * tokens, width), 0, full, keep)

        def remote_block(r, q):
            here = slice(q * span, (q + 1) * span)

            def keep(cols, total):
                accr[:, cols] = total[0:span]
                sendc[r - 1, here, cols] = total[span:].astype(BF16)

            experts(grows_ref[m, r, :, here, :].reshape(2 * span, width), r, here, keep)
            return lambda: accr[...]

        ex.run(local_block, remote_block, complete, last)
        move(range(1, 2))
        for q in range(BACKWARD_CHUNKS):
            ex.arrived(q)
        total = accl[...] + retl[...].astype(F32)
        for r in range(1, ny):
            total = total + rety[r - 1].astype(F32)
        dgates = total[:, width:]
        dgates = dgates + pltpu.roll(dgates, 64, 1)
        gates_t = gates_ref[m, 0, 0]
        gates = jnp.transpose(
            jnp.concatenate([gates_t, jnp.zeros((128 - ROUTER_ROWS, tokens), F32)], 0)
        )
        dlog = gates * (dgates - jnp.sum(gates * dgates, -1, keepdims=True))
        dlog = dlog[:, 0:SMALL_ROWS]
        high = dlog.astype(BF16)
        low = (dlog - high.astype(F32)).astype(BF16)
        router = small_ref[...]
        dxm = total[:, 0:width] + dot(high, router) + dot(low, router)
        xm = xm_s[0, 0]
        gsmall_ref[0:ROUTER_ROWS, :] += (dot_tn(high, xm) + dot_tn(low, xm))[0:ROUTER_ROWS]
        h1 = h1_ref[m]
        rinv = lax.rsqrt(jnp.mean(h1 * h1, -1, keepdims=True) + EPS)
        n2 = h1 * rinv
        gsmall_ref[ROUTER_ROWS + 1 : ROUTER_ROWS + 2, :] += jnp.sum(dxm * n2, 0, keepdims=True)
        scaled = dxm * gain_m
        dh1 = grows_ref[m, 0, 0].astype(F32) + rinv * (scaled - n2 * jnp.mean(scaled * n2, -1, keepdims=True))
        dh1_s[...] = dh1
        dattn = dh1.astype(BF16)
        dattn_ref[m] = dattn

        @pl.when(m == 0)
        def _():
            for load in loads[3:]:
                load.wait()

        @pl.when(jnp.logical_not(open_end))
        def _():
            move(range(2, min(3, nz)))

        @pl.when(first)
        def _():
            gather.passes(m, range(1, 2))

        @pl.when(first & (m > 0))
        def _():
            gather.passes(m - 1, range(3, nz))

        @pl.when(first & (m < micro - 1))
        def _():
            gather.passes(m, range(2, min(3, nz)))

        for copy in partner(m)[:1]:
            copy.start()
        bias = mask_bias(segc_ref[m], segr_ref[m])
        bias6 = jnp.concatenate([bias] * GROUP, 0)
        qkv = qkv_ref.at[m]
        turned = QUERY_HEADS + KEY_VALUE_HEADS

        def unturn(part):
            return part * cos - pltpu.roll(part, HEAD // 2, 1) * sin

        for kv in range(KEY_VALUE_HEADS):
            wide = GROUP * HEAD
            dob = dot_nt(dattn, wout[kv * wide : (kv + 1) * wide, :]).astype(BF16)
            dob6 = heads_of(dob, 0, GROUP)
            q6 = heads_of(qkv, kv * GROUP, GROUP)
            k = heads_of(qkv, QUERY_HEADS + kv, 1)
            v = heads_of(qkv, turned + kv, 1)
            shares = attention_shares(q6, k, bias6)
            dshares = dot_nt(dob6, v)
            dv = dot_tn(shares.astype(BF16), dob6)
            ds = (shares * (dshares - jnp.sum(shares * dshares, -1, keepdims=True))).astype(BF16)
            dq6 = dot(ds, k) * SCALE
            dk = dot_tn(ds, q6) * SCALE
            for i in range(GROUP):
                head = kv * GROUP + i
                dqkv_ref[m, :, head * HEAD : (head + 1) * HEAD] = unturn(
                    dq6[i * tokens : (i + 1) * tokens]
                ).astype(BF16)
            head = QUERY_HEADS + kv
            dqkv_ref[m, :, head * HEAD : (head + 1) * HEAD] = unturn(dk).astype(BF16)
            head = turned + kv
            dqkv_ref[m, :, head * HEAD : (head + 1) * HEAD] = dv.astype(BF16)

        h = hin_ref[m].astype(F32)
        rinv = lax.rsqrt(jnp.mean(h * h, -1, keepdims=True) + EPS)
        n1 = h * rinv
        xa = (n1 * gain_a).astype(BF16)
        block = xab_ref.shape[3]
        for i in range(2 * ny):
            xab_ref[m, i] = xa[:, i * block : (i + 1) * block]
        n_s[...] = n1
        dqkv = dqkv_ref[m]
        for n in range(width // 512):
            cols = slice(n * 512, (n + 1) * 512)
            accl[:, cols] = dot_nt(dqkv, wqkv[cols, :])
        dxa = accl[:, 0:width]
        n1 = n_s[...]
        gsmall_ref[ROUTER_ROWS : ROUTER_ROWS + 1, :] += jnp.sum(dxa * n1, 0, keepdims=True)
        scaled = dxa * gain_a
        grad = dh1_s[...] + rinv * (scaled - n1 * jnp.mean(scaled * n1, -1, keepdims=True))
        gin_ref[m] = grad.astype(BF16)

        @pl.when(g.s > 0)
        def _():
            for q in range(HOP_CHUNKS):
                hop(m, q).start()

        for copy in partner(m)[1:]:
            copy.start()

        @pl.when(last)
        def _():
            move(range(3, nz))

        @pl.when(open_end)
        def _():
            for h in range(2, min(3, nz)):
                gather.step(m, h, whole=False, forward=False)

        ex.finish()
        return carry

    lax.fori_loop(0, micro, body, 0)

    @pl.when(g.s > 0)
    def _():
        for m in range(micro):
            for q in range(HOP_CHUNKS):
                hop(m, q).wait_send()

    few = range(1, min(3, nz))

    @pl.when(last)
    def _():
        for m in range(micro):
            gather.passes(m, range(1, nz))
        for m in range(1, micro):
            for r in every:
                gather.start(micro + m, r, grows_ref.at[m, r, 0])
            for h in few:
                gather.step(micro + m, h, forward=m < micro - 1 or h < few[-1])
            if m < micro - 1:
                for h in range(3, nz):
                    gather.step(micro + m, h)

    for m in range(micro - 1):
        gather.finish(m, every, whole=False)
    for m in range(1, micro - 1):
        gather.finish(micro + m, every)

    @pl.when(first)
    def _():
        for r in every:
            gather.near(micro - 1, r, grows_ref.at[micro - 1, r, 0]).wait()
        for r in every:
            gather.line(micro - 1, r, False).finish(few)
        gather.finish_passes(micro - 1, range(1, 2))
        gather.finish(2 * micro - 1, every)

    @pl.when(last)
    def _():
        gather.finish(micro - 1, every, whole=False)
        gather.finish(2 * micro - 1, every, hops=few)

    for m in range(micro):
        for copy in partner(m):
            copy.wait()


def tail_kernel(
    ny, nz, sections, span,
    route_ref, small_ref, gsmall_ref,
    zf_h, zb_in, slices_h, partner_h, wd_h, xab_h, obb_h, dqkv_h, dattn_h, xap_h, obp_h, dqp_h, dtp_h,
    gate_ref, up_ref, down_ref, attn_ref, small_out, zb_h,
    w4, x_s, g_s, da_s, db_s, gh_s, acc_g, acc_u, acc_d, csend, cland, dsend, dland,
    xa_s, ob_s, dq_s, dt_s, own_s, ysend, yland, zland, sm_s, smy, smz,
    wsem, xsem, asem, ss, sr, cs, cr, ts, tr, ys, yr, zs, zr, hs, hr, hys, hyr, hl,
):
    micro, tokens, width = dqkv_h.shape[0], zf_h.shape[3], zf_h.shape[4]
    hidden = slices_h.shape[1]
    turns = nz // 2
    half = hidden // turns
    slice_h = half // 2
    both = 2 * half
    wide = 2 * hidden
    tile = 256 if both % 256 == 0 else 128
    qkv_width = dqkv_h.shape[2]
    shard = width // (2 * ny * nz)
    part = width // nz
    rows = span * ny * tokens
    groups = nz // span
    g = Place(ny, nz)
    first = g.s == 0
    pieces = []
    for t in range(turns):
        own, other = 2 * t, 2 * t + 1
        rows_t = slice(t * half, (t + 1) * half)
        pieces.append((slices_h.at[:, rows_t], w4.at[0:2, own * half : (own + 1) * half]))
        pieces.append((partner_h.at[:, rows_t], w4.at[:, other * half : (other + 1) * half]))
        here = pl.ds(pl.multiple_of(g.z_of(2 * t) * slice_h, slice_h), slice_h)
        for j in range(2):
            at = own * half + j * slice_h
            pieces.append((wd_h.at[j, here], w4.at[2, at : at + slice_h]))
    mine = [pltpu.make_async_copy(src, dst, wsem.at[n]) for n, (src, dst) in enumerate(pieces)]

    def load(i):
        m, k = lax.div(i, groups), pl.ds(lax.rem(i, groups) * span, span)
        early = [(first, x_s, 0), (jnp.logical_not(first), g_s, 1)]
        late = [(first, g_s, 1), (jnp.logical_not(first), x_s, 0)]
        copies = [(when, pltpu.make_async_copy(zb_h.at[m, k], dst, xsem.at[n])) for when, dst, n in late]
        for when, dst, n in early:
            copies.append((when & (m == 0), pltpu.make_async_copy(zf_h.at[0, k], dst, xsem.at[n])))
            copies.append((when & (m > 0), pltpu.make_async_copy(zb_h.at[micro + m, k], dst, xsem.at[n])))
        return copies

    def start_load(i):
        for when, copy in load(i):
            @pl.when(when)
            def _():
                copy.start()

    def wait_load():
        pltpu.make_async_copy(zf_h.at[0, pl.ds(0, span)], x_s, xsem.at[0]).wait()
        pltpu.make_async_copy(zf_h.at[0, pl.ds(0, span)], g_s, xsem.at[1]).wait()

    acts = []
    for m in range(micro):
        for yy in range(ny):
            own = yy * 2 + g.c
            acts.append((xab_h.at[m, own], xa_s.at[yy, 0, m]))
            acts.append((xap_h.at[m, yy], xa_s.at[yy, 1, m]))
            acts.append((obb_h.at[m, own], ob_s.at[yy, 0, m]))
            acts.append((obp_h.at[m, yy], ob_s.at[yy, 1, m]))
    acts += [(dqkv_h, dq_s.at[0]), (dqp_h, dq_s.at[1]), (dattn_h, dt_s.at[0]), (dtp_h, dt_s.at[1])]
    acts = [pltpu.make_async_copy(src, dst, asem.at[i]) for i, (src, dst) in enumerate(acts)]
    for copy in acts:
        copy.start()
    g.greet(with_x=False)
    gather = Gather(g, zb_h, hs, hr, hys, hyr, hl)
    late_hops = range(3, nz)
    newest = micro - 1

    @pl.when(first)
    def _():
        gather.passes(newest, range(2, min(3, nz)))
        for h in late_hops[:1]:
            gather.go_on(newest, h, whole=False)

    @pl.when(jnp.logical_not(first))
    def _():
        for h in late_hops[:1]:
            gather.go_on(micro + newest, h)
    sm_core = remote(gsmall_ref, sm_s.at[1], ss.at[0], sr.at[0], g.core)
    sm_core.start()

    def sm_y(r):
        return remote(sm_s.at[0], smy.at[ny - r - 1], ss.at[r], sr.at[ny - r], g.ahead(r))

    def sm_y_arrival(r):
        return remote(sm_s.at[0], smy.at[r - 1], ss.at[r], sr.at[r], g.ahead(r))

    def sm_z(k):
        return remote(sm_s.at[1], smz.at[k - 1], ss.at[ny + k], sr.at[ny + k], g.z_behind(k))

    for copy in acts:
        copy.wait()
    for copy in mine:
        copy.start()
    start_load(0)

    count = 2 * micro * tokens

    def attn_rows(yy, dst):
        for src, grad, at in ((xa_s, dq_s, 0), (ob_s, dt_s, qkv_width)):
            left = src[yy].reshape(count, shard * nz)
            wide = grad.shape[3]
            for n in range(wide // 512):
                cols = slice(n * 512, (n + 1) * 512)
                got = dot_tn(left, grad[:, :, :, cols].reshape(count, 512)).astype(BF16)
                for zi in range(nz):
                    dst[zi, 0:shard, at + n * 512 : at + (n + 1) * 512] = got[zi * shard : (zi + 1) * shard]

    def flipped(mask):
        place = g.d
        for b in range(nz.bit_length()):
            if mask >> b & 1:
                place = place + (1 << b) - (2 << b) * lax.rem(lax.div(g.d, 1 << b), 2)
        return place

    def y_copy(r, k):
        zi = flipped(k)
        return remote(ysend.at[r - 1, zi], yland.at[ny - r - 1, zi], ys.at[r, k], yr.at[ny - r, k], g.ahead(r))

    def y_arrival(r, k):
        zi = flipped(k)
        return remote(ysend.at[r - 1, zi], yland.at[r - 1, zi], ys.at[r, k], yr.at[r, k], g.ahead(r))

    order = list(range(1, nz)) + [0]
    masks = list(range(nz - 1, -1, -1))

    def y_start(k):
        for r in range(1, ny):
            y_copy(r, k).start()

    for r in range(1, ny):
        attn_rows(lax.rem(g.y + r, ny), ysend.at[r - 1])
    y_start(masks[0])
    sm_core.wait_recv()
    sm_s[0] = gsmall_ref[...] + sm_s[1]
    sm_core.wait_send()
    for r in range(1, ny):
        sm_y(r).start()
    attn_rows(g.y, own_s)

    bits = nz.bit_length() - 1

    def low(mask):
        return (mask & -mask).bit_length() - 1 if mask else bits

    landings = [(mask, b) for mask in range(nz) for b in range(low(mask))]

    def z_copy(mask):
        b = low(mask)
        at = landings.index((mask - (1 << b), b))
        device = (g.s, g.e, flipped(1 << b))
        return remote(own_s.at[flipped(mask)], zland.at[at], zs.at[0, mask], zr.at[0, at], device)

    def z_arrival(mask, b):
        at = landings.index((mask, b))
        device = (g.s, g.e, flipped(1 << b))
        return remote(own_s.at[flipped(mask)], zland.at[at], zs.at[0, mask], zr.at[0, at], device)

    def advance(mask):
        for r in range(1, ny):
            y_arrival(r, mask).wait_recv()
        zi = flipped(mask)
        for b in range(low(mask)):
            z_arrival(mask, b).wait_recv()
        for n in range((qkv_width + width) // 512):
            cols = slice(n * 512, (n + 1) * 512)
            total = own_s[zi, :, cols].astype(F32)
            for r in range(1, ny):
                total = total + yland[r - 1, zi, :, cols].astype(F32)
            for b in range(low(mask)):
                total = total + zland[landings.index((mask, b)), :, cols].astype(F32)
            own_s[zi, :, cols] = total.astype(BF16)
        if mask:
            z_copy(mask).start()

    for copy in mine:
        copy.wait()
    acc_g[...] = jnp.zeros_like(acc_g)
    acc_u[...] = jnp.zeros_like(acc_u)
    acc_d[...] = jnp.zeros_like(acc_d)
    column = lax.rem(lax.broadcasted_iota(jnp.int32, (ROUTER_ROWS, wide), 1), both)
    expert = lax.broadcasted_iota(jnp.int32, (ROUTER_ROWS, wide), 0)
    owner = jnp.where(column < half, g.e, 2 * g.y + 1 - g.c)
    local = jnp.where(column < half, column, column - half)
    chosen = 2 * owner + jnp.where(local < slice_h, 0, 1)
    spread = jnp.where(expert == chosen, 1.0, 0.0).astype(BF16)
    spread = jnp.concatenate([spread, spread], 0)

    last_group = micro * groups - 1
    accs = (acc_g, acc_u)
    parity = lax.rem(g.d, 2)

    def rows_of(x):
        at = parity if x == 0 else 1 - parity
        return pl.ds(pl.multiple_of(at * part, part), part)

    def cols_of(t, o):
        return slice((2 * t + o) * half, (2 * t + o + 1) * half)

    def core_copy(n, x, t):
        return remote(csend.at[n, x, t], cland.at[n, x, t], cs.at[n, x * turns + t], cr.at[n, x * turns + t], g.core)

    def give_half(n):
        for x in (1, 0):
            for t in range(turns):
                csend[n, x, t] = accs[n][rows_of(x), cols_of(t, 1)].astype(BF16)
                core_copy(n, x, t).start()

    def turn_copy(n, t):
        dst = (gate_ref, up_ref)[n]
        device = (g.s, g.e, flipped(1))
        return remote(cland.at[n, 1, t], dst.at[g.z_of(2 * t)], ts.at[n, t], tr.at[n, t], device)

    def turn_arrival(n, t):
        dst = (gate_ref, up_ref)[n]
        device = (g.s, g.e, flipped(1))
        return remote(cland.at[n, 1, t], dst.at[lax.rem(flipped(1) + 2 * t, nz)], ts.at[n, t], tr.at[n, t], device)

    def turn_near(n, t):
        dst = (gate_ref, up_ref)[n]
        return pltpu.make_async_copy(cland.at[n, 0, t], dst.at[g.z_of(2 * t)], ts.at[n, turns + t])

    def take_half(n):
        for x in (1, 0):
            for t in range(turns):
                core_copy(n, x, t).wait_recv()
                total = accs[n][rows_of(x), cols_of(t, 0)] + cland[n, x, t].astype(F32)
                cland[n, x, t] = total.astype(BF16)
                if x:
                    turn_copy(n, t).start()
                else:
                    turn_near(n, t).start()

    def small_z():
        for r in range(1, ny):
            sm_y_arrival(r).wait_recv()
        total = sm_s[0]
        for r in range(1, ny):
            total = total + smy[r - 1]
        sm_s[1] = total
        for k in range(1, nz):
            sm_z(k).start()

    def group(i, carry):
        m = lax.div(i, groups)
        wait_load()

        def block(b, carry):
            k = lax.rem(i, groups) * span + b
            x = x_s[b].reshape(ny * tokens, width)
            gr = g_s[b].reshape(ny * tokens, width)
            places = [(lax.rem(g.y + r, ny) * 2 + g.c) * nz + k for r in range(ny)]
            route = jnp.concatenate([route_ref[place, m] for place in places], 1)
            gates_t = chosen_gates(dot_nt(small_ref[0:ROUTER_ROWS, :], x), route)
            high = gates_t.astype(BF16)
            gates_b = jnp.concatenate([high, (gates_t - high.astype(F32)).astype(BF16)], 0)
            here = pl.ds(pl.multiple_of(b * ny * tokens, ny * tokens), ny * tokens)
            for n in range(wide // tile):
                cols = slice(n * tile, (n + 1) * tile)
                a = dot_nt(x, w4[0, cols])
                bb = dot_nt(x, w4[1, cols])
                gate = dot_tn(gates_b, spread[:, cols])
                u = dot_nt(gr, w4[2, cols]) * gate
                square = a * a
                th = jnp.tanh(GELU_C * (a + GELU_A * square * a))
                hf = 0.5 * (1.0 + th)
                act = a * hf
                slope = hf + (0.5 * GELU_C) * a * (1.0 - th * th) * (1.0 + (3.0 * GELU_A) * square)
                da_s[here, cols] = (u * slope * bb).astype(BF16)
                db_s[here, cols] = (u * act).astype(BF16)
                if (n + 1) * tile <= both:
                    gh_s[here, cols] = ((act * bb).astype(BF16).astype(F32) * gate).astype(BF16)
            return carry

        lax.fori_loop(0, span, block, 0)

        @pl.when(first & (i == newest * groups - 1))
        def _():
            for h in late_hops:
                gather.step(newest, h, whole=False)
            gather.passes(newest, late_hops)

        @pl.when(jnp.logical_not(first) & (i == newest * groups - 1))
        def _():
            for h in late_hops:
                gather.step(micro + newest, h)

        size = 256 if (2 * part) % 256 == 0 else 128
        base = lax.div(g.d, 2) * (2 * part)

        def x_columns(n):
            cols = pl.ds(pl.multiple_of(base + n * size, size), size)
            return x_s[:, :, :, cols].reshape(rows, size)

        def sum_rows(acc, right):
            def columns(n, carry):
                at = pl.ds(pl.multiple_of(n * size, size), size)
                acc[at, :] += dot_tn(x_columns(n), right[...])
                return carry

            lax.fori_loop(0, 2 * part // size, columns, 0)

        def down():
            def columns(n, carry):
                cols = pl.ds(pl.multiple_of(n * tile, tile), tile)
                acc_d[cols, :] += dot_tn(gh_s[:, cols], g_s[...].reshape(rows, width))
                return carry

            lax.fori_loop(0, both // tile, columns, 0)

        sum_rows(acc_g, da_s)

        @pl.when(i == last_group)
        def _():
            give_half(0)

        sum_rows(acc_u, db_s)

        @pl.when(i == last_group)
        def _():
            give_half(1)
            take_half(0)

        down()

        @pl.when(first & (i == newest * groups - 1))
        def _():
            for r in range(ny):
                gather.line(newest, r, False).finish(late_hops)
            gather.finish_passes(newest, range(2, nz))

        @pl.when(jnp.logical_not(first) & (i == newest * groups - 1))
        def _():
            gather.finish(micro + newest, [], hops=late_hops)

        @pl.when(i < last_group)
        def _():
            start_load(i + 1)

        for n in range(min(3, last_group)):
            @pl.when(i == n)
            def _():
                advance(masks[n])
                y_start(masks[n + 1])
                if n == 1:
                    small_z()

        return carry

    lax.fori_loop(0, micro * groups, group, 0)
    polled = min(3, last_group)
    for mask in masks[polled + 1 :]:
        y_start(mask)

    down_copy = remote(dsend, dland, cs.at[2, 0], cr.at[2, 0], g.core)
    dsend[...] = acc_d[half:both, :].astype(BF16)
    down_copy.start()
    take_half(1)
    for mask in masks[polled:-1]:
        advance(mask)
    down_copy.wait_recv()
    dland[...] = (acc_d[0:half, :] + dland[...].astype(F32)).astype(BF16)
    down_near = pltpu.make_async_copy(dland, down_ref, ts.at[0, nz])
    down_near.start()

    total = sm_s[1]
    for k in range(1, nz):
        sm_z(k).wait_recv()
        total = total + smz[k - 1]
    small_out[...] = total

    advance(0)
    attn_near = pltpu.make_async_copy(own_s.at[g.d], attn_ref, ts.at[1, nz])
    attn_near.start()
    for t in range(turns):
        for n in range(2):
            turn_arrival(n, t).wait_recv()

    for r in range(1, ny):
        sm_y(r).wait_send()
        for k in range(nz):
            y_copy(r, k).wait_send()
    for k in range(1, nz):
        sm_z(k).wait_send()
        z_copy(k).wait_send()
    for n in range(2):
        for t in range(turns):
            turn_copy(n, t).wait_send()
            turn_near(n, t).wait()
            for x in range(2):
                core_copy(n, x, t).wait_send()
    down_copy.wait_send()
    down_near.wait()
    attn_near.wait()


def finish_kernel(nz, experts, gate_in, up_in, down_in, attn_in, small_in, gate, up, down, qkv, out, router, again, mgain):
    slice_h = gate_in.shape[2] // 2
    for src, dst in ((gate_in, gate), (up_in, up)):
        for j in range(2):
            cols = slice(j * slice_h, (j + 1) * slice_h)
            dst[0, j] = jnp.concatenate([src[z, :, cols].astype(F32) for z in range(nz)], 1)
    down[0, 0] = down_in[...].astype(F32)
    shard, split = qkv.shape[1], qkv.shape[2]
    qkv[0] = attn_in[0:shard, 0:split].astype(F32)
    out[0] = attn_in[0:shard, split:].astype(F32)
    rows, width = small_in.shape
    base = (lax.axis_index("expert") * nz + lax.axis_index("dp")) * shard
    at = lax.broadcasted_iota(jnp.int32, (width, 128), 0)
    lane = lax.broadcasted_iota(jnp.int32, (width, 128), 1)
    pick = jnp.where(at == base + lane, 1.0, 0.0).astype(F32)
    got = jnp.dot(small_in[...], pick, precision=lax.Precision.HIGHEST, preferred_element_type=F32)
    again[...] = got[ROUTER_ROWS : ROUTER_ROWS + 1, 0:shard]
    mgain[...] = got[ROUTER_ROWS + 1 : ROUTER_ROWS + 2, 0:shard]
    turned = jnp.transpose(jnp.concatenate([got, jnp.zeros((128 - rows, 128), F32)], 0))
    router[0] = turned[0:shard, 0:experts]


VMEM = pl.BlockSpec(memory_space=pltpu.VMEM)
ANY = pl.BlockSpec(memory_space=pl.ANY)
DMA = pltpu.SemaphoreType.DMA


def per_device(
    ne, nz, sections,
    layer_input, cotangent, segments, routes, attn_gain, w_qkv, w_out, moe_gain, w_router, w_gate, w_up, w_down,
):
    ny = ne // 2
    micro, _, tokens, width = layer_input.shape
    total_experts = w_router.shape[2]
    hidden = w_gate.shape[3]
    owners = ("expert", "dp")
    shard = w_qkv.shape[1]
    place_e, place_d = lax.axis_index("expert"), lax.axis_index("dp")
    small = jnp.concatenate(
        [
            w_router[0],
            jnp.zeros((shard, ROUTER_ROWS - total_experts), BF16),
            attn_gain[0][:, None],
            moe_gain[0][:, None],
            jnp.zeros((shard, 128 - ROUTER_ROWS - 2), BF16),
        ],
        1,
    ).astype(F32)
    own_routes = jnp.transpose(routes[0, :, 0], (0, 2, 1))
    cos, sin = rotary_tables(tokens)
    segs = segments[:, 0]
    segc, segr = segs[:, :, None], segs[:, None, :]
    x = layer_input[:, 0]
    cot = cotangent[:, 0]
    wg, wu, wd = w_gate[0], w_up[0], w_down[0]
    qkv_width = w_qkv.shape[2]
    slice_h = hidden // nz
    half = 2 * slice_h

    def shape(*dims, dtype=BF16):
        return jax.ShapeDtypeStruct(dims, dtype)

    grid_sems = [DMA((5, 2, nz, ny)) for _ in range(4)]
    small, routes_all, wqkv, wout, slices = pl.pallas_call(
        functools.partial(gather_kernel, ny, nz),
        out_shape=(
            shape(SMALL_ROWS, width),
            shape(ne, nz, *own_routes.shape, dtype=jnp.int32),
            shape(ne, nz, shard, qkv_width),
            shape(ne, nz, shard, width),
            shape(2, hidden, width),
        ),
        in_specs=[VMEM] + [ANY] * 5,
        out_specs=tuple([VMEM] + [ANY] * 4),
        scratch_shapes=[
            pltpu.VMEM((ne, nz, shard, 128), F32),
            pltpu.VMEM(wg.shape, BF16),
            pltpu.VMEM(wu.shape, BF16),
            pltpu.VMEM((2, 2, hidden, width), BF16),
            DMA((2,)), DMA((5,)),
        ]
        + grid_sems
        + [DMA((5, ny, 2, nz)), DMA((5, ny, 2, nz)), DMA((2, nz))],
        compiler_params=pltpu.CompilerParams(
            collective_id=3, has_side_effects=True, vmem_limit_bytes=60 * 2**20
        ),
        name="gather_weights",
    )(small, own_routes, w_qkv[0], w_out[0], wg, wu)
    wqkv = wqkv.reshape(width, qkv_width)
    wout = wout.reshape(width, width)
    routes_all = routes_all.reshape((ne * nz,) + own_routes.shape)
    weights = [pltpu.VMEM(w.shape, BF16) for w in (wqkv, wout, wg, wu, wd)]
    hop_sems = [DMA((micro, HOP_CHUNKS)) for _ in range(2)]
    block = width // ne

    def gather_sems(count):
        return [DMA((count, ny, 2, nz))] * 2 + [DMA((count, 2, nz, ny))] * 2 + [DMA((count, ny))]

    def returns(wide):
        return [
            pltpu.VMEM((tokens, wide), BF16),
            pltpu.VMEM((max(1, ny - 1), tokens, wide), BF16),
            pltpu.VMEM((max(1, ny - 1), tokens, wide), BF16),
            pltpu.VMEM((tokens, wide), BF16),
            pltpu.VMEM((max(1, ny - 1), tokens, wide), BF16),
            pltpu.VMEM((max(1, ny - 1), tokens, wide), BF16),
        ]

    out, hin, h1, qkv, obb, xm, gates, zf, obp, partner = pl.pallas_call(
        functools.partial(forward_kernel, ny, nz, sections),
        out_shape=(
            shape(micro, tokens, width),
            shape(micro, tokens, width),
            shape(micro, tokens, width, dtype=F32),
            shape(micro, tokens, qkv_width),
            shape(micro, ne, tokens, block),
            shape(micro, ny, 2, tokens, width),
            shape(micro, ny, 2, ROUTER_ROWS, tokens, dtype=F32),
            shape(1, nz, ny, tokens, width),
            shape(micro, ny, tokens, block),
            shape(3, hidden, width),
        ),
        in_specs=[VMEM] * 7 + [ANY] * 7,
        out_specs=tuple([VMEM] * 7 + [ANY] * 3),
        scratch_shapes=weights
        + [
            pltpu.VMEM((tokens, width), BF16),
            pltpu.VMEM((2, 2 * tokens, hidden), BF16),
            pltpu.VMEM((tokens, width), F32),
            pltpu.VMEM((tokens // FORWARD_CHUNKS, width), F32),
        ]
        + returns(width)
        + [DMA((5,))]
        + gather_sems(1)
        + [DMA((ny,)), DMA((ny,))]
        + hop_sems
        + [DMA((micro, ny))] * 2
        + [DMA((nz + 2,))] * 2
        + sem_shapes(micro, ny, FORWARD_CHUNKS),
        compiler_params=pltpu.CompilerParams(
            collective_id=0, has_side_effects=True, vmem_limit_bytes=60 * 2**20
        ),
        name="layers_forward",
    )(x, segc, segr, routes_all, small, cos, sin, cot, slices, wqkv, wout, wg, wu, wd)

    wide = width + 128
    every = (2, ny, 2, tokens, hidden)
    gin, grows, xab, dqkv, dattn, gsmall, zb, xap, dqp, dtp = pl.pallas_call(
        functools.partial(backward_kernel, ny, nz, sections),
        out_shape=(
            shape(micro, tokens, width),
            shape(micro, ny, 2, tokens, width),
            shape(micro, ne, tokens, block),
            shape(micro, tokens, qkv_width),
            shape(micro, tokens, width),
            shape(SMALL_ROWS, width, dtype=F32),
            shape(2 * micro, nz, ny, tokens, width),
            shape(micro, ny, tokens, block),
            shape(micro, tokens, qkv_width),
            shape(micro, tokens, width),
        ),
        in_specs=[VMEM] * 10 + [ANY] * 6,
        out_specs=tuple([VMEM] * 6 + [ANY] * 4),
        scratch_shapes=weights
        + [
            pltpu.VMEM((ny, 2, tokens, width), BF16),
            pltpu.VMEM(every, BF16),
            pltpu.VMEM(every, BF16),
            pltpu.VMEM(every, BF16),
            pltpu.VMEM((2, 2 * tokens, hidden), BF16),
            pltpu.VMEM((2, 2 * tokens, hidden), BF16),
            pltpu.VMEM((tokens, wide), F32),
            pltpu.VMEM((tokens // BACKWARD_CHUNKS, wide), F32),
            pltpu.VMEM((tokens, width), F32),
            pltpu.VMEM((tokens, width), F32),
        ]
        + returns(wide)
        + [DMA((5,)), DMA]
        + gather_sems(2 * micro)
        + hop_sems
        + [DMA((micro, ny + 2))] * 2
        + sem_shapes(micro, ny, BACKWARD_CHUNKS * HOP_CHUNKS),
        compiler_params=pltpu.CompilerParams(
            collective_id=1, has_side_effects=True, vmem_limit_bytes=62 * 2**20
        ),
        name="layers_backward",
    )(cot, segc, segr, small, cos, sin, hin, h1, qkv, gates, xm, wqkv, wout, wg, wu, wd)

    span_z = max(1, min(nz, 512 // (ny * tokens)))
    rows = span_z * ny * tokens
    padded = -(-shard // 16) * 16
    attn_width = qkv_width + width
    part = width // nz
    small_shape = (SMALL_ROWS, width)
    gate_g, up_g, down_g, attn_g, small_g, _ = pl.pallas_call(
        functools.partial(tail_kernel, ny, nz, sections, span_z),
        out_shape=(
            shape(nz, part, half),
            shape(nz, part, half),
            shape(half, width),
            shape(padded, attn_width),
            shape(*small_shape, dtype=F32),
            shape(*zb.shape),
        ),
        in_specs=[VMEM] * 3 + [ANY] * 13,
        out_specs=tuple([ANY] * 4 + [VMEM] + [ANY]),
        input_output_aliases={4: 5},
        scratch_shapes=[
            pltpu.VMEM((3, 2 * hidden, width), BF16),
            pltpu.VMEM((span_z, ny, tokens, width), BF16),
            pltpu.VMEM((span_z, ny, tokens, width), BF16),
            pltpu.VMEM((rows, 2 * hidden), BF16),
            pltpu.VMEM((rows, 2 * hidden), BF16),
            pltpu.VMEM((rows, 2 * half), BF16),
            pltpu.VMEM((2 * part, 2 * hidden), F32),
            pltpu.VMEM((2 * part, 2 * hidden), F32),
            pltpu.VMEM((2 * half, width), F32),
            pltpu.VMEM((2, 2, nz // 2, part, half), BF16),
            pltpu.VMEM((2, 2, nz // 2, part, half), BF16),
            pltpu.VMEM((half, width), BF16),
            pltpu.VMEM((half, width), BF16),
            pltpu.VMEM((ny, 2, micro, tokens, block), BF16),
            pltpu.VMEM((ny, 2, micro, tokens, block), BF16),
            pltpu.VMEM((2, micro, tokens, qkv_width), BF16),
            pltpu.VMEM((2, micro, tokens, width), BF16),
            pltpu.VMEM((nz, padded, attn_width), BF16),
            pltpu.VMEM((max(1, ny - 1), nz, padded, attn_width), BF16),
            pltpu.VMEM((max(1, ny - 1), nz, padded, attn_width), BF16),
            pltpu.VMEM((max(1, nz - 1), padded, attn_width), BF16),
            pltpu.VMEM((2,) + small_shape, F32),
            pltpu.VMEM((max(1, ny - 1),) + small_shape, F32),
            pltpu.VMEM((max(1, nz - 1),) + small_shape, F32),
            DMA((2 * nz,)), DMA((2,)),
            DMA((4 * ny * micro + 4,)),
            DMA((ny + nz,)), DMA((ny + nz,)),
            DMA((3, nz)), DMA((3, nz)),
            DMA((2, nz + 1)), DMA((2, nz)),
            DMA((ny, nz)), DMA((ny, nz)),
            DMA((1, nz)), DMA((1, nz)),
        ]
        + gather_sems(2 * micro),
        compiler_params=pltpu.CompilerParams(
            collective_id=2, has_side_effects=True, vmem_limit_bytes=63 * 2**20
        ),
        name="weight_gradients",
    )(routes_all, small, gsmall, zf, zb, slices, partner, wd, xab, obb, dqkv, dattn, xap, obp, dqp, dtp)

    steps = 2
    finals = pl.pallas_call(
        functools.partial(finish_kernel, nz, total_experts),
        grid=(steps,),
        out_shape=(
            shape(1, 2, part, hidden, dtype=F32),
            shape(1, 2, part, hidden, dtype=F32),
            shape(1, 2, slice_h, width, dtype=F32),
            shape(1, shard, qkv_width, dtype=F32),
            shape(1, shard, width, dtype=F32),
            shape(1, shard, total_experts, dtype=F32),
            shape(1, shard, dtype=F32),
            shape(1, shard, dtype=F32),
        ),
        in_specs=[
            pl.BlockSpec((nz, part // steps, half), lambda i: (0, i, 0)),
            pl.BlockSpec((nz, part // steps, half), lambda i: (0, i, 0)),
            pl.BlockSpec((slice_h, width), lambda i: (i, 0)),
            pl.BlockSpec((padded, attn_width), lambda i: (0, 0)),
            pl.BlockSpec(small_shape, lambda i: (0, 0)),
        ],
        out_specs=(
            pl.BlockSpec((1, 2, part // steps, hidden), lambda i: (0, 0, i, 0)),
            pl.BlockSpec((1, 2, part // steps, hidden), lambda i: (0, 0, i, 0)),
            pl.BlockSpec((1, 1, slice_h, width), lambda i: (0, i, 0, 0)),
            pl.BlockSpec((1, shard, qkv_width), lambda i: (0, 0, 0)),
            pl.BlockSpec((1, shard, width), lambda i: (0, 0, 0)),
            pl.BlockSpec((1, shard, total_experts), lambda i: (0, 0, 0)),
            pl.BlockSpec((1, shard), lambda i: (0, 0)),
            pl.BlockSpec((1, shard), lambda i: (0, 0)),
        ),
        compiler_params=pltpu.CompilerParams(vmem_limit_bytes=60 * 2**20),
        name="finish_gradients",
    )(gate_g, up_g, down_g, attn_g, small_g)
    grad_gate, grad_up, grad_down, grad_qkv, grad_out, grad_router, grad_again, grad_mgain = finals
    return (
        out[None, :, None],
        gin[None, :, None],
        grad_again,
        grad_qkv,
        grad_out,
        grad_mgain,
        grad_router,
        grad_gate,
        grad_up,
        grad_down,
    )


def solution(mesh):
    owners = ("expert", "dp")
    return jax.shard_map(
        functools.partial(per_device, mesh.shape["expert"], mesh.shape["dp"], mesh.shape["section"]),
        mesh=mesh,
        in_specs=(
            P(None, owners, None, None),
            P(None, owners, None, None),
            P(None, owners, None),
            P("section", None, owners, None, None),
            P("section", owners),
            P("section", owners, None),
            P("section", owners, None),
            P("section", owners),
            P("section", owners, None),
            P("section", "expert", None, None),
            P("section", "expert", None, None),
            P("section", "expert", None, None),
        ),
        out_specs=(
            P("section", None, owners, None, None),
            P("section", None, owners, None, None),
            P("section", owners),
            P("section", owners, None),
            P("section", owners, None),
            P("section", owners),
            P("section", owners, None),
            P("section", "expert", "dp", None),
            P("section", "expert", "dp", None),
            P("section", "expert", "dp", None),
        ),
        check_vma=False,
    )
```

```python
import functools

import jax
import jax.numpy as jnp
import numpy as np
from jax import lax
from jax.experimental import pallas as pl
from jax.experimental.pallas import tpu as pltpu
from jax.sharding import PartitionSpec as P

HEAD = 128
QUERY_HEADS = 12
KEY_VALUE_HEADS = 2
GROUP = QUERY_HEADS // KEY_VALUE_HEADS
EPS = 1e-06
THETA = 1000000.0
NEGATIVE = -1e30
SCALE = HEAD ** (-0.5)
ROUTER_ROWS = 16
SMALL_ROWS = 32
FORWARD_CHUNKS = 2
BACKWARD_CHUNKS = 1
HOP_CHUNKS = 2
MESH = pl.DeviceIdType.MESH
F32 = jnp.float32
BF16 = jnp.bfloat16
GELU_C = float(np.sqrt(2.0 / np.pi))
GELU_A = 0.044715


def dot(a, b):
    return jnp.dot(a, b, preferred_element_type=F32)


def dot_nt(a, b):
    return lax.dot_general(a, b, (((1,), (1,)), ((), ())), preferred_element_type=F32)


def dot_tn(a, b):
    return lax.dot_general(a, b, (((0,), (0,)), ((), ())), preferred_element_type=F32)


def rotary_tables(tokens):
    places = np.arange(tokens, dtype=np.float64)
    inverse = THETA ** (-2.0 * np.arange(HEAD // 2, dtype=np.float64) / HEAD)
    angles = places[:, None] * inverse[None, :]
    cosine, sine = np.cos(angles), np.sin(angles)
    return (
        jnp.asarray(np.concatenate([cosine, cosine], 1), F32),
        jnp.asarray(np.concatenate([-sine, sine], 1), F32),
    )


def mask_bias(row):
    tokens = row.shape[1]
    row = jnp.broadcast_to(row.astype(F32), (tokens, tokens))
    col = jnp.transpose(row)
    ti = lax.broadcasted_iota(jnp.int32, (tokens, tokens), 0)
    ui = lax.broadcasted_iota(jnp.int32, (tokens, tokens), 1)
    return jnp.where((col == row) & (ui <= ti), 0.0, NEGATIVE).astype(F32)


def heads_of(value, first, count):
    return jnp.concatenate(
        [value[:, (first + i) * HEAD : (first + i + 1) * HEAD] for i in range(count)], 0
    )


def attention_shares(q6, k, bias6):
    scores = dot_nt(q6, k) * SCALE + bias6
    top = jnp.max(scores, -1, keepdims=True)
    raised = jnp.exp(scores - top)
    return raised / jnp.sum(raised, -1, keepdims=True)


class Place:
    def __init__(self, ny, nz):
        self.ny = ny
        self.nz = nz
        self.s = lax.axis_index("section")
        self.e = lax.axis_index("expert")
        self.d = lax.axis_index("dp")
        self.y = lax.div(self.e, 2)
        self.c = lax.rem(self.e, 2)
        self.core = (self.s, self.y * 2 + 1 - self.c, self.d)
        self.x = (1 - self.s, self.e, self.d)

    def ahead(self, r):
        return (self.s, lax.rem(self.y + r, self.ny) * 2 + self.c, self.d)

    def behind(self, r):
        return (self.s, lax.rem(self.y + self.ny - r, self.ny) * 2 + self.c, self.d)

    def pack(self, r, other):
        core = 1 - self.c if other else self.c
        return lax.rem(self.y + r, self.ny) * 2 + core

    def z_of(self, k):
        return lax.rem(self.d + k, self.nz)

    def z_ahead(self, k):
        return (self.s, self.e, self.z_of(k))

    def z_behind(self, k):
        return (self.s, self.e, self.z_of(self.nz - k))

    def greet(self, with_x=True):
        barrier = pltpu.get_barrier_semaphore()
        partners = [self.core] + ([self.x] if with_x else [])
        partners += [self.ahead(r) for r in range(1, self.ny)]
        partners += [self.z_ahead(k) for k in range(1, self.nz)]
        for partner in partners:
            pl.semaphore_signal(barrier, inc=1, device_id=partner, device_id_type=MESH)
        pl.semaphore_wait(barrier, len(partners))


def remote(src, dst, send, recv, device):
    return pltpu.make_async_remote_copy(
        src_ref=src, dst_ref=dst, send_sem=send, recv_sem=recv, device_id=device, device_id_type=MESH
    )


class Line:
    def __init__(self, place, slot, send, recv):
        self.place, self.slot, self.send, self.recv = place, slot, send, recv

    def origin(self, way, h):
        return self.place.d - h if way == 0 else self.place.d + h

    def comes(self, way, h):
        return self.place.d >= h if way == 0 else self.place.d + h < self.place.nz

    def leaves(self, way, h):
        d, nz = self.place.d, self.place.nz
        return (d + 1 < nz) & (d >= h - 1) if way == 0 else (d >= 1) & (d + h - 1 < nz)

    def out(self, way, h, src=None):
        g = self.place
        at = self.slot(self.origin(way, h - 1))
        next_door = (g.s, g.e, g.d + 1 if way == 0 else g.d - 1)
        return remote(at if src is None else src, at, self.send.at[way, h], self.recv.at[way, h], next_door)

    def came(self, way, h):
        g = self.place
        at = self.slot(self.origin(way, h))
        return remote(at, at, self.send.at[way, h], self.recv.at[way, h], g.core)

    def start(self, src):
        for way in range(2):
            @pl.when(self.leaves(way, 1))
            def _():
                self.out(way, 1, src).start()

    def go_on(self, h):
        for way in range(2):
            @pl.when(self.leaves(way, h))
            def _():
                self.out(way, h).start()

    def step(self, h, then=None, forward=True):
        for way in range(2):
            @pl.when(self.comes(way, h))
            def _():
                self.came(way, h).wait_recv()
                if forward and h + 1 < self.place.nz:
                    @pl.when(self.leaves(way, h + 1))
                    def _():
                        self.out(way, h + 1).start()
                if then is not None:
                    then(way, h)

    def finish(self, hops=None):
        for way in range(2):
            for h in range(1, self.place.nz) if hops is None else hops:
                @pl.when(self.leaves(way, h))
                def _():
                    self.out(way, h).wait_send()


class Gather:
    def __init__(self, place, buf, send, recv, ysend, yrecv, local):
        self.place, self.buf, self.local = place, buf, local
        self.send, self.recv, self.ysend, self.yrecv = send, recv, ysend, yrecv
        self.tokens = buf.shape[3]
        self.cut = self.tokens // 2

    def rows(self, r, whole):
        return pl.ds(0, self.tokens if whole or r == 0 else self.cut)

    def line(self, i, r, whole=True):
        rows = self.rows(r, whole)
        return Line(self.place, lambda zz: self.buf.at[i, zz, r, rows], self.send.at[i, r], self.recv.at[i, r])

    def near(self, i, r, src):
        return pltpu.make_async_copy(src, self.buf.at[i, self.place.d, r], self.local.at[i, r])

    def across(self, i, way, h, r):
        at = self.line(i, 0).origin(way, h)
        rest = pl.ds(self.cut, self.tokens - self.cut)
        return remote(
            self.buf.at[i, at, 0, rest], self.buf.at[i, at, r, rest],
            self.ysend.at[i, way, h, r], self.yrecv.at[i, way, h, r], self.place.behind(r),
        )

    def start(self, i, r, src, keep=True, whole=True):
        if keep:
            self.near(i, r, src).start()
        self.line(i, r, whole).start(src.at[self.rows(r, whole)])

    def step(self, i, h, whole=True, forward=True):
        for r in range(self.place.ny):
            self.line(i, r, whole).step(h, forward=forward)

    def go_on(self, i, h, whole=True):
        for r in range(self.place.ny):
            self.line(i, r, whole).go_on(h)

    def passes(self, i, hops):
        line = self.line(i, 0)
        for h in hops:
            for way in range(2):
                @pl.when(line.comes(way, h))
                def _():
                    for r in range(1, self.place.ny):
                        self.across(i, way, h, r).start()

    def finish(self, i, kept, whole=True, hops=None):
        for r in kept:
            self.near(i, r, self.buf.at[i, self.place.d, r]).wait()
        for r in range(self.place.ny):
            self.line(i, r, whole).finish(hops)
        if not whole:
            self.finish_passes(i, hops)

    def finish_passes(self, i, hops=None):
        g = self.place
        line = self.line(i, 0)
        for h in range(1, g.nz) if hops is None else hops:
            for way in range(2):
                @pl.when(line.comes(way, h))
                def _():
                    for r in range(1, g.ny):
                        self.across(i, way, h, r).wait()


class Exchange:
    def __init__(self, place, chunks, rows_ref, retl, retc, rety, sendl, sendc, sendy, sems, parts=1):
        self.place, self.chunks, self.parts = place, chunks, parts
        self.rows_ref = rows_ref
        self.retl, self.retc, self.rety = retl, retc, rety
        self.sendl, self.sendc, self.sendy = sendl, sendc, sendy
        self.sems = sems
        self.tokens = rows_ref.shape[2]
        self.span = self.tokens // chunks

    def rows(self, q):
        return pl.ds(q * self.span, self.span)

    def core_own(self):
        g = self.place
        return remote(
            self.rows_ref.at[0, 0], self.rows_ref.at[0, 1], self.sems.cs.at[0, 0], self.sems.cr.at[0, 0], g.core
        )

    def y_part(self, r, i):
        g = self.place
        size = self.span // self.parts
        rows = pl.ds(i * size, size)
        return remote(
            self.rows_ref.at[0, 0, rows],
            self.rows_ref.at[r, 0, rows],
            self.sems.ys.at[r, i],
            self.sems.yr.at[r, i],
            g.behind(r),
        )

    def y_parts(self, r, q):
        return [self.y_part(r, q * self.parts + p) for p in range(self.parts)]

    def forward(self, r, q):
        g = self.place
        return remote(
            self.rows_ref.at[r, 0, self.rows(q)],
            self.rows_ref.at[r, 1, self.rows(q)],
            self.sems.cs.at[r, q],
            self.sems.cr.at[r, q],
            g.core,
        )

    def back_local(self):
        return remote(self.sendl, self.retl, self.sems.bs.at[0, 0], self.sems.br.at[0, 0], self.place.core)

    def back_core(self, r, q):
        return remote(
            self.sendc.at[r - 1, self.rows(q)],
            self.retc.at[r - 1, self.rows(q)],
            self.sems.bs.at[r, q],
            self.sems.br.at[r, q],
            self.place.core,
        )

    def back_y(self, r, q):
        g = self.place
        return remote(
            self.sendy.at[r - 1, self.rows(q)],
            self.rety.at[g.ny - r - 1, self.rows(q)],
            self.sems.zs.at[r, q],
            self.sems.zr.at[g.ny - r, q],
            g.ahead(r),
        )

    def back_y_arrival(self, r, q):
        g = self.place
        return remote(
            self.sendy.at[r - 1, self.rows(q)],
            self.rety.at[r - 1, self.rows(q)],
            self.sems.zs.at[r, q],
            self.sems.zr.at[r, q],
            g.ahead(r),
        )

    def send_own(self):
        for i in range(self.chunks * self.parts):
            self.send_part(i)
        self.core_own().start()

    def send_part(self, i):
        for r in range(1, self.place.ny):
            self.y_part(r, i).start()

    def run(self, local_block, remote_block, complete, early=None):
        ny = self.place.ny
        items = [(r, q) for q in range(self.chunks) for r in range(1, ny)]
        def arrive(r, q):
            for part in self.y_parts(r, q):
                part.wait_recv()
            self.forward(r, q).start()
            if q == self.chunks - 1:
                complete(r)

        if items and early is not None:
            @pl.when(early)
            def _():
                arrive(*items[0])

        self.core_own().wait_recv()
        local_block()
        self.back_local().start()
        if items and early is None:
            arrive(*items[0])
        if items and early is not None:
            @pl.when(jnp.logical_not(early))
            def _():
                arrive(*items[0])

        for i, (r, q) in enumerate(items):
            self.forward(r, q).wait_recv()
            own = remote_block(r, q)
            self.back_core(r, q).start()
            if i + 1 < len(items):
                arrive(*items[i + 1])
            self.back_core(r, q).wait_recv()
            here = self.rows(q)
            self.sendy[r - 1, here, :] = (own() + self.retc[r - 1, here, :].astype(F32)).astype(BF16)
            self.back_y(r, q).start()
        self.back_local().wait_recv()

    def arrived(self, q):
        for r in range(1, self.place.ny):
            self.back_y_arrival(r, q).wait_recv()

    def finish(self):
        ny = self.place.ny
        self.core_own().wait_send()
        self.back_local().wait_send()
        for q in range(self.chunks):
            for r in range(1, ny):
                for part in self.y_parts(r, q):
                    part.wait_send()
                self.forward(r, q).wait_send()
                self.back_core(r, q).wait_send()
                self.back_y(r, q).wait_send()


class Sems:
    def __init__(self, refs, m):
        self.cs, self.cr, self.ys, self.yr, self.bs, self.br, self.zs, self.zr = [ref.at[m] for ref in refs]


def sem_shapes(micro, ny, chunks):
    return [pltpu.SemaphoreType.DMA((micro, ny, chunks)) for _ in range(8)]


def chosen_gates(logits_t, route):
    experts = lax.broadcasted_iota(jnp.int32, logits_t.shape, 0)
    chosen = route[0:1, :] == experts
    for k in range(1, route.shape[0]):
        chosen = chosen | (route[k : k + 1, :] == experts)
    masked = jnp.where(chosen, logits_t, NEGATIVE)
    raised = jnp.where(chosen, jnp.exp(masked - jnp.max(masked, 0, keepdims=True)), 0.0)
    return raised / jnp.sum(raised, 0, keepdims=True)


def gate_lanes(gates_t, expert):
    rows = lax.broadcasted_iota(jnp.int32, gates_t.shape, 0)
    one = jnp.sum(jnp.where(rows == expert, gates_t, 0.0), 0, keepdims=True)
    return jnp.transpose(jnp.broadcast_to(one, (128, one.shape[1])))


def widen(lanes, width):
    return jnp.concatenate([lanes] * (width // 128), 1)


def gather_kernel(
    ny, nz,
    small_ref, route_h, wqkv_h, wout_h, wg_h, wu_h,
    small_t, route_o, wqkv_o, wout_o, slices_o,
    small_s, wg, wu, turned,
    lsem, own_sem, cs, cr, ys, yr, zs, zr, sls,
):
    g = Place(ny, nz)
    hidden, width = turned.shape[2], turned.shape[3]
    slice_h = hidden // nz
    loads = [pltpu.make_async_copy(src, dst, lsem.at[i]) for i, (src, dst) in enumerate(((wg_h, wg), (wu_h, wu)))]
    for copy in loads:
        copy.start()
    g.greet(with_x=False)
    split = width * 2 // 3
    arrays = (
        (small_ref, lambda e, zz: small_s.at[e, zz]),
        (route_h, lambda e, zz: route_o.at[e, zz]),
        (wqkv_h, lambda e, zz: wqkv_o.at[e, zz]),
        (wout_h.at[:, 0:split], lambda e, zz: wout_o.at[e, zz, :, 0:split]),
        (wout_h.at[:, split:width], lambda e, zz: wout_o.at[e, zz, :, split:width]),
    )
    count = len(arrays)
    turned_way = count - 1
    plain = range(turned_way)

    def near(n):
        src, slot = arrays[n]
        return pltpu.make_async_copy(src, slot(g.e, g.d), own_sem.at[n])

    lines = [
        Line(g, lambda zz, slot=slot: slot(g.e, zz), zs.at[n, 0], zr.at[n, 0]) for n, (_, slot) in enumerate(arrays)
    ]
    turned_lines = [
        Line(g, lambda zz, r=r: arrays[turned_way][1](g.pack(r, False), zz), zs.at[turned_way, r], zr.at[turned_way, r])
        for r in range(ny)
    ]

    def along_y(n, way, h, r):
        src, slot = arrays[n]
        at = slot(g.e, lines[n].origin(way, h))
        return remote(src if h == 0 else at, at, ys.at[n, way, h, r], yr.at[n, way, h, r], g.behind(r))

    def to_core(n, way, h, r):
        src, slot = arrays[n]
        at = slot(g.pack(r, False), lines[n].origin(way, h))
        own = h == 0 and r == 0
        return remote(src if own else at, at, cs.at[n, way, h, r], cr.at[n, way, h, r], g.core)

    for n in [turned_way] + list(plain):
        for r in range(1, ny):
            along_y(n, 0, 0, r).start()
        lines[n].start(arrays[n][0])
        near(n).start()
        to_core(n, 0, 0, 0).start()

    def got_z(n, h):
        if n == turned_way:
            for r, line in enumerate(turned_lines):
                line.step(h, lambda way, h, r=r: to_core(n, way, h, r).start())
            return

        def then(way, h):
            for r in range(1, ny):
                along_y(n, way, h, r).start()
            to_core(n, way, h, 0).start()

        lines[n].step(h, then)

    def got_y(n, h):
        for way in range(1 if h == 0 else 2):
            def pass_on():
                for r in range(1, ny):
                    along_y(n, way, h, r).wait_recv()
                    to_core(n, way, h, r).start()
                    if n == turned_way:
                        turned_lines[r].start(arrays[n][1](g.pack(r, False), g.d))

            if h == 0:
                pass_on()
            else:
                pl.when(lines[n].comes(way, h))(pass_on)

    parts = []
    for i in range(2):
        for t in range(nz // 2):
            here = pl.ds(pl.multiple_of(g.z_of(2 * t) * slice_h, slice_h), slice_h)
            for j in range(2):
                n = 2 * t + j
                to = slice(n * slice_h, (n + 1) * slice_h)
                parts.append(pltpu.make_async_copy(turned.at[i, j, here], slices_o.at[i, to], sls.at[i, n]))

    def turn(i, j, n):
        src = (wg, wu)[i]
        if j == 0 and n == 0:
            loads[i].wait()
        cols = slice(n * 256, (n + 1) * 256)
        turned[i, j, cols, :] = jnp.transpose(src[j, :, cols])

    turns = [(i, j, n) for i in range(2) for j in range(2) for n in range(hidden // 256)]

    z_items = [(n, h) for h in range(1, nz) for n in range(count)]
    y_items = [(n, h) for h in range(nz) for n in plain]
    done = 0
    for i, item in enumerate(z_items):
        if item == (2, 1):
            got_y(turned_way, 0)
        got_z(*item)
        if (i % 2 == 1 or i >= count) and item[0] != turned_way:
            got_y(*y_items[done])
            done += 1
        for piece in turns[:2]:
            turn(*piece)
        turns = turns[2:]
        if not turns and parts:
            for copy in parts:
                copy.start()
            started, parts = parts, []
    for item in y_items[done:]:
        got_y(*item)

    def each(act):
        for n in range(count):
            for h in range(nz):
                for way in range(1 if h == 0 else 2):
                    if h == 0:
                        act(n, way, h)
                    else:
                        pl.when(lines[n].comes(way, h))(lambda: act(n, way, h))

    def arrived(n, way, h):
        for r in range(ny):
            to_core(n, way, h, r).wait_recv()

    def sent(n, way, h):
        for r in range(ny):
            to_core(n, way, h, r).wait_send()
            if r and (h == 0 or n != turned_way):
                along_y(n, way, h, r).wait_send()

    each(arrived)
    for n in range(count):
        near(n).wait()
    gathered = small_s[...].reshape(width, small_s.shape[3])
    small_t[...] = jnp.transpose(gathered)[0:SMALL_ROWS].astype(BF16)
    each(sent)
    for line in lines[:turned_way] + turned_lines:
        line.finish()
    for copy in started:
        copy.wait()


def forward_kernel(
    ny, nz, sections,
    x_ref, segr_ref, route_ref, small_ref, cos_ref, sin_ref,
    cot_h, slices_h, wqkv_h, wout_h, wg_h, wu_h, wd_h,
    out_ref, hin_ref, h1_ref, qkv_ref, obb_ref, xm_ref, gates_ref, zf_h, obp_h, share_h,
    wqkv, wout, wg, wu, wd, ob_s, hid, accl, accr, retl, retc, rety, sendl, sendc, sendy,
    wsem, zs, zr, zys, zyr, zl, gs, gr, xs, xr, ps, pr, hs, hr, *sem_refs,
):
    micro, tokens, width = x_ref.shape
    hidden = wg.shape[2]
    span = tokens // FORWARD_CHUNKS
    loads = [
        pltpu.make_async_copy(src, dst, wsem.at[i])
        for i, (src, dst) in enumerate([(wqkv_h, wqkv), (wout_h, wout), (wg_h, wg), (wu_h, wu), (wd_h, wd)])
    ]
    for load in loads:
        load.start()
    g = Place(ny, nz)
    g.greet()
    gain_a = small_ref[ROUTER_ROWS : ROUTER_ROWS + 1, :].astype(F32)
    gain_m = small_ref[ROUTER_ROWS + 1 : ROUTER_ROWS + 2, :].astype(F32)
    cos, sin = cos_ref[...], sin_ref[...]
    gather = Gather(g, zf_h, zs, zr, zys, zyr, zl)
    every = range(ny)
    first, last = g.s == 0, g.s == sections - 1

    slice_h = hidden // nz
    shares = [remote(slices_h.at[i], share_h.at[i], hs.at[i], hr.at[i], g.core) for i in range(2)]
    for t in range(nz // 2):
        here = pl.ds(pl.multiple_of(g.z_of(2 * t) * slice_h, slice_h), slice_h)
        for j in range(2):
            n = 2 * t + j
            to = slice(n * slice_h, (n + 1) * slice_h)
            shares.append(remote(wd_h.at[j, here], share_h.at[2, to], hs.at[2 + n], hr.at[2 + n], g.core))

    def cot_copy(r):
        return remote(cot_h.at[0], zf_h.at[0, g.d, r], gs.at[r], gr.at[r], g.behind(r))

    @pl.when(last)
    def _():
        for r in range(1, ny):
            cot_copy(r).start()
        gather.start(0, 0, cot_h.at[0])
        for r in range(1, ny):
            cot_copy(r).wait_recv()
            gather.start(0, r, zf_h.at[0, g.d, r], keep=False)
        for copy in shares:
            copy.start()
        gather.step(0, 1)

    def hop(m, q):
        here = pl.ds(q * (tokens // HOP_CHUNKS), tokens // HOP_CHUNKS)
        return remote(out_ref.at[m, here], hin_ref.at[m, here], xs.at[m, q], xr.at[m, q], g.x)

    def experts(rows, lanes, keep):
        count = rows.shape[0]
        for j in range(2):
            for n in range(hidden // 256):
                cols = slice(n * 256, (n + 1) * 256)
                a = dot(rows, wg[j, :, cols])
                b = dot(rows, wu[j, :, cols])
                act = 0.5 * a * (1.0 + jnp.tanh(GELU_C * (a + GELU_A * a * a * a)))
                hid[j, 0:count, cols] = (act * b).astype(BF16)
        for n in range(width // 512):
            cols = slice(n * 512, (n + 1) * 512)
            total = None
            for j in range(2):
                eo = dot(hid[j, 0:count, :], wd[j, :, cols]).astype(BF16).astype(F32)
                term = widen(lanes[j], 512) * eo
                total = term if total is None else total + term
            keep(cols, total)

    def partner(m, yy):
        return remote(obb_ref.at[m, yy * 2 + 1 - g.c], obp_h.at[m, yy], ps.at[m, yy], pr.at[m, yy], g.core)

    def body(m, carry):
        @pl.when(g.s == 0)
        def _():
            hin_ref[m] = x_ref[m]

        @pl.when(g.s > 0)
        def _():
            for q in range(HOP_CHUNKS):
                hop(m, q).wait_recv()

        h = hin_ref[m].astype(F32)
        xa = (h * lax.rsqrt(jnp.mean(h * h, -1, keepdims=True) + EPS) * gain_a).astype(BF16)

        @pl.when(m == 0)
        def _():
            loads[0].wait()

        turned = QUERY_HEADS + KEY_VALUE_HEADS
        for i in range(wqkv.shape[1] // 256):
            mixed = dot(xa, wqkv[:, i * 256 : (i + 1) * 256])
            for half in range(2):
                head = 2 * i + half
                part = mixed[:, half * HEAD : (half + 1) * HEAD]
                if head < turned:
                    part = part * cos + pltpu.roll(part, HEAD // 2, 1) * sin
                qkv_ref[m, :, head * HEAD : (head + 1) * HEAD] = part.astype(BF16)
        bias = mask_bias(segr_ref[m])
        bias6 = jnp.concatenate([bias] * GROUP, 0)
        qkv = qkv_ref.at[m]
        for kv in range(KEY_VALUE_HEADS):
            q6 = heads_of(qkv, kv * GROUP, GROUP)
            k = heads_of(qkv, QUERY_HEADS + kv, 1)
            v = heads_of(qkv, turned + kv, 1)
            shares = attention_shares(q6, k, bias6).astype(BF16)
            o6 = dot(shares, v).astype(BF16)
            for i in range(GROUP):
                head = kv * GROUP + i
                ob_s[:, head * HEAD : (head + 1) * HEAD] = o6[i * tokens : (i + 1) * tokens]

        @pl.when(m == 0)
        def _():
            loads[1].wait()

        ob = ob_s[...]
        block = obb_ref.shape[3]
        for i in range(2 * ny):
            obb_ref[m, i] = ob[:, i * block : (i + 1) * block]
        for n in range(width // 512):
            cols = slice(n * 512, (n + 1) * 512)
            h1_ref[m, :, cols] = hin_ref[m, :, cols].astype(F32) + dot(ob, wout[:, cols])
        h1 = h1_ref[m]
        xm_ref[m, 0, 0] = (h1 * lax.rsqrt(jnp.mean(h1 * h1, -1, keepdims=True) + EPS) * gain_m).astype(BF16)

        ex = Exchange(g, FORWARD_CHUNKS, xm_ref.at[m], retl, retc, rety, sendl, sendc, sendy, Sems(sem_refs, m))
        ex.send_own()

        def complete(r):
            @pl.when(first & (m == 0))
            def _():
                gather.start(0, r, xm_ref.at[0, r, 0])

        def move(h):
            if h + 1 < nz:
                @pl.when(last & (m == 0))
                def _():
                    gather.step(0, h + 1)

            if h < nz:
                @pl.when(first & (m == 1))
                def _():
                    gather.step(0, h)

        complete(0)
        move(1)

        @pl.when(m == 0)
        def _():
            for load in loads[2:]:
                load.wait()

        def gates_for(r, other, here):
            rows = xm_ref[m, r, other, here, :]
            logits_t = dot_nt(small_ref[0:ROUTER_ROWS, :], rows)
            gates_t = chosen_gates(logits_t, route_ref[g.pack(r, other) * nz + g.d, m][:, here])
            return gates_t

        def lanes_of(blocks):
            return [
                jnp.concatenate([gate_lanes(gates_t, 2 * g.e + j) for gates_t in blocks], 0) for j in range(2)
            ]

        full = slice(0, tokens)

        def local_block():
            blocks = []
            for other in range(2):
                gates_t = gates_for(0, other, full)
                gates_ref[m, 0, other] = gates_t
                blocks.append(gates_t)

            def keep(cols, total):
                accl[:, cols] = total[0:tokens]
                sendl[:, cols] = total[tokens:].astype(BF16)

            experts(xm_ref[m, 0].reshape(2 * tokens, width), lanes_of(blocks), keep)

        def remote_block(r, q):
            here = slice(q * span, (q + 1) * span)
            blocks = []
            for other in range(2):
                gates_t = gates_for(r, other, here)
                gates_ref[m, r, other, :, here] = gates_t
                blocks.append(jnp.concatenate([gates_t] * (128 // span), 1))
            lanes = [
                jnp.concatenate([gate_lanes(gates_t, 2 * g.e + j)[0:span] for gates_t in blocks], 0)
                for j in range(2)
            ]

            def keep(cols, total):
                accr[:, cols] = total[0:span]
                sendc[r - 1, here, cols] = total[span:].astype(BF16)

            experts(xm_ref[m, r, :, here, :].reshape(2 * span, width), lanes, keep)
            return lambda: accr[...]

        ex.run(local_block, remote_block, complete)
        for q in range(HOP_CHUNKS):
            here = slice(q * span, (q + 1) * span)
            ex.arrived(q)
            total = h1_ref[m, here, :] + accl[here, :] + retl[here, :].astype(F32)
            for r in range(1, ny):
                total = total + rety[r - 1, here, :].astype(F32)
            out_ref[m, here, :] = total.astype(BF16)

            @pl.when(g.s < sections - 1)
            def _():
                hop(m, q).start()

        ex.finish()
        for yy in range(ny):
            partner(m, yy).start()
        move(2)
        return carry

    lax.fori_loop(0, micro, body, 0)

    @pl.when(jnp.logical_not(last))
    def _():
        for copy in shares:
            copy.start()

    for m in range(micro):
        for yy in range(ny):
            partner(m, yy).wait()

    @pl.when(g.s < sections - 1)
    def _():
        for m in range(micro):
            for q in range(HOP_CHUNKS):
                hop(m, q).wait_send()

    @pl.when(first)
    def _():
        for h in range(3, nz):
            gather.step(0, h)
        gather.finish(0, every)

    for copy in shares:
        copy.wait()

    @pl.when(last)
    def _():
        for r in range(1, ny):
            cot_copy(r).wait_send()
        for h in range(4, nz):
            gather.step(0, h)
        gather.finish(0, [0])


def backward_kernel(
    ny, nz, sections,
    cot_ref, segr_ref, small_ref, cos_ref, sin_ref,
    hin_ref, h1_ref, qkv_ref, gates_ref,
    xm_h, wqkv_h, wout_h, wg_h, wu_h, wd_h,
    gin_ref, grows_ref, xab_ref, dqkv_ref, dattn_ref, gsmall_ref, zb_h, xap_h, dqp_h, dtp_h,
    wqkv, wout, wg, wu, wd, xm_s, hid, act_s, slope_s, da_s, db_s, accl, accr, dh1_s, n_s,
    retl, retc, rety, sendl, sendc, sendy,
    wsem, xmsem, zs, zr, zys, zyr, zl, xs, xr, ps, pr, *sem_refs,
):
    micro, tokens, width = cot_ref.shape
    hidden = wg.shape[2]
    span = tokens // BACKWARD_CHUNKS
    loads = [
        pltpu.make_async_copy(src, dst, wsem.at[i])
        for i, (src, dst) in enumerate([(wg_h, wg), (wu_h, wu), (wd_h, wd), (wout_h, wout), (wqkv_h, wqkv)])
    ]
    for load in loads:
        load.start()
    g = Place(ny, nz)
    g.greet()
    gain_a = small_ref[ROUTER_ROWS : ROUTER_ROWS + 1, :].astype(F32)
    gain_m = small_ref[ROUTER_ROWS + 1 : ROUTER_ROWS + 2, :].astype(F32)
    cos, sin = cos_ref[...], sin_ref[...]
    gsmall_ref[...] = jnp.zeros_like(gsmall_ref)
    gather = Gather(g, zb_h, zs, zr, zys, zyr, zl)
    every = range(ny)
    first, last = g.s == 0, g.s == sections - 1

    @pl.when(first)
    def _():
        for m in range(1, micro):
            for r in every:
                gather.start(micro + m, r, xm_h.at[m, r, 0])
            for h in range(1, nz):
                gather.step(micro + m, h)

    def hop(m, q):
        here = pl.ds(q * (tokens // HOP_CHUNKS), tokens // HOP_CHUNKS)
        return remote(gin_ref.at[m, here], grows_ref.at[m, 0, 0, here], xs.at[m, q], xr.at[m, q], g.x)

    def partner(m):
        pairs = [(dattn_ref.at[m], dtp_h.at[m]), (dqkv_ref.at[m], dqp_h.at[m])]
        pairs += [(xab_ref.at[m, yy * 2 + 1 - g.c], xap_h.at[m, yy]) for yy in range(ny)]
        return [remote(src, dst, ps.at[m, n], pr.at[m, n], g.core) for n, (src, dst) in enumerate(pairs)]

    def late(m):
        for h in range(3, nz):
            gather.step(m, h, whole=False)

    def body(m, carry):
        load_xm = pltpu.make_async_copy(xm_h.at[m], xm_s, xmsem)
        load_xm.start()

        @pl.when(last)
        def _():
            grows_ref[m, 0, 0] = cot_ref[m]
            for r in every:
                gather.start(m, r, xm_h.at[m, r, 0], whole=False)

        ex = Exchange(
            g, BACKWARD_CHUNKS, grows_ref.at[m], retl, retc, rety, sendl, sendc, sendy, Sems(sem_refs, m), HOP_CHUNKS
        )

        @pl.when(last)
        def _():
            ex.send_own()

        @pl.when(m == 0)
        def _():
            for load in loads[:3]:
                load.wait()

        load_xm.wait()

        def again(r, _):
            rows = xm_s[r].reshape(2 * tokens, width)
            for j in range(2):
                for n in range(hidden // 256):
                    cols = slice(n * 256, (n + 1) * 256)
                    a = dot(rows, wg[j, :, cols])
                    b = dot(rows, wu[j, :, cols])
                    square = a * a
                    th = jnp.tanh(GELU_C * (a + GELU_A * square * a))
                    half = 0.5 * (1.0 + th)
                    act = a * half
                    slope = half + (0.5 * GELU_C) * a * (1.0 - th * th) * (1.0 + (3.0 * GELU_A) * square)
                    shape = (2, tokens, 256)
                    hid[j, r, :, :, cols] = (act * b).astype(BF16).reshape(shape)
                    act_s[j, r, :, :, cols] = act.astype(BF16).reshape(shape)
                    slope_s[j, r, :, :, cols] = (slope * b).astype(BF16).reshape(shape)
            return 0

        @pl.when(first)
        def _():
            lax.fori_loop(0, ny, again, 0)

            @pl.when(m > 0)
            def _():
                late(m - 1)

            for q in range(HOP_CHUNKS):
                hop(m, q).wait_recv()
                ex.send_part(q)
            ex.core_own().start()

        def complete(r):
            src = grows_ref.at[m, r, 0]

            @pl.when(first)
            def _():
                gather.start(m, r, src, whole=False)

        open_end = first & (m == micro - 1)

        def move(hops):
            for h in hops:
                gather.step(m, h, whole=False)

        complete(0)

        @pl.when(last)
        def _():
            lax.fori_loop(0, ny, again, 0)


        def experts(rows, r, here, keep):
            count = 2 * (here.stop - here.start)
            part = slice(0, count)
            lane = lax.broadcasted_iota(jnp.int32, (count, 128), 1)
            gate_grads = jnp.zeros((count, 128), F32)
            for j in range(2):
                expert = 2 * g.e + j
                lanes = []
                for other in range(2):
                    gates_t = gates_ref[m, r, other]
                    lanes.append(gate_lanes(gates_t, expert)[here])
                lanes = widen(jnp.concatenate(lanes, 0), 256)
                summed = jnp.zeros((count, 1), F32)
                for n in range(hidden // 256):
                    cols = slice(n * 256, (n + 1) * 256)
                    u = dot_nt(rows, wd[j, cols, :])
                    inner = hid[j, r, :, here, cols].reshape(count, 256).astype(F32)
                    summed = summed + jnp.sum(u * inner, -1, keepdims=True)
                    u = u * lanes
                    slope = slope_s[j, r, :, here, cols].reshape(count, 256).astype(F32)
                    act = act_s[j, r, :, here, cols].reshape(count, 256).astype(F32)
                    da_s[j, part, cols] = (u * slope).astype(BF16)
                    db_s[j, part, cols] = (u * act).astype(BF16)
                high = summed.astype(BF16).astype(F32)
                gate_grads = jnp.where(lane == expert, high, gate_grads)
                gate_grads = jnp.where(lane == expert + 64, summed - high, gate_grads)
            for n in range(width // 512):
                cols = slice(n * 512, (n + 1) * 512)
                total = None
                for j in range(2):
                    term = dot_nt(da_s[j, part, :], wg[j, cols, :]) + dot_nt(db_s[j, part, :], wu[j, cols, :])
                    total = term if total is None else total + term
                keep(cols, total)
            keep(slice(width, width + 128), gate_grads)

        full = slice(0, tokens)

        def local_block():
            def keep(cols, total):
                accl[:, cols] = total[0:tokens]
                sendl[:, cols] = total[tokens:].astype(BF16)

            experts(grows_ref[m, 0].reshape(2 * tokens, width), 0, full, keep)

        def remote_block(r, q):
            here = slice(q * span, (q + 1) * span)

            def keep(cols, total):
                accr[:, cols] = total[0:span]
                sendc[r - 1, here, cols] = total[span:].astype(BF16)

            experts(grows_ref[m, r, :, here, :].reshape(2 * span, width), r, here, keep)
            return lambda: accr[...]

        ex.run(local_block, remote_block, complete, last)
        move(range(1, 2))
        for q in range(BACKWARD_CHUNKS):
            ex.arrived(q)
        total = accl[...] + retl[...].astype(F32)
        for r in range(1, ny):
            total = total + rety[r - 1].astype(F32)
        dgates = total[:, width:]
        dgates = dgates + pltpu.roll(dgates, 64, 1)
        gates_t = gates_ref[m, 0, 0]
        gates = jnp.transpose(
            jnp.concatenate([gates_t, jnp.zeros((128 - ROUTER_ROWS, tokens), F32)], 0)
        )
        dlog = gates * (dgates - jnp.sum(gates * dgates, -1, keepdims=True))
        dlog = dlog[:, 0:SMALL_ROWS]
        high = dlog.astype(BF16)
        low = (dlog - high.astype(F32)).astype(BF16)
        router = small_ref[...]
        dxm = total[:, 0:width] + dot(high, router) + dot(low, router)
        xm = xm_s[0, 0]
        gsmall_ref[0:ROUTER_ROWS, :] += (dot_tn(high, xm) + dot_tn(low, xm))[0:ROUTER_ROWS]
        h1 = h1_ref[m]
        rinv = lax.rsqrt(jnp.mean(h1 * h1, -1, keepdims=True) + EPS)
        n2 = h1 * rinv
        gsmall_ref[ROUTER_ROWS + 1 : ROUTER_ROWS + 2, :] += jnp.sum(dxm * n2, 0, keepdims=True)
        scaled = dxm * gain_m
        dh1 = grows_ref[m, 0, 0].astype(F32) + rinv * (scaled - n2 * jnp.mean(scaled * n2, -1, keepdims=True))
        dh1_s[...] = dh1
        dattn = dh1.astype(BF16)
        dattn_ref[m] = dattn

        @pl.when(m == 0)
        def _():
            for load in loads[3:]:
                load.wait()

        @pl.when(jnp.logical_not(open_end))
        def _():
            move(range(2, min(3, nz)))

        @pl.when(first)
        def _():
            gather.passes(m, range(1, 2))

        @pl.when(first & (m > 0))
        def _():
            gather.passes(m - 1, range(3, nz))

        @pl.when(first & (m < micro - 1))
        def _():
            gather.passes(m, range(2, min(3, nz)))

        for copy in partner(m)[:1]:
            copy.start()
        bias = mask_bias(segr_ref[m])
        bias6 = jnp.concatenate([bias] * GROUP, 0)
        qkv = qkv_ref.at[m]
        turned = QUERY_HEADS + KEY_VALUE_HEADS

        def unturn(part):
            return part * cos - pltpu.roll(part, HEAD // 2, 1) * sin

        for kv in range(KEY_VALUE_HEADS):
            wide = GROUP * HEAD
            dob = dot_nt(dattn, wout[kv * wide : (kv + 1) * wide, :]).astype(BF16)
            dob6 = heads_of(dob, 0, GROUP)
            q6 = heads_of(qkv, kv * GROUP, GROUP)
            k = heads_of(qkv, QUERY_HEADS + kv, 1)
            v = heads_of(qkv, turned + kv, 1)
            shares = attention_shares(q6, k, bias6)
            dshares = dot_nt(dob6, v)
            dv = dot_tn(shares.astype(BF16), dob6)
            ds = (shares * (dshares - jnp.sum(shares * dshares, -1, keepdims=True))).astype(BF16)
            dq6 = dot(ds, k) * SCALE
            dk = dot_tn(ds, q6) * SCALE
            for i in range(GROUP):
                head = kv * GROUP + i
                dqkv_ref[m, :, head * HEAD : (head + 1) * HEAD] = unturn(
                    dq6[i * tokens : (i + 1) * tokens]
                ).astype(BF16)
            head = QUERY_HEADS + kv
            dqkv_ref[m, :, head * HEAD : (head + 1) * HEAD] = unturn(dk).astype(BF16)
            head = turned + kv
            dqkv_ref[m, :, head * HEAD : (head + 1) * HEAD] = dv.astype(BF16)

        h = hin_ref[m].astype(F32)
        rinv = lax.rsqrt(jnp.mean(h * h, -1, keepdims=True) + EPS)
        n1 = h * rinv
        xa = (n1 * gain_a).astype(BF16)
        block = xab_ref.shape[3]
        for i in range(2 * ny):
            xab_ref[m, i] = xa[:, i * block : (i + 1) * block]
        n_s[...] = n1
        dqkv = dqkv_ref[m]
        for n in range(width // 512):
            cols = slice(n * 512, (n + 1) * 512)
            accl[:, cols] = dot_nt(dqkv, wqkv[cols, :])
        dxa = accl[:, 0:width]
        n1 = n_s[...]
        gsmall_ref[ROUTER_ROWS : ROUTER_ROWS + 1, :] += jnp.sum(dxa * n1, 0, keepdims=True)
        scaled = dxa * gain_a
        grad = dh1_s[...] + rinv * (scaled - n1 * jnp.mean(scaled * n1, -1, keepdims=True))
        gin_ref[m] = grad.astype(BF16)

        @pl.when(g.s > 0)
        def _():
            for q in range(HOP_CHUNKS):
                hop(m, q).start()

        for copy in partner(m)[1:]:
            copy.start()

        @pl.when(last)
        def _():
            move(range(3, nz))

        @pl.when(open_end)
        def _():
            for h in range(2, min(3, nz)):
                gather.step(m, h, whole=False, forward=False)

        ex.finish()
        return carry

    lax.fori_loop(0, micro, body, 0)

    @pl.when(g.s > 0)
    def _():
        for m in range(micro):
            for q in range(HOP_CHUNKS):
                hop(m, q).wait_send()

    few = range(1, min(3, nz))

    @pl.when(last)
    def _():
        for m in range(micro):
            gather.passes(m, range(1, nz))
        for m in range(1, micro):
            for r in every:
                gather.start(micro + m, r, grows_ref.at[m, r, 0])
            for h in few:
                gather.step(micro + m, h, forward=m < micro - 1 or h < few[-1])
            if m < micro - 1:
                for h in range(3, nz):
                    gather.step(micro + m, h)

    for m in range(micro - 1):
        gather.finish(m, every, whole=False)
    for m in range(1, micro - 1):
        gather.finish(micro + m, every)

    @pl.when(first)
    def _():
        for r in every:
            gather.near(micro - 1, r, grows_ref.at[micro - 1, r, 0]).wait()
        for r in every:
            gather.line(micro - 1, r, False).finish(few)
        gather.finish_passes(micro - 1, range(1, 2))
        gather.finish(2 * micro - 1, every)

    @pl.when(last)
    def _():
        gather.finish(micro - 1, every, whole=False)
        gather.finish(2 * micro - 1, every, hops=few)

    for m in range(micro):
        for copy in partner(m):
            copy.wait()


def tail_kernel(
    ny, nz, sections, span,
    route_ref, small_ref, gsmall_ref,
    zf_h, zb_in, slices_h, partner_h, wd_h, xab_h, obb_h, dqkv_h, dattn_h, xap_h, obp_h, dqp_h, dtp_h,
    gate_ref, up_ref, down_ref, attn_ref, small_out, zb_h,
    w4, x_s, g_s, da_s, db_s, gh_s, acc_g, acc_u, acc_d, csend, cland, dsend, dland,
    xa_s, ob_s, dq_s, dt_s, own_s, ysend, yland, zland, sm_s, smy, smz,
    wsem, xsem, asem, ss, sr, cs, cr, ts, tr, ys, yr, zs, zr, hs, hr, hys, hyr, hl,
):
    micro, tokens, width = dqkv_h.shape[0], zf_h.shape[3], zf_h.shape[4]
    hidden = slices_h.shape[1]
    turns = nz // 2
    half = hidden // turns
    slice_h = half // 2
    both = 2 * half
    wide = 2 * hidden
    tile = 256 if both % 256 == 0 else 128
    qkv_width = dqkv_h.shape[2]
    shard = width // (2 * ny * nz)
    part = width // nz
    rows = span * ny * tokens
    groups = nz // span
    g = Place(ny, nz)
    first = g.s == 0
    pieces = []
    for t in range(turns):
        own, other = 2 * t, 2 * t + 1
        rows_t = slice(t * half, (t + 1) * half)
        pieces.append((slices_h.at[:, rows_t], w4.at[0:2, own * half : (own + 1) * half]))
        pieces.append((partner_h.at[:, rows_t], w4.at[:, other * half : (other + 1) * half]))
        here = pl.ds(pl.multiple_of(g.z_of(2 * t) * slice_h, slice_h), slice_h)
        for j in range(2):
            at = own * half + j * slice_h
            pieces.append((wd_h.at[j, here], w4.at[2, at : at + slice_h]))
    mine = [pltpu.make_async_copy(src, dst, wsem.at[n]) for n, (src, dst) in enumerate(pieces)]

    def load(i):
        m, k = lax.div(i, groups), pl.ds(lax.rem(i, groups) * span, span)
        early = [(first, x_s, 0), (jnp.logical_not(first), g_s, 1)]
        late = [(first, g_s, 1), (jnp.logical_not(first), x_s, 0)]
        copies = [(when, pltpu.make_async_copy(zb_h.at[m, k], dst, xsem.at[n])) for when, dst, n in late]
        for when, dst, n in early:
            copies.append((when & (m == 0), pltpu.make_async_copy(zf_h.at[0, k], dst, xsem.at[n])))
            copies.append((when & (m > 0), pltpu.make_async_copy(zb_h.at[micro + m, k], dst, xsem.at[n])))
        return copies

    def start_load(i):
        for when, copy in load(i):
            @pl.when(when)
            def _():
                copy.start()

    def wait_load():
        pltpu.make_async_copy(zf_h.at[0, pl.ds(0, span)], x_s, xsem.at[0]).wait()
        pltpu.make_async_copy(zf_h.at[0, pl.ds(0, span)], g_s, xsem.at[1]).wait()

    acts = []
    for m in range(micro):
        for yy in range(ny):
            own = yy * 2 + g.c
            acts.append((xab_h.at[m, own], xa_s.at[yy, 0, m]))
            acts.append((xap_h.at[m, yy], xa_s.at[yy, 1, m]))
            acts.append((obb_h.at[m, own], ob_s.at[yy, 0, m]))
            acts.append((obp_h.at[m, yy], ob_s.at[yy, 1, m]))
    acts += [(dqkv_h, dq_s.at[0]), (dqp_h, dq_s.at[1]), (dattn_h, dt_s.at[0]), (dtp_h, dt_s.at[1])]
    acts = [pltpu.make_async_copy(src, dst, asem.at[i]) for i, (src, dst) in enumerate(acts)]
    for copy in acts:
        copy.start()
    g.greet(with_x=False)
    gather = Gather(g, zb_h, hs, hr, hys, hyr, hl)
    late_hops = range(3, nz)
    newest = micro - 1

    @pl.when(first)
    def _():
        gather.passes(newest, range(2, min(3, nz)))
        for h in late_hops[:1]:
            gather.go_on(newest, h, whole=False)

    @pl.when(jnp.logical_not(first))
    def _():
        for h in late_hops[:1]:
            gather.go_on(micro + newest, h)
    sm_core = remote(gsmall_ref, sm_s.at[1], ss.at[0], sr.at[0], g.core)
    sm_core.start()

    def sm_y(r):
        return remote(sm_s.at[0], smy.at[ny - r - 1], ss.at[r], sr.at[ny - r], g.ahead(r))

    def sm_y_arrival(r):
        return remote(sm_s.at[0], smy.at[r - 1], ss.at[r], sr.at[r], g.ahead(r))

    def sm_z(k):
        return remote(sm_s.at[1], smz.at[k - 1], ss.at[ny + k], sr.at[ny + k], g.z_behind(k))

    acc_g[...] = jnp.zeros_like(acc_g)
    acc_u[...] = jnp.zeros_like(acc_u)
    acc_d[...] = jnp.zeros_like(acc_d)
    for copy in acts:
        copy.wait()
    for copy in mine:
        copy.start()
    start_load(0)

    count = 2 * micro * tokens

    def attn_rows(yy, dst):
        for src, grad, at in ((xa_s, dq_s, 0), (ob_s, dt_s, qkv_width)):
            left = src[yy].reshape(count, shard * nz)
            wide = grad.shape[3]
            for n in range(wide // 512):
                cols = slice(n * 512, (n + 1) * 512)
                got = dot_tn(left, grad[:, :, :, cols].reshape(count, 512)).astype(BF16)
                for zi in range(nz):
                    dst[zi, 0:shard, at + n * 512 : at + (n + 1) * 512] = got[zi * shard : (zi + 1) * shard]

    def flipped(mask):
        place = g.d
        for b in range(nz.bit_length()):
            if mask >> b & 1:
                place = place + (1 << b) - (2 << b) * lax.rem(lax.div(g.d, 1 << b), 2)
        return place

    def y_copy(r, k):
        zi = flipped(k)
        return remote(ysend.at[r - 1, zi], yland.at[ny - r - 1, zi], ys.at[r, k], yr.at[ny - r, k], g.ahead(r))

    def y_arrival(r, k):
        zi = flipped(k)
        return remote(ysend.at[r - 1, zi], yland.at[r - 1, zi], ys.at[r, k], yr.at[r, k], g.ahead(r))

    order = list(range(1, nz)) + [0]
    masks = list(range(nz - 1, -1, -1))

    def y_start(k):
        for r in range(1, ny):
            y_copy(r, k).start()

    for r in range(1, ny):
        attn_rows(lax.rem(g.y + r, ny), ysend.at[r - 1])
    y_start(masks[0])
    sm_core.wait_recv()
    sm_s[0] = gsmall_ref[...] + sm_s[1]
    sm_core.wait_send()
    for r in range(1, ny):
        sm_y(r).start()
    attn_rows(g.y, own_s)

    bits = nz.bit_length() - 1

    def low(mask):
        return (mask & -mask).bit_length() - 1 if mask else bits

    landings = [(mask, b) for mask in range(nz) for b in range(low(mask))]

    def z_copy(mask):
        b = low(mask)
        at = landings.index((mask - (1 << b), b))
        device = (g.s, g.e, flipped(1 << b))
        return remote(own_s.at[flipped(mask)], zland.at[at], zs.at[0, mask], zr.at[0, at], device)

    def z_arrival(mask, b):
        at = landings.index((mask, b))
        device = (g.s, g.e, flipped(1 << b))
        return remote(own_s.at[flipped(mask)], zland.at[at], zs.at[0, mask], zr.at[0, at], device)

    def advance(mask):
        for r in range(1, ny):
            y_arrival(r, mask).wait_recv()
        zi = flipped(mask)
        for b in range(low(mask)):
            z_arrival(mask, b).wait_recv()
        for n in range((qkv_width + width) // 512):
            cols = slice(n * 512, (n + 1) * 512)
            total = own_s[zi, :, cols].astype(F32)
            for r in range(1, ny):
                total = total + yland[r - 1, zi, :, cols].astype(F32)
            for b in range(low(mask)):
                total = total + zland[landings.index((mask, b)), :, cols].astype(F32)
            own_s[zi, :, cols] = total.astype(BF16)
        if mask:
            z_copy(mask).start()

    for copy in mine:
        copy.wait()
    column = lax.rem(lax.broadcasted_iota(jnp.int32, (ROUTER_ROWS, wide), 1), both)
    expert = lax.broadcasted_iota(jnp.int32, (ROUTER_ROWS, wide), 0)
    owner = jnp.where(column < half, g.e, 2 * g.y + 1 - g.c)
    local = jnp.where(column < half, column, column - half)
    chosen = 2 * owner + jnp.where(local < slice_h, 0, 1)
    spread = jnp.where(expert == chosen, 1.0, 0.0).astype(BF16)
    spread = jnp.concatenate([spread, spread], 0)

    last_group = micro * groups - 1
    accs = (acc_g, acc_u)
    parity = lax.rem(g.d, 2)

    def rows_of(x):
        at = parity if x == 0 else 1 - parity
        return pl.ds(pl.multiple_of(at * part, part), part)

    def cols_of(t, o):
        return slice((2 * t + o) * half, (2 * t + o + 1) * half)

    def core_copy(n, x, t):
        return remote(csend.at[n, x, t], cland.at[n, x, t], cs.at[n, x * turns + t], cr.at[n, x * turns + t], g.core)

    def give_half(n):
        for x in (1, 0):
            for t in range(turns):
                csend[n, x, t] = accs[n][rows_of(x), cols_of(t, 1)].astype(BF16)
                core_copy(n, x, t).start()

    def turn_copy(n, t):
        dst = (gate_ref, up_ref)[n]
        device = (g.s, g.e, flipped(1))
        return remote(cland.at[n, 1, t], dst.at[g.z_of(2 * t)], ts.at[n, t], tr.at[n, t], device)

    def turn_arrival(n, t):
        dst = (gate_ref, up_ref)[n]
        device = (g.s, g.e, flipped(1))
        return remote(cland.at[n, 1, t], dst.at[lax.rem(flipped(1) + 2 * t, nz)], ts.at[n, t], tr.at[n, t], device)

    def turn_near(n, t):
        dst = (gate_ref, up_ref)[n]
        return pltpu.make_async_copy(cland.at[n, 0, t], dst.at[g.z_of(2 * t)], ts.at[n, turns + t])

    def take_half(n):
        for x in (1, 0):
            for t in range(turns):
                core_copy(n, x, t).wait_recv()
                total = accs[n][rows_of(x), cols_of(t, 0)] + cland[n, x, t].astype(F32)
                cland[n, x, t] = total.astype(BF16)
                if x:
                    turn_copy(n, t).start()
                else:
                    turn_near(n, t).start()

    def small_z():
        for r in range(1, ny):
            sm_y_arrival(r).wait_recv()
        total = sm_s[0]
        for r in range(1, ny):
            total = total + smy[r - 1]
        sm_s[1] = total
        for k in range(1, nz):
            sm_z(k).start()

    def group(i, carry):
        m = lax.div(i, groups)
        wait_load()

        def block(b, carry):
            k = lax.rem(i, groups) * span + b
            x = x_s[b].reshape(ny * tokens, width)
            gr = g_s[b].reshape(ny * tokens, width)
            places = [(lax.rem(g.y + r, ny) * 2 + g.c) * nz + k for r in range(ny)]
            route = jnp.concatenate([route_ref[place, m] for place in places], 1)
            gates_t = chosen_gates(dot_nt(small_ref[0:ROUTER_ROWS, :], x), route)
            high = gates_t.astype(BF16)
            gates_b = jnp.concatenate([high, (gates_t - high.astype(F32)).astype(BF16)], 0)
            here = pl.ds(pl.multiple_of(b * ny * tokens, ny * tokens), ny * tokens)
            for n in range(wide // tile):
                cols = slice(n * tile, (n + 1) * tile)
                a = dot_nt(x, w4[0, cols])
                bb = dot_nt(x, w4[1, cols])
                gate = dot_tn(gates_b, spread[:, cols])
                u = dot_nt(gr, w4[2, cols]) * gate
                square = a * a
                th = jnp.tanh(GELU_C * (a + GELU_A * square * a))
                hf = 0.5 * (1.0 + th)
                act = a * hf
                slope = hf + (0.5 * GELU_C) * a * (1.0 - th * th) * (1.0 + (3.0 * GELU_A) * square)
                da_s[here, cols] = (u * slope * bb).astype(BF16)
                db_s[here, cols] = (u * act).astype(BF16)
                if (n + 1) * tile <= both:
                    gh_s[here, cols] = ((act * bb).astype(BF16).astype(F32) * gate).astype(BF16)
            return carry

        lax.fori_loop(0, span, block, 0)

        @pl.when(first & (i == newest * groups - 1))
        def _():
            for h in late_hops:
                gather.step(newest, h, whole=False)
            gather.passes(newest, late_hops)

        @pl.when(jnp.logical_not(first) & (i == newest * groups - 1))
        def _():
            for h in late_hops:
                gather.step(micro + newest, h)

        size = 256 if (2 * part) % 256 == 0 else 128
        base = lax.div(g.d, 2) * (2 * part)

        def x_columns(n):
            cols = pl.ds(pl.multiple_of(base + n * size, size), size)
            return x_s[:, :, :, cols].reshape(rows, size)

        def sum_rows(acc, right):
            def columns(n, carry):
                at = pl.ds(pl.multiple_of(n * size, size), size)
                acc[at, :] += dot_tn(x_columns(n), right[...])
                return carry

            lax.fori_loop(0, 2 * part // size, columns, 0)

        def down():
            def columns(n, carry):
                cols = pl.ds(pl.multiple_of(n * tile, tile), tile)
                acc_d[cols, :] += dot_tn(gh_s[:, cols], g_s[...].reshape(rows, width))
                return carry

            lax.fori_loop(0, both // tile, columns, 0)

        sum_rows(acc_g, da_s)

        @pl.when(i == last_group)
        def _():
            give_half(0)

        sum_rows(acc_u, db_s)

        @pl.when(i == last_group)
        def _():
            give_half(1)
            take_half(0)

        down()

        @pl.when(first & (i == newest * groups - 1))
        def _():
            for r in range(ny):
                gather.line(newest, r, False).finish(late_hops)
            gather.finish_passes(newest, range(2, nz))

        @pl.when(jnp.logical_not(first) & (i == newest * groups - 1))
        def _():
            gather.finish(micro + newest, [], hops=late_hops)

        @pl.when(i < last_group)
        def _():
            start_load(i + 1)

        for n in range(min(3, last_group)):
            @pl.when(i == n)
            def _():
                advance(masks[n])
                y_start(masks[n + 1])
                if n == 1:
                    small_z()

        return carry

    lax.fori_loop(0, micro * groups, group, 0)
    polled = min(3, last_group)
    for mask in masks[polled + 1 :]:
        y_start(mask)

    down_copy = remote(dsend, dland, cs.at[2, 0], cr.at[2, 0], g.core)
    dsend[...] = acc_d[half:both, :].astype(BF16)
    down_copy.start()
    take_half(1)
    for mask in masks[polled:-1]:
        advance(mask)
    down_copy.wait_recv()
    dland[...] = (acc_d[0:half, :] + dland[...].astype(F32)).astype(BF16)
    down_near = pltpu.make_async_copy(dland, down_ref, ts.at[0, nz])
    down_near.start()

    total = sm_s[1]
    for k in range(1, nz):
        sm_z(k).wait_recv()
        total = total + smz[k - 1]
    small_out[...] = total

    advance(0)
    attn_near = pltpu.make_async_copy(own_s.at[g.d], attn_ref, ts.at[1, nz])
    attn_near.start()
    for t in range(turns):
        for n in range(2):
            turn_arrival(n, t).wait_recv()

    for r in range(1, ny):
        sm_y(r).wait_send()
        for k in range(nz):
            y_copy(r, k).wait_send()
    for k in range(1, nz):
        sm_z(k).wait_send()
        z_copy(k).wait_send()
    for n in range(2):
        for t in range(turns):
            turn_copy(n, t).wait_send()
            turn_near(n, t).wait()
            for x in range(2):
                core_copy(n, x, t).wait_send()
    down_copy.wait_send()
    down_near.wait()
    attn_near.wait()


def finish_kernel(nz, experts, gate_in, up_in, down_in, attn_in, small_in, gate, up, down, qkv, out, router, again, mgain):
    slice_h = gate_in.shape[2] // 2
    for src, dst in ((gate_in, gate), (up_in, up)):
        for j in range(2):
            cols = slice(j * slice_h, (j + 1) * slice_h)
            dst[0, j] = jnp.concatenate([src[z, :, cols].astype(F32) for z in range(nz)], 1)
    down[0, 0] = down_in[...].astype(F32)
    shard, split = qkv.shape[1], qkv.shape[2]
    qkv[0] = attn_in[0:shard, 0:split].astype(F32)
    out[0] = attn_in[0:shard, split:].astype(F32)
    rows, width = small_in.shape
    base = (lax.axis_index("expert") * nz + lax.axis_index("dp")) * shard
    at = lax.broadcasted_iota(jnp.int32, (width, 128), 0)
    lane = lax.broadcasted_iota(jnp.int32, (width, 128), 1)
    pick = jnp.where(at == base + lane, 1.0, 0.0).astype(F32)
    got = jnp.dot(small_in[...], pick, precision=lax.Precision.HIGHEST, preferred_element_type=F32)
    again[...] = got[ROUTER_ROWS : ROUTER_ROWS + 1, 0:shard]
    mgain[...] = got[ROUTER_ROWS + 1 : ROUTER_ROWS + 2, 0:shard]
    turned = jnp.transpose(jnp.concatenate([got, jnp.zeros((128 - rows, 128), F32)], 0))
    router[0] = turned[0:shard, 0:experts]


VMEM = pl.BlockSpec(memory_space=pltpu.VMEM)
ANY = pl.BlockSpec(memory_space=pl.ANY)
DMA = pltpu.SemaphoreType.DMA


def per_device(
    ne, nz, sections,
    layer_input, cotangent, segments, routes, attn_gain, w_qkv, w_out, moe_gain, w_router, w_gate, w_up, w_down,
):
    ny = ne // 2
    micro, _, tokens, width = layer_input.shape
    total_experts = w_router.shape[2]
    hidden = w_gate.shape[3]
    owners = ("expert", "dp")
    shard = w_qkv.shape[1]
    place_e, place_d = lax.axis_index("expert"), lax.axis_index("dp")
    small = jnp.concatenate(
        [
            w_router[0],
            jnp.zeros((shard, ROUTER_ROWS - total_experts), BF16),
            attn_gain[0][:, None],
            moe_gain[0][:, None],
            jnp.zeros((shard, 128 - ROUTER_ROWS - 2), BF16),
        ],
        1,
    ).astype(F32)
    own_routes = jnp.transpose(routes[0, :, 0], (0, 2, 1))
    cos, sin = rotary_tables(tokens)
    segs = segments[:, 0]
    segr = segs[:, None, :]
    x = layer_input[:, 0]
    cot = cotangent[:, 0]
    wg, wu, wd = w_gate[0], w_up[0], w_down[0]
    qkv_width = w_qkv.shape[2]
    slice_h = hidden // nz
    half = 2 * slice_h

    def shape(*dims, dtype=BF16):
        return jax.ShapeDtypeStruct(dims, dtype)

    grid_sems = [DMA((5, 2, nz, ny)) for _ in range(4)]
    small, routes_all, wqkv, wout, slices = pl.pallas_call(
        functools.partial(gather_kernel, ny, nz),
        out_shape=(
            shape(SMALL_ROWS, width),
            shape(ne, nz, *own_routes.shape, dtype=jnp.int32),
            shape(ne, nz, shard, qkv_width),
            shape(ne, nz, shard, width),
            shape(2, hidden, width),
        ),
        in_specs=[VMEM] + [ANY] * 5,
        out_specs=tuple([VMEM] + [ANY] * 4),
        scratch_shapes=[
            pltpu.VMEM((ne, nz, shard, 128), F32),
            pltpu.VMEM(wg.shape, BF16),
            pltpu.VMEM(wu.shape, BF16),
            pltpu.VMEM((2, 2, hidden, width), BF16),
            DMA((2,)), DMA((5,)),
        ]
        + grid_sems
        + [DMA((5, ny, 2, nz)), DMA((5, ny, 2, nz)), DMA((2, nz))],
        compiler_params=pltpu.CompilerParams(
            collective_id=3, has_side_effects=True, vmem_limit_bytes=60 * 2**20
        ),
        name="gather_weights",
    )(small, own_routes, w_qkv[0], w_out[0], wg, wu)
    wqkv = wqkv.reshape(width, qkv_width)
    wout = wout.reshape(width, width)
    routes_all = routes_all.reshape((ne * nz,) + own_routes.shape)
    weights = [pltpu.VMEM(w.shape, BF16) for w in (wqkv, wout, wg, wu, wd)]
    hop_sems = [DMA((micro, HOP_CHUNKS)) for _ in range(2)]
    block = width // ne

    def gather_sems(count):
        return [DMA((count, ny, 2, nz))] * 2 + [DMA((count, 2, nz, ny))] * 2 + [DMA((count, ny))]

    def returns(wide):
        return [
            pltpu.VMEM((tokens, wide), BF16),
            pltpu.VMEM((max(1, ny - 1), tokens, wide), BF16),
            pltpu.VMEM((max(1, ny - 1), tokens, wide), BF16),
            pltpu.VMEM((tokens, wide), BF16),
            pltpu.VMEM((max(1, ny - 1), tokens, wide), BF16),
            pltpu.VMEM((max(1, ny - 1), tokens, wide), BF16),
        ]

    out, hin, h1, qkv, obb, xm, gates, zf, obp, partner = pl.pallas_call(
        functools.partial(forward_kernel, ny, nz, sections),
        out_shape=(
            shape(micro, tokens, width),
            shape(micro, tokens, width),
            shape(micro, tokens, width, dtype=F32),
            shape(micro, tokens, qkv_width),
            shape(micro, ne, tokens, block),
            shape(micro, ny, 2, tokens, width),
            shape(micro, ny, 2, ROUTER_ROWS, tokens, dtype=F32),
            shape(1, nz, ny, tokens, width),
            shape(micro, ny, tokens, block),
            shape(3, hidden, width),
        ),
        in_specs=[VMEM] * 6 + [ANY] * 7,
        out_specs=tuple([VMEM] * 7 + [ANY] * 3),
        scratch_shapes=weights
        + [
            pltpu.VMEM((tokens, width), BF16),
            pltpu.VMEM((2, 2 * tokens, hidden), BF16),
            pltpu.VMEM((tokens, width), F32),
            pltpu.VMEM((tokens // FORWARD_CHUNKS, width), F32),
        ]
        + returns(width)
        + [DMA((5,))]
        + gather_sems(1)
        + [DMA((ny,)), DMA((ny,))]
        + hop_sems
        + [DMA((micro, ny))] * 2
        + [DMA((nz + 2,))] * 2
        + sem_shapes(micro, ny, FORWARD_CHUNKS),
        compiler_params=pltpu.CompilerParams(
            collective_id=0, has_side_effects=True, vmem_limit_bytes=60 * 2**20
        ),
        name="layers_forward",
    )(x, segr, routes_all, small, cos, sin, cot, slices, wqkv, wout, wg, wu, wd)

    wide = width + 128
    every = (2, ny, 2, tokens, hidden)
    gin, grows, xab, dqkv, dattn, gsmall, zb, xap, dqp, dtp = pl.pallas_call(
        functools.partial(backward_kernel, ny, nz, sections),
        out_shape=(
            shape(micro, tokens, width),
            shape(micro, ny, 2, tokens, width),
            shape(micro, ne, tokens, block),
            shape(micro, tokens, qkv_width),
            shape(micro, tokens, width),
            shape(SMALL_ROWS, width, dtype=F32),
            shape(2 * micro, nz, ny, tokens, width),
            shape(micro, ny, tokens, block),
            shape(micro, tokens, qkv_width),
            shape(micro, tokens, width),
        ),
        in_specs=[VMEM] * 9 + [ANY] * 6,
        out_specs=tuple([VMEM] * 6 + [ANY] * 4),
        scratch_shapes=weights
        + [
            pltpu.VMEM((ny, 2, tokens, width), BF16),
            pltpu.VMEM(every, BF16),
            pltpu.VMEM(every, BF16),
            pltpu.VMEM(every, BF16),
            pltpu.VMEM((2, 2 * tokens, hidden), BF16),
            pltpu.VMEM((2, 2 * tokens, hidden), BF16),
            pltpu.VMEM((tokens, wide), F32),
            pltpu.VMEM((tokens // BACKWARD_CHUNKS, wide), F32),
            pltpu.VMEM((tokens, width), F32),
            pltpu.VMEM((tokens, width), F32),
        ]
        + returns(wide)
        + [DMA((5,)), DMA]
        + gather_sems(2 * micro)
        + hop_sems
        + [DMA((micro, ny + 2))] * 2
        + sem_shapes(micro, ny, BACKWARD_CHUNKS * HOP_CHUNKS),
        compiler_params=pltpu.CompilerParams(
            collective_id=1, has_side_effects=True, vmem_limit_bytes=62 * 2**20
        ),
        name="layers_backward",
    )(cot, segr, small, cos, sin, hin, h1, qkv, gates, xm, wqkv, wout, wg, wu, wd)

    span_z = max(1, min(nz, 512 // (ny * tokens)))
    rows = span_z * ny * tokens
    padded = -(-shard // 16) * 16
    attn_width = qkv_width + width
    part = width // nz
    small_shape = (SMALL_ROWS, width)
    gate_g, up_g, down_g, attn_g, small_g, _ = pl.pallas_call(
        functools.partial(tail_kernel, ny, nz, sections, span_z),
        out_shape=(
            shape(nz, part, half),
            shape(nz, part, half),
            shape(half, width),
            shape(padded, attn_width),
            shape(*small_shape, dtype=F32),
            shape(*zb.shape),
        ),
        in_specs=[VMEM] * 3 + [ANY] * 13,
        out_specs=tuple([ANY] * 4 + [VMEM] + [ANY]),
        input_output_aliases={4: 5},
        scratch_shapes=[
            pltpu.VMEM((3, 2 * hidden, width), BF16),
            pltpu.VMEM((span_z, ny, tokens, width), BF16),
            pltpu.VMEM((span_z, ny, tokens, width), BF16),
            pltpu.VMEM((rows, 2 * hidden), BF16),
            pltpu.VMEM((rows, 2 * hidden), BF16),
            pltpu.VMEM((rows, 2 * half), BF16),
            pltpu.VMEM((2 * part, 2 * hidden), F32),
            pltpu.VMEM((2 * part, 2 * hidden), F32),
            pltpu.VMEM((2 * half, width), F32),
            pltpu.VMEM((2, 2, nz // 2, part, half), BF16),
            pltpu.VMEM((2, 2, nz // 2, part, half), BF16),
            pltpu.VMEM((half, width), BF16),
            pltpu.VMEM((half, width), BF16),
            pltpu.VMEM((ny, 2, micro, tokens, block), BF16),
            pltpu.VMEM((ny, 2, micro, tokens, block), BF16),
            pltpu.VMEM((2, micro, tokens, qkv_width), BF16),
            pltpu.VMEM((2, micro, tokens, width), BF16),
            pltpu.VMEM((nz, padded, attn_width), BF16),
            pltpu.VMEM((max(1, ny - 1), nz, padded, attn_width), BF16),
            pltpu.VMEM((max(1, ny - 1), nz, padded, attn_width), BF16),
            pltpu.VMEM((max(1, nz - 1), padded, attn_width), BF16),
            pltpu.VMEM((2,) + small_shape, F32),
            pltpu.VMEM((max(1, ny - 1),) + small_shape, F32),
            pltpu.VMEM((max(1, nz - 1),) + small_shape, F32),
            DMA((2 * nz,)), DMA((2,)),
            DMA((4 * ny * micro + 4,)),
            DMA((ny + nz,)), DMA((ny + nz,)),
            DMA((3, nz)), DMA((3, nz)),
            DMA((2, nz + 1)), DMA((2, nz)),
            DMA((ny, nz)), DMA((ny, nz)),
            DMA((1, nz)), DMA((1, nz)),
        ]
        + gather_sems(2 * micro),
        compiler_params=pltpu.CompilerParams(
            collective_id=2, has_side_effects=True, vmem_limit_bytes=63 * 2**20
        ),
        name="weight_gradients",
    )(routes_all, small, gsmall, zf, zb, slices, partner, wd, xab, obb, dqkv, dattn, xap, obp, dqp, dtp)

    steps = 4
    finals = pl.pallas_call(
        functools.partial(finish_kernel, nz, total_experts),
        grid=(steps,),
        out_shape=(
            shape(1, 2, part, hidden, dtype=F32),
            shape(1, 2, part, hidden, dtype=F32),
            shape(1, 2, slice_h, width, dtype=F32),
            shape(1, shard, qkv_width, dtype=F32),
            shape(1, shard, width, dtype=F32),
            shape(1, shard, total_experts, dtype=F32),
            shape(1, shard, dtype=F32),
            shape(1, shard, dtype=F32),
        ),
        in_specs=[
            pl.BlockSpec((nz, part // steps, half), lambda i: (0, i, 0)),
            pl.BlockSpec((nz, part // steps, half), lambda i: (0, i, 0)),
            pl.BlockSpec((half // steps, width), lambda i: (i, 0)),
            pl.BlockSpec((padded, attn_width), lambda i: (0, 0)),
            pl.BlockSpec(small_shape, lambda i: (0, 0)),
        ],
        out_specs=(
            pl.BlockSpec((1, 2, part // steps, hidden), lambda i: (0, 0, i, 0)),
            pl.BlockSpec((1, 2, part // steps, hidden), lambda i: (0, 0, i, 0)),
            pl.BlockSpec((1, 1, half // steps, width), lambda i: (0, i // 2, i % 2, 0)),
            pl.BlockSpec((1, shard, qkv_width), lambda i: (0, 0, 0)),
            pl.BlockSpec((1, shard, width), lambda i: (0, 0, 0)),
            pl.BlockSpec((1, shard, total_experts), lambda i: (0, 0, 0)),
            pl.BlockSpec((1, shard), lambda i: (0, 0)),
            pl.BlockSpec((1, shard), lambda i: (0, 0)),
        ),
        compiler_params=pltpu.CompilerParams(vmem_limit_bytes=60 * 2**20),
        name="finish_gradients",
    )(gate_g, up_g, down_g, attn_g, small_g)
    grad_gate, grad_up, grad_down, grad_qkv, grad_out, grad_router, grad_again, grad_mgain = finals
    return (
        out[None, :, None],
        gin[None, :, None],
        grad_again,
        grad_qkv,
        grad_out,
        grad_mgain,
        grad_router,
        grad_gate,
        grad_up,
        grad_down,
    )


def solution(mesh):
    owners = ("expert", "dp")
    return jax.shard_map(
        functools.partial(per_device, mesh.shape["expert"], mesh.shape["dp"], mesh.shape["section"]),
        mesh=mesh,
        in_specs=(
            P(None, owners, None, None),
            P(None, owners, None, None),
            P(None, owners, None),
            P("section", None, owners, None, None),
            P("section", owners),
            P("section", owners, None),
            P("section", owners, None),
            P("section", owners),
            P("section", owners, None),
            P("section", "expert", None, None),
            P("section", "expert", None, None),
            P("section", "expert", None, None),
        ),
        out_specs=(
            P("section", None, owners, None, None),
            P("section", None, owners, None, None),
            P("section", owners),
            P("section", owners, None),
            P("section", owners, None),
            P("section", owners),
            P("section", owners, None),
            P("section", "expert", "dp", None),
            P("section", "expert", "dp", None),
            P("section", "expert", "dp", None),
        ),
        check_vma=False,
    )
```
